32 devices in a mesh: ctx: 16 (over z, y, x), fsdp: 2 (over core).
Axes of the slice: x: 2, y: 2, z: 4, core: 2. Of those that a mesh axis runs over, the one named last changes fastest.
Arguments:
- tokens: bfloat16 [2, 2048, 1600], P('fsdp', 'ctx'), may hold values from -6 to 6
- qkv_weight: bfloat16 [1600, 4800], P('ctx', 'fsdp'), may hold values from -0.15625 to 0.15625
- proj_weight: bfloat16 [1600, 1600], P('ctx', 'fsdp'), may hold values from -3 to 3
- fc_weight: bfloat16 [1600, 6400], P('ctx', 'fsdp'), may hold values from -0.15625 to 0.15625
- out_weight: bfloat16 [6400, 1600], P('ctx', 'fsdp'), may hold values from -0.078125 to 0.078125
- gains: bfloat16 [2, 1600], P('fsdp', 'ctx'), may hold values from 0.5 to 1.5
- biases: bfloat16 [6, 1600], P('fsdp', 'ctx'), may hold values from -0.119628906 to 0.119628906
- fc_bias: bfloat16 [6400], P(('ctx', 'fsdp')), may hold values from -3 to 3
- cotangent: bfloat16 [2, 2048, 1600], P('fsdp', 'ctx'), may hold values from -6 to 6
Outputs:
- mixed: bfloat16 [2, 2048, 1600], P('fsdp', 'ctx')
- input_grad: float32 [2, 2048, 1600], P('fsdp', 'ctx')
- qkv_weight_grad: float32 [1600, 4800], P('ctx', 'fsdp')
- proj_weight_grad: float32 [1600, 1600], P('ctx', 'fsdp')
- fc_weight_grad: float32 [1600, 6400], P('ctx', 'fsdp')
- out_weight_grad: float32 [6400, 1600], P('ctx', 'fsdp')
- gains_grad: float32 [2, 1600], P('fsdp', 'ctx')
- biases_grad: float32 [6, 1600], P('fsdp', 'ctx')
- fc_bias_grad: float32 [6400], P(('ctx', 'fsdp'))
The draws below stay inside these ranges and needn't reach their ends.
All inputs are finite; a program needn't handle non-finite values.
Results may differ from the reference program's by a relative error of at most 0.019.
Values may be sent and summed in bfloat16 or wider, within the bound.
A program may use at most 576 MiB of HBM per device.

```python
import math
import jax
import jax.numpy as jnp
from jax import lax

D = 1600
HEADS = 25
HEAD_DIM = 64
FF = 6400
SEQS = 2
LENGTH = 2048


def levels(rng, dims, shards, smallest, largest):
    level, own = 1.0, jax.random.fold_in(rng, 6)
    for dim, parts in shards:
        steps = jnp.exp(jax.random.uniform(jax.random.fold_in(own, dim), (parts,), jnp.float32, smallest / len(shards), largest / len(shards)))
        level = level * jnp.repeat(steps, dims[dim] // parts).reshape([-1 if axis == dim else 1 for axis in range(len(dims))])
    return level


def normal_values(rng, extent, scale, reach, pieces=(), kind=jnp.bfloat16):
    values = jax.random.normal(rng, extent, jnp.float32) * scale
    if len(pieces) > 0:
        values = levels(rng, extent, pieces, -0.22, 0.18) * values
    return jnp.clip(values, min=-reach, max=reach).astype(kind)


def setup_inputs(seed: int = 0) -> dict:
    streams_of = jax.random.split(jax.random.key(seed), 10)
    return {
        "tokens": normal_values(streams_of[0], (SEQS, LENGTH, D), 1.0, 6.0, ((0, 2), (1, 16))),
        "qkv_weight": normal_values(streams_of[1], (D, 3 * D), D ** -0.5, 0.15625, ((0, 16), (1, 2))),
        "proj_weight": normal_values(streams_of[2], (D, D), 4 ** -0.5, 3.0, ((0, 16), (1, 2))),
        "fc_weight": normal_values(streams_of[3], (D, FF), D ** -0.5, 0.15625, ((0, 16), (1, 2))),
        "out_weight": normal_values(streams_of[4], (FF, D), FF ** -0.5, 0.078125, ((0, 16), (1, 2))),
        "gains": jnp.clip(1.0 + 0.1 * jax.random.normal(streams_of[5], (2, D), jnp.float32), 0.5, 1.5).astype(jnp.bfloat16),
        "biases": normal_values(streams_of[6], (6, D), 0.02, 0.119628906, ((0, 2), (1, 16))),
        "fc_bias": normal_values(streams_of[7], (FF,), 0.5, 3.0, ((0, 32),)),
        "cotangent": normal_values(streams_of[8], (SEQS, LENGTH, D), 1.0, 6.0, ((0, 2), (1, 16))),
    }


EPS = 1e-05
PRECISE = lax.Precision.HIGHEST

@jax.custom_vjp
def low(v):
    return lax.optimization_barrier(v.astype(jnp.bfloat16)).astype(jnp.float32)

@jax.custom_vjp
def low_back(v):
    return v

def low_keep(v):
    return (low(v), None)

def low_pass(kept, grad):
    return (grad,)

def back_keep(v):
    return (v, None)

def back_low(kept, grad):
    return (low(grad),)
low.defvjp(low_keep, low_pass)
low_back.defvjp(back_keep, back_low)

def layer_norm(values, gain, bias):
    centre = values - lax.optimization_barrier(jnp.mean(values, axis=-1, keepdims=True))
    spread = lax.rsqrt(lax.optimization_barrier(jnp.mean(centre * centre, axis=-1, keepdims=True)) + EPS)
    return centre * spread * gain + bias

def attention(queries, keys, values):
    length = queries.shape[0]
    block = min(512, length)
    scale = 1.0 / math.sqrt(HEAD_DIM)
    query_heads = queries.reshape(length, HEADS, HEAD_DIM)
    key_heads = keys.reshape(length, HEADS, HEAD_DIM)
    value_heads = values.reshape(length, HEADS, HEAD_DIM)
    key_pos = jnp.arange(length, dtype=jnp.int32)

    def one_block(start):
        query_block = lax.dynamic_slice_in_dim(query_heads, start, block, 0)
        scores = low_back(jnp.einsum('qhd,khd->hqk', query_block, key_heads, precision=PRECISE) * scale)
        query_pos = start + jnp.arange(block, dtype=jnp.int32)
        visible = key_pos[None, :] <= query_pos[:, None]
        scores = jnp.where(visible[None], scores, -1e+30)
        shifted = jnp.exp(scores - lax.optimization_barrier(jnp.max(scores, axis=-1, keepdims=True)))
        probs = shifted / lax.optimization_barrier(jnp.sum(shifted, axis=-1, keepdims=True))
        out_heads = jnp.einsum('hqk,khd->qhd', low(probs), value_heads, precision=PRECISE)
        return out_heads.reshape(block, HEADS * HEAD_DIM)
    starts = jnp.arange(length // block, dtype=jnp.int32) * block
    return lax.map(jax.checkpoint(one_block), starts).reshape(length, HEADS * HEAD_DIM)

def forward(tokens, qkv_weight, proj_weight, fc_weight, out_weight, gains, biases, fc_bias):
    seq_count, length, width = tokens.shape
    flat_rows = tokens.reshape(seq_count * length, width)
    normed_one = low(layer_norm(flat_rows, gains[0], biases[0]))
    projected = jnp.dot(normed_one, qkv_weight, precision=PRECISE)
    queries = low(low_back(projected[:, :width] + biases[1]))
    keys = low(low_back(projected[:, width:2 * width]))
    values = low(low_back(projected[:, 2 * width:] + biases[2]))
    mixed_parts = []
    for member in range(seq_count):
        lower = member * length
        upper = lower + length
        mixed_parts.append(attention(queries[lower:upper], keys[lower:upper], values[lower:upper]))
    attended = low(low_back(jnp.concatenate(mixed_parts, axis=0)))
    branch = low_back(jnp.dot(attended, proj_weight, precision=PRECISE) + biases[3])
    middle = flat_rows + branch
    normed_two = low(layer_norm(middle, gains[1], biases[4]))
    hidden_pre = low_back(jnp.dot(normed_two, fc_weight, precision=PRECISE) + fc_bias)
    hidden = low(jax.nn.gelu(hidden_pre, approximate=True))
    output = low_back(jnp.dot(hidden, out_weight, precision=PRECISE) + biases[5])
    return (middle + output).reshape(seq_count, length, width)

def reference(tokens, qkv_weight, proj_weight, fc_weight, out_weight, gains, biases, fc_bias, cotangent):
    result, pull_back = jax.vjp(forward, tokens.astype(jnp.float32), qkv_weight.astype(jnp.float32), proj_weight.astype(jnp.float32), fc_weight.astype(jnp.float32), out_weight.astype(jnp.float32), gains.astype(jnp.float32), biases.astype(jnp.float32), fc_bias.astype(jnp.float32))
    grads = pull_back(cotangent.astype(jnp.float32))
    return (result.astype(jnp.bfloat16), grads[0], grads[1], grads[2], grads[3], grads[4], grads[5], grads[6], grads[7])
```

```python
import functools
import math

import jax
import jax.numpy as jnp
from jax import lax
from jax.experimental import pallas as pl
from jax.experimental.pallas import tpu as pltpu
from jax.sharding import PartitionSpec as P

D = 1600
HEADS = 25
HEAD_DIM = 64
FF = 6400
EPS = 1e-05
UNITS = 8
HU = -(-HEADS // UNITS)
QKV = 3 * HEAD_DIM
TP_BITS = (1, 4)
MESH = pl.DeviceIdType.MESH
BF = jnp.bfloat16
F32 = jnp.float32
VMEM_LIMIT = 56 * 1024 * 1024
LOG2E = 1.0 / math.log(2.0)


class Layout:
    def __init__(self, n_ctx):
        self.n_ctx = n_ctx
        self.tp_bits = TP_BITS
        bits = [1 << i for i in range(n_ctx.bit_length() - 1)]
        self.dp_bits = tuple(b for b in bits if b not in TP_BITS)[::-1]
        self.n_dp = n_ctx // 4
        self.dp_order = [(b, b) for b in self.dp_bits]
        a, b = TP_BITS
        self.tp_order = [(a, b), (b, a)]
        self.tp_masks = [[], [(a, a)], [(b, b)], [(a, a), (b, b)]]

    def tp_index(self, c):
        return sum(((c // b) % 2) * (1 << i) for i, b in enumerate(self.tp_bits))

    def dp_index(self, c):
        return sum(((c // b) % 2) * (1 << i) for i, b in enumerate(self.dp_bits))

    def compose(self, t, d):
        return sum(((t // (1 << i)) % 2) * b for i, b in enumerate(self.tp_bits)) + sum(
            ((d // (1 << i)) % 2) * b for i, b in enumerate(self.dp_bits)
        )

    def head_rank(self, h):
        u, j = h // HU, h % HU
        return self.compose(u // 2, j) * 2 + u % 2

    def to_natural(self, x):
        labels = list(self.dp_bits[::-1]) + list(self.tp_bits[::-1])
        k = len(labels)
        rest = x.shape[2:]
        x = x.reshape((2,) * k + rest)
        order = sorted(range(k), key=lambda i: -labels[i])
        x = jnp.transpose(x, order + list(range(k, k + len(rest))))
        return x.reshape((self.n_ctx,) + rest)

    def from_natural(self, x):
        labels = list(self.dp_bits[::-1]) + list(self.tp_bits[::-1])
        k = len(labels)
        rest = x.shape[1:]
        x = x.reshape((2,) * k + rest)
        natural = sorted(labels, reverse=True)
        order = [natural.index(b) for b in labels]
        x = jnp.transpose(x, order + list(range(k, k + len(rest))))
        return x.reshape((self.n_dp, 4) + rest)


def flip(c, sym, s):
    def one(b):
        return c + b * (1 - 2 * ((c // b) % 2))

    if sym[0] == sym[1]:
        return one(sym[0])
    return one(sym[0]) * (1 - s) + one(sym[1]) * s


def flips(c, masks, s):
    for sym in masks:
        c = flip(c, sym, s)
    return c


class Env:
    def __init__(self, layout):
        self.lay = layout
        self.c = lax.axis_index("ctx")
        self.s = lax.axis_index("fsdp")
        self.t = layout.tp_index(self.c)
        self.d = layout.dp_index(self.c)
        self.rank = self.c * 2 + self.s
        self.n_dev = layout.n_ctx * 2

    def other(self):
        return (self.c, 1 - self.s)


class Links:
    def __init__(self, sems):
        self.send_sems, self.recv_sems, self.local_sems = sems
        self.count = 0
        self.local_count = 0
        self.sent = []
        self.locals = []

    def send(self, src, dst, device):
        copy = pltpu.make_async_remote_copy(
            src_ref=src,
            dst_ref=dst,
            send_sem=self.send_sems.at[self.count],
            recv_sem=self.recv_sems.at[self.count],
            device_id=device,
            device_id_type=MESH,
        )
        copy.start()
        self.count += 1
        self.sent.append(copy)
        return copy

    def local(self, src, dst):
        copy = pltpu.make_async_copy(src, dst, self.local_sems.at[self.local_count])
        copy.start()
        self.local_count += 1
        self.locals.append(copy)
        return copy

    def finish(self):
        for copy in self.locals:
            copy.wait()
        for copy in self.sent:
            copy.wait_send()


def sem_shapes(sends, local=1):
    sends = max(sends, 1)
    return [
        pltpu.SemaphoreType.DMA((sends,)),
        pltpu.SemaphoreType.DMA((sends,)),
        pltpu.SemaphoreType.DMA((local,)),
    ]


def meet(env, devices):
    barrier = pltpu.get_barrier_semaphore()
    for device in devices:
        pl.semaphore_signal(barrier, inc=1, device_id=device, device_id_type=MESH)
    pl.semaphore_wait(barrier, len(devices))


def meet_all(env):
    barrier = pltpu.get_barrier_semaphore()

    def hail(i, carry):
        rank = (env.rank + i) % env.n_dev
        pl.semaphore_signal(barrier, inc=1, device_id=(rank // 2, rank % 2), device_id_type=MESH)
        return carry

    lax.fori_loop(1, env.n_dev, hail, 0)
    pl.semaphore_wait(barrier, env.n_dev - 1)


def tp_partners(env):
    return [(flips(env.c, m, env.s), env.s) for m in env.lay.tp_masks[1:]]


def dp_partners(env):
    return [(flip(env.c, sym, env.s), env.s) for sym in env.lay.dp_order]


def run(generators):
    active = list(generators)
    while active:
        left = []
        for g in active:
            try:
                next(g)
                left.append(g)
            except StopIteration:
                pass
        active = left


def gather_sends(have, bits, core, rows):
    return (3 if rows else 0) + have * ((1 << bits) - 1) + (have << bits if core else 0)


def gather(env, src, buf, sems, bits, slot, core=False, rows=False):
    c, s = env.c, env.s
    links = Links(sems)

    def place(masks):
        index = slot(flips(c, masks, s))
        return buf.at[s, index] if core else buf.at[index]

    own = src.at[env.t] if rows else src
    links.local(own, place([]))
    levels = [[([], None)]] + [[] for _ in bits]
    if rows:
        for m in env.lay.tp_masks[1:]:
            there = flips(c, m, s)
            copy = links.send(src.at[env.lay.tp_index(there)], place([]), (there, s))
            levels[0].append((m, copy))
    crossing = []
    for k in range(len(bits) + 1):
        for masks, copy in levels[k]:
            if copy is None:
                ref = own
            else:
                copy.wait_recv()
                ref = place(masks)
            for j in range(k, len(bits)):
                forward = links.send(ref, place(masks), (flip(c, bits[j], s), s))
                levels[j + 1].append((masks + [bits[j]], forward))
            if core:
                crossing.append(links.send(ref, place(masks), env.other()))
            yield
    for copy in crossing:
        copy.wait_recv()
    links.finish()
    yield


def reduce_sends(have, bits, core, rows, halves):
    return (have << bits if core else 0) + have * ((1 << bits) - 1) + (3 + 4 if rows else 0) + (1 if halves else 0)


def reduce_scratch(have, bits, core, block):
    counts = [have << j for j in range(bits + (1 if core else 0))]
    return [pltpu.VMEM((n,) + block, BF) for n in counts]


def reduce(env, inp, out, parts, sems, bits, slot, core=False, rows=False, halves=False):
    c, s = env.c, env.s
    links = Links(sems)
    levels = [list(env.lay.tp_masks) if rows else [[]]]
    for sym in bits:
        levels.append(levels[-1] + [m + [sym] for m in levels[-1]])

    def at(side, masks):
        index = slot(flips(c, masks, side))
        return inp.at[side, index] if core else inp.at[index]

    last = levels[-1]
    now = [at(s, m) for m in last]
    copies = {}
    if core:
        stage = len(bits)
        for i in reversed(range(len(last))):
            copies[i] = links.send(at(1 - s, last[i]), parts[stage].at[i], env.other())
    else:
        stage = len(bits) - 1
        n = len(levels[stage])
        for i in reversed(range(n)):
            copies[i] = links.send(now[n + i], parts[stage].at[i], (flip(c, bits[stage], s), s))
    yield
    while stage >= 0:
        n = len(levels[stage])
        got = parts[stage]
        after = {}
        for i in reversed(range(n)):
            copies[i].wait_recv()
            got[i] = got[i] + now[i][...]
            if stage > 0 and i >= n // 2:
                after[i - n // 2] = links.send(
                    got.at[i], parts[stage - 1].at[i - n // 2], (flip(c, bits[stage - 1], s), s)
                )
            yield
        now = [got.at[i] for i in range(n)]
        copies = after
        stage -= 1
    if rows:
        arrivals = []
        links.local(now[0], out.at[s, env.t])
        arrivals.append((env.t, None, now[0]))
        for i, m in enumerate(env.lay.tp_masks):
            if i > 0:
                there = flips(c, m, s)
                copy = links.send(now[i], out.at[s, env.t], (there, s))
                index = env.lay.tp_index(there)
                arrivals.append((index, copy, out.at[s, index]))
        yield
        crossing = []
        for index, copy, ref in arrivals:
            if copy is not None:
                copy.wait_recv()
            crossing.append(links.send(ref, out.at[s, index], env.other()))
            yield
        for copy in crossing:
            copy.wait_recv()
    elif halves:
        links.local(now[0], out.at[s])
        copy = links.send(now[0], out.at[s], env.other())
        yield
        copy.wait_recv()
    else:
        out[...] = now[0][...]
    links.finish()
    yield


def to_everyone(env, src, out, sems, same):
    send_sems, recv_sems, local_sems = sems

    def own(ref):
        return ref if same else ref.at[env.rank]

    def copy(i):
        rank = (env.rank + i) % env.n_dev
        return pltpu.make_async_remote_copy(
            src_ref=src if same else src.at[rank],
            dst_ref=out.at[env.rank],
            send_sem=send_sems.at[i],
            recv_sem=recv_sems.at[i],
            device_id=(rank // 2, rank % 2),
            device_id_type=MESH,
        )

    def begin(i, carry):
        copy(i).start()
        return carry

    def end(i, carry):
        copy(i).wait()
        return carry

    lax.fori_loop(1, env.n_dev, begin, 0)
    local = pltpu.make_async_copy(own(src), out.at[env.rank], local_sems.at[0])
    local.start()
    yield
    lax.fori_loop(1, env.n_dev, end, 0)
    local.wait()
    yield


def own_head(env):
    h = (env.t * 2 + env.s) * HU + env.d
    return h, jnp.logical_and(env.d < HU, h < HEADS)


def heads_to_tokens(env, src, out, sems):
    send_sems, recv_sems, local_sems = sems
    h, active = own_head(env)
    lay = env.lay

    def copy(i):
        rank = (env.rank + i) % env.n_dev
        return pltpu.make_async_remote_copy(
            src_ref=src.at[rank % 2, rank // 2],
            dst_ref=out.at[h],
            send_sem=send_sems.at[i],
            recv_sem=recv_sems.at[h],
            device_id=(rank // 2, rank % 2),
            device_id_type=MESH,
        )

    @pl.when(active)
    def _():
        def begin(i, carry):
            copy(i).start()
            return carry

        lax.fori_loop(1, env.n_dev, begin, 0)
        local = pltpu.make_async_copy(src.at[env.s, env.c], out.at[h], local_sems.at[0])
        local.start()
        local.wait()

    def receive(j, carry):
        @pl.when(lay.head_rank(j) != env.rank)
        def _():
            pltpu.make_async_remote_copy(
                src_ref=src.at[0, 0],
                dst_ref=out.at[j],
                send_sem=send_sems.at[0],
                recv_sem=recv_sems.at[j],
                device_id=env.other(),
                device_id_type=MESH,
            ).wait_recv()

        return carry

    lax.fori_loop(0, HEADS, receive, 0)

    @pl.when(active)
    def _():
        def end(i, carry):
            copy(i).wait_send()
            return carry

        lax.fori_loop(1, env.n_dev, end, 0)


def tokens_to_heads(env, src, out, sems):
    send_sems, recv_sems, local_sems = sems
    h, active = own_head(env)
    lay = env.lay

    def copy(j):
        rank = lay.head_rank(j)
        return rank, pltpu.make_async_remote_copy(
            src_ref=src.at[j],
            dst_ref=out.at[env.s, env.c],
            send_sem=send_sems.at[j],
            recv_sem=recv_sems.at[(rank - env.rank + env.n_dev) % env.n_dev],
            device_id=(rank // 2, rank % 2),
            device_id_type=MESH,
        )

    def begin(i, carry):
        rank, cp = copy((env.rank + i) % HEADS)

        @pl.when(rank != env.rank)
        def _():
            cp.start()

        return carry

    lax.fori_loop(0, HEADS, begin, 0)

    @pl.when(active)
    def _():
        local = pltpu.make_async_copy(src.at[h], out.at[env.s, env.c], local_sems.at[0])
        local.start()
        local.wait()

        def receive(i, carry):
            rank = (env.rank - i + env.n_dev) % env.n_dev
            pltpu.make_async_remote_copy(
                src_ref=src.at[0],
                dst_ref=out.at[rank % 2, rank // 2],
                send_sem=send_sems.at[0],
                recv_sem=recv_sems.at[i],
                device_id=env.other(),
                device_id_type=MESH,
            ).wait_recv()
            return carry

        lax.fori_loop(1, env.n_dev, receive, 0)

    def end(j, carry):
        rank, cp = copy(j)

        @pl.when(rank != env.rank)
        def _():
            cp.wait_send()

        return carry

    lax.fori_loop(0, HEADS, end, 0)


def data_partners(env):
    lay = env.lay
    return [(lay.compose(env.t, (env.d + i) % lay.n_dp), env.s) for i in range(1, lay.n_dp)]


def group_to_heads(env, src, out, sems):
    send_sems, recv_sems, local_sems = sems
    lay = env.lay

    def copy(j, source, target):
        return pltpu.make_async_remote_copy(
            src_ref=src.at[j],
            dst_ref=out.at[source],
            send_sem=send_sems.at[j],
            recv_sem=recv_sems.at[source],
            device_id=(lay.compose(env.t, target), env.s),
            device_id_type=MESH,
        )

    for i in range(1, HU + 1):
        j = (env.d + i) % HU

        @pl.when(j != env.d)
        def _():
            copy(j, env.d, j).start()

    @pl.when(env.d < HU)
    def _():
        local = pltpu.make_async_copy(src.at[env.d], out.at[env.d], local_sems.at[0])
        local.start()
        local.wait()
        for i in range(1, lay.n_dp):
            source = (env.d + i) % lay.n_dp
            copy(0, source, source).wait_recv()

    for j in range(HU):

        @pl.when(j != env.d)
        def _():
            copy(j, env.d, j).wait_send()


def heads_to_group(env, src, out, sems):
    send_sems, recv_sems, local_sems = sems
    lay = env.lay

    def copy(there, j, target):
        return pltpu.make_async_remote_copy(
            src_ref=src.at[there],
            dst_ref=out.at[j],
            send_sem=send_sems.at[there],
            recv_sem=recv_sems.at[j],
            device_id=(lay.compose(env.t, target), env.s),
            device_id_type=MESH,
        )

    @pl.when(env.d < HU)
    def _():
        for i in range(1, lay.n_dp):
            there = (env.d + i) % lay.n_dp
            copy(there, env.d, there).start()
        local = pltpu.make_async_copy(src.at[env.d], out.at[env.d], local_sems.at[0])
        local.start()
        local.wait()

    for j in range(HU):

        @pl.when(j != env.d)
        def _():
            copy(0, j, j).wait_recv()

    @pl.when(env.d < HU)
    def _():
        for i in range(1, lay.n_dp):
            there = (env.d + i) % lay.n_dp
            copy(there, env.d, there).wait_send()


ANY = pl.BlockSpec(memory_space=pl.ANY)
VM = pl.BlockSpec(memory_space=pltpu.VMEM)


def struct(*shape, dtype=BF):
    return jax.ShapeDtypeStruct(shape, dtype)


def call(name, cid, body, args, in_specs, outs, out_specs, scratch):
    return pl.pallas_call(
        body,
        out_shape=outs,
        in_specs=in_specs,
        out_specs=out_specs,
        scratch_shapes=scratch,
        compiler_params=pltpu.CompilerParams(
            collective_id=cid, has_side_effects=True, vmem_limit_bytes=VMEM_LIMIT
        ),
        name=name,
    )(*args)


def exchange_start(lay, small, qkv, fc, out):
    def body(small_r, qkv_r, fc_r, out_r, small_o, qkv_o, fc_o, out_o, *sems):
        env = Env(lay)
        meet_all(env)
        links = Links((sems[0], sems[1], sems[2]))
        copies = [
            links.send(a, b, env.other()) for a, b in ((qkv_r, qkv_o), (fc_r, fc_o), (out_r, out_o))
        ]
        run([to_everyone(env, small_r, small_o, sems[3:6], True)])
        for copy in copies:
            copy.wait_recv()
        links.finish()

    n_dev = lay.n_ctx * 2
    return call(
        "exchange_start",
        0,
        body,
        (small, qkv, fc, out),
        [ANY] * 4,
        [struct(n_dev, *small.shape), struct(*qkv.shape), struct(*fc.shape), struct(*out.shape)],
        [ANY] * 4,
        sem_shapes(3) + sem_shapes(n_dev),
    )


def gather_weights(lay, qkv, fc, out, proj, h1, dy):
    n_ctx, n_dp = lay.n_ctx, lay.n_dp
    k = len(lay.dp_bits)

    def natural(c):
        return c

    def body(qkv_r, fc_r, out_r, proj_r, h1_r, dy_r, qkv_o, fc_o, out_o, proj_o, h1_o, dy_o, *sems):
        env = Env(lay)
        meet(env, tp_partners(env) + dp_partners(env) + [env.other()])
        groups = [sems[3 * i : 3 * i + 3] for i in range(6)]
        run(
            [
                gather(env, qkv_r, qkv_o, groups[0], lay.dp_order, natural, rows=True),
                gather(env, h1_r, h1_o, groups[4], lay.tp_order, lay.tp_index, core=True),
                gather(env, proj_r, proj_o, groups[3], lay.dp_order + lay.tp_order, natural, core=True),
                gather(env, fc_r, fc_o, groups[1], lay.dp_order, natural, rows=True),
                gather(env, out_r, out_o, groups[2], lay.dp_order, lay.dp_index),
                gather(env, dy_r, dy_o, groups[5], lay.tp_order, lay.tp_index, core=True),
            ]
        )

    outs = [
        struct(n_ctx, *qkv.shape[1:]),
        struct(n_ctx, *fc.shape[1:]),
        struct(n_dp, *out.shape),
        struct(2, n_ctx, *proj.shape),
        struct(2, 4, *h1.shape),
        struct(2, 4, *dy.shape),
    ]
    scratch = (
        sem_shapes(gather_sends(4, k, False, True)) * 2
        + sem_shapes(gather_sends(1, k, False, False))
        + sem_shapes(gather_sends(1, k + 2, True, False))
        + sem_shapes(gather_sends(1, 2, True, False)) * 2
    )
    return call(
        "gather_weights", 1, body, (qkv, fc, out, proj, h1, dy), [ANY] * 6, outs, [ANY] * 6, scratch
    )


def gather_rows(lay, h2):
    def body(h2_r, h2_o, *sems):
        env = Env(lay)
        meet(env, tp_partners(env) + [env.other()])
        run([gather(env, h2_r, h2_o, sems, lay.tp_order, lay.tp_index, core=True)])

    return call(
        "gather_rows",
        2,
        body,
        (h2,),
        [ANY],
        struct(2, 4, *h2.shape),
        ANY,
        sem_shapes(gather_sends(1, 2, True, False)),
    )


def reduce_rows(lay, first, second):
    block = first.shape[2:]

    def body(a_r, b_r, a_o, b_o, *rest):
        env = Env(lay)
        meet(env, tp_partners(env) + [env.other()])
        run(
            [
                reduce(env, a_r, a_o, rest[0:3], rest[6:9], lay.tp_order, lay.tp_index, core=True),
                reduce(env, b_r, b_o, rest[3:6], rest[9:12], lay.tp_order, lay.tp_index, core=True),
            ]
        )

    return call(
        "reduce_rows",
        3,
        body,
        (first, second),
        [VM] * 2,
        [struct(*block)] * 2,
        [VM] * 2,
        reduce_scratch(1, 2, True, block) * 2 + sem_shapes(reduce_sends(1, 2, True, False, False)) * 2,
    )


def exchange(lay, name, cid, op, partners, src, out, counts):
    def body(src_r, out_r, *sems):
        env = Env(lay)
        if partners is None:
            meet_all(env)
        else:
            meet(env, partners(env))
        op(env, src_r, out_r, sems)

    scratch = [
        pltpu.SemaphoreType.DMA((counts[0],)),
        pltpu.SemaphoreType.DMA((counts[1],)),
        pltpu.SemaphoreType.DMA((1,)),
    ]
    return call(name, cid, body, (src,), [ANY], out, ANY, scratch)


def reduce_grads(lay, rows, qkv, fc, out, proj, small):
    n_ctx = lay.n_ctx
    k = len(lay.dp_bits)
    n_dev = 2 * n_ctx

    def natural(c):
        return c

    plan = [
        (rows.shape[2:], 1, 2, True, False, False),
        (qkv.shape[1:], 4, k, False, True, False),
        (fc.shape[1:], 4, k, False, True, False),
        (out.shape[1:], 1, k, False, False, True),
        (proj.shape[2:], 1, k + 2, True, False, False),
    ]
    scratch, spans = [], []
    for block, have, bits, core, is_rows, halves in plan:
        part = reduce_scratch(have, bits, core, block)
        sems = sem_shapes(reduce_sends(have, bits, core, is_rows, halves))
        spans.append((len(scratch), len(part)))
        scratch = scratch + part + sems
    scratch = scratch + sem_shapes(n_dev)

    def body(rows_r, qkv_r, fc_r, out_r, proj_r, small_r, rows_o, qkv_o, fc_o, out_o, proj_o, small_o, *rest):
        env = Env(lay)
        meet_all(env)

        def space(i):
            first, n = spans[i]
            return rest[first : first + n], rest[first + n : first + n + 3]

        run(
            [
                to_everyone(env, small_r, small_o, rest[-3:], False),
                reduce(env, qkv_r, qkv_o, *space(1), lay.dp_order, natural, rows=True),
                reduce(env, rows_r, rows_o, *space(0), lay.tp_order, lay.tp_index, core=True),
                reduce(env, proj_r, proj_o, *space(4), lay.dp_order + lay.tp_order, natural, core=True),
                reduce(env, fc_r, fc_o, *space(2), lay.dp_order, natural, rows=True),
                reduce(env, out_r, out_o, *space(3), lay.dp_order, lay.dp_index, halves=True),
            ]
        )

    outs = [
        struct(*rows.shape[2:]),
        struct(2, 4, *qkv.shape[1:]),
        struct(2, 4, *fc.shape[1:]),
        struct(2, *out.shape[1:]),
        struct(*proj.shape[2:]),
        struct(*small.shape, dtype=F32),
    ]
    return call(
        "reduce_grads",
        8,
        body,
        (rows, qkv, fc, out, proj, small),
        [VM] * 5 + [ANY],
        outs,
        [VM, ANY, ANY, ANY, VM, ANY],
        scratch,
    )


def dot(left, right, dims):
    return lax.dot_general(left, right, (dims, ((), ())), preferred_element_type=F32)


NN = ((1,), (0,))
NT = ((1,), (1,))
TN = ((0,), (0,))
SCALE = 1.0 / math.sqrt(HEAD_DIM)
TILE = 512


def attend(lay, q, k, v, rows):
    length = q.shape[2]
    tile = min(TILE, length)
    n = length // tile
    per = tile // rows

    def body(q_ref, k_ref, v_ref, o_ref, low_ref, lse_ref, keys):
        i = pl.program_id(1)

        @pl.when(i == 0)
        def _():
            keys[...] = k_ref[0].T

        qt = q_ref[0]

        def step(j, carry, masked):
            peak, total, acc = carry
            first = pl.multiple_of(j * tile, tile)
            st = dot(keys[pl.ds(first, tile), :], qt, NN) * (SCALE * LOG2E)
            if masked:
                row = lax.broadcasted_iota(jnp.int32, (tile, tile), 0)
                col = lax.broadcasted_iota(jnp.int32, (tile, tile), 1)
                st = jnp.where(row <= col, st, -1e30)
            new = jnp.maximum(peak, jnp.max(st, axis=0, keepdims=True))
            p = jnp.exp2(st - new)
            shrink = jnp.exp2(peak - new)
            total = total * shrink + jnp.sum(p, axis=0, keepdims=True)
            acc = acc * shrink + dot(v_ref[0, :, pl.ds(first, tile)], p.astype(BF), NN)
            return new, total, acc

        start = (
            jnp.full((1, tile), -1e30, F32),
            jnp.zeros((1, tile), F32),
            jnp.zeros((HEAD_DIM, tile), F32),
        )
        carry = lax.fori_loop(0, i, functools.partial(step, masked=False), start)
        peak, total, acc = step(i, carry, True)
        o = acc / total
        o_ref[0] = o
        low = o.astype(BF)
        for b in range(per):
            low_ref[0, b] = low[:, b * rows : (b + 1) * rows]
        lse_ref[0] = peak + jnp.log2(total)

    whole = pl.BlockSpec((1, HEAD_DIM, length), lambda b, i: (b, 0, 0))
    tiled = pl.BlockSpec((1, HEAD_DIM, tile), lambda b, i: (b, 0, i))
    return pl.pallas_call(
        body,
        grid=(2, n),
        in_specs=[tiled, whole, whole],
        out_specs=[
            tiled,
            pl.BlockSpec((1, per, HEAD_DIM, rows), lambda b, i: (b, i, 0, 0)),
            pl.BlockSpec((1, 1, tile), lambda b, i: (b, 0, i)),
        ],
        out_shape=[
            struct(2, HEAD_DIM, length, dtype=F32),
            struct(2, length // rows, HEAD_DIM, rows),
            struct(2, 1, length, dtype=F32),
        ],
        scratch_shapes=[pltpu.VMEM((length, HEAD_DIM), BF)],
        compiler_params=pltpu.CompilerParams(vmem_limit_bytes=VMEM_LIMIT),
        name="attend",
    )(q, k, v)


def attend_back(lay, q, k, v, o, lse, dob):
    length = q.shape[2]
    tile = min(TILE, length)
    n = length // tile

    def body(q_ref, k_ref, v_ref, o_ref, lse_ref, dob_ref, dq_ref, dk_ref, dv_ref, qs, dobs, delta, dq_acc):
        j = pl.program_id(1)

        @pl.when(j == 0)
        def _():
            qs[...] = q_ref[0].T
            dobs[...] = dob_ref[0].T
            delta[...] = jnp.sum(dob_ref[0].astype(F32) * o_ref[0], axis=0, keepdims=True)
            dq_acc[...] = jnp.zeros_like(dq_acc)

        kt = k_ref[0]
        keys = kt.T
        values = v_ref[0].T

        def step(i, carry, masked):
            dk, dv = carry
            at = pl.ds(pl.multiple_of(i * tile, tile), tile)
            st = dot(keys, q_ref[0, :, at], NN) * (SCALE * LOG2E)
            p = jnp.exp2(st - lse_ref[0, :, at])
            if masked:
                row = lax.broadcasted_iota(jnp.int32, (tile, tile), 0)
                col = lax.broadcasted_iota(jnp.int32, (tile, tile), 1)
                p = jnp.where(row <= col, p, 0.0)
            dp = dot(values, dob_ref[0, :, at], NN)
            ds = (p * (dp - delta[:, at])).astype(BF)
            dv = dv + dot(p.astype(BF), dobs[at, :], NN)
            dk = dk + dot(ds, qs[at, :], NN)
            dq_acc[:, at] += dot(kt, ds, NN)
            return dk, dv

        zero = jnp.zeros((tile, HEAD_DIM), F32)
        carry = step(j, (zero, zero), True)
        dk, dv = lax.fori_loop(j + 1, n, functools.partial(step, masked=False), carry)
        dk_ref[0] = (dk * SCALE).T.astype(BF)
        dv_ref[0] = dv.T.astype(BF)

        @pl.when(j == n - 1)
        def _():
            dq_ref[0] = (dq_acc[...] * SCALE).astype(BF)

    whole = pl.BlockSpec((1, HEAD_DIM, length), lambda b, i: (b, 0, 0))
    tiled = pl.BlockSpec((1, HEAD_DIM, tile), lambda b, i: (b, 0, i))
    line = pl.BlockSpec((1, 1, length), lambda b, i: (b, 0, 0))
    return pl.pallas_call(
        body,
        grid=(2, n),
        in_specs=[whole, tiled, tiled, whole, line, whole],
        out_specs=[whole, tiled, tiled],
        out_shape=[struct(2, HEAD_DIM, length)] * 3,
        scratch_shapes=[
            pltpu.VMEM((length, HEAD_DIM), BF),
            pltpu.VMEM((length, HEAD_DIM), BF),
            pltpu.VMEM((1, length), F32),
            pltpu.VMEM((HEAD_DIM, length), F32),
        ],
        compiler_params=pltpu.CompilerParams(vmem_limit_bytes=VMEM_LIMIT),
        name="attend_back",
    )(q, k, v, o, lse, dob)


def norm_forward(values, gain, bias):
    centre = values - jnp.mean(values, axis=-1, keepdims=True)
    spread = lax.rsqrt(jnp.mean(centre * centre, axis=-1, keepdims=True) + EPS)
    normed = centre * spread
    return (normed * gain + bias, normed, spread)


def norm_back(grad_out, normed, spread, gain):
    scaled = grad_out * gain
    grad_in = spread * (
        scaled
        - jnp.mean(scaled, axis=-1, keepdims=True)
        - normed * jnp.mean(scaled * normed, axis=-1, keepdims=True)
    )
    return (grad_in, jnp.sum(grad_out * normed, axis=0), jnp.sum(grad_out, axis=0))


def gelu_tanh(values):
    return jax.nn.gelu(values, approximate=True)


def pad_to(x, axis, size):
    if x.shape[axis] == size:
        return x
    widths = [(0, 0)] * x.ndim
    widths[axis] = (0, size - x.shape[axis])
    return jnp.pad(x, widths)


def shards(lay, tokens, qkv_weight, proj_weight, fc_weight, out_weight, gains, biases, fc_bias, cotangent):
    n_ctx, n_dp = lay.n_ctx, lay.n_dp
    c = lax.axis_index("ctx")
    s = lax.axis_index("fsdp")
    t = lay.tp_index(c)
    unit = 2 * t + s
    T = tokens.shape[1]
    M = 8 * T
    R = D // n_ctx
    FB = FF // n_ctx
    FH = FB // 2
    W = HU * HEAD_DIM
    length = n_ctx * T

    def both(own, other, axis):
        return jnp.where(
            s == 0, jnp.concatenate([own, other], axis), jnp.concatenate([other, own], axis)
        )

    def side(x, axis):
        return lax.dynamic_index_in_dim(x, s, axis, keepdims=False)

    x = tokens.reshape(T, D).astype(F32)
    dy = cotangent.reshape(T, D)

    small = jnp.concatenate([gains.reshape(-1), biases.reshape(-1), fc_bias])
    small = pad_to(small, 0, 2048).reshape(16, 128)
    small_all, qkv_other, fc_other, out_other = exchange_start(
        lay, small, qkv_weight, fc_weight, out_weight
    )
    small_all = small_all.reshape(n_ctx, 2, 2048)
    gain_rows = jnp.transpose(small_all[:, :, :R], (1, 0, 2)).reshape(2, D).astype(F32)
    bias_rows = (
        jnp.transpose(small_all[:, :, R : 4 * R].reshape(n_ctx, 2, 3, R), (1, 2, 0, 3))
        .reshape(6, D)
        .astype(F32)
    )
    fcb = side(small_all[:, :, 4 * R : 4 * R + FH], 1)
    fc_shift = lax.dynamic_index_in_dim(
        lay.from_natural(fcb), t, 1, keepdims=False
    ).reshape(n_dp * FH).astype(F32)

    normed_one, hat_one, spread_one = norm_forward(x, gain_rows[0], bias_rows[0])
    h1 = normed_one.astype(BF)

    qkv_full = both(qkv_weight, qkv_other, 1).reshape(R, 3, D)
    qkv_full = pad_to(qkv_full, 2, UNITS * W).reshape(R, 3, 4, 2, W)
    qkv_src = jnp.transpose(side(qkv_full, 3), (2, 0, 1, 3)).reshape(4, R, 3 * W)
    fc_full = side(both(fc_weight, fc_other, 1).reshape(R, n_ctx, 2, FH), 2)
    fc_src = jnp.stack(
        [
            jnp.concatenate([fc_full[:, lay.compose(u, d)] for d in range(n_dp)], axis=1)
            for u in range(4)
        ]
    )
    out_src = side(both(out_weight, out_other, 1).reshape(2, FH, D), 0)

    qkv_buf, fc_buf, out_buf, proj_buf, h1_all, dy_all = gather_weights(
        lay, qkv_src, fc_src, out_src, proj_weight, h1, dy
    )
    w_qkv = qkv_buf.reshape(D, 3 * W)
    w_fc = fc_buf.reshape(D, n_dp * FH)
    w_out = out_buf.reshape(n_dp * FH, D)
    w_proj = jnp.transpose(proj_buf, (1, 2, 0, 3)).reshape(D, D)
    h1_rows = h1_all.reshape(M, D)
    dy_rows = dy_all.reshape(M, D)

    def unit_bias(row):
        return lax.dynamic_slice_in_dim(pad_to(row, 0, UNITS * W), unit * W, W)

    shift = jnp.concatenate([unit_bias(bias_rows[1]), jnp.zeros((W,), F32), unit_bias(bias_rows[2])])
    qkv = (dot(w_qkv, h1_rows, ((0,), (1,))) + shift[:, None]).astype(BF)
    qkv = jnp.transpose(qkv.reshape(3, HU, HEAD_DIM, M), (1, 0, 2, 3)).reshape(HU, QKV, M)
    mine = exchange(
        lay, "group_to_heads", 4, group_to_heads, data_partners, qkv, struct(n_dp, QKV, M), (HU, n_dp)
    )
    mine = jnp.transpose(mine.reshape(n_dp, 3, HEAD_DIM, 2, 4, T), (0, 4, 1, 3, 2, 5))
    mine = jnp.transpose(lay.to_natural(mine), (1, 2, 3, 0, 4)).reshape(3, 2, HEAD_DIM, length)
    q, k, v = mine[0], mine[1], mine[2]
    o, o_low, lse = attend(lay, q, k, v, T)
    n_dev = 2 * n_ctx
    ob = exchange(
        lay,
        "heads_to_tokens",
        5,
        heads_to_tokens,
        None,
        o_low,
        struct(HEADS, HEAD_DIM, T),
        (n_dev, HEADS),
    ).reshape(D, T)
    x1 = x + dot(ob, w_proj, TN) + bias_rows[3]
    normed_two, hat_two, spread_two = norm_forward(x1, gain_rows[1], bias_rows[4])
    h2_rows = gather_rows(lay, normed_two.astype(BF)).reshape(M, D)
    hidden_pre = dot(h2_rows, w_fc, NN) + fc_shift
    hidden, gelu_back = jax.vjp(gelu_tanh, hidden_pre)
    gb = hidden.astype(BF)
    mixed_part = dot(gb, w_out, NN).astype(BF).reshape(2, 4, T, D)
    du = gelu_back(dot(dy_rows, w_out, NT))[0].astype(BF)
    dh2_part = dot(du, w_fc, NT).astype(BF).reshape(2, 4, T, D)
    mixed_sum, dh2 = reduce_rows(lay, mixed_part, dh2_part)
    fc_grad = dot(h2_rows, du, TN).astype(BF).reshape(n_ctx, R, n_dp * FH)
    out_grad = dot(gb, dy_rows, TN).astype(BF).reshape(n_dp, FH, D)
    fc_bias_part = jnp.sum(du.astype(F32), axis=0)
    mixed = (x1 + mixed_sum.astype(F32) + bias_rows[5]).astype(BF)
    back_two, gain_two_g, bias_two_g = norm_back(dh2.astype(F32), hat_two, spread_two, gain_rows[1])
    dx1 = dy.astype(F32) + back_two
    da = dx1.astype(BF)
    proj_grad = jnp.transpose(dot(ob, da, NN).astype(BF).reshape(n_ctx, R, 2, D // 2), (2, 0, 1, 3))
    proj_bias_g = jnp.sum(da.astype(F32), axis=0)
    dob = dot(w_proj, da, NT).astype(BF).reshape(HEADS, HEAD_DIM, T)
    dob = exchange(
        lay,
        "tokens_to_heads",
        6,
        tokens_to_heads,
        None,
        dob,
        struct(2, n_ctx, HEAD_DIM, T),
        (HEADS, n_dev),
    )
    dob = jnp.transpose(dob, (0, 2, 1, 3)).reshape(2, HEAD_DIM, length)
    dq, dk, dv = attend_back(lay, q, k, v, o, lse, dob)
    grads = jnp.stack([dq, dk, dv]).reshape(3, 2, HEAD_DIM, n_ctx, T)
    grads = lay.from_natural(jnp.transpose(grads, (3, 0, 2, 1, 4)))
    grads = jnp.transpose(grads, (0, 2, 3, 4, 1, 5)).reshape(n_dp, QKV, M)
    dqkv = exchange(
        lay, "heads_to_group", 7, heads_to_group, data_partners, grads, struct(HU, QKV, M), (n_dp, HU)
    )
    dqkv = jnp.transpose(dqkv.reshape(HU, 3, HEAD_DIM, M), (1, 0, 2, 3)).reshape(3 * W, M)
    dh1_part = dot(dqkv, w_qkv, ((0,), (1,))).astype(BF).reshape(2, 4, T, D)
    qkv_grad = dot(h1_rows, dqkv, ((0,), (1,))).astype(BF).reshape(n_ctx, R, 3 * W)
    qkv_bias_part = jnp.sum(dqkv.astype(F32), axis=1)

    def unit_row(part):
        row = lax.dynamic_update_slice_in_dim(jnp.zeros((UNITS * W,), F32), part, unit * W, 0)
        return row[:D]

    dy_sum = jnp.sum(dy.astype(F32), axis=0)
    gains_part = jnp.stack([jnp.zeros((D,), F32), gain_two_g])
    biases_part = jnp.stack(
        [
            jnp.zeros((D,), F32),
            unit_row(qkv_bias_part[:W]),
            unit_row(qkv_bias_part[2 * W :]),
            proj_bias_g,
            bias_two_g,
            dy_sum,
        ]
    )
    parts = lay.from_natural(jnp.zeros((n_ctx, 2, FH), F32))
    mask = (jnp.arange(4)[None, :, None, None] == t) & (jnp.arange(2)[None, None, :, None] == s)
    parts = jnp.where(mask, fc_bias_part.reshape(n_dp, 1, 1, FH), parts)
    fc_bias_full = lay.to_natural(parts)
    small_parts = jnp.concatenate(
        [
            jnp.transpose(gains_part.reshape(2, n_ctx, R), (1, 0, 2)),
            jnp.transpose(biases_part.reshape(2, 3, n_ctx, R), (2, 0, 1, 3)).reshape(n_ctx, 2, 3 * R),
            fc_bias_full,
        ],
        axis=2,
    )
    small_parts = pad_to(small_parts, 2, 1024).reshape(n_dev, 8, 128)
    dh1, qkv_sum, fc_sum, out_sum, proj_sum, small_sum = reduce_grads(
        lay, dh1_part, qkv_grad, fc_grad, out_grad, proj_grad, small_parts
    )
    back_one, gain_one_g, bias_one_g = norm_back(dh1.astype(F32), hat_one, spread_one, gain_rows[0])
    input_grad = (dx1 + back_one).reshape(tokens.shape)
    first_rows = jnp.stack([gain_one_g, bias_one_g])
    first_rows = lax.psum(first_rows, ("ctx", "fsdp"))
    small_sum = jnp.sum(small_sum.reshape(n_dev, 1024), axis=0)
    own_cols = lax.dynamic_slice_in_dim(first_rows, c * R, R, 1)
    first_side = (s == 0).astype(F32)
    gains_out = (small_sum[:R] + own_cols[0] * first_side).reshape(1, R)
    biases_out = small_sum[R : 4 * R].reshape(3, R)
    biases_out = biases_out.at[0].add(own_cols[1] * first_side)
    fc_bias_out = small_sum[4 * R : 4 * R + FH]

    qkv_out = jnp.transpose(qkv_sum.reshape(2, 4, R, 3, W), (2, 3, 1, 0, 4))
    qkv_out = qkv_out.reshape(R, 3, UNITS * W)[:, :, :D].reshape(R, 2, 3 * D // 2)
    qkv_out = side(qkv_out, 1).astype(F32)
    fc_out = fc_sum.reshape(2, 4, R, n_dp, FH)
    fc_cols = []
    for b in range(n_ctx):
        for half in range(2):
            fc_cols.append(fc_sum[half, lay.tp_index(b), :, lay.dp_index(b) * FH : (lay.dp_index(b) + 1) * FH])
    half = n_ctx
    fc_out = jnp.where(
        s == 0, jnp.concatenate(fc_cols[:half], axis=1), jnp.concatenate(fc_cols[half:], axis=1)
    ).astype(F32)
    out_out = side(out_sum.reshape(FB, 2, D // 2), 1).astype(F32)
    proj_out = proj_sum.astype(F32)
    return (
        mixed.reshape(tokens.shape),
        input_grad,
        qkv_out,
        proj_out,
        fc_out,
        out_out,
        gains_out,
        biases_out,
        fc_bias_out,
    )


def solution(mesh):
    lay = Layout(mesh.shape["ctx"])
    in_specs = (
        P("fsdp", "ctx", None),
        P("ctx", "fsdp"),
        P("ctx", "fsdp"),
        P("ctx", "fsdp"),
        P("ctx", "fsdp"),
        P("fsdp", "ctx"),
        P("fsdp", "ctx"),
        P(("ctx", "fsdp")),
        P("fsdp", "ctx", None),
    )
    out_specs = (
        P("fsdp", "ctx", None),
        P("fsdp", "ctx", None),
        P("ctx", "fsdp"),
        P("ctx", "fsdp"),
        P("ctx", "fsdp"),
        P("ctx", "fsdp"),
        P("fsdp", "ctx"),
        P("fsdp", "ctx"),
        P(("ctx", "fsdp")),
    )
    return jax.shard_map(
        functools.partial(shards, lay), mesh=mesh, in_specs=in_specs, out_specs=out_specs, check_vma=False
    )
```

```python
import functools
import math

import jax
import jax.numpy as jnp
from jax import lax
from jax.experimental import pallas as pl
from jax.experimental.pallas import tpu as pltpu
from jax.sharding import PartitionSpec as P

D = 1600
HEADS = 25
HEAD_DIM = 64
FF = 6400
EPS = 1e-05
UNITS = 8
HU = -(-HEADS // UNITS)
QKV = 3 * HEAD_DIM
MESH = pl.DeviceIdType.MESH
BF = jnp.bfloat16
F32 = jnp.float32
VMEM_LIMIT = 56 * 1024 * 1024
LOG2E = 1.0 / math.log(2.0)


class Layout:
    def __init__(self, n_ctx):
        self.n_ctx = n_ctx
        a, b = n_ctx // 4, n_ctx // 2
        self.tp_bits = (a, b)
        self.dp_bits = tuple(1 << i for i in range(n_ctx.bit_length() - 3))
        self.n_dp = n_ctx // 4
        self.dp_order = list(zip(self.dp_bits, self.dp_bits[::-1]))
        self.tp_order = [(b, b), (a, a)]
        self.tp_masks = [[], [(a, a)], [(b, b)], [(a, a), (b, b)]]

    def tp_index(self, c):
        return sum(((c // b) % 2) * (1 << i) for i, b in enumerate(self.tp_bits))

    def dp_index(self, c):
        return sum(((c // b) % 2) * (1 << i) for i, b in enumerate(self.dp_bits))

    def compose(self, t, d):
        return sum(((t // (1 << i)) % 2) * b for i, b in enumerate(self.tp_bits)) + sum(
            ((d // (1 << i)) % 2) * b for i, b in enumerate(self.dp_bits)
        )

    def head_rank(self, h):
        u, j = h // HU, h % HU
        return self.compose(u // 2, j) * 2 + u % 2

    def to_natural(self, x):
        labels = list(self.dp_bits[::-1]) + list(self.tp_bits[::-1])
        k = len(labels)
        rest = x.shape[2:]
        x = x.reshape((2,) * k + rest)
        order = sorted(range(k), key=lambda i: -labels[i])
        x = jnp.transpose(x, order + list(range(k, k + len(rest))))
        return x.reshape((self.n_ctx,) + rest)

    def from_natural(self, x):
        labels = list(self.dp_bits[::-1]) + list(self.tp_bits[::-1])
        k = len(labels)
        rest = x.shape[1:]
        x = x.reshape((2,) * k + rest)
        natural = sorted(labels, reverse=True)
        order = [natural.index(b) for b in labels]
        x = jnp.transpose(x, order + list(range(k, k + len(rest))))
        return x.reshape((self.n_dp, 4) + rest)


def flip(c, sym, s):
    def one(b):
        return c + b * (1 - 2 * ((c // b) % 2))

    if sym[0] == sym[1]:
        return one(sym[0])
    return one(sym[0]) * (1 - s) + one(sym[1]) * s


def flips(c, masks, s):
    for sym in masks:
        c = flip(c, sym, s)
    return c


class Env:
    def __init__(self, layout):
        self.lay = layout
        self.c = lax.axis_index("ctx")
        self.s = lax.axis_index("fsdp")
        self.t = layout.tp_index(self.c)
        self.d = layout.dp_index(self.c)
        self.rank = self.c * 2 + self.s
        self.n_dev = layout.n_ctx * 2

    def other(self):
        return (self.c, 1 - self.s)


class Links:
    def __init__(self, sems):
        self.send_sems, self.recv_sems, self.local_sems = sems
        self.count = 0
        self.local_count = 0
        self.sent = []
        self.locals = []

    def send(self, src, dst, device):
        copy = pltpu.make_async_remote_copy(
            src_ref=src,
            dst_ref=dst,
            send_sem=self.send_sems.at[self.count],
            recv_sem=self.recv_sems.at[self.count],
            device_id=device,
            device_id_type=MESH,
        )
        copy.start()
        self.count += 1
        self.sent.append(copy)
        return copy

    def local(self, src, dst):
        copy = pltpu.make_async_copy(src, dst, self.local_sems.at[self.local_count])
        copy.start()
        self.local_count += 1
        self.locals.append(copy)
        return copy

    def finish(self):
        for copy in self.locals:
            copy.wait()
        for copy in self.sent:
            copy.wait_send()


def sem_shapes(sends, local=1):
    sends = max(sends, 1)
    return [
        pltpu.SemaphoreType.DMA((sends,)),
        pltpu.SemaphoreType.DMA((sends,)),
        pltpu.SemaphoreType.DMA((local,)),
    ]


def meet(env, devices):
    barrier = pltpu.get_barrier_semaphore()
    for device in devices:
        pl.semaphore_signal(barrier, inc=1, device_id=device, device_id_type=MESH)
    pl.semaphore_wait(barrier, len(devices))


def meet_all(env):
    barrier = pltpu.get_barrier_semaphore()

    def hail(i, carry):
        rank = (env.rank + i) % env.n_dev
        pl.semaphore_signal(barrier, inc=1, device_id=(rank // 2, rank % 2), device_id_type=MESH)
        return carry

    lax.fori_loop(1, env.n_dev, hail, 0)
    pl.semaphore_wait(barrier, env.n_dev - 1)


def tp_partners(env):
    return [(flips(env.c, m, env.s), env.s) for m in env.lay.tp_masks[1:]]


def dp_partners(env):
    return [(flip(env.c, sym, env.s), env.s) for sym in env.lay.dp_order]


def run(generators):
    active = list(generators)
    while active:
        left = []
        for g in active:
            try:
                next(g)
                left.append(g)
            except StopIteration:
                pass
        active = left


def gather_sends(have, bits, core, rows):
    return (3 if rows else 0) + have * ((1 << bits) - 1) + (have << bits if core else 0)


def gather(env, src, buf, sems, bits, slot, core=False, rows=False):
    c, s = env.c, env.s
    links = Links(sems)

    def place(masks):
        index = slot(flips(c, masks, s))
        return buf.at[s, index] if core else buf.at[index]

    own = src.at[env.t] if rows else src
    links.local(own, place([]))
    levels = [[([], None)]] + [[] for _ in bits]
    if rows:
        for m in env.lay.tp_masks[1:]:
            there = flips(c, m, s)
            copy = links.send(src.at[env.lay.tp_index(there)], place([]), (there, s))
            levels[0].append((m, copy))
    crossing = []
    for k in range(len(bits) + 1):
        for masks, copy in levels[k]:
            if copy is None:
                ref = own
            else:
                copy.wait_recv()
                ref = place(masks)
            for j in range(k, len(bits)):
                forward = links.send(ref, place(masks), (flip(c, bits[j], s), s))
                levels[j + 1].append((masks + [bits[j]], forward))
            if core:
                crossing.append(links.send(ref, place(masks), env.other()))
            yield
    for copy in crossing:
        copy.wait_recv()
    links.finish()
    yield


def reduce_sends(have, bits, core, rows, halves):
    return (have << bits if core else 0) + have * ((1 << bits) - 1) + (3 + 4 if rows else 0) + (1 if halves else 0)


def reduce_scratch(have, bits, core, block):
    counts = [have << j for j in range(bits + (1 if core else 0))]
    return [pltpu.VMEM((n,) + block, BF) for n in counts]


def reduce(env, inp, out, parts, sems, bits, slot, core=False, rows=False, halves=False):
    c, s = env.c, env.s
    links = Links(sems)
    levels = [list(env.lay.tp_masks) if rows else [[]]]
    for sym in bits:
        levels.append(levels[-1] + [m + [sym] for m in levels[-1]])

    def at(side, masks):
        index = slot(flips(c, masks, side))
        return inp.at[side, index] if core else inp.at[index]

    last = levels[-1]
    now = [at(s, m) for m in last]
    copies = {}
    if core:
        stage = len(bits)
        for i in reversed(range(len(last))):
            copies[i] = links.send(at(1 - s, last[i]), parts[stage].at[i], env.other())
    else:
        stage = len(bits) - 1
        n = len(levels[stage])
        for i in reversed(range(n)):
            copies[i] = links.send(now[n + i], parts[stage].at[i], (flip(c, bits[stage], s), s))
    yield
    while stage >= 0:
        n = len(levels[stage])
        got = parts[stage]
        after = {}
        for i in reversed(range(n)):
            copies[i].wait_recv()
            got[i] = got[i] + now[i][...]
            if stage > 0 and i >= n // 2:
                after[i - n // 2] = links.send(
                    got.at[i], parts[stage - 1].at[i - n // 2], (flip(c, bits[stage - 1], s), s)
                )
            yield
        now = [got.at[i] for i in range(n)]
        copies = after
        stage -= 1
    if rows:
        arrivals = []
        links.local(now[0], out.at[s, env.t])
        arrivals.append((env.t, None, now[0]))
        for i, m in enumerate(env.lay.tp_masks):
            if i > 0:
                there = flips(c, m, s)
                copy = links.send(now[i], out.at[s, env.t], (there, s))
                index = env.lay.tp_index(there)
                arrivals.append((index, copy, out.at[s, index]))
        yield
        crossing = []
        for index, copy, ref in arrivals:
            if copy is not None:
                copy.wait_recv()
            crossing.append(links.send(ref, out.at[s, index], env.other()))
            yield
        for copy in crossing:
            copy.wait_recv()
    elif halves:
        links.local(now[0], out.at[s])
        copy = links.send(now[0], out.at[s], env.other())
        yield
        copy.wait_recv()
    else:
        out[...] = now[0][...]
    links.finish()
    yield


def to_everyone(env, src, out, sems, same):
    send_sems, recv_sems, local_sems = sems

    def own(ref):
        return ref if same else ref.at[env.rank]

    def copy(i):
        rank = (env.rank + i) % env.n_dev
        return pltpu.make_async_remote_copy(
            src_ref=src if same else src.at[rank],
            dst_ref=out.at[env.rank],
            send_sem=send_sems.at[i],
            recv_sem=recv_sems.at[i],
            device_id=(rank // 2, rank % 2),
            device_id_type=MESH,
        )

    def begin(i, carry):
        copy(i).start()
        return carry

    def end(i, carry):
        copy(i).wait()
        return carry

    lax.fori_loop(1, env.n_dev, begin, 0)
    local = pltpu.make_async_copy(own(src), out.at[env.rank], local_sems.at[0])
    local.start()
    yield
    lax.fori_loop(1, env.n_dev, end, 0)
    local.wait()
    yield


def own_head(env):
    h = (env.t * 2 + env.s) * HU + env.d
    return h, jnp.logical_and(env.d < HU, h < HEADS)


def tokens_to_heads(env, src, out, sems):
    send_sems, recv_sems, local_sems = sems
    h, active = own_head(env)
    lay = env.lay

    def copy(j):
        rank = lay.head_rank(j)
        return rank, pltpu.make_async_remote_copy(
            src_ref=src.at[j],
            dst_ref=out.at[env.s, env.c],
            send_sem=send_sems.at[j],
            recv_sem=recv_sems.at[(rank - env.rank + env.n_dev) % env.n_dev],
            device_id=(rank // 2, rank % 2),
            device_id_type=MESH,
        )

    def begin(i, carry):
        rank, cp = copy((env.rank + i) % HEADS)

        @pl.when(rank != env.rank)
        def _():
            cp.start()

        return carry

    lax.fori_loop(0, HEADS, begin, 0)

    @pl.when(active)
    def _():
        local = pltpu.make_async_copy(src.at[h], out.at[env.s, env.c], local_sems.at[0])
        local.start()
        local.wait()

        def receive(i, carry):
            rank = (env.rank - i + env.n_dev) % env.n_dev
            pltpu.make_async_remote_copy(
                src_ref=src.at[0],
                dst_ref=out.at[rank % 2, rank // 2],
                send_sem=send_sems.at[0],
                recv_sem=recv_sems.at[i],
                device_id=env.other(),
                device_id_type=MESH,
            ).wait_recv()
            return carry

        lax.fori_loop(1, env.n_dev, receive, 0)

    def end(j, carry):
        rank, cp = copy(j)

        @pl.when(rank != env.rank)
        def _():
            cp.wait_send()

        return carry

    lax.fori_loop(0, HEADS, end, 0)


def data_partners(env):
    lay = env.lay
    return [(lay.compose(env.t, (env.d + i) % lay.n_dp), env.s) for i in range(1, lay.n_dp)]


def heads_to_group(env, src, out, sems):
    send_sems, recv_sems, local_sems = sems
    lay = env.lay

    def copy(there, j, target):
        return pltpu.make_async_remote_copy(
            src_ref=src.at[there],
            dst_ref=out.at[j],
            send_sem=send_sems.at[there],
            recv_sem=recv_sems.at[j],
            device_id=(lay.compose(env.t, target), env.s),
            device_id_type=MESH,
        )

    @pl.when(env.d < HU)
    def _():
        for i in range(1, lay.n_dp):
            there = (env.d + i) % lay.n_dp
            copy(there, env.d, there).start()
        local = pltpu.make_async_copy(src.at[env.d], out.at[env.d], local_sems.at[0])
        local.start()
        local.wait()

    for j in range(HU):

        @pl.when(j != env.d)
        def _():
            copy(0, j, j).wait_recv()

    @pl.when(env.d < HU)
    def _():
        for i in range(1, lay.n_dp):
            there = (env.d + i) % lay.n_dp
            copy(there, env.d, there).wait_send()


ANY = pl.BlockSpec(memory_space=pl.ANY)
VM = pl.BlockSpec(memory_space=pltpu.VMEM)


def struct(*shape, dtype=BF):
    return jax.ShapeDtypeStruct(shape, dtype)


def call(name, cid, body, args, in_specs, outs, out_specs, scratch):
    return pl.pallas_call(
        body,
        out_shape=outs,
        in_specs=in_specs,
        out_specs=out_specs,
        scratch_shapes=scratch,
        compiler_params=pltpu.CompilerParams(
            collective_id=cid, has_side_effects=True, vmem_limit_bytes=VMEM_LIMIT
        ),
        name=name,
    )(*args)


def reduce_rows(lay, first, second):
    block = first.shape[2:]

    def body(a_r, b_r, a_o, b_o, *rest):
        env = Env(lay)
        meet(env, tp_partners(env) + [env.other()])
        run(
            [
                reduce(env, a_r, a_o, rest[0:3], rest[6:9], lay.tp_order, lay.tp_index, core=True),
                reduce(env, b_r, b_o, rest[3:6], rest[9:12], lay.tp_order, lay.tp_index, core=True),
            ]
        )

    return call(
        "reduce_rows",
        3,
        body,
        (first, second),
        [VM] * 2,
        [struct(*block)] * 2,
        [VM] * 2,
        reduce_scratch(1, 2, True, block) * 2 + sem_shapes(reduce_sends(1, 2, True, False, False)) * 2,
    )


def exchange(lay, name, cid, op, partners, src, out, counts):
    def body(src_r, out_r, *sems):
        env = Env(lay)
        if partners is None:
            meet_all(env)
        else:
            meet(env, partners(env))
        op(env, src_r, out_r, sems)

    scratch = [
        pltpu.SemaphoreType.DMA((counts[0],)),
        pltpu.SemaphoreType.DMA((counts[1],)),
        pltpu.SemaphoreType.DMA((1,)),
    ]
    return call(name, cid, body, (src,), [ANY], out, ANY, scratch)


def reduce_grads(lay, rows, qkv, fc, out, proj, small):
    n_ctx = lay.n_ctx
    k = len(lay.dp_bits)
    n_dev = 2 * n_ctx

    def natural(c):
        return c

    plan = [
        (rows.shape[2:], 1, 2, True, False, False),
        (qkv.shape[1:], 4, k, False, True, False),
        (fc.shape[1:], 4, k, False, True, False),
        (out.shape[1:], 1, k, False, False, True),
        (proj.shape[2:], 1, k + 2, True, False, False),
    ]
    scratch, spans = [], []
    for block, have, bits, core, is_rows, halves in plan:
        part = reduce_scratch(have, bits, core, block)
        sems = sem_shapes(reduce_sends(have, bits, core, is_rows, halves))
        spans.append((len(scratch), len(part)))
        scratch = scratch + part + sems
    scratch = scratch + sem_shapes(n_dev)

    def body(rows_r, qkv_r, fc_r, out_r, proj_r, small_r, rows_o, qkv_o, fc_o, out_o, proj_o, small_o, *rest):
        env = Env(lay)
        meet_all(env)

        def space(i):
            first, n = spans[i]
            return rest[first : first + n], rest[first + n : first + n + 3]

        run(
            [
                to_everyone(env, small_r, small_o, rest[-3:], False),
                reduce(env, qkv_r, qkv_o, *space(1), lay.dp_order, natural, rows=True),
                reduce(env, rows_r, rows_o, *space(0), lay.tp_order, lay.tp_index, core=True),
                reduce(env, proj_r, proj_o, *space(4), lay.tp_order + lay.dp_order, natural, core=True),
                reduce(env, fc_r, fc_o, *space(2), lay.dp_order, natural, rows=True),
                reduce(env, out_r, out_o, *space(3), lay.dp_order, lay.dp_index, halves=True),
            ]
        )

    outs = [
        struct(*rows.shape[2:]),
        struct(2, 4, *qkv.shape[1:]),
        struct(2, 4, *fc.shape[1:]),
        struct(2, *out.shape[1:]),
        struct(*proj.shape[2:]),
        struct(*small.shape, dtype=F32),
    ]
    return call(
        "reduce_grads",
        8,
        body,
        (rows, qkv, fc, out, proj, small),
        [VM] * 5 + [ANY],
        outs,
        [VM, ANY, ANY, ANY, VM, ANY],
        scratch,
    )


def dot(left, right, dims):
    return lax.dot_general(left, right, (dims, ((), ())), preferred_element_type=F32)


NN = ((1,), (0,))
NT = ((1,), (1,))
TN = ((0,), (0,))
SCALE = 1.0 / math.sqrt(HEAD_DIM)
TILE = 512


def attend_back(lay, q, k, v, o, lse, dob):
    length = q.shape[2]
    tile = min(TILE, length)
    n = length // tile

    def body(q_ref, k_ref, v_ref, o_ref, lse_ref, dob_ref, dq_ref, dk_ref, dv_ref, qs, dobs, delta, dq_acc):
        j = pl.program_id(1)

        @pl.when(j == 0)
        def _():
            qs[...] = q_ref[0].T
            dobs[...] = dob_ref[0].T
            delta[...] = jnp.sum(dob_ref[0].astype(F32) * o_ref[0], axis=0, keepdims=True)
            dq_acc[...] = jnp.zeros_like(dq_acc)

        kt = k_ref[0]
        keys = kt.T
        values = v_ref[0].T

        def step(i, carry, masked):
            dk, dv = carry
            at = pl.ds(pl.multiple_of(i * tile, tile), tile)
            st = dot(keys, q_ref[0, :, at], NN) * (SCALE * LOG2E)
            p = jnp.exp2(st - lse_ref[0, :, at])
            if masked:
                row = lax.broadcasted_iota(jnp.int32, (tile, tile), 0)
                col = lax.broadcasted_iota(jnp.int32, (tile, tile), 1)
                p = jnp.where(row <= col, p, 0.0)
            dp = dot(values, dob_ref[0, :, at], NN)
            ds = (p * (dp - delta[:, at])).astype(BF)
            dv = dv + dot(p.astype(BF), dobs[at, :], NN)
            dk = dk + dot(ds, qs[at, :], NN)
            dq_acc[:, at] += dot(kt, ds, NN)
            return dk, dv

        zero = jnp.zeros((tile, HEAD_DIM), F32)
        carry = step(j, (zero, zero), True)
        dk, dv = lax.fori_loop(j + 1, n, functools.partial(step, masked=False), carry)
        dk_ref[0] = (dk * SCALE).T.astype(BF)
        dv_ref[0] = dv.T.astype(BF)

        @pl.when(j == n - 1)
        def _():
            dq_ref[0] = (dq_acc[...] * SCALE).astype(BF)

    whole = pl.BlockSpec((1, HEAD_DIM, length), lambda b, i: (b, 0, 0))
    tiled = pl.BlockSpec((1, HEAD_DIM, tile), lambda b, i: (b, 0, i))
    line = pl.BlockSpec((1, 1, length), lambda b, i: (b, 0, 0))
    return pl.pallas_call(
        body,
        grid=(2, n),
        in_specs=[whole, tiled, tiled, whole, line, whole],
        out_specs=[whole, tiled, tiled],
        out_shape=[struct(2, HEAD_DIM, length)] * 3,
        scratch_shapes=[
            pltpu.VMEM((length, HEAD_DIM), BF),
            pltpu.VMEM((length, HEAD_DIM), BF),
            pltpu.VMEM((1, length), F32),
            pltpu.VMEM((HEAD_DIM, length), F32),
        ],
        compiler_params=pltpu.CompilerParams(vmem_limit_bytes=VMEM_LIMIT),
        name="attend_back",
    )(q, k, v, o, lse, dob)


class Background:
    def __init__(self):
        self.active = []

    def add(self, generator):
        self.active.append(generator)

    def step(self, count=1):
        for _ in range(count):
            if not self.active:
                return
            g = self.active.pop(0)
            try:
                next(g)
                self.active.append(g)
            except StopIteration:
                pass

    def finish(self):
        while self.active:
            self.step()


def finish(generator):
    for _ in generator:
        pass


def group_to_heads(env, src, out, sems, q):
    send_sems, recv_sems, local_sems = sems
    lay = env.lay

    def copy(j, source, target):
        return pltpu.make_async_remote_copy(
            src_ref=src.at[q, j],
            dst_ref=out.at[q, source],
            send_sem=send_sems.at[q, j],
            recv_sem=recv_sems.at[q, source],
            device_id=(lay.compose(env.t, target), env.s),
            device_id_type=MESH,
        )

    for i in range(1, HU + 1):
        j = (env.d + i) % HU

        @pl.when(j != env.d)
        def _():
            copy(j, env.d, j).start()

    local = pltpu.make_async_copy(src.at[q, env.d % HU], out.at[q, env.d], local_sems.at[q])

    @pl.when(env.d < HU)
    def _():
        local.start()

    yield

    @pl.when(env.d < HU)
    def _():
        local.wait()
        for i in range(1, lay.n_dp):
            source = (env.d + i) % lay.n_dp
            copy(0, source, source).wait_recv()

    yield
    for j in range(HU):

        @pl.when(j != env.d)
        def _():
            copy(j, env.d, j).wait_send()


def heads_out(env, src, out, sems, q):
    send_sems, recv_sems, local_sems = sems
    h, active = own_head(env)
    n_ctx = env.lay.n_ctx

    def copy(i):
        there = (env.c + i) % n_ctx
        return pltpu.make_async_remote_copy(
            src_ref=src.at[q, there],
            dst_ref=out.at[h],
            send_sem=send_sems.at[q, i],
            recv_sem=recv_sems.at[h],
            device_id=(there, q),
            device_id_type=MESH,
        )

    local = pltpu.make_async_copy(src.at[q, env.c], out.at[h], local_sems.at[q])
    mine = jnp.logical_and(active, env.s == q)
    theirs = jnp.logical_and(active, env.s != q)

    def begin(i, carry):
        copy(i).start()
        return carry

    def end(i, carry):
        copy(i).wait_send()
        return carry

    @pl.when(mine)
    def _():
        local.start()

    @pl.when(theirs)
    def _():
        copy(0).start()

    @pl.when(active)
    def _():
        lax.fori_loop(1, n_ctx, begin, 0)

    yield

    @pl.when(mine)
    def _():
        local.wait()

    @pl.when(theirs)
    def _():
        copy(0).wait_send()

    @pl.when(active)
    def _():
        lax.fori_loop(1, n_ctx, end, 0)


def heads_in(env, src, out, sems):
    def receive(j, carry):
        @pl.when(env.lay.head_rank(j) != env.rank)
        def _():
            pltpu.make_async_remote_copy(
                src_ref=src.at[0, 0],
                dst_ref=out.at[j],
                send_sem=sems[0].at[0, 0],
                recv_sem=sems[1].at[j],
                device_id=env.other(),
                device_id_type=MESH,
            ).wait_recv()

        return carry

    lax.fori_loop(0, HEADS, receive, 0)


def norm_stats(values):
    centre = values - jnp.mean(values, axis=-1, keepdims=True)
    spread = lax.rsqrt(jnp.mean(centre * centre, axis=-1, keepdims=True) + EPS)
    return centre * spread, spread


def attend_tile(i, tile, qt, keys, v_ref):
    def step(j, carry, masked):
        peak, total, acc = carry
        at = pl.ds(pl.multiple_of(j * tile, tile), tile)
        st = dot(keys[at, :], qt, NN) * (SCALE * LOG2E)
        if masked:
            row = lax.broadcasted_iota(jnp.int32, (tile, tile), 0)
            col = lax.broadcasted_iota(jnp.int32, (tile, tile), 1)
            st = jnp.where(row <= col, st, -1e30)
        new = jnp.maximum(peak, jnp.max(st, axis=0, keepdims=True))
        p = jnp.exp2(st - new)
        shrink = jnp.exp2(peak - new)
        total = total * shrink + jnp.sum(p, axis=0, keepdims=True)
        acc = acc * shrink + dot(v_ref[:, at], p.astype(BF), NN)
        return new, total, acc

    start = (
        jnp.full((1, tile), -1e30, F32),
        jnp.zeros((1, tile), F32),
        jnp.zeros((HEAD_DIM, tile), F32),
    )
    carry = start
    if i > 0:
        carry = lax.fori_loop(0, i, functools.partial(step, masked=False), carry)
    peak, total, acc = step(i, carry, True)
    return acc / total, peak + jnp.log2(total)


def forward(lay, x, gains, biases, fc_bias, qkv, fc, out, proj, dy):
    n_ctx, n_dp = lay.n_ctx, lay.n_dp
    n_dev = 2 * n_ctx
    k = len(lay.dp_bits)
    T = x.shape[0]
    R, FB = D // n_ctx, FF // n_ctx
    FH = FB // 2
    W = HU * HEAD_DIM
    G = 4 * T
    length = n_ctx * T
    tile = min(TILE, length)
    n_tiles = length // tile
    half = D // 2
    wide = UNITS * W

    def natural(c):
        return c

    def body(*refs):
        (x_r, gains_r, biases_r, fcb_r, qkv_r, fc_r, out_r, proj_r, dy_r) = refs[:9]
        (h1_o, wq_o, heads_o, o_o, lse_o, ob_o, pj_o, x1_o, h2_o, fc_o, out_o, dy_o, shift_o, par_o) = refs[9:23]
        (
            pack, small, qkv_x, fc_x, out_x, qkv_s, fc_s, out_s, wq_b, h1_s, par_w,
            parts, mine, keys, o_low, ob_b, proj_b, h2_s,
        ) = refs[23:41]
        sems = refs[41:]
        groups = [sems[3 * i : 3 * i + 3] for i in range(len(sems) // 3)]
        env = Env(lay)
        s = env.s

        pack[...] = jnp.zeros_like(pack)
        pack[0:1, :R] = gains_r[...].astype(F32)
        pack[1:4, :R] = biases_r[...].astype(F32)
        pack[4:6, : FH // 2] = fcb_r[...].astype(F32)
        meet_all(env)
        links = Links(groups[0])
        crossing = [
            links.send(a, b, env.other()) for a, b in ((qkv_r, qkv_x), (fc_r, fc_x), (out_r, out_x))
        ]
        everyone = to_everyone(env, pack, small, groups[1], True)
        next(everyone)
        hat, _ = norm_stats(x_r[...].astype(F32))

        def fill_qkv(a, b, side):
            q = a[:, :D]
            keys_all = jnp.concatenate([a[:, D:], b[:, : D // 2]], axis=1)
            v = b[:, D // 2 :]
            for u in range(4):
                first = (2 * u + side) * W
                width = max(0, min(W, D - first))
                for n, part in enumerate((q, keys_all, v)):
                    if width < W:
                        qkv_s[u, :, n * W : (n + 1) * W] = jnp.zeros((R, W), BF)
                    if width > 0:
                        qkv_s[u, :, n * W : n * W + width] = part[:, first : first + width]

        def fill_rest(a, b, oa, ob, side):
            for u in range(4):
                for d in range(n_dp):
                    first = lay.compose(u, d) * FB + side * FH
                    source, first = (a, first) if first < FF // 2 else (b, first - FF // 2)
                    fc_s[u, :, d * FH : (d + 1) * FH] = source[:, first : first + FH]
            out_s[:, :half] = oa[side * FH : (side + 1) * FH, :]
            out_s[:, half:] = ob[side * FH : (side + 1) * FH, :]

        def by_side(f, own, other):
            @pl.when(s == 0)
            def _():
                f(*own_other(own, other), 0)

            @pl.when(s == 1)
            def _():
                f(*own_other(other, own), 1)

        def own_other(first, second):
            return [r for pair in zip(first, second) for r in pair]

        crossing[0].wait_recv()
        by_side(fill_qkv, (qkv_r,), (qkv_x,))
        weights = gather(env, qkv_s, wq_b, groups[2], lay.dp_order, natural, rows=True)
        next(weights)
        finish(everyone)
        for f in range(2):
            rows = jnp.concatenate([small[2 * c + f][:, :R] for c in range(n_ctx)], axis=1)
            par_o[f] = rows
        par_w[...] = jnp.zeros_like(par_w)
        par_w[:, :D] = par_o[0]
        h1_s[...] = (hat * par_o[0, 0:1, :] + par_o[0, 1:2, :]).astype(BF)
        rows_h1 = gather(env, h1_s, h1_o, groups[3], lay.tp_order, lay.tp_index, core=True)
        next(rows_h1)
        shift_parts = []
        for d in range(n_dp):
            block = small[lay.compose(env.t, d) * 2 + s]
            shift_parts += [block[4:5, : FH // 2], block[5:6, : FH // 2]]
        shift_o[...] = jnp.concatenate(shift_parts, axis=1)
        run([weights, rows_h1])
        crossing[1].wait_recv()
        crossing[2].wait_recv()
        by_side(fill_rest, (fc_r, out_r), (fc_x, out_x))
        bg = Background()
        bg.add(gather(env, dy_r, dy_o, groups[4], lay.tp_order, lay.tp_index, core=True))
        bg.add(gather(env, fc_s, fc_o, groups[5], lay.dp_order, natural, rows=True))
        bg.step(2)
        for c in range(n_ctx):
            wq_o[c * R : (c + 1) * R, :] = wq_b[c]
        unit = 2 * env.t + s
        cols = pl.ds(pl.multiple_of(unit * W, W), W)
        shift = jnp.concatenate(
            [par_w[2:3, cols], jnp.zeros((1, W), F32), par_w[3:4, cols]], axis=1
        )
        moving = []
        for q in range(2):
            rows = h1_o[q].reshape(G, D)
            made = (dot(rows, wq_o[...], NN) + shift).astype(BF).T
            for n in range(3):
                for j in range(HU):
                    first = n * W + j * HEAD_DIM
                    parts[q, j, n * HEAD_DIM : (n + 1) * HEAD_DIM, :] = made[first : first + HEAD_DIM]
            g = group_to_heads(env, parts, mine, groups[6], q)
            next(g)
            moving.append(g)
        bg.add(gather(env, proj_r, proj_b, groups[7], lay.tp_order + lay.dp_order, natural, core=True))
        bg.add(gather(env, out_s, out_o, groups[8], lay.dp_order, lay.dp_index))
        bg.step(4)
        leaving = []
        for q in range(2):
            next(moving[q])
            for c in range(n_ctx):
                tc, dc = lay.tp_index(c), lay.dp_index(c)
                for n in range(3):
                    heads_o[n, q, :, c * T : (c + 1) * T] = mine[
                        q, dc, n * HEAD_DIM : (n + 1) * HEAD_DIM, tc * T : (tc + 1) * T
                    ]
            keys[...] = heads_o[1, q].T
            for i in range(n_tiles):
                at = slice(i * tile, (i + 1) * tile)
                o, lse = attend_tile(i, tile, heads_o[0, q, :, at], keys, heads_o.at[2, q])
                o_o[q, :, at] = o
                lse_o[q, :, at] = lse
                low = o.astype(BF)
                for b in range(tile // T):
                    o_low[q, i * (tile // T) + b] = low[:, b * T : (b + 1) * T]
                bg.step(3)
            g = heads_out(env, o_low, ob_b, groups[9], q)
            next(g)
            leaving.append(g)
        bg.finish()
        for g in moving + leaving:
            finish(g)
        for n in range(2):
            for c in range(n_ctx):
                pj_o[n, c * R : (c + 1) * R, :] = proj_b[n, c]
        heads_in(env, o_low, ob_b, groups[9])
        ob_o[...] = ob_b[...].reshape(D, T).T
        branch = jnp.concatenate([dot(ob_o[...], pj_o[n], NN) for n in range(2)], axis=1)
        x1 = x_r[...].astype(F32) + branch + par_o[1, 1:2, :]
        x1_o[...] = x1
        hat, _ = norm_stats(x1)
        h2_s[...] = (hat * par_o[1, 0:1, :] + par_o[1, 2:3, :]).astype(BF)
        finish(gather(env, h2_s, h2_o, groups[10], lay.tp_order, lay.tp_index, core=True))
        links.finish()

    outs = [
        struct(2, 4, T, D),
        struct(D, 3 * W),
        struct(3, 2, HEAD_DIM, length),
        struct(2, HEAD_DIM, length, dtype=F32),
        struct(2, 1, length, dtype=F32),
        struct(T, D),
        struct(2, D, half),
        struct(T, D, dtype=F32),
        struct(2, 4, T, D),
        struct(n_ctx, R, n_dp * FH),
        struct(n_dp, FH, D),
        struct(2, 4, T, D),
        struct(1, n_dp * FH, dtype=F32),
        struct(2, 8, D, dtype=F32),
    ]
    out_specs = [VM] * 8 + [ANY] * 4 + [VM] * 2
    scratch = [
        pltpu.VMEM((8, 128), F32),
        pltpu.VMEM((n_dev, 8, 128), F32),
        pltpu.VMEM(qkv.shape, BF),
        pltpu.VMEM(fc.shape, BF),
        pltpu.VMEM(out.shape, BF),
        pltpu.VMEM((4, R, 3 * W), BF),
        pltpu.VMEM((4, R, n_dp * FH), BF),
        pltpu.VMEM((FH, D), BF),
        pltpu.VMEM((n_ctx, R, 3 * W), BF),
        pltpu.VMEM((T, D), BF),
        pltpu.VMEM((8, wide), F32),
        pltpu.VMEM((2, HU, QKV, G), BF),
        pltpu.VMEM((2, n_dp, QKV, G), BF),
        pltpu.VMEM((length, HEAD_DIM), BF),
        pltpu.VMEM((2, n_ctx, HEAD_DIM, T), BF),
        pltpu.VMEM((HEADS, HEAD_DIM, T), BF),
        pltpu.VMEM((2, n_ctx, R, half), BF),
        pltpu.VMEM((T, D), BF),
    ]
    DMA = pltpu.SemaphoreType.DMA
    scratch += sem_shapes(3) + sem_shapes(n_dev)
    scratch += sem_shapes(gather_sends(4, k, False, True))
    scratch += sem_shapes(gather_sends(1, 2, True, False)) * 2
    scratch += sem_shapes(gather_sends(4, k, False, True))
    scratch += [DMA((2, HU)), DMA((2, n_dp)), DMA((2,))]
    scratch += sem_shapes(gather_sends(1, k + 2, True, False))
    scratch += sem_shapes(gather_sends(1, k, False, False))
    scratch += [DMA((2, n_ctx)), DMA((HEADS,)), DMA((2,))]
    scratch += sem_shapes(gather_sends(1, 2, True, False))
    return call(
        "forward", 0, body, (x, gains, biases, fc_bias, qkv, fc, out, proj, dy), [VM] * 9, outs, out_specs, scratch
    )


def norm_forward(values, gain, bias):
    centre = values - jnp.mean(values, axis=-1, keepdims=True)
    spread = lax.rsqrt(jnp.mean(centre * centre, axis=-1, keepdims=True) + EPS)
    normed = centre * spread
    return (normed * gain + bias, normed, spread)


def norm_back(grad_out, normed, spread, gain):
    scaled = grad_out * gain
    grad_in = spread * (
        scaled
        - jnp.mean(scaled, axis=-1, keepdims=True)
        - normed * jnp.mean(scaled * normed, axis=-1, keepdims=True)
    )
    return (grad_in, jnp.sum(grad_out * normed, axis=0), jnp.sum(grad_out, axis=0))


def gelu_tanh(values):
    return jax.nn.gelu(values, approximate=True)


def pad_to(x, axis, size):
    if x.shape[axis] == size:
        return x
    widths = [(0, 0)] * x.ndim
    widths[axis] = (0, size - x.shape[axis])
    return jnp.pad(x, widths)


def shards(lay, tokens, qkv_weight, proj_weight, fc_weight, out_weight, gains, biases, fc_bias, cotangent):
    n_ctx, n_dp = lay.n_ctx, lay.n_dp
    c = lax.axis_index("ctx")
    s = lax.axis_index("fsdp")
    t = lay.tp_index(c)
    unit = 2 * t + s
    T = tokens.shape[1]
    M = 8 * T
    R = D // n_ctx
    FB = FF // n_ctx
    FH = FB // 2
    W = HU * HEAD_DIM
    length = n_ctx * T

    def side(x, axis):
        return lax.dynamic_index_in_dim(x, s, axis, keepdims=False)

    x = tokens.reshape(T, D)
    dy = cotangent.reshape(T, D)
    n_dev = 2 * n_ctx
    (h1_all, w_qkv, heads, o, lse, ob, w_proj, x1, h2_all, fc_buf, out_buf, dy_all, fc_shift, par) = forward(
        lay, x, gains, biases, fc_bias.reshape(2, FH // 2), qkv_weight, fc_weight, out_weight, proj_weight, dy
    )
    q, k, v = heads[0], heads[1], heads[2]
    w_fc = fc_buf.reshape(D, n_dp * FH)
    w_out = out_buf.reshape(n_dp * FH, D)
    h1_rows = h1_all.reshape(M, D)
    h2_rows = h2_all.reshape(M, D)
    dy_rows = dy_all.reshape(M, D)
    gain_rows = par[:, 0]
    bias_rows = par[:, 1:4].reshape(6, D)
    _, hat_one, spread_one = norm_forward(x.astype(F32), gain_rows[0], bias_rows[0])
    _, hat_two, spread_two = norm_forward(x1, gain_rows[1], bias_rows[4])
    hidden_pre = dot(h2_rows, w_fc, NN) + fc_shift
    hidden, gelu_back = jax.vjp(gelu_tanh, hidden_pre)
    gb = hidden.astype(BF)
    mixed_part = dot(gb, w_out, NN).astype(BF).reshape(2, 4, T, D)
    du = gelu_back(dot(dy_rows, w_out, NT))[0].astype(BF)
    dh2_part = dot(du, w_fc, NT).astype(BF).reshape(2, 4, T, D)
    mixed_sum, dh2 = reduce_rows(lay, mixed_part, dh2_part)
    fc_grad = dot(h2_rows, du, TN).astype(BF).reshape(n_ctx, R, n_dp * FH)
    out_grad = dot(gb, dy_rows, TN).astype(BF).reshape(n_dp, FH, D)
    fc_bias_part = jnp.sum(du.astype(F32), axis=0)
    mixed = (x1 + mixed_sum.astype(F32) + bias_rows[5]).astype(BF)
    back_two, gain_two_g, bias_two_g = norm_back(dh2.astype(F32), hat_two, spread_two, gain_rows[1])
    dx1 = dy.astype(F32) + back_two
    da = dx1.astype(BF)
    proj_grad = jnp.stack([dot(ob, da[:, n * (D // 2) : (n + 1) * (D // 2)], TN) for n in range(2)])
    proj_grad = proj_grad.astype(BF).reshape(2, n_ctx, R, D // 2)
    proj_bias_g = jnp.sum(da.astype(F32), axis=0)
    dob = dot(w_proj[0], da[:, : D // 2], NT) + dot(w_proj[1], da[:, D // 2 :], NT)
    dob = dob.astype(BF).reshape(HEADS, HEAD_DIM, T)
    dob = exchange(
        lay,
        "tokens_to_heads",
        6,
        tokens_to_heads,
        None,
        dob,
        struct(2, n_ctx, HEAD_DIM, T),
        (HEADS, n_dev),
    )
    dob = jnp.transpose(dob, (0, 2, 1, 3)).reshape(2, HEAD_DIM, length)
    dq, dk, dv = attend_back(lay, q, k, v, o, lse, dob)
    grads = jnp.stack([dq, dk, dv]).reshape(3, 2, HEAD_DIM, n_ctx, T)
    grads = lay.from_natural(jnp.transpose(grads, (3, 0, 2, 1, 4)))
    grads = jnp.transpose(grads, (0, 2, 3, 4, 1, 5)).reshape(n_dp, QKV, M)
    dqkv = exchange(
        lay, "heads_to_group", 7, heads_to_group, data_partners, grads, struct(HU, QKV, M), (n_dp, HU)
    )
    dqkv = jnp.transpose(dqkv.reshape(HU, 3, HEAD_DIM, M), (1, 0, 2, 3)).reshape(3 * W, M)
    dh1_part = dot(dqkv, w_qkv, ((0,), (1,))).astype(BF).reshape(2, 4, T, D)
    qkv_grad = dot(h1_rows, dqkv, ((0,), (1,))).astype(BF).reshape(n_ctx, R, 3 * W)
    qkv_bias_part = jnp.sum(dqkv.astype(F32), axis=1)

    def unit_row(part):
        row = lax.dynamic_update_slice_in_dim(jnp.zeros((UNITS * W,), F32), part, unit * W, 0)
        return row[:D]

    dy_sum = jnp.sum(dy.astype(F32), axis=0)
    gains_part = jnp.stack([jnp.zeros((D,), F32), gain_two_g])
    biases_part = jnp.stack(
        [
            jnp.zeros((D,), F32),
            unit_row(qkv_bias_part[:W]),
            unit_row(qkv_bias_part[2 * W :]),
            proj_bias_g,
            bias_two_g,
            dy_sum,
        ]
    )
    parts = lay.from_natural(jnp.zeros((n_ctx, 2, FH), F32))
    mask = (jnp.arange(4)[None, :, None, None] == t) & (jnp.arange(2)[None, None, :, None] == s)
    parts = jnp.where(mask, fc_bias_part.reshape(n_dp, 1, 1, FH), parts)
    fc_bias_full = lay.to_natural(parts)
    small_parts = jnp.concatenate(
        [
            jnp.transpose(gains_part.reshape(2, n_ctx, R), (1, 0, 2)),
            jnp.transpose(biases_part.reshape(2, 3, n_ctx, R), (2, 0, 1, 3)).reshape(n_ctx, 2, 3 * R),
            fc_bias_full,
        ],
        axis=2,
    )
    small_parts = pad_to(small_parts, 2, 1024).reshape(n_dev, 8, 128)
    dh1, qkv_sum, fc_sum, out_sum, proj_sum, small_sum = reduce_grads(
        lay, dh1_part, qkv_grad, fc_grad, out_grad, proj_grad, small_parts
    )
    back_one, gain_one_g, bias_one_g = norm_back(dh1.astype(F32), hat_one, spread_one, gain_rows[0])
    input_grad = (dx1 + back_one).reshape(tokens.shape)
    first_rows = jnp.stack([gain_one_g, bias_one_g])
    first_rows = lax.psum(first_rows, ("ctx", "fsdp"))
    small_sum = jnp.sum(small_sum.reshape(n_dev, 1024), axis=0)
    own_cols = lax.dynamic_slice_in_dim(first_rows, c * R, R, 1)
    first_side = (s == 0).astype(F32)
    gains_out = (small_sum[:R] + own_cols[0] * first_side).reshape(1, R)
    biases_out = small_sum[R : 4 * R].reshape(3, R)
    biases_out = biases_out.at[0].add(own_cols[1] * first_side)
    fc_bias_out = small_sum[4 * R : 4 * R + FH]

    qkv_out = jnp.transpose(qkv_sum.reshape(2, 4, R, 3, W), (2, 3, 1, 0, 4))
    qkv_out = qkv_out.reshape(R, 3, UNITS * W)[:, :, :D].reshape(R, 2, 3 * D // 2)
    qkv_out = side(qkv_out, 1).astype(F32)
    fc_out = fc_sum.reshape(2, 4, R, n_dp, FH)
    fc_cols = []
    for b in range(n_ctx):
        for half in range(2):
            fc_cols.append(fc_sum[half, lay.tp_index(b), :, lay.dp_index(b) * FH : (lay.dp_index(b) + 1) * FH])
    half = n_ctx
    fc_out = jnp.where(
        s == 0, jnp.concatenate(fc_cols[:half], axis=1), jnp.concatenate(fc_cols[half:], axis=1)
    ).astype(F32)
    out_out = side(out_sum.reshape(FB, 2, D // 2), 1).astype(F32)
    proj_out = proj_sum.astype(F32)
    return (
        mixed.reshape(tokens.shape),
        input_grad,
        qkv_out,
        proj_out,
        fc_out,
        out_out,
        gains_out,
        biases_out,
        fc_bias_out,
    )


def solution(mesh):
    lay = Layout(mesh.shape["ctx"])
    in_specs = (
        P("fsdp", "ctx", None),
        P("ctx", "fsdp"),
        P("ctx", "fsdp"),
        P("ctx", "fsdp"),
        P("ctx", "fsdp"),
        P("fsdp", "ctx"),
        P("fsdp", "ctx"),
        P(("ctx", "fsdp")),
        P("fsdp", "ctx", None),
    )
    out_specs = (
        P("fsdp", "ctx", None),
        P("fsdp", "ctx", None),
        P("ctx", "fsdp"),
        P("ctx", "fsdp"),
        P("ctx", "fsdp"),
        P("ctx", "fsdp"),
        P("fsdp", "ctx"),
        P("fsdp", "ctx"),
        P(("ctx", "fsdp")),
    )
    return jax.shard_map(
        functools.partial(shards, lay), mesh=mesh, in_specs=in_specs, out_specs=out_specs, check_vma=False
    )
```

```python
import functools
import math

import jax
import jax.numpy as jnp
from jax import lax
from jax.experimental import pallas as pl
from jax.experimental.pallas import tpu as pltpu
from jax.sharding import PartitionSpec as P

D = 1600
HEADS = 25
HEAD_DIM = 64
FF = 6400
EPS = 1e-05
UNITS = 8
HU = -(-HEADS // UNITS)
QKV = 3 * HEAD_DIM
MESH = pl.DeviceIdType.MESH
BF = jnp.bfloat16
F32 = jnp.float32
VMEM_LIMIT = 60 * 1024 * 1024
LOG2E = 1.0 / math.log(2.0)


class Layout:
    def __init__(self, n_ctx):
        self.n_ctx = n_ctx
        a, b = n_ctx // 4, n_ctx // 2
        self.tp_bits = (a, b)
        self.dp_bits = tuple(1 << i for i in range(n_ctx.bit_length() - 3))
        self.n_dp = n_ctx // 4
        self.dp_order = list(zip(self.dp_bits, self.dp_bits[::-1]))
        self.tp_order = [(b, b), (a, a)]
        self.tp_masks = [[], [(a, a)], [(b, b)], [(a, a), (b, b)]]

    def tp_index(self, c):
        return sum(((c // b) % 2) * (1 << i) for i, b in enumerate(self.tp_bits))

    def dp_index(self, c):
        return sum(((c // b) % 2) * (1 << i) for i, b in enumerate(self.dp_bits))

    def compose(self, t, d):
        return sum(((t // (1 << i)) % 2) * b for i, b in enumerate(self.tp_bits)) + sum(
            ((d // (1 << i)) % 2) * b for i, b in enumerate(self.dp_bits)
        )

    def head_rank(self, h):
        u, j = h // HU, h % HU
        return self.compose(u // 2, j) * 2 + u % 2

    def to_natural(self, x):
        labels = list(self.dp_bits[::-1]) + list(self.tp_bits[::-1])
        k = len(labels)
        rest = x.shape[2:]
        x = x.reshape((2,) * k + rest)
        order = sorted(range(k), key=lambda i: -labels[i])
        x = jnp.transpose(x, order + list(range(k, k + len(rest))))
        return x.reshape((self.n_ctx,) + rest)

    def from_natural(self, x):
        labels = list(self.dp_bits[::-1]) + list(self.tp_bits[::-1])
        k = len(labels)
        rest = x.shape[1:]
        x = x.reshape((2,) * k + rest)
        natural = sorted(labels, reverse=True)
        order = [natural.index(b) for b in labels]
        x = jnp.transpose(x, order + list(range(k, k + len(rest))))
        return x.reshape((self.n_dp, 4) + rest)


def flip(c, sym, s):
    def one(b):
        return c + b * (1 - 2 * ((c // b) % 2))

    if sym[0] == sym[1]:
        return one(sym[0])
    return one(sym[0]) * (1 - s) + one(sym[1]) * s


def flips(c, masks, s):
    for sym in masks:
        c = flip(c, sym, s)
    return c


class Env:
    def __init__(self, layout):
        self.lay = layout
        self.c = lax.axis_index("ctx")
        self.s = lax.axis_index("fsdp")
        self.t = layout.tp_index(self.c)
        self.d = layout.dp_index(self.c)
        self.rank = self.c * 2 + self.s
        self.n_dev = layout.n_ctx * 2

    def other(self):
        return (self.c, 1 - self.s)


class Links:
    def __init__(self, sems):
        self.send_sems, self.recv_sems, self.local_sems = sems
        self.count = 0
        self.local_count = 0
        self.sent = []
        self.locals = []

    def send(self, src, dst, device):
        copy = pltpu.make_async_remote_copy(
            src_ref=src,
            dst_ref=dst,
            send_sem=self.send_sems.at[self.count],
            recv_sem=self.recv_sems.at[self.count],
            device_id=device,
            device_id_type=MESH,
        )
        copy.start()
        self.count += 1
        self.sent.append(copy)
        return copy

    def local(self, src, dst):
        copy = pltpu.make_async_copy(src, dst, self.local_sems.at[self.local_count])
        copy.start()
        self.local_count += 1
        self.locals.append(copy)
        return copy

    def finish(self):
        for copy in self.locals:
            copy.wait()
        for copy in self.sent:
            copy.wait_send()


def sem_shapes(sends, local=1):
    sends = max(sends, 1)
    return [
        pltpu.SemaphoreType.DMA((sends,)),
        pltpu.SemaphoreType.DMA((sends,)),
        pltpu.SemaphoreType.DMA((local,)),
    ]


def meet(env, devices):
    barrier = pltpu.get_barrier_semaphore()
    for device in devices:
        pl.semaphore_signal(barrier, inc=1, device_id=device, device_id_type=MESH)
    pl.semaphore_wait(barrier, len(devices))


def meet_all(env):
    barrier = pltpu.get_barrier_semaphore()

    def hail(i, carry):
        rank = (env.rank + i) % env.n_dev
        pl.semaphore_signal(barrier, inc=1, device_id=(rank // 2, rank % 2), device_id_type=MESH)
        return carry

    lax.fori_loop(1, env.n_dev, hail, 0)
    pl.semaphore_wait(barrier, env.n_dev - 1)


def tp_partners(env):
    return [(flips(env.c, m, env.s), env.s) for m in env.lay.tp_masks[1:]]


def dp_partners(env):
    return [(flip(env.c, sym, env.s), env.s) for sym in env.lay.dp_order]


def run(generators):
    active = list(generators)
    while active:
        left = []
        for g in active:
            try:
                next(g)
                left.append(g)
            except StopIteration:
                pass
        active = left


def gather_sends(have, bits, core, rows):
    return (3 if rows else 0) + have * ((1 << bits) - 1) + (have << bits if core else 0)


def gather(env, src, buf, sems, bits, slot, core=False, rows=False):
    c, s = env.c, env.s
    links = Links(sems)

    def place(masks):
        index = slot(flips(c, masks, s))
        return buf.at[s, index] if core else buf.at[index]

    own = src.at[env.t] if rows else src
    links.local(own, place([]))
    levels = [[([], None)]] + [[] for _ in bits]
    if rows:
        for m in env.lay.tp_masks[1:]:
            there = flips(c, m, s)
            copy = links.send(src.at[env.lay.tp_index(there)], place([]), (there, s))
            levels[0].append((m, copy))
    crossing = []
    for k in range(len(bits) + 1):
        for masks, copy in levels[k]:
            if copy is None:
                ref = own
            else:
                copy.wait_recv()
                ref = place(masks)
            for j in range(k, len(bits)):
                forward = links.send(ref, place(masks), (flip(c, bits[j], s), s))
                levels[j + 1].append((masks + [bits[j]], forward))
            if core:
                crossing.append(links.send(ref, place(masks), env.other()))
            yield
    for copy in crossing:
        copy.wait_recv()
    links.finish()
    yield


def reduce_sends(have, bits, core, rows, halves):
    return (have << bits if core else 0) + have * ((1 << bits) - 1) + (3 + 4 if rows else 0) + (1 if halves else 0)


def reduce_scratch(have, bits, core, block):
    counts = [have << j for j in range(bits + (1 if core else 0))]
    return [pltpu.VMEM((n,) + block, BF) for n in counts]


def reduce(env, inp, out, parts, sems, bits, slot, core=False, rows=False, halves=False):
    c, s = env.c, env.s
    links = Links(sems)
    levels = [list(env.lay.tp_masks) if rows else [[]]]
    for sym in bits:
        levels.append(levels[-1] + [m + [sym] for m in levels[-1]])

    def at(side, masks):
        index = slot(flips(c, masks, side))
        return inp.at[side, index] if core else inp.at[index]

    last = levels[-1]
    now = [at(s, m) for m in last]
    copies = {}
    if core:
        stage = len(bits)
        for i in reversed(range(len(last))):
            copies[i] = links.send(at(1 - s, last[i]), parts[stage].at[i], env.other())
    else:
        stage = len(bits) - 1
        n = len(levels[stage])
        for i in reversed(range(n)):
            copies[i] = links.send(now[n + i], parts[stage].at[i], (flip(c, bits[stage], s), s))
    yield
    while stage >= 0:
        n = len(levels[stage])
        got = parts[stage]
        after = {}
        for i in reversed(range(n)):
            copies[i].wait_recv()
            got[i] = got[i] + now[i][...]
            if stage > 0 and i >= n // 2:
                after[i - n // 2] = links.send(
                    got.at[i], parts[stage - 1].at[i - n // 2], (flip(c, bits[stage - 1], s), s)
                )
            yield
        now = [got.at[i] for i in range(n)]
        copies = after
        stage -= 1
    if rows:
        arrivals = []
        links.local(now[0], out.at[s, env.t])
        arrivals.append((env.t, None, now[0]))
        for i, m in enumerate(env.lay.tp_masks):
            if i > 0:
                there = flips(c, m, s)
                copy = links.send(now[i], out.at[s, env.t], (there, s))
                index = env.lay.tp_index(there)
                arrivals.append((index, copy, out.at[s, index]))
        yield
        crossing = []
        for index, copy, ref in arrivals:
            if copy is not None:
                copy.wait_recv()
            crossing.append(links.send(ref, out.at[s, index], env.other()))
            yield
        for copy in crossing:
            copy.wait_recv()
    elif halves:
        links.local(now[0], out.at[s])
        copy = links.send(now[0], out.at[s], env.other())
        yield
        copy.wait_recv()
    else:
        out[...] = now[0][...].astype(out.dtype)
    links.finish()
    yield


def to_everyone(env, src, out, sems, same):
    send_sems, recv_sems, local_sems = sems

    def own(ref):
        return ref if same else ref.at[env.rank]

    def copy(i):
        rank = (env.rank + i) % env.n_dev
        return pltpu.make_async_remote_copy(
            src_ref=src if same else src.at[rank],
            dst_ref=out.at[env.rank],
            send_sem=send_sems.at[i],
            recv_sem=recv_sems.at[i],
            device_id=(rank // 2, rank % 2),
            device_id_type=MESH,
        )

    def begin(i, carry):
        copy(i).start()
        return carry

    def end(i, carry):
        copy(i).wait()
        return carry

    lax.fori_loop(1, env.n_dev, begin, 0)
    local = pltpu.make_async_copy(own(src), out.at[env.rank], local_sems.at[0])
    local.start()
    yield
    lax.fori_loop(1, env.n_dev, end, 0)
    local.wait()
    yield


def own_head(env):
    h = (env.t * 2 + env.s) * HU + env.d
    return h, jnp.logical_and(env.d < HU, h < HEADS)


def tokens_to_heads(env, src, out, sems):
    send_sems, recv_sems, local_sems = sems
    h, active = own_head(env)
    lay = env.lay

    def copy(j):
        rank = lay.head_rank(j)
        return rank, pltpu.make_async_remote_copy(
            src_ref=src.at[j],
            dst_ref=out.at[env.s, env.c],
            send_sem=send_sems.at[j],
            recv_sem=recv_sems.at[(rank - env.rank + env.n_dev) % env.n_dev],
            device_id=(rank // 2, rank % 2),
            device_id_type=MESH,
        )

    def begin(i, carry):
        rank, cp = copy((env.rank + i) % HEADS)

        @pl.when(rank != env.rank)
        def _():
            cp.start()

        return carry

    lax.fori_loop(0, HEADS, begin, 0)
    yield

    @pl.when(active)
    def _():
        local = pltpu.make_async_copy(src.at[h], out.at[env.s, env.c], local_sems.at[0])
        local.start()
        local.wait()

        def receive(i, carry):
            rank = (env.rank - i + env.n_dev) % env.n_dev
            pltpu.make_async_remote_copy(
                src_ref=src.at[0],
                dst_ref=out.at[rank % 2, rank // 2],
                send_sem=send_sems.at[0],
                recv_sem=recv_sems.at[i],
                device_id=env.other(),
                device_id_type=MESH,
            ).wait_recv()
            return carry

        lax.fori_loop(1, env.n_dev, receive, 0)

    def end(j, carry):
        rank, cp = copy(j)

        @pl.when(rank != env.rank)
        def _():
            cp.wait_send()

        return carry

    lax.fori_loop(0, HEADS, end, 0)


def data_partners(env):
    lay = env.lay
    return [(lay.compose(env.t, (env.d + i) % lay.n_dp), env.s) for i in range(1, lay.n_dp)]


ANY = pl.BlockSpec(memory_space=pl.ANY)
VM = pl.BlockSpec(memory_space=pltpu.VMEM)


def struct(*shape, dtype=BF):
    return jax.ShapeDtypeStruct(shape, dtype)


def call(name, cid, body, args, in_specs, outs, out_specs, scratch):
    return pl.pallas_call(
        body,
        out_shape=outs,
        in_specs=in_specs,
        out_specs=out_specs,
        scratch_shapes=scratch,
        compiler_params=pltpu.CompilerParams(
            collective_id=cid, has_side_effects=True, vmem_limit_bytes=VMEM_LIMIT
        ),
        name=name,
    )(*args)


def dot(left, right, dims):
    return lax.dot_general(left, right, (dims, ((), ())), preferred_element_type=F32)


NN = ((1,), (0,))
NT = ((1,), (1,))
TN = ((0,), (0,))
SCALE = 1.0 / math.sqrt(HEAD_DIM)
TILE = 512


class Background:
    def __init__(self):
        self.active = []

    def add(self, generator):
        self.active.append(generator)

    def step(self, count=1):
        for _ in range(count):
            if not self.active:
                return
            g = self.active.pop(0)
            try:
                next(g)
                self.active.append(g)
            except StopIteration:
                pass

    def finish(self):
        while self.active:
            self.step()


def finish(generator):
    for _ in generator:
        pass


def group_to_heads(env, src, out, sems, q):
    send_sems, recv_sems, local_sems = sems
    lay = env.lay

    def copy(j, source, target):
        return pltpu.make_async_remote_copy(
            src_ref=src.at[q, j],
            dst_ref=out.at[q, source],
            send_sem=send_sems.at[q, j],
            recv_sem=recv_sems.at[q, source],
            device_id=(lay.compose(env.t, target), env.s),
            device_id_type=MESH,
        )

    for i in range(1, HU + 1):
        j = (env.d + i) % HU

        @pl.when(j != env.d)
        def _():
            copy(j, env.d, j).start()

    local = pltpu.make_async_copy(src.at[q, env.d % HU], out.at[q, env.d], local_sems.at[q])

    @pl.when(env.d < HU)
    def _():
        local.start()

    yield

    @pl.when(env.d < HU)
    def _():
        local.wait()
        for i in range(1, lay.n_dp):
            source = (env.d + i) % lay.n_dp
            copy(0, source, source).wait_recv()

    yield
    for j in range(HU):

        @pl.when(j != env.d)
        def _():
            copy(j, env.d, j).wait_send()


def heads_out(env, src, out, sems, q):
    send_sems, recv_sems, local_sems = sems
    h, active = own_head(env)
    n_ctx = env.lay.n_ctx

    def copy(i):
        there = (env.c + i) % n_ctx
        return pltpu.make_async_remote_copy(
            src_ref=src.at[q, there],
            dst_ref=out.at[h],
            send_sem=send_sems.at[q, i],
            recv_sem=recv_sems.at[h],
            device_id=(there, q),
            device_id_type=MESH,
        )

    local = pltpu.make_async_copy(src.at[q, env.c], out.at[h], local_sems.at[q])
    mine = jnp.logical_and(active, env.s == q)
    theirs = jnp.logical_and(active, env.s != q)

    def begin(i, carry):
        copy(i).start()
        return carry

    def end(i, carry):
        copy(i).wait_send()
        return carry

    @pl.when(mine)
    def _():
        local.start()

    @pl.when(theirs)
    def _():
        copy(0).start()

    @pl.when(active)
    def _():
        lax.fori_loop(1, n_ctx, begin, 0)

    yield

    @pl.when(mine)
    def _():
        local.wait()

    @pl.when(theirs)
    def _():
        copy(0).wait_send()

    @pl.when(active)
    def _():
        lax.fori_loop(1, n_ctx, end, 0)


def heads_in(env, src, out, sems):
    def receive(j, carry):
        @pl.when(env.lay.head_rank(j) != env.rank)
        def _():
            pltpu.make_async_remote_copy(
                src_ref=src.at[0, 0],
                dst_ref=out.at[j],
                send_sem=sems[0].at[0, 0],
                recv_sem=sems[1].at[j],
                device_id=env.other(),
                device_id_type=MESH,
            ).wait_recv()

        return carry

    lax.fori_loop(0, HEADS, receive, 0)


def norm_stats(values):
    centre = values - jnp.mean(values, axis=-1, keepdims=True)
    spread = lax.rsqrt(jnp.mean(centre * centre, axis=-1, keepdims=True) + EPS)
    return centre * spread, spread


def attend_tile(i, tile, qt, keys, v_ref):
    def step(j, carry, masked):
        peak, total, acc = carry
        at = pl.ds(pl.multiple_of(j * tile, tile), tile)
        st = dot(keys[at, :], qt, NN) * (SCALE * LOG2E)
        if masked:
            row = lax.broadcasted_iota(jnp.int32, (tile, tile), 0)
            col = lax.broadcasted_iota(jnp.int32, (tile, tile), 1)
            st = jnp.where(row <= col, st, -1e30)
        new = jnp.maximum(peak, jnp.max(st, axis=0, keepdims=True))
        p = jnp.exp2(st - new)
        shrink = jnp.exp2(peak - new)
        total = total * shrink + jnp.sum(p, axis=0, keepdims=True)
        acc = acc * shrink + dot(v_ref[:, at], p.astype(BF), NN)
        return new, total, acc

    start = (
        jnp.full((1, tile), -1e30, F32),
        jnp.zeros((1, tile), F32),
        jnp.zeros((HEAD_DIM, tile), F32),
    )
    carry = start
    if i > 0:
        carry = lax.fori_loop(0, i, functools.partial(step, masked=False), carry)
    peak, total, acc = step(i, carry, True)
    return acc / total, peak + jnp.log2(total)


def forward(lay, x, gains, biases, fc_bias, qkv, fc, out, proj, dy):
    n_ctx, n_dp = lay.n_ctx, lay.n_dp
    n_dev = 2 * n_ctx
    k = len(lay.dp_bits)
    T = x.shape[0]
    R, FB = D // n_ctx, FF // n_ctx
    FH = FB // 2
    W = HU * HEAD_DIM
    G = 4 * T
    length = n_ctx * T
    tile = min(TILE, length)
    n_tiles = length // tile
    half = D // 2
    wide = UNITS * W

    def natural(c):
        return c

    def body(*refs):
        (x_r, gains_r, biases_r, fcb_r, qkv_r, fc_r, out_r, proj_r, dy_r) = refs[:9]
        (h1_o, wq_o, heads_o, o_o, lse_o, ob_o, pj_o, x1_o, h2_o, fc_o, out_o, dy_o, shift_o, par_o) = refs[9:23]
        (
            pack, small, qkv_x, fc_x, out_x, qkv_s, fc_s, out_s, wq_b, h1_s, par_w,
            parts, mine, keys, o_low, ob_b, proj_b, h2_s,
        ) = refs[23:41]
        sems = refs[41:]
        groups = [sems[3 * i : 3 * i + 3] for i in range(len(sems) // 3)]
        env = Env(lay)
        s = env.s

        pack[...] = jnp.zeros_like(pack)
        pack[0:1, :R] = gains_r[...].astype(F32)
        pack[1:4, :R] = biases_r[...].astype(F32)
        pack[4:6, : FH // 2] = fcb_r[...].astype(F32)
        meet_all(env)
        links = Links(groups[0])
        crossing = [
            links.send(a, b, env.other()) for a, b in ((qkv_r, qkv_x), (fc_r, fc_x), (out_r, out_x))
        ]
        everyone = to_everyone(env, pack, small, groups[1], True)
        next(everyone)
        hat, _ = norm_stats(x_r[...].astype(F32))

        def fill_qkv(a, b, side):
            q = a[:, :D]
            keys_all = jnp.concatenate([a[:, D:], b[:, : D // 2]], axis=1)
            v = b[:, D // 2 :]
            for u in range(4):
                first = (2 * u + side) * W
                width = max(0, min(W, D - first))
                for n, part in enumerate((q, keys_all, v)):
                    if width < W:
                        qkv_s[u, :, n * W : (n + 1) * W] = jnp.zeros((R, W), BF)
                    if width > 0:
                        qkv_s[u, :, n * W : n * W + width] = part[:, first : first + width]

        def fill_rest(a, b, oa, ob, side):
            for u in range(4):
                for d in range(n_dp):
                    first = lay.compose(u, d) * FB + side * FH
                    source, first = (a, first) if first < FF // 2 else (b, first - FF // 2)
                    fc_s[u, :, d * FH : (d + 1) * FH] = source[:, first : first + FH]
            out_s[:, :half] = oa[side * FH : (side + 1) * FH, :]
            out_s[:, half:] = ob[side * FH : (side + 1) * FH, :]

        def by_side(f, own, other):
            @pl.when(s == 0)
            def _():
                f(*own_other(own, other), 0)

            @pl.when(s == 1)
            def _():
                f(*own_other(other, own), 1)

        def own_other(first, second):
            return [r for pair in zip(first, second) for r in pair]

        crossing[0].wait_recv()
        by_side(fill_qkv, (qkv_r,), (qkv_x,))
        weights = gather(env, qkv_s, wq_b, groups[2], lay.dp_order, natural, rows=True)
        next(weights)
        finish(everyone)
        for f in range(2):
            rows = jnp.concatenate([small[2 * c + f][:, :R] for c in range(n_ctx)], axis=1)
            par_o[f] = rows
        par_w[...] = jnp.zeros_like(par_w)
        par_w[:, :D] = par_o[0]
        h1_s[...] = (hat * par_o[0, 0:1, :] + par_o[0, 1:2, :]).astype(BF)
        rows_h1 = gather(env, h1_s, h1_o, groups[3], lay.tp_order, lay.tp_index, core=True)
        next(rows_h1)
        shift_parts = []
        for d in range(n_dp):
            block = small[lay.compose(env.t, d) * 2 + s]
            shift_parts += [block[4:5, : FH // 2], block[5:6, : FH // 2]]
        shift_o[...] = jnp.concatenate(shift_parts, axis=1)
        run([weights, rows_h1])
        crossing[1].wait_recv()
        crossing[2].wait_recv()
        by_side(fill_rest, (fc_r, out_r), (fc_x, out_x))
        bg = Background()
        bg.add(gather(env, dy_r, dy_o, groups[4], lay.tp_order, lay.tp_index, core=True))
        bg.add(gather(env, fc_s, fc_o, groups[5], lay.dp_order, natural, rows=True))
        bg.step(2)
        for c in range(n_ctx):
            wq_o[c * R : (c + 1) * R, :] = wq_b[c]
        unit = 2 * env.t + s
        cols = pl.ds(pl.multiple_of(unit * W, W), W)
        shift = jnp.concatenate(
            [par_w[2:3, cols], jnp.zeros((1, W), F32), par_w[3:4, cols]], axis=1
        )
        moving = []
        for q in range(2):
            rows = h1_o[q].reshape(G, D)
            made = (dot(rows, wq_o[...], NN) + shift).astype(BF).T
            for n in range(3):
                for j in range(HU):
                    first = n * W + j * HEAD_DIM
                    parts[q, j, n * HEAD_DIM : (n + 1) * HEAD_DIM, :] = made[first : first + HEAD_DIM]
            g = group_to_heads(env, parts, mine, groups[6], q)
            next(g)
            moving.append(g)
        bg.add(gather(env, proj_r, proj_b, groups[7], lay.tp_order + lay.dp_order, natural, core=True))
        bg.add(gather(env, out_s, out_o, groups[8], lay.dp_order, lay.dp_index))
        bg.step(4)
        leaving = []
        for q in range(2):
            next(moving[q])
            for c in range(n_ctx):
                tc, dc = lay.tp_index(c), lay.dp_index(c)
                for n in range(3):
                    heads_o[n, q, :, c * T : (c + 1) * T] = mine[
                        q, dc, n * HEAD_DIM : (n + 1) * HEAD_DIM, tc * T : (tc + 1) * T
                    ]
            keys[...] = heads_o[1, q].T
            for i in range(n_tiles):
                at = slice(i * tile, (i + 1) * tile)
                o, lse = attend_tile(i, tile, heads_o[0, q, :, at], keys, heads_o.at[2, q])
                o_o[q, :, at] = o
                lse_o[q, :, at] = lse
                low = o.astype(BF)
                for b in range(tile // T):
                    o_low[q, i * (tile // T) + b] = low[:, b * T : (b + 1) * T]
                bg.step(3)
            g = heads_out(env, o_low, ob_b, groups[9], q)
            next(g)
            leaving.append(g)
        bg.finish()
        for g in moving + leaving:
            finish(g)
        for n in range(2):
            for c in range(n_ctx):
                pj_o[n, c * R : (c + 1) * R, :] = proj_b[n, c]
        heads_in(env, o_low, ob_b, groups[9])
        ob_o[...] = ob_b[...].reshape(D, T).T
        branch = jnp.concatenate([dot(ob_o[...], pj_o[n], NN) for n in range(2)], axis=1)
        x1 = x_r[...].astype(F32) + branch + par_o[1, 1:2, :]
        x1_o[...] = x1
        hat, _ = norm_stats(x1)
        h2_s[...] = (hat * par_o[1, 0:1, :] + par_o[1, 2:3, :]).astype(BF)
        finish(gather(env, h2_s, h2_o, groups[10], lay.tp_order, lay.tp_index, core=True))
        links.finish()

    outs = [
        struct(2, 4, T, D),
        struct(D, 3 * W),
        struct(3, 2, HEAD_DIM, length),
        struct(2, HEAD_DIM, length, dtype=F32),
        struct(2, 1, length, dtype=F32),
        struct(T, D),
        struct(2, D, half),
        struct(T, D, dtype=F32),
        struct(2, 4, T, D),
        struct(n_ctx, R, n_dp * FH),
        struct(n_dp, FH, D),
        struct(2, 4, T, D),
        struct(1, n_dp * FH, dtype=F32),
        struct(2, 8, D, dtype=F32),
    ]
    out_specs = [VM] * 8 + [ANY] * 4 + [VM] * 2
    scratch = [
        pltpu.VMEM((8, 128), F32),
        pltpu.VMEM((n_dev, 8, 128), F32),
        pltpu.VMEM(qkv.shape, BF),
        pltpu.VMEM(fc.shape, BF),
        pltpu.VMEM(out.shape, BF),
        pltpu.VMEM((4, R, 3 * W), BF),
        pltpu.VMEM((4, R, n_dp * FH), BF),
        pltpu.VMEM((FH, D), BF),
        pltpu.VMEM((n_ctx, R, 3 * W), BF),
        pltpu.VMEM((T, D), BF),
        pltpu.VMEM((8, wide), F32),
        pltpu.VMEM((2, HU, QKV, G), BF),
        pltpu.VMEM((2, n_dp, QKV, G), BF),
        pltpu.VMEM((length, HEAD_DIM), BF),
        pltpu.VMEM((2, n_ctx, HEAD_DIM, T), BF),
        pltpu.VMEM((HEADS, HEAD_DIM, T), BF),
        pltpu.VMEM((2, n_ctx, R, half), BF),
        pltpu.VMEM((T, D), BF),
    ]
    DMA = pltpu.SemaphoreType.DMA
    scratch += sem_shapes(3) + sem_shapes(n_dev)
    scratch += sem_shapes(gather_sends(4, k, False, True))
    scratch += sem_shapes(gather_sends(1, 2, True, False)) * 2
    scratch += sem_shapes(gather_sends(4, k, False, True))
    scratch += [DMA((2, HU)), DMA((2, n_dp)), DMA((2,))]
    scratch += sem_shapes(gather_sends(1, k + 2, True, False))
    scratch += sem_shapes(gather_sends(1, k, False, False))
    scratch += [DMA((2, n_ctx)), DMA((HEADS,)), DMA((2,))]
    scratch += sem_shapes(gather_sends(1, 2, True, False))
    return call(
        "forward", 0, body, (x, gains, biases, fc_bias, qkv, fc, out, proj, dy), [VM] * 9, outs, out_specs, scratch
    )


def drive(generator, background):
    for _ in generator:
        background.step()


def by_side(s, f):
    for side in range(2):

        @pl.when(s == side)
        def _():
            f(side)


def middle(lay, x, h2, dy_all, fc, out, shift, x1, dy, pj, par):
    n_ctx, n_dp = lay.n_ctx, lay.n_dp
    n_dev = 2 * n_ctx
    k = len(lay.dp_bits)
    T = x.shape[0]
    R, FB = D // n_ctx, FF // n_ctx
    FH = FB // 2
    U = n_dp * FH
    G = 4 * T
    half = D // 2
    chunk = 2 * T

    def natural(c):
        return c

    def body(*refs):
        (h2_r, dya_r, fc_r, out_r, pj_r, shift_r, x1_r, dy_r, par_r) = refs[:9]
        (mixed_o, dx1_o, dob_o, fc_o, out_o, vec_o, fcb_o) = refs[9:16]
        (
            h2_v, dy_v, fc_b, fc_w, out_b, out_w, pj_v, gb_v, du_v, back_p, dh2_v, mix_v, dob_s, fc_v, out_v,
        ) = refs[16:31]
        rest = refs[31:]
        plan = [
            (0, 3, 3),
            (1, 3, 3),
            (2, k, 3),
            (3, k, 3),
        ]
        spans, first = [], 0
        for _, n, m in plan:
            spans.append((rest[first : first + n], rest[first + n : first + n + m]))
            first += n + m
        sems = rest[first:]
        env = Env(lay)
        s = env.s
        loads = Links((None, None, sems[3]))
        load = {}
        for name, a, b in (
            ("h2", h2_r, h2_v),
            ("fc", fc_r, fc_b),
            ("dy", dya_r, dy_v),
            ("out", out_r, out_b),
            ("pj", pj_r, pj_v),
        ):
            load[name] = loads.local(a, b)
        meet_all(env)
        load["fc"].wait()
        for c in range(n_ctx):
            fc_w[c * R : (c + 1) * R, :] = fc_b[c]
        load["out"].wait()
        for d in range(n_dp):
            out_w[d * FH : (d + 1) * FH, :] = out_b[d]
        load["h2"].wait()
        load["dy"].wait()

        def forth_and_back(q):
            @pl.loop(0, G // chunk)
            def _(i):
                rows = h2_v[q, pl.ds(2 * i, 2)].reshape(chunk, D)
                u = dot(rows, fc_w[...], NN) + shift_r[...]
                square = u * u
                th = jnp.tanh(math.sqrt(2 / math.pi) * (u + 0.044715 * square * u))
                up = 0.5 * (1.0 + th)
                at = pl.ds(pl.multiple_of(i * chunk, chunk), chunk)
                gb_v[q, at, :] = (u * up).astype(BF)
                slope = up + (0.5 * math.sqrt(2 / math.pi)) * u * (1.0 - th * th) * (
                    1.0 + (3 * 0.044715) * square
                )
                dact = dot(dy_v[q, pl.ds(2 * i, 2)].reshape(chunk, D), out_w[...], NT)
                du = (dact * slope).astype(BF)
                du_v[q, at, :] = du
                back = dot(du, fc_w[...], NT).astype(BF)
                back_p[q, pl.ds(2 * i, 2)] = back.reshape(2, T, D)

        forth_and_back(1 - s)
        rows = reduce(env, back_p, dh2_v, *spans[0], lay.tp_order, lay.tp_index, core=True)
        next(rows)
        forth_and_back(s)
        next(rows)
        bg = Background()
        for d in range(n_dp):
            left = gb_v[:, :, d * FH : (d + 1) * FH].reshape(2 * G, FH)
            out_b[d] = dot(left, dy_v[...].reshape(2 * G, D), TN).astype(BF)
        bg.add(reduce(env, out_b, out_v, *spans[3], lay.dp_order, lay.dp_index, halves=True))
        bg.step()
        next(rows)
        for c in range(0, n_ctx, 4):
            left = h2_v[:, :, :, c * R : (c + 4) * R].reshape(2 * G, 4 * R)
            made = dot(left, du_v[...].reshape(2 * G, U), TN).astype(BF)
            for i in range(4):
                fc_b[c + i] = made[i * R : (i + 1) * R, :]
        bg.add(reduce(env, fc_b, fc_v, *spans[2], lay.dp_order, natural, rows=True))
        bg.step()
        for _ in range(2):
            next(rows)
        fcb_o[...] = jnp.sum(du_v[...].reshape(2 * G, U).astype(F32), axis=0, keepdims=True)
        x1 = x1_r[...]
        hat, spread = norm_stats(x1)
        dy_own = dy_r[...].astype(F32)
        vec_o[...] = jnp.zeros_like(vec_o)
        vec_o[3:4, :] = jnp.sum(dy_own, axis=0, keepdims=True)
        for _ in range(2):
            next(rows)
        for q in range(2):

            @pl.loop(0, G // chunk)
            def _(i):
                at = pl.ds(pl.multiple_of(i * chunk, chunk), chunk)
                part = dot(gb_v[q, at, :], out_w[...], NN).astype(BF)
                h2_v[q, pl.ds(2 * i, 2)] = part.reshape(2, T, D)

        finish(rows)
        dh2 = dh2_v[...].astype(F32)
        scaled = dh2 * par_r[1, 0:1, :]
        dx1 = dy_own + spread * (
            scaled
            - jnp.mean(scaled, axis=-1, keepdims=True)
            - hat * jnp.mean(scaled * hat, axis=-1, keepdims=True)
        )
        dx1_o[...] = dx1
        da = dx1.astype(BF)
        load["pj"].wait()
        dob = dot(da[:, :half], pj_v[0], NT) + dot(da[:, half:], pj_v[1], NT)
        dob_s[...] = dob.astype(BF).T.reshape(HEADS, HEAD_DIM, T)
        heads = tokens_to_heads(env, dob_s, dob_o, sems[0:3])
        next(heads)
        mixing = reduce(env, h2_v, mix_v, *spans[1], lay.tp_order, lay.tp_index, core=True)
        next(mixing)
        bg.add(mixing)
        vec_o[0:1, :] = jnp.sum(dh2 * hat, axis=0, keepdims=True)
        vec_o[1:2, :] = jnp.sum(da.astype(F32), axis=0, keepdims=True)
        vec_o[2:3, :] = jnp.sum(dh2, axis=0, keepdims=True)
        bg.finish()
        finish(heads)
        mixed_o[...] = (x1 + mix_v[...].astype(F32) + par_r[1, 3:4, :]).astype(BF)

        def last(side):
            pieces = []
            for c in range(n_ctx // 2 * side, n_ctx // 2 * (side + 1)):
                for h in range(2):
                    first = lay.dp_index(c) * FH
                    pieces.append(fc_v[h, lay.tp_index(c)][:, first : first + FH])
            fc_o[...] = jnp.concatenate(pieces, axis=1).astype(F32)
            out_o[...] = jnp.concatenate(
                [out_v[h][:, side * half : (side + 1) * half] for h in range(2)], axis=0
            ).astype(F32)

        by_side(s, last)

    outs = [
        struct(T, D),
        struct(T, D, dtype=F32),
        struct(2, n_ctx, HEAD_DIM, T),
        struct(R, FF // 2, dtype=F32),
        struct(FB, half, dtype=F32),
        struct(8, D, dtype=F32),
        struct(1, U, dtype=F32),
    ]
    scratch = [
        pltpu.VMEM((2, 4, T, D), BF),
        pltpu.VMEM((2, 4, T, D), BF),
        pltpu.VMEM((n_ctx, R, U), BF),
        pltpu.VMEM((D, U), BF),
        pltpu.VMEM((n_dp, FH, D), BF),
        pltpu.VMEM((U, D), BF),
        pltpu.VMEM((2, D, half), BF),
        pltpu.VMEM((2, G, U), BF),
        pltpu.VMEM((2, G, U), BF),
        pltpu.VMEM((2, 4, T, D), BF),
        pltpu.VMEM((T, D), BF),
        pltpu.VMEM((T, D), BF),
        pltpu.VMEM((HEADS, HEAD_DIM, T), BF),
        pltpu.VMEM((2, 4, R, U), BF),
        pltpu.VMEM((2, FH, D), BF),
    ]
    for _ in range(2):
        scratch += reduce_scratch(1, 2, True, (T, D)) + sem_shapes(reduce_sends(1, 2, True, False, False))
    scratch += reduce_scratch(4, k, False, (R, U)) + sem_shapes(reduce_sends(4, k, False, True, False))
    scratch += reduce_scratch(1, k, False, (FH, D)) + sem_shapes(reduce_sends(1, k, False, False, True))
    DMA = pltpu.SemaphoreType.DMA
    scratch += [DMA((HEADS,)), DMA((n_dev,)), DMA((1,)), DMA((5,))]
    args = (h2, dy_all, fc, out, pj, shift, x1, dy, par)
    out_specs = [VM] * 2 + [ANY] + [VM] * 4
    return call("middle", 1, body, args, [ANY] * 5 + [VM] * 4, outs, out_specs, scratch)


def heads_to_group(env, src, out, sems, q):
    send_sems, recv_sems, local_sems = sems
    lay = env.lay

    def copy(there, j, target):
        return pltpu.make_async_remote_copy(
            src_ref=src.at[q, there],
            dst_ref=out.at[q, j],
            send_sem=send_sems.at[q, there],
            recv_sem=recv_sems.at[q, j],
            device_id=(lay.compose(env.t, target), env.s),
            device_id_type=MESH,
        )

    local = pltpu.make_async_copy(src.at[q, env.d], out.at[q, env.d % HU], local_sems.at[q])

    @pl.when(env.d < HU)
    def _():
        for i in range(1, lay.n_dp):
            there = (env.d + i) % lay.n_dp
            copy(there, env.d, there).start()
        local.start()

    yield

    @pl.when(env.d < HU)
    def _():
        local.wait()

    for j in range(HU):

        @pl.when(j != env.d)
        def _():
            copy(0, j, j).wait_recv()

    yield

    @pl.when(env.d < HU)
    def _():
        for i in range(1, lay.n_dp):
            there = (env.d + i) % lay.n_dp
            copy(there, env.d, there).wait_send()


def backward(lay, x, heads, o, lse, dob, wq, h1, ob, vec, fcb, dx1, par):
    n_ctx, n_dp = lay.n_ctx, lay.n_dp
    n_dev = 2 * n_ctx
    k = len(lay.dp_bits)
    T = x.shape[0]
    R, FB = D // n_ctx, FF // n_ctx
    FH = FB // 2
    W = HU * HEAD_DIM
    G = 4 * T
    half = D // 2
    length = n_ctx * T
    tile = TILE if length <= 4 * TILE else TILE // 2
    n_tiles = length // tile
    wide = UNITS * W

    def natural(c):
        return c

    def body(*refs):
        (x_r, heads_r, o_r, lse_r, dob_r, wq_r, h1_r, ob_r, vec_r, fcb_r, dx1_r, par_r) = refs[:12]
        (grad_o, qkv_o, proj_o, small_o) = refs[12:16]
        (
            heads_v, o_v, dob_n, qs, dobs, delta, dq_acc, parts, land, dqkv, dh1_p, dh1_v, q_g, q_v, wide_v,
            small_s, small_v, pg,
        ) = refs[16:34]
        rest = refs[34:]
        spans, first = [], 0
        for n in (3, k, k + 3):
            spans.append((rest[first : first + n], rest[first + n : first + n + 3]))
            first += n + 3
        sems = rest[first:]
        env = Env(lay)
        s = env.s
        meet_all(env)
        bg = Background()
        for n in range(2):
            right = dx1_r[:, n * half : (n + 1) * half].astype(BF)
            for c in range(0, n_ctx, 4):
                made = dot(ob_r[:, c * R : (c + 4) * R], right, TN).astype(BF)
                for i in range(4):
                    pg[n, c + i] = made[i * R : (i + 1) * R, :]
        bg.add(reduce(env, pg, proj_o, *spans[2], lay.tp_order + lay.dp_order, natural, core=True))
        bg.step()
        small_s[...] = jnp.zeros_like(small_s)
        wide_v[...] = jnp.zeros_like(wide_v)
        moving = []
        _, active = own_head(env)

        def loads(q):
            copies = [pltpu.make_async_copy(heads_r.at[n, q], heads_v.at[n], sems[6].at[n]) for n in range(3)]
            copies.append(pltpu.make_async_copy(o_r.at[q], o_v, sems[6].at[3]))
            for c in range(n_ctx):
                copies.append(
                    pltpu.make_async_copy(
                        dob_r.at[q, c], dob_n.at[:, pl.ds(c * T, T)], sems[6].at[4 + c]
                    )
                )
            return copies

        for copy in loads(0):
            copy.start()
        for q in range(2):
            for copy in loads(q):
                copy.wait()

            @pl.when(jnp.logical_not(active))
            def _():
                dob_n[...] = jnp.zeros_like(dob_n)

            qs[...] = heads_v[0].T
            dobs[...] = dob_n[...].T
            delta[...] = jnp.sum(dob_n[...].astype(F32) * o_v[...], axis=0, keepdims=True)
            dq_acc[...] = jnp.zeros_like(dq_acc)

            def put(n, first, block):
                for b in range(block.shape[1] // T):
                    c = first // T + b
                    tc, dc = lay.tp_index(c), lay.dp_index(c)
                    parts[q, dc, n * HEAD_DIM : (n + 1) * HEAD_DIM, tc * T : (tc + 1) * T] = block[
                        :, b * T : (b + 1) * T
                    ]

            for j in range(n_tiles):
                here = slice(j * tile, (j + 1) * tile)
                kt = heads_v[1, :, here]
                keys = kt.T
                values = heads_v[2, :, here].T

                def step(i, carry, masked):
                    dk, dv = carry
                    at = pl.ds(pl.multiple_of(i * tile, tile), tile)
                    st = dot(keys, heads_v[0, :, at], NN) * (SCALE * LOG2E)
                    p = jnp.exp2(st - lse_r[q, :, at])
                    if masked:
                        row = lax.broadcasted_iota(jnp.int32, (tile, tile), 0)
                        col = lax.broadcasted_iota(jnp.int32, (tile, tile), 1)
                        p = jnp.where(row <= col, p, 0.0)
                    dp = dot(values, dob_n[:, at], NN)
                    ds = (p * (dp - delta[:, at])).astype(BF)
                    dv = dv + dot(p.astype(BF), dobs[at, :], NN)
                    dk = dk + dot(ds, qs[at, :], NN)
                    dq_acc[:, at] += dot(kt, ds, NN)
                    return dk, dv

                zero = jnp.zeros((tile, HEAD_DIM), F32)
                carry = step(j, (zero, zero), True)
                if j + 1 < n_tiles:
                    carry = lax.fori_loop(j + 1, n_tiles, functools.partial(step, masked=False), carry)
                put(1, j * tile, (carry[0] * SCALE).T.astype(BF))
                put(2, j * tile, carry[1].T.astype(BF))
                bg.step(4)
            put(0, 0, (dq_acc[...] * SCALE).astype(BF))
            if q == 0:
                for copy in loads(1):
                    copy.start()
            g = heads_to_group(env, parts, land, sems[0:3], q)
            next(g)
            moving.append(g)
        for q in range(2):
            next(moving[q])
            rows = []
            for n in range(3):
                for j in range(HU):
                    rows.append(land[q, j, n * HEAD_DIM : (n + 1) * HEAD_DIM, :])
            dqkv[q] = jnp.concatenate(rows, axis=0).T
            dh1_p[q] = dot(dqkv[q], wq_r[...], NT).astype(BF).reshape(4, T, D)
        rows_h1 = reduce(env, dh1_p, dh1_v, *spans[0], lay.tp_order, lay.tp_index, core=True)
        next(rows_h1)
        for c in range(0, n_ctx, 4):
            left = h1_r[:, :, :, c * R : (c + 4) * R].reshape(2 * G, 4 * R)
            made = dot(left, dqkv[...].reshape(2 * G, 3 * W), TN).astype(BF)
            for i in range(4):
                q_g[c + i] = made[i * R : (i + 1) * R, :]
        grads = reduce(env, q_g, q_v, *spans[1], lay.dp_order, natural, rows=True)
        next(grads)
        bg.add(grads)
        unit = 2 * env.t + s
        sums = jnp.sum(dqkv[0].astype(F32), axis=0, keepdims=True) + jnp.sum(
            dqkv[1].astype(F32), axis=0, keepdims=True
        )
        cols = pl.ds(pl.multiple_of(unit * W, W), W)
        wide_v[2:3, cols] = sums[:, :W]
        wide_v[3:4, cols] = sums[:, 2 * W :]
        hat, spread = norm_stats(x_r[...].astype(F32))
        drive(rows_h1, bg)
        dh1 = dh1_v[...].astype(F32)
        scaled = dh1 * par_r[0, 0:1, :]
        grad_o[...] = dx1_r[...] + spread * (
            scaled
            - jnp.mean(scaled, axis=-1, keepdims=True)
            - hat * jnp.mean(scaled * hat, axis=-1, keepdims=True)
        )
        wide_v[0:1, :D] = jnp.sum(dh1 * hat, axis=0, keepdims=True)
        wide_v[1:2, :D] = jnp.sum(dh1, axis=0, keepdims=True)
        for c in range(n_ctx):
            small_s[2 * c, 0:4, :R] = wide_v[0:4, c * R : (c + 1) * R]
            small_s[2 * c + 1, 0:4, :R] = vec_r[0:4, c * R : (c + 1) * R]
        for d in range(n_dp):
            owner = lay.compose(env.t, d) * 2 + s
            for h in range(2):
                first = d * FH + h * (FH // 2)
                small_s[owner, 4 + h : 5 + h, : FH // 2] = fcb_r[:, first : first + FH // 2]
        everyone = to_everyone(env, small_s, small_v, sems[3:6], False)
        next(everyone)
        bg.finish()
        for g in moving:
            finish(g)

        def last(side):
            parts_all = []
            for n in range(3):
                pieces = [q_v[h, u][:, n * W : (n + 1) * W] for u in range(4) for h in range(2)]
                parts_all.append(jnp.concatenate(pieces, axis=1)[:, :D])
            whole = jnp.concatenate(parts_all, axis=1)
            qkv_o[...] = whole[:, side * (3 * half) : (side + 1) * (3 * half)].astype(F32)

        by_side(s, last)
        finish(everyone)
        total = small_v[0]
        for r in range(1, n_dev):
            total = total + small_v[r]
        small_o[...] = total

    outs = [
        struct(T, D, dtype=F32),
        struct(R, 3 * half, dtype=F32),
        struct(R, half, dtype=F32),
        struct(8, 128, dtype=F32),
    ]
    scratch = [
        pltpu.VMEM((3, HEAD_DIM, length), BF),
        pltpu.VMEM((HEAD_DIM, length), F32),
        pltpu.VMEM((HEAD_DIM, length), BF),
        pltpu.VMEM((length, HEAD_DIM), BF),
        pltpu.VMEM((length, HEAD_DIM), BF),
        pltpu.VMEM((1, length), F32),
        pltpu.VMEM((HEAD_DIM, length), F32),
        pltpu.VMEM((2, n_dp, QKV, G), BF),
        pltpu.VMEM((2, HU, QKV, G), BF),
        pltpu.VMEM((2, G, 3 * W), BF),
        pltpu.VMEM((2, 4, T, D), BF),
        pltpu.VMEM((T, D), BF),
        pltpu.VMEM((n_ctx, R, 3 * W), BF),
        pltpu.VMEM((2, 4, R, 3 * W), BF),
        pltpu.VMEM((8, wide), F32),
        pltpu.VMEM((n_dev, 8, 128), F32),
        pltpu.VMEM((n_dev, 8, 128), F32),
        pltpu.VMEM((2, n_ctx, R, half), BF),
    ]
    scratch += reduce_scratch(1, 2, True, (T, D)) + sem_shapes(reduce_sends(1, 2, True, False, False))
    scratch += reduce_scratch(4, k, False, (R, 3 * W)) + sem_shapes(reduce_sends(4, k, False, True, False))
    scratch += reduce_scratch(1, k + 2, True, (R, half)) + sem_shapes(
        reduce_sends(1, k + 2, True, False, False)
    )
    DMA = pltpu.SemaphoreType.DMA
    scratch += [DMA((2, n_dp)), DMA((2, HU)), DMA((2,))] + sem_shapes(n_dev) + [DMA((4 + n_ctx,))]
    args = (x, heads, o, lse, dob, wq, h1, ob, vec, fcb, dx1, par)
    in_specs = [VM, ANY, ANY, VM, ANY] + [VM] * 7
    return call("backward", 2, body, args, in_specs, outs, [VM] * 4, scratch)


def shards(lay, tokens, qkv_weight, proj_weight, fc_weight, out_weight, gains, biases, fc_bias, cotangent):
    T = tokens.shape[1]
    R = D // lay.n_ctx
    FH = FF // lay.n_ctx // 2
    x = tokens.reshape(T, D)
    dy = cotangent.reshape(T, D)
    (h1, wq, heads, o, lse, ob, pj, x1, h2, fc, out, dy_all, shift, par) = forward(
        lay, x, gains, biases, fc_bias.reshape(2, FH // 2), qkv_weight, fc_weight, out_weight, proj_weight, dy
    )
    mixed, dx1, dob, fc_grad, out_grad, vec, fcb = middle(
        lay, x, h2, dy_all, fc, out, shift, x1, dy, pj, par
    )
    input_grad, qkv_grad, proj_grad, small = backward(lay, x, heads, o, lse, dob, wq, h1, ob, vec, fcb, dx1, par)
    return (
        mixed.reshape(tokens.shape),
        input_grad.reshape(tokens.shape),
        qkv_grad,
        proj_grad,
        fc_grad,
        out_grad,
        small[0:1, :R],
        small[1:4, :R],
        small[4:6, : FH // 2].reshape(FH),
    )


def solution(mesh):
    lay = Layout(mesh.shape["ctx"])
    in_specs = (
        P("fsdp", "ctx", None),
        P("ctx", "fsdp"),
        P("ctx", "fsdp"),
        P("ctx", "fsdp"),
        P("ctx", "fsdp"),
        P("fsdp", "ctx"),
        P("fsdp", "ctx"),
        P(("ctx", "fsdp")),
        P("fsdp", "ctx", None),
    )
    out_specs = (
        P("fsdp", "ctx", None),
        P("fsdp", "ctx", None),
        P("ctx", "fsdp"),
        P("ctx", "fsdp"),
        P("ctx", "fsdp"),
        P("ctx", "fsdp"),
        P("fsdp", "ctx"),
        P("fsdp", "ctx"),
        P(("ctx", "fsdp")),
    )
    return jax.shard_map(
        functools.partial(shards, lay), mesh=mesh, in_specs=in_specs, out_specs=out_specs, check_vma=False
    )
```

```python
import functools
import math

import jax
import jax.numpy as jnp
from jax import lax
from jax.experimental import pallas as pl
from jax.experimental.pallas import tpu as pltpu
from jax.sharding import PartitionSpec as P

D = 1600
HEADS = 25
HEAD_DIM = 64
FF = 6400
EPS = 1e-05
UNITS = 8
HU = -(-HEADS // UNITS)
QKV = 3 * HEAD_DIM
MESH = pl.DeviceIdType.MESH
BF = jnp.bfloat16
F32 = jnp.float32
VMEM_LIMIT = 60 * 1024 * 1024
LOG2E = 1.0 / math.log(2.0)


class Layout:
    def __init__(self, n_ctx):
        self.n_ctx = n_ctx
        a, b = n_ctx // 4, n_ctx // 2
        self.tp_bits = (a, b)
        self.dp_bits = tuple(1 << i for i in range(n_ctx.bit_length() - 3))
        self.n_dp = n_ctx // 4
        self.dp_order = list(zip(self.dp_bits, self.dp_bits[::-1]))
        self.tp_order = [(b, b), (a, a)]
        self.tp_masks = [[], [(a, a)], [(b, b)], [(a, a), (b, b)]]

    def tp_index(self, c):
        return sum(((c // b) % 2) * (1 << i) for i, b in enumerate(self.tp_bits))

    def dp_index(self, c):
        return sum(((c // b) % 2) * (1 << i) for i, b in enumerate(self.dp_bits))

    def compose(self, t, d):
        return sum(((t // (1 << i)) % 2) * b for i, b in enumerate(self.tp_bits)) + sum(
            ((d // (1 << i)) % 2) * b for i, b in enumerate(self.dp_bits)
        )

    def head_rank(self, h):
        u, j = h // HU, h % HU
        return self.compose(u // 2, j) * 2 + u % 2

    def to_natural(self, x):
        labels = list(self.dp_bits[::-1]) + list(self.tp_bits[::-1])
        k = len(labels)
        rest = x.shape[2:]
        x = x.reshape((2,) * k + rest)
        order = sorted(range(k), key=lambda i: -labels[i])
        x = jnp.transpose(x, order + list(range(k, k + len(rest))))
        return x.reshape((self.n_ctx,) + rest)

    def from_natural(self, x):
        labels = list(self.dp_bits[::-1]) + list(self.tp_bits[::-1])
        k = len(labels)
        rest = x.shape[1:]
        x = x.reshape((2,) * k + rest)
        natural = sorted(labels, reverse=True)
        order = [natural.index(b) for b in labels]
        x = jnp.transpose(x, order + list(range(k, k + len(rest))))
        return x.reshape((self.n_dp, 4) + rest)


def flip(c, sym, s):
    def one(b):
        return c + b * (1 - 2 * ((c // b) % 2))

    if sym[0] == sym[1]:
        return one(sym[0])
    return one(sym[0]) * (1 - s) + one(sym[1]) * s


def flips(c, masks, s):
    for sym in masks:
        c = flip(c, sym, s)
    return c


class Env:
    def __init__(self, layout):
        self.lay = layout
        self.c = lax.axis_index("ctx")
        self.s = lax.axis_index("fsdp")
        self.t = layout.tp_index(self.c)
        self.d = layout.dp_index(self.c)
        self.rank = self.c * 2 + self.s
        self.n_dev = layout.n_ctx * 2

    def other(self):
        return (self.c, 1 - self.s)


class Links:
    def __init__(self, sems):
        self.send_sems, self.recv_sems, self.local_sems = sems
        self.count = 0
        self.local_count = 0
        self.sent = []
        self.locals = []

    def send(self, src, dst, device):
        copy = pltpu.make_async_remote_copy(
            src_ref=src,
            dst_ref=dst,
            send_sem=self.send_sems.at[self.count],
            recv_sem=self.recv_sems.at[self.count],
            device_id=device,
            device_id_type=MESH,
        )
        copy.start()
        self.count += 1
        self.sent.append(copy)
        return copy

    def local(self, src, dst):
        copy = pltpu.make_async_copy(src, dst, self.local_sems.at[self.local_count])
        copy.start()
        self.local_count += 1
        self.locals.append(copy)
        return copy

    def finish(self):
        for copy in self.locals:
            copy.wait()
        for copy in self.sent:
            copy.wait_send()


def sem_shapes(sends, local=1):
    sends = max(sends, 1)
    return [
        pltpu.SemaphoreType.DMA((sends,)),
        pltpu.SemaphoreType.DMA((sends,)),
        pltpu.SemaphoreType.DMA((local,)),
    ]


def meet(env, devices):
    barrier = pltpu.get_barrier_semaphore()
    for device in devices:
        pl.semaphore_signal(barrier, inc=1, device_id=device, device_id_type=MESH)
    pl.semaphore_wait(barrier, len(devices))


def hail_all(env):
    barrier = pltpu.get_barrier_semaphore()

    def hail(i, carry):
        rank = (env.rank + i) % env.n_dev
        pl.semaphore_signal(barrier, inc=1, device_id=(rank // 2, rank % 2), device_id_type=MESH)
        return carry

    lax.fori_loop(1, env.n_dev, hail, 0)


def meet_all(env):
    pl.semaphore_wait(pltpu.get_barrier_semaphore(), env.n_dev - 1)


def tp_partners(env):
    return [(flips(env.c, m, env.s), env.s) for m in env.lay.tp_masks[1:]]


def dp_partners(env):
    return [(flip(env.c, sym, env.s), env.s) for sym in env.lay.dp_order]


def run(generators):
    active = list(generators)
    while active:
        left = []
        for g in active:
            try:
                next(g)
                left.append(g)
            except StopIteration:
                pass
        active = left


def gather_sends(have, bits, core, rows):
    return (3 if rows else 0) + have * ((1 << bits) - 1) + (have << bits if core else 0)


def gather(env, src, buf, sems, bits, slot, core=False, rows=False, half=None):
    c, s = env.c, env.s
    links = Links(sems)

    def place(masks):
        index = slot(flips(c, masks, s))
        return buf.at[s, index] if core else buf.at[index]

    own = src.at[env.t] if rows else src
    links.local(own, place([]))
    levels = [[([], None)]] + [[] for _ in bits]
    if rows:
        for m in env.lay.tp_masks[1:]:
            there = flips(c, m, s)
            copy = links.send(src.at[env.lay.tp_index(there)], place([]), (there, s))
            levels[0].append((m, copy))
    crossing = []
    for k in range(len(bits) + 1):
        for masks, copy in levels[k]:
            if copy is None:
                ref = own
            else:
                copy.wait_recv()
                ref = place(masks)
            for j in range(k, len(bits)):
                forward = links.send(ref, place(masks), (flip(c, bits[j], s), s))
                levels[j + 1].append((masks + [bits[j]], forward))
            if core:
                crossing.append(links.send(ref, place(masks), env.other()))
            if half is not None:
                there = half.at[slot(flips(c, masks, s))]
                crossing.append(links.send(ref.at[1 - s], there, env.other()))
            yield
    for copy in crossing:
        copy.wait_recv()
    links.finish()
    yield


def reduce_sends(have, bits, core, rows, halves):
    return (have << bits if core else 0) + have * ((1 << bits) - 1) + (3 + 4 if rows else 0) + (1 if halves else 0)


def reduce_scratch(have, bits, core, block):
    counts = [have << j for j in range(bits + (1 if core else 0))]
    return [pltpu.VMEM((n,) + block, BF) for n in counts]


def reduce(env, inp, out, parts, sems, bits, slot, core=False, rows=False, halves=False, own=None):
    c, s = env.c, env.s
    links = Links(sems)
    levels = [list(env.lay.tp_masks) if rows else [[]]]
    for sym in bits:
        levels.append(levels[-1] + [m + [sym] for m in levels[-1]])

    def at(side, masks):
        index = slot(flips(c, masks, side))
        return inp.at[side, index] if core else inp.at[index]

    last = levels[-1]
    if own is None:
        now = [at(s, m) for m in last]
    else:
        now = [own.at[slot(flips(c, m, s))] for m in last]
    copies = {}
    if core:
        stage = len(bits)
        for i in reversed(range(len(last))):
            copies[i] = links.send(at(1 - s, last[i]), parts[stage].at[i], env.other())
    else:
        stage = len(bits) - 1
        n = len(levels[stage])
        for i in reversed(range(n)):
            copies[i] = links.send(now[n + i], parts[stage].at[i], (flip(c, bits[stage], s), s))
    yield
    while stage >= 0:
        n = len(levels[stage])
        got = parts[stage]
        after = {}
        for i in reversed(range(n)):
            copies[i].wait_recv()
            got[i] = got[i] + now[i][...]
            if stage > 0 and i >= n // 2:
                after[i - n // 2] = links.send(
                    got.at[i], parts[stage - 1].at[i - n // 2], (flip(c, bits[stage - 1], s), s)
                )
            yield
        now = [got.at[i] for i in range(n)]
        copies = after
        stage -= 1
    if rows:
        arrivals = []
        links.local(now[0], out.at[s, env.t])
        arrivals.append((env.t, None, now[0]))
        for i, m in enumerate(env.lay.tp_masks):
            if i > 0:
                there = flips(c, m, s)
                copy = links.send(now[i], out.at[s, env.t], (there, s))
                index = env.lay.tp_index(there)
                arrivals.append((index, copy, out.at[s, index]))
        yield
        crossing = []
        for index, copy, ref in arrivals:
            if copy is not None:
                copy.wait_recv()
            crossing.append(links.send(ref, out.at[s, index], env.other()))
            yield
        for copy in crossing:
            copy.wait_recv()
    elif halves:
        links.local(now[0], out.at[s])
        copy = links.send(now[0], out.at[s], env.other())
        yield
        copy.wait_recv()
    else:
        out[...] = now[0][...].astype(out.dtype)
    links.finish()
    yield


def to_everyone(env, src, out, sems, same):
    send_sems, recv_sems, local_sems = sems

    def own(ref):
        return ref if same else ref.at[env.rank]

    def copy(i):
        rank = (env.rank + i) % env.n_dev
        return pltpu.make_async_remote_copy(
            src_ref=src if same else src.at[rank],
            dst_ref=out.at[env.rank],
            send_sem=send_sems.at[i],
            recv_sem=recv_sems.at[i],
            device_id=(rank // 2, rank % 2),
            device_id_type=MESH,
        )

    def begin(i, carry):
        copy(i).start()
        return carry

    def end(i, carry):
        copy(i).wait()
        return carry

    lax.fori_loop(1, env.n_dev, begin, 0)
    local = pltpu.make_async_copy(own(src), out.at[env.rank], local_sems.at[0])
    local.start()
    yield
    lax.fori_loop(1, env.n_dev, end, 0)
    local.wait()
    yield


def own_head(env):
    h = (env.t * 2 + env.s) * HU + env.d
    return h, jnp.logical_and(env.d < HU, h < HEADS)


def tokens_to_heads(env, src, out, sems):
    send_sems, recv_sems, local_sems = sems
    h, active = own_head(env)
    lay = env.lay

    def copy(j):
        rank = lay.head_rank(j)
        return rank, pltpu.make_async_remote_copy(
            src_ref=src.at[j],
            dst_ref=out.at[env.s, env.c],
            send_sem=send_sems.at[j],
            recv_sem=recv_sems.at[(rank - env.rank + env.n_dev) % env.n_dev],
            device_id=(rank // 2, rank % 2),
            device_id_type=MESH,
        )

    def begin(i, carry):
        rank, cp = copy((env.rank + i) % HEADS)

        @pl.when(rank != env.rank)
        def _():
            cp.start()

        return carry

    lax.fori_loop(0, HEADS, begin, 0)
    yield

    @pl.when(active)
    def _():
        local = pltpu.make_async_copy(src.at[h], out.at[env.s, env.c], local_sems.at[0])
        local.start()
        local.wait()

        def receive(i, carry):
            rank = (env.rank - i + env.n_dev) % env.n_dev
            pltpu.make_async_remote_copy(
                src_ref=src.at[0],
                dst_ref=out.at[rank % 2, rank // 2],
                send_sem=send_sems.at[0],
                recv_sem=recv_sems.at[i],
                device_id=env.other(),
                device_id_type=MESH,
            ).wait_recv()
            return carry

        lax.fori_loop(1, env.n_dev, receive, 0)

    def end(j, carry):
        rank, cp = copy(j)

        @pl.when(rank != env.rank)
        def _():
            cp.wait_send()

        return carry

    lax.fori_loop(0, HEADS, end, 0)


def data_partners(env):
    lay = env.lay
    return [(lay.compose(env.t, (env.d + i) % lay.n_dp), env.s) for i in range(1, lay.n_dp)]


ANY = pl.BlockSpec(memory_space=pl.ANY)
VM = pl.BlockSpec(memory_space=pltpu.VMEM)


def struct(*shape, dtype=BF):
    return jax.ShapeDtypeStruct(shape, dtype)


def call(name, cid, body, args, in_specs, outs, out_specs, scratch):
    return pl.pallas_call(
        body,
        out_shape=outs,
        in_specs=in_specs,
        out_specs=out_specs,
        scratch_shapes=scratch,
        compiler_params=pltpu.CompilerParams(
            collective_id=cid, has_side_effects=True, vmem_limit_bytes=VMEM_LIMIT
        ),
        name=name,
    )(*args)


def dot(left, right, dims):
    return lax.dot_general(left, right, (dims, ((), ())), preferred_element_type=F32)


NN = ((1,), (0,))
NT = ((1,), (1,))
TN = ((0,), (0,))
SCALE = 1.0 / math.sqrt(HEAD_DIM)
TILE = 512


class Background:
    def __init__(self):
        self.active = []

    def add(self, generator):
        self.active.append(generator)

    def step(self, count=1):
        for _ in range(count):
            if not self.active:
                return
            g = self.active.pop(0)
            try:
                next(g)
                self.active.append(g)
            except StopIteration:
                pass

    def finish(self):
        while self.active:
            self.step()


def finish(generator):
    for _ in generator:
        pass


def group_to_heads(env, src, out, sems, q):
    send_sems, recv_sems, local_sems = sems
    lay = env.lay

    def copy(j, source, target):
        return pltpu.make_async_remote_copy(
            src_ref=src.at[q, j],
            dst_ref=out.at[q, source],
            send_sem=send_sems.at[q, j],
            recv_sem=recv_sems.at[q, source],
            device_id=(lay.compose(env.t, target), env.s),
            device_id_type=MESH,
        )

    for i in range(1, HU + 1):
        j = (env.d + i) % HU

        @pl.when(j != env.d)
        def _():
            copy(j, env.d, j).start()

    local = pltpu.make_async_copy(src.at[q, env.d % HU], out.at[q, env.d], local_sems.at[q])

    @pl.when(env.d < HU)
    def _():
        local.start()

    yield

    @pl.when(env.d < HU)
    def _():
        local.wait()
        for i in range(1, lay.n_dp):
            source = (env.d + i) % lay.n_dp
            copy(0, source, source).wait_recv()

    yield
    for j in range(HU):

        @pl.when(j != env.d)
        def _():
            copy(j, env.d, j).wait_send()


def heads_out(env, src, out, sems, q):
    send_sems, recv_sems, local_sems = sems
    h, active = own_head(env)
    n_ctx = env.lay.n_ctx

    def copy(i):
        there = (env.c + i) % n_ctx
        return pltpu.make_async_remote_copy(
            src_ref=src.at[q, there],
            dst_ref=out.at[h],
            send_sem=send_sems.at[q, i],
            recv_sem=recv_sems.at[h],
            device_id=(there, q),
            device_id_type=MESH,
        )

    local = pltpu.make_async_copy(src.at[q, env.c], out.at[h], local_sems.at[q])
    mine = jnp.logical_and(active, env.s == q)
    theirs = jnp.logical_and(active, env.s != q)

    def begin(i, carry):
        copy(i).start()
        return carry

    def end(i, carry):
        copy(i).wait_send()
        return carry

    @pl.when(mine)
    def _():
        local.start()

    @pl.when(theirs)
    def _():
        copy(0).start()

    @pl.when(active)
    def _():
        lax.fori_loop(1, n_ctx, begin, 0)

    yield

    @pl.when(mine)
    def _():
        local.wait()

    @pl.when(theirs)
    def _():
        copy(0).wait_send()

    @pl.when(active)
    def _():
        lax.fori_loop(1, n_ctx, end, 0)


def heads_in(env, src, out, sems):
    def receive(j, carry):
        @pl.when(env.lay.head_rank(j) != env.rank)
        def _():
            pltpu.make_async_remote_copy(
                src_ref=src.at[0, 0],
                dst_ref=out.at[j],
                send_sem=sems[0].at[0, 0],
                recv_sem=sems[1].at[j],
                device_id=env.other(),
                device_id_type=MESH,
            ).wait_recv()

        return carry

    lax.fori_loop(0, HEADS, receive, 0)


def norm_stats(values):
    centre = values - jnp.mean(values, axis=-1, keepdims=True)
    spread = lax.rsqrt(jnp.mean(centre * centre, axis=-1, keepdims=True) + EPS)
    return centre * spread, spread


def attend_tile(i, tile, qt, keys, v_ref):
    def step(j, carry, masked):
        peak, total, acc = carry
        at = pl.ds(pl.multiple_of(j * tile, tile), tile)
        st = dot(keys[at, :], qt, NN) * (SCALE * LOG2E)
        if masked:
            row = lax.broadcasted_iota(jnp.int32, (tile, tile), 0)
            col = lax.broadcasted_iota(jnp.int32, (tile, tile), 1)
            st = jnp.where(row <= col, st, -1e30)
        new = jnp.maximum(peak, jnp.max(st, axis=0, keepdims=True))
        p = jnp.exp2(st - new)
        shrink = jnp.exp2(peak - new)
        total = total * shrink + jnp.sum(p, axis=0, keepdims=True)
        acc = acc * shrink + dot(v_ref[:, at], p.astype(BF), NN)
        return new, total, acc

    start = (
        jnp.full((1, tile), -1e30, F32),
        jnp.zeros((1, tile), F32),
        jnp.zeros((HEAD_DIM, tile), F32),
    )
    carry = start
    if i > 0:
        carry = lax.fori_loop(0, i, functools.partial(step, masked=False), carry)
    peak, total, acc = step(i, carry, True)
    return acc / total, peak + jnp.log2(total)


def forward(lay, x, gains, biases, fc_bias, qkv, fc, out, proj, dy):
    n_ctx, n_dp = lay.n_ctx, lay.n_dp
    n_dev = 2 * n_ctx
    k = len(lay.dp_bits)
    T = x.shape[0]
    R, FB = D // n_ctx, FF // n_ctx
    FH = FB // 2
    W = HU * HEAD_DIM
    G = 4 * T
    length = n_ctx * T
    tile = min(TILE, length)
    n_tiles = length // tile
    half = D // 2
    wide = UNITS * W

    def natural(c):
        return c

    def body(*refs):
        (x_r, gains_r, biases_r, fcb_r, qkv_r, fc_r, out_r, proj_r, dy_r) = refs[:9]
        (h1_o, wq_o, heads_o, o_o, pj_o, h2_o, fc_o, out_o, outx_o, dy_o, lse_o, ob_o, x1_o, shift_o, par_o) = refs[9:24]
        (
            pack, small, qkv_x, fc_x, qkv_s, fc_s, out_s, wq_b, wq_v, x_v, h1_v, par_w,
            parts, mine, keys, heads_v, o_v, o_low, ob_b, proj_b, pj_v, h2_s,
        ) = refs[24:46]
        sems = refs[46:]
        groups = [sems[3 * i : 3 * i + 3] for i in range(len(sems) // 3)]
        env = Env(lay)
        s = env.s

        hail_all(env)
        pack[...] = jnp.zeros_like(pack)
        pack[0:1, :R] = gains_r[...].astype(F32)
        pack[1:4, :R] = biases_r[...].astype(F32)
        pack[4:6, : FH // 2] = fcb_r[...].astype(F32)
        for h in range(2):
            out_s[h] = out_r[h * FH : (h + 1) * FH, :]
        par_w[...] = jnp.zeros_like(par_w)
        meet_all(env)
        links = Links(groups[0])
        crossing = [links.send(a, b, env.other()) for a, b in ((qkv_r, qkv_x), (fc_r, fc_x))]
        rows_x = gather(env, x_r, x_v, groups[3], lay.tp_order, lay.tp_index, core=True)
        next(rows_x)
        everyone = to_everyone(env, pack, small, groups[1], True)
        next(everyone)
        bg = Background()
        bg.add(gather(env, out_s, out_o, groups[8], lay.dp_order, lay.dp_index, half=outx_o))
        bg.step()

        def fill_qkv(a, b, side):
            q = a[:, :D]
            keys_all = jnp.concatenate([a[:, D:], b[:, : D // 2]], axis=1)
            v = b[:, D // 2 :]
            for u in range(4):
                first = (2 * u + side) * W
                width = max(0, min(W, D - first))
                for n, part in enumerate((q, keys_all, v)):
                    if width < W:
                        qkv_s[u, :, n * W : (n + 1) * W] = jnp.zeros((R, W), BF)
                    if width > 0:
                        qkv_s[u, :, n * W : n * W + width] = part[:, first : first + width]

        def fill_fc(a, b, side):
            for u in range(4):
                for d in range(n_dp):
                    first = lay.compose(u, d) * FB + side * FH
                    source, first = (a, first) if first < FF // 2 else (b, first - FF // 2)
                    fc_s[u, :, d * FH : (d + 1) * FH] = source[:, first : first + FH]

        crossing[0].wait_recv()
        by_side(s, lambda side: fill_qkv(*((qkv_r, qkv_x) if side == 0 else (qkv_x, qkv_r)), side))
        weights = gather(env, qkv_s, wq_b, groups[2], lay.dp_order, natural, rows=True)
        next(weights)
        crossing[1].wait_recv()
        by_side(s, lambda side: fill_fc(*((fc_r, fc_x) if side == 0 else (fc_x, fc_r)), side))
        finish(everyone)
        for f in range(2):
            rows = jnp.concatenate([small[2 * c + f][:, :R] for c in range(n_ctx)], axis=1)
            par_o[f] = rows
        par_w[:, :D] = par_o[0]
        shift_parts = []
        for d in range(n_dp):
            block = small[lay.compose(env.t, d) * 2 + s]
            shift_parts += [block[4:5, : FH // 2], block[5:6, : FH // 2]]
        shift_o[...] = jnp.concatenate(shift_parts, axis=1)
        steps(weights, 3)
        bg.step()
        steps(rows_x, 1)
        steps(weights, 4)
        bg.step(2)
        finish(rows_x)
        proj = gather(env, proj_r, proj_b, groups[7], lay.tp_order + lay.dp_order, natural, core=True)
        next(proj)
        bg.add(gather(env, fc_s, fc_o, groups[5], lay.dp_order, natural, rows=True))
        bg.step(2)

        @pl.loop(0, 8)
        def _(i):
            hat, _ = norm_stats(x_v[i // 4, i % 4].astype(F32))
            h1_v[i // 4, i % 4] = (hat * par_o[0, 0:1, :] + par_o[0, 1:2, :]).astype(BF)

        finish(weights)
        for c in range(n_ctx):
            wq_v[c * R : (c + 1) * R, :] = wq_b[c]
        leave = Links((None, None, groups[11][2]))
        leave.local(h1_v, h1_o)
        leave.local(wq_v, wq_o)
        unit = 2 * env.t + s
        cols = pl.ds(pl.multiple_of(unit * W, W), W)
        shift = jnp.concatenate(
            [par_w[2:3, cols], jnp.zeros((1, W), F32), par_w[3:4, cols]], axis=1
        )
        moving = []
        for q in range(2):
            rows = h1_v[q].reshape(G, D)
            made = (dot(rows, wq_v[...], NN) + shift).astype(BF).T
            for n in range(3):
                for j in range(HU):
                    first = n * W + j * HEAD_DIM
                    parts[q, j, n * HEAD_DIM : (n + 1) * HEAD_DIM, :] = made[first : first + HEAD_DIM]
            g = group_to_heads(env, parts, mine, groups[6], q)
            next(g)
            moving.append(g)
        steps(proj, 1)
        bg.step(4)
        bg.add(gather(env, dy_r, dy_o, groups[4], lay.tp_order, lay.tp_index, core=True))
        leaving = []
        for q in range(2):
            next(moving[q])
            for c in range(n_ctx):
                tc, dc = lay.tp_index(c), lay.dp_index(c)
                for n in range(3):
                    heads_v[n, q, :, c * T : (c + 1) * T] = mine[
                        q, dc, n * HEAD_DIM : (n + 1) * HEAD_DIM, tc * T : (tc + 1) * T
                    ]
            keys[...] = heads_v[1, q].T
            for i in range(n_tiles):
                at = slice(i * tile, (i + 1) * tile)
                o, lse = attend_tile(i, tile, heads_v[0, q, :, at], keys, heads_v.at[2, q])
                o_v[q, :, at] = o
                lse_o[q, :, at] = lse
                low = o.astype(BF)
                for b in range(tile // T):
                    o_low[q, i * (tile // T) + b] = low[:, b * T : (b + 1) * T]
                steps(proj, 2)
                bg.step(2)
            g = heads_out(env, o_low, ob_b, groups[9], q)
            next(g)
            leaving.append(g)
        leave.local(heads_v, heads_o)
        leave.local(o_v, o_o)
        finish(proj)
        for n in range(2):
            for c in range(n_ctx):
                pj_v[n, c * R : (c + 1) * R, :] = proj_b[n, c]
        leave.local(pj_v, pj_o)
        for g in leaving:
            finish(g)
        heads_in(env, o_low, ob_b, groups[9])
        ob_o[...] = ob_b[...].reshape(D, T).T
        branch = jnp.concatenate([dot(ob_o[...], pj_v[n], NN) for n in range(2)], axis=1)
        x1 = x_r[...].astype(F32) + branch + par_o[1, 1:2, :]
        x1_o[...] = x1
        hat, _ = norm_stats(x1)
        h2_s[...] = (hat * par_o[1, 0:1, :] + par_o[1, 2:3, :]).astype(BF)
        rows_h2 = gather(env, h2_s, h2_o, groups[10], lay.tp_order, lay.tp_index, core=True)
        next(rows_h2)
        bg.step(4)
        next(rows_h2)
        bg.finish()
        finish(rows_h2)
        for g in moving:
            finish(g)
        leave.finish()
        links.finish()

    outs = [
        struct(2, 4, T, D),
        struct(D, 3 * W),
        struct(3, 2, HEAD_DIM, length),
        struct(2, HEAD_DIM, length, dtype=F32),
        struct(2, D, half),
        struct(2, 4, T, D),
        struct(n_ctx, R, n_dp * FH),
        struct(n_dp, 2, FH, half),
        struct(n_dp, FH, half),
        struct(2, 4, T, D),
        struct(2, 1, length, dtype=F32),
        struct(T, D),
        struct(T, D, dtype=F32),
        struct(1, n_dp * FH, dtype=F32),
        struct(2, 8, D, dtype=F32),
    ]
    out_specs = [ANY] * 10 + [VM] * 5
    scratch = [
        pltpu.VMEM((8, 128), F32),
        pltpu.VMEM((n_dev, 8, 128), F32),
        pltpu.VMEM(qkv.shape, BF),
        pltpu.VMEM(fc.shape, BF),
        pltpu.VMEM((4, R, 3 * W), BF),
        pltpu.VMEM((4, R, n_dp * FH), BF),
        pltpu.VMEM((2, FH, half), BF),
        pltpu.VMEM((n_ctx, R, 3 * W), BF),
        pltpu.VMEM((D, 3 * W), BF),
        pltpu.VMEM((2, 4, T, D), BF),
        pltpu.VMEM((2, 4, T, D), BF),
        pltpu.VMEM((8, wide), F32),
        pltpu.VMEM((2, HU, QKV, G), BF),
        pltpu.VMEM((2, n_dp, QKV, G), BF),
        pltpu.VMEM((length, HEAD_DIM), BF),
        pltpu.VMEM((3, 2, HEAD_DIM, length), BF),
        pltpu.VMEM((2, HEAD_DIM, length), F32),
        pltpu.VMEM((2, n_ctx, HEAD_DIM, T), BF),
        pltpu.VMEM((HEADS, HEAD_DIM, T), BF),
        pltpu.VMEM((2, n_ctx, R, half), BF),
        pltpu.VMEM((2, D, half), BF),
        pltpu.VMEM((T, D), BF),
    ]
    DMA = pltpu.SemaphoreType.DMA
    scratch += sem_shapes(2) + sem_shapes(n_dev)
    scratch += sem_shapes(gather_sends(4, k, False, True))
    scratch += sem_shapes(gather_sends(1, 2, True, False)) * 2
    scratch += sem_shapes(gather_sends(4, k, False, True))
    scratch += [DMA((2, HU)), DMA((2, n_dp)), DMA((2,))]
    scratch += sem_shapes(gather_sends(1, k + 2, True, False))
    scratch += sem_shapes(gather_sends(1, k, True, False))
    scratch += [DMA((2, n_ctx)), DMA((HEADS,)), DMA((2,))]
    scratch += sem_shapes(gather_sends(1, 2, True, False))
    scratch += sem_shapes(1, 5)
    in_specs = [VM] * 7 + [ANY] * 2
    return call(
        "forward", 0, body, (x, gains, biases, fc_bias, qkv, fc, out, proj, dy), in_specs, outs, out_specs, scratch
    )


def steps(generator, count):
    for _ in range(count):
        next(generator, None)


def by_side(s, f):
    for side in range(2):

        @pl.when(s == side)
        def _():
            f(side)


def middle(lay, x, h2, dy_all, fc, out, out_x, shift, x1, dy, pj, par):
    n_ctx, n_dp = lay.n_ctx, lay.n_dp
    n_dev = 2 * n_ctx
    k = len(lay.dp_bits)
    T = x.shape[0]
    R, FB = D // n_ctx, FF // n_ctx
    FH = FB // 2
    U = n_dp * FH
    G = 4 * T
    half = D // 2
    chunk = 2 * T

    def natural(c):
        return c

    def body(*refs):
        (h2_r, dya_r, fc_r, out_r, outx_r, pj_r, shift_r, x1_r, dy_r, par_r) = refs[:10]
        (mix_o, dob_o, fc_o, out_o, dx1_o, vec_o, fcb_o) = refs[10:17]
        (h2_v, dy_v, fc_b, fc_w, out_b, out_w, out_g, pj_v, gb_v, du_v, back_p, dh2_v, dob_s) = refs[17:30]
        rest = refs[30:]
        spans, first = [], 0
        for n in (3, k, k):
            spans.append((rest[first : first + n], rest[first + n : first + n + 3]))
            first += n + 3
        sems = rest[first:]
        env = Env(lay)
        s = env.s
        hail_all(env)
        loads = Links((None, None, sems[3]))
        load_fc = loads.local(fc_r, fc_b)
        load_h2 = loads.local(h2_r, h2_v)
        load_out = [loads.local(out_r.at[d, s], out_b.at[0, d]) for d in range(n_dp)]
        load_out += [loads.local(outx_r.at[d], out_b.at[1, d]) for d in range(n_dp)]
        load_dy = loads.local(dya_r, dy_v)
        load_pj = loads.local(pj_r, pj_v)
        load_fc.wait()
        for c in range(n_ctx):
            fc_w[c * R : (c + 1) * R, :] = fc_b[c]
        for copy in load_out:
            copy.wait()

        def fill_out(side):
            for d in range(n_dp):
                at = slice(d * FH, (d + 1) * FH)
                pair = (out_b[0, d], out_b[1, d]) if side == 0 else (out_b[1, d], out_b[0, d])
                out_w[at, :] = jnp.concatenate(pair, axis=1)

        by_side(s, fill_out)
        load_h2.wait()
        load_dy.wait()

        def forth_and_back(q):
            @pl.loop(0, G // chunk)
            def _(i):
                rows = h2_v[q, pl.ds(2 * i, 2)].reshape(chunk, D)
                u = dot(rows, fc_w[...], NN) + shift_r[...]
                square = u * u
                th = jnp.tanh(math.sqrt(2 / math.pi) * (u + 0.044715 * square * u))
                up = 0.5 * (1.0 + th)
                at = pl.ds(pl.multiple_of(i * chunk, chunk), chunk)
                gb_v[q, at, :] = (u * up).astype(BF)
                slope = up + (0.5 * math.sqrt(2 / math.pi)) * u * (1.0 - th * th) * (
                    1.0 + (3 * 0.044715) * square
                )
                dact = dot(dy_v[q, pl.ds(2 * i, 2)].reshape(chunk, D), out_w[...], NT)
                du = (dact * slope).astype(BF)
                du_v[q, at, :] = du
                back = dot(du, fc_w[...], NT).astype(BF)
                back_p[q, pl.ds(2 * i, 2)] = back.reshape(2, T, D)

        forth_and_back(1 - s)
        meet_all(env)
        rows = reduce(env, back_p, dh2_v, *spans[0], lay.tp_order, lay.tp_index, core=True)
        next(rows)
        forth_and_back(s)
        steps(rows, 4)
        for c in range(0, n_ctx, 4):
            left = h2_v[:, :, :, c * R : (c + 4) * R].reshape(2 * G, 4 * R)
            made = dot(left, du_v[...].reshape(2 * G, U), TN).astype(BF)
            for i in range(4):
                fc_b[c + i] = made[i * R : (i + 1) * R, :]
        fc_sum = reduce(env, fc_b, fc_o, *spans[1], lay.dp_order, natural, rows=True)
        next(fc_sum)
        for d in range(n_dp):
            left = gb_v[:, :, d * FH : (d + 1) * FH].reshape(2 * G, FH)
            out_g[d] = dot(left, dy_v[...].reshape(2 * G, D), TN).astype(BF)
        out_sum = reduce(env, out_g, out_o, *spans[2], lay.dp_order, lay.dp_index, halves=True)
        next(out_sum)
        fcb_o[...] = jnp.sum(du_v[...].reshape(2 * G, U).astype(F32), axis=0, keepdims=True)
        x1 = x1_r[...]
        hat, spread = norm_stats(x1)
        dy_own = dy_r[...].astype(F32)
        vec_o[...] = jnp.zeros_like(vec_o)
        vec_o[3:4, :] = jnp.sum(dy_own, axis=0, keepdims=True)
        for q in range(2):

            @pl.loop(0, G // chunk)
            def _(i):
                at = pl.ds(pl.multiple_of(i * chunk, chunk), chunk)
                part = dot(gb_v[q, at, :], out_w[...], NN).astype(BF)
                h2_v[q, pl.ds(2 * i, 2)] = part.reshape(2, T, D)

        leave = loads.local(h2_v, mix_o)
        steps(rows, 2)
        steps(fc_sum, 8)
        finish(rows)
        dh2 = dh2_v[...].astype(F32)
        scaled = dh2 * par_r[1, 0:1, :]
        dx1 = dy_own + spread * (
            scaled
            - jnp.mean(scaled, axis=-1, keepdims=True)
            - hat * jnp.mean(scaled * hat, axis=-1, keepdims=True)
        )
        dx1_o[...] = dx1
        da = dx1.astype(BF)
        load_pj.wait()
        dob = dot(da[:, :half], pj_v[0], NT) + dot(da[:, half:], pj_v[1], NT)
        dob_s[...] = dob.astype(BF).T.reshape(HEADS, HEAD_DIM, T)
        heads = tokens_to_heads(env, dob_s, dob_o, sems[0:3])
        next(heads)
        vec_o[0:1, :] = jnp.sum(dh2 * hat, axis=0, keepdims=True)
        vec_o[1:2, :] = jnp.sum(da.astype(F32), axis=0, keepdims=True)
        vec_o[2:3, :] = jnp.sum(dh2, axis=0, keepdims=True)
        steps(fc_sum, 4)
        steps(out_sum, 2)
        run([fc_sum, out_sum])
        finish(heads)
        leave.wait()

    outs = [
        struct(2, 4, T, D),
        struct(2, n_ctx, HEAD_DIM, T),
        struct(2, 4, R, U),
        struct(2, FH, D),
        struct(T, D, dtype=F32),
        struct(8, D, dtype=F32),
        struct(1, U, dtype=F32),
    ]
    scratch = [
        pltpu.VMEM((2, 4, T, D), BF),
        pltpu.VMEM((2, 4, T, D), BF),
        pltpu.VMEM((n_ctx, R, U), BF),
        pltpu.VMEM((D, U), BF),
        pltpu.VMEM((2, n_dp, FH, half), BF),
        pltpu.VMEM((U, D), BF),
        pltpu.VMEM((n_dp, FH, D), BF),
        pltpu.VMEM((2, D, half), BF),
        pltpu.VMEM((2, G, U), BF),
        pltpu.VMEM((2, G, U), BF),
        pltpu.VMEM((2, 4, T, D), BF),
        pltpu.VMEM((T, D), BF),
        pltpu.VMEM((HEADS, HEAD_DIM, T), BF),
    ]
    scratch += reduce_scratch(1, 2, True, (T, D)) + sem_shapes(reduce_sends(1, 2, True, False, False))
    scratch += reduce_scratch(4, k, False, (R, U)) + sem_shapes(reduce_sends(4, k, False, True, False))
    scratch += reduce_scratch(1, k, False, (FH, D)) + sem_shapes(reduce_sends(1, k, False, False, True))
    DMA = pltpu.SemaphoreType.DMA
    scratch += [DMA((HEADS,)), DMA((n_dev,)), DMA((1,)), DMA((2 * n_dp + 5,))]
    args = (h2, dy_all, fc, out, out_x, pj, shift, x1, dy, par)
    out_specs = [ANY] * 4 + [VM] * 3
    return call("middle", 1, body, args, [ANY] * 6 + [VM] * 4, outs, out_specs, scratch)


def heads_to_group(env, src, out, sems, q):
    send_sems, recv_sems, local_sems = sems
    lay = env.lay
    held = q % src.shape[0]

    def copy(there, j, target):
        return pltpu.make_async_remote_copy(
            src_ref=src.at[held, there],
            dst_ref=out.at[q, j],
            send_sem=send_sems.at[q, there],
            recv_sem=recv_sems.at[q, j],
            device_id=(lay.compose(env.t, target), env.s),
            device_id_type=MESH,
        )

    local = pltpu.make_async_copy(src.at[held, env.d], out.at[q, env.d % HU], local_sems.at[q])

    @pl.when(env.d < HU)
    def _():
        for i in range(1, lay.n_dp):
            there = (env.d + i) % lay.n_dp
            copy(there, env.d, there).start()
        local.start()

    yield

    @pl.when(env.d < HU)
    def _():
        local.wait()

    for j in range(HU):

        @pl.when(j != env.d)
        def _():
            copy(0, j, j).wait_recv()

    yield

    @pl.when(env.d < HU)
    def _():
        for i in range(1, lay.n_dp):
            there = (env.d + i) % lay.n_dp
            copy(there, env.d, there).wait_send()


def backward(lay, x, heads, o, lse, dob, wq, h1, ob, vec, fcb, dx1, par, mix):
    n_ctx, n_dp = lay.n_ctx, lay.n_dp
    n_dev = 2 * n_ctx
    k = len(lay.dp_bits)
    T = x.shape[0]
    R, FB = D // n_ctx, FF // n_ctx
    FH = FB // 2
    W = HU * HEAD_DIM
    G = 4 * T
    half = D // 2
    length = n_ctx * T
    tile = TILE if length <= 4 * TILE else TILE // 2
    n_tiles = length // tile
    wide = UNITS * W

    def natural(c):
        return c

    def body(*refs):
        (x_r, heads_r, o_r, lse_r, dob_r, wqh_r, h1h_r, ob_r, vec_r, fcb_r, dx1_r, par_r, mix_r) = refs[:13]
        (grad_o, q_v, proj_o, small_o, mix_s) = refs[13:18]
        (
            heads_v, o_v, dob_n, qs, dobs, delta, dq_acc, parts, land, dqkv, dh1_p, dh1_v, q_g, wide_v,
            small_s, small_v, pg, wq_r, h1_r,
        ) = refs[18:37]
        rest = refs[37:]
        spans, first = [], 0
        for n in (3, k, k + 3, 3):
            spans.append((rest[first : first + n], rest[first + n : first + n + 3]))
            first += n + 3
        sems = rest[first:]
        env = Env(lay)
        s = env.s
        hail_all(env)
        early = Links((None, None, sems[7]))
        mix_v = dh1_p.at[0]
        load_mix = early.local(mix_r.at[s], mix_v)
        load_wq = early.local(wqh_r, wq_r)
        load_h1 = early.local(h1h_r, h1_r)
        for n in range(2):
            right = dx1_r[:, n * half : (n + 1) * half].astype(BF)
            for c in range(0, n_ctx, 4):
                made = dot(ob_r[:, c * R : (c + 4) * R], right, TN).astype(BF)
                for i in range(4):
                    pg[n, c + i] = made[i * R : (i + 1) * R, :]
        small_s[...] = jnp.zeros_like(small_s)
        wide_v[...] = jnp.zeros_like(wide_v)
        meet_all(env)
        proj = reduce(env, pg, proj_o, *spans[2], lay.tp_order + lay.dp_order, natural, core=True)
        next(proj)
        mixing = reduce(env, mix_r, mix_s, *spans[3], lay.tp_order, lay.tp_index, core=True, own=mix_v)
        next(mixing)
        load_mix.wait()
        moving = []
        _, active = own_head(env)

        def loads(q):
            copies = [pltpu.make_async_copy(heads_r.at[n, q], heads_v.at[n], sems[6].at[n]) for n in range(3)]
            copies.append(pltpu.make_async_copy(o_r.at[q], o_v, sems[6].at[3]))
            for c in range(n_ctx):
                copies.append(
                    pltpu.make_async_copy(
                        dob_r.at[q, c], dob_n.at[:, pl.ds(c * T, T)], sems[6].at[4 + c]
                    )
                )
            return copies

        for copy in loads(0):
            copy.start()
        for q in range(2):
            for copy in loads(q):
                copy.wait()

            @pl.when(jnp.logical_not(active))
            def _():
                dob_n[...] = jnp.zeros_like(dob_n)

            qs[...] = heads_v[0].T
            dobs[...] = dob_n[...].T
            delta[...] = jnp.sum(dob_n[...].astype(F32) * o_v[...], axis=0, keepdims=True)
            dq_acc[...] = jnp.zeros_like(dq_acc)

            if q == 1 and parts.shape[0] == 1:
                finish(moving[0])

            def put(n, first, block):
                for b in range(block.shape[1] // T):
                    c = first // T + b
                    tc, dc = lay.tp_index(c), lay.dp_index(c)
                    parts[q % parts.shape[0], dc, n * HEAD_DIM : (n + 1) * HEAD_DIM, tc * T : (tc + 1) * T] = block[
                        :, b * T : (b + 1) * T
                    ]

            for j in range(n_tiles):
                here = slice(j * tile, (j + 1) * tile)
                kt = heads_v[1, :, here]
                keys = kt.T
                values = heads_v[2, :, here].T

                def step(i, carry, masked):
                    dk, dv = carry
                    at = pl.ds(pl.multiple_of(i * tile, tile), tile)
                    st = dot(keys, heads_v[0, :, at], NN) * (SCALE * LOG2E)
                    p = jnp.exp2(st - lse_r[q, :, at])
                    if masked:
                        row = lax.broadcasted_iota(jnp.int32, (tile, tile), 0)
                        col = lax.broadcasted_iota(jnp.int32, (tile, tile), 1)
                        p = jnp.where(row <= col, p, 0.0)
                    dp = dot(values, dob_n[:, at], NN)
                    ds = (p * (dp - delta[:, at])).astype(BF)
                    dv = dv + dot(p.astype(BF), dobs[at, :], NN)
                    dk = dk + dot(ds, qs[at, :], NN)
                    dq_acc[:, at] += dot(kt, ds, NN)
                    return dk, dv

                zero = jnp.zeros((tile, HEAD_DIM), F32)
                carry = step(j, (zero, zero), True)
                if j + 1 < n_tiles:
                    carry = lax.fori_loop(j + 1, n_tiles, functools.partial(step, masked=False), carry)
                put(1, j * tile, (carry[0] * SCALE).T.astype(BF))
                put(2, j * tile, carry[1].T.astype(BF))
                if q == 0:
                    steps(proj, n_ctx // n_tiles)
                    steps(mixing, 1)
                else:
                    steps(proj, n_ctx // 2 // n_tiles)
                    steps(mixing, 1)
            put(0, 0, (dq_acc[...] * SCALE).astype(BF))
            if q == 0:
                for copy in loads(1):
                    copy.start()
            g = heads_to_group(env, parts, land, sems[0:3], q)
            next(g)
            moving.append(g)
        load_wq.wait()
        load_h1.wait()
        for q in range(2):
            next(moving[q], None)
            rows = []
            for n in range(3):
                for j in range(HU):
                    rows.append(land[q, j, n * HEAD_DIM : (n + 1) * HEAD_DIM, :])
            dqkv[q] = jnp.concatenate(rows, axis=0).T
            dh1_p[q] = dot(dqkv[q], wq_r[...], NT).astype(BF).reshape(4, T, D)
        rows_h1 = reduce(env, dh1_p, dh1_v, *spans[0], lay.tp_order, lay.tp_index, core=True)
        next(rows_h1)
        for c in range(0, n_ctx, 4):
            left = h1_r[:, :, :, c * R : (c + 4) * R].reshape(2 * G, 4 * R)
            made = dot(left, dqkv[...].reshape(2 * G, 3 * W), TN).astype(BF)
            for i in range(4):
                q_g[c + i] = made[i * R : (i + 1) * R, :]
        grads = reduce(env, q_g, q_v, *spans[1], lay.dp_order, natural, rows=True)
        next(grads)
        steps(rows_h1, 4)
        unit = 2 * env.t + s
        sums = jnp.sum(dqkv[0].astype(F32), axis=0, keepdims=True) + jnp.sum(
            dqkv[1].astype(F32), axis=0, keepdims=True
        )
        cols = pl.ds(pl.multiple_of(unit * W, W), W)
        wide_v[2:3, cols] = sums[:, :W]
        wide_v[3:4, cols] = sums[:, 2 * W :]
        hat, spread = norm_stats(x_r[...].astype(F32))
        finish(mixing)
        steps(proj, n_ctx // 4)
        steps(grads, n_ctx // 2)
        steps(rows_h1, 2)
        steps(grads, n_ctx // 4)
        finish(rows_h1)
        dh1 = dh1_v[...].astype(F32)
        scaled = dh1 * par_r[0, 0:1, :]
        grad_o[...] = dx1_r[...] + spread * (
            scaled
            - jnp.mean(scaled, axis=-1, keepdims=True)
            - hat * jnp.mean(scaled * hat, axis=-1, keepdims=True)
        )
        wide_v[0:1, :D] = jnp.sum(dh1 * hat, axis=0, keepdims=True)
        wide_v[1:2, :D] = jnp.sum(dh1, axis=0, keepdims=True)
        for c in range(n_ctx):
            small_s[2 * c, 0:4, :R] = wide_v[0:4, c * R : (c + 1) * R]
            small_s[2 * c + 1, 0:4, :R] = vec_r[0:4, c * R : (c + 1) * R]
        for d in range(n_dp):
            owner = lay.compose(env.t, d) * 2 + s
            for h in range(2):
                first = d * FH + h * (FH // 2)
                small_s[owner, 4 + h : 5 + h, : FH // 2] = fcb_r[:, first : first + FH // 2]
        everyone = to_everyone(env, small_s, small_v, sems[3:6], False)
        next(everyone)
        finish(grads)
        finish(proj)
        for g in moving:
            finish(g)
        finish(everyone)
        total = small_v[0]
        for r in range(1, n_dev):
            total = total + small_v[r]
        small_o[...] = total

    outs = [
        struct(T, D, dtype=F32),
        struct(2, 4, R, 3 * W),
        struct(R, half),
        struct(8, 128, dtype=F32),
        struct(T, D),
    ]
    scratch = [
        pltpu.VMEM((3, HEAD_DIM, length), BF),
        pltpu.VMEM((HEAD_DIM, length), F32),
        pltpu.VMEM((HEAD_DIM, length), BF),
        pltpu.VMEM((length, HEAD_DIM), BF),
        pltpu.VMEM((length, HEAD_DIM), BF),
        pltpu.VMEM((1, length), F32),
        pltpu.VMEM((HEAD_DIM, length), F32),
        pltpu.VMEM((2 if n_ctx <= 16 else 1, n_dp, QKV, G), BF),
        pltpu.VMEM((2, HU, QKV, G), BF),
        pltpu.VMEM((2, G, 3 * W), BF),
        pltpu.VMEM((2, 4, T, D), BF),
        pltpu.VMEM((T, D), BF),
        pltpu.VMEM((n_ctx, R, 3 * W), BF),
        pltpu.VMEM((8, wide), F32),
        pltpu.VMEM((n_dev, 8, 128), F32),
        pltpu.VMEM((n_dev, 8, 128), F32),
        pltpu.VMEM((2, n_ctx, R, half), BF),
        pltpu.VMEM((D, 3 * W), BF),
        pltpu.VMEM((2, 4, T, D), BF),
    ]
    scratch += reduce_scratch(1, 2, True, (T, D)) + sem_shapes(reduce_sends(1, 2, True, False, False))
    scratch += reduce_scratch(4, k, False, (R, 3 * W)) + sem_shapes(reduce_sends(4, k, False, True, False))
    scratch += reduce_scratch(1, k + 2, True, (R, half)) + sem_shapes(
        reduce_sends(1, k + 2, True, False, False)
    )
    scratch += reduce_scratch(1, 2, True, (T, D)) + sem_shapes(reduce_sends(1, 2, True, False, False))
    DMA = pltpu.SemaphoreType.DMA
    scratch += [DMA((2, n_dp)), DMA((2, HU)), DMA((2,))] + sem_shapes(n_dev) + [DMA((4 + n_ctx,)), DMA((3,))]
    args = (x, heads, o, lse, dob, wq, h1, ob, vec, fcb, dx1, par, mix)
    in_specs = [VM, ANY, ANY, VM, ANY, ANY, ANY] + [VM] * 5 + [ANY]
    return call("backward", 2, body, args, in_specs, outs, [VM, ANY, VM, VM, VM], scratch)


def assemble(lay, q, fc, out, proj, grad, mix, x1, par, small):
    n_ctx, n_dp = lay.n_ctx, lay.n_dp
    T = grad.shape[0]
    R, FB = D // n_ctx, FF // n_ctx
    FH = FB // 2
    W = HU * HEAD_DIM
    half = D // 2

    def body(*refs):
        (q_r, fc_r, out_r, proj_r, grad_r, mix_r, x1_r, par_r, small_r) = refs[:9]
        (mixed_o, grad_o, qkv_o, proj_o, fc_o, out_o, gains_o, biases_o, fcb_o) = refs[9:]
        mixed_o[...] = (x1_r[...] + mix_r[...].astype(F32) + par_r[1, 3:4, :]).astype(BF)
        grad_o[...] = grad_r[...]
        proj_o[...] = proj_r[...].astype(F32)
        gains_o[...] = small_r[0:1, :R]
        biases_o[...] = small_r[1:4, :R]
        fcb_o[...] = small_r[4:6, : FH // 2]

        def last(side):
            thirds = []
            for n in range(3):
                pieces = [q_r[h, u][:, n * W : (n + 1) * W] for u in range(4) for h in range(2)]
                thirds.append(jnp.concatenate(pieces, axis=1)[:, :D])
            whole = jnp.concatenate(thirds, axis=1)
            qkv_o[...] = whole[:, side * (3 * half) : (side + 1) * (3 * half)].astype(F32)
            pieces = []
            for c in range(n_ctx // 2 * side, n_ctx // 2 * (side + 1)):
                for h in range(2):
                    first = lay.dp_index(c) * FH
                    pieces.append(fc_r[h, lay.tp_index(c)][:, first : first + FH])
            fc_o[...] = jnp.concatenate(pieces, axis=1).astype(F32)
            out_o[...] = jnp.concatenate(
                [out_r[h][:, side * half : (side + 1) * half] for h in range(2)], axis=0
            ).astype(F32)

        by_side(lax.axis_index("fsdp"), last)

    outs = [
        struct(T, D),
        struct(T, D, dtype=F32),
        struct(R, 3 * half, dtype=F32),
        struct(R, half, dtype=F32),
        struct(R, FF // 2, dtype=F32),
        struct(FB, half, dtype=F32),
        struct(1, R, dtype=F32),
        struct(3, R, dtype=F32),
        struct(2, FH // 2, dtype=F32),
    ]
    return pl.pallas_call(
        body,
        out_shape=outs,
        in_specs=[VM] * 9,
        out_specs=[VM] * 9,
        compiler_params=pltpu.CompilerParams(vmem_limit_bytes=VMEM_LIMIT),
        name="assemble",
    )(q, fc, out, proj, grad, mix, x1, par, small)


def shards(lay, tokens, qkv_weight, proj_weight, fc_weight, out_weight, gains, biases, fc_bias, cotangent):
    T = tokens.shape[1]
    R = D // lay.n_ctx
    FH = FF // lay.n_ctx // 2
    x = tokens.reshape(T, D)
    dy = cotangent.reshape(T, D)
    (h1, wq, heads, o, pj, h2, fc, out, out_x, dy_all, lse, ob, x1, shift, par) = forward(
        lay, x, gains, biases, fc_bias.reshape(2, FH // 2), qkv_weight, fc_weight, out_weight, proj_weight, dy
    )
    mix, dob, fc_sum, out_sum, dx1, vec, fcb = middle(
        lay, x, h2, dy_all, fc, out, out_x, shift, x1, dy, pj, par
    )
    grad, q_sum, proj_sum, small, mix_sum = backward(
        lay, x, heads, o, lse, dob, wq, h1, ob, vec, fcb, dx1, par, mix
    )
    (mixed, grad, qkv_grad, proj_grad, fc_grad, out_grad, gains_grad, biases_grad, fc_bias_grad) = assemble(
        lay, q_sum, fc_sum, out_sum, proj_sum, grad, mix_sum, x1, par, small
    )
    return (
        mixed.reshape(tokens.shape),
        grad.reshape(tokens.shape),
        qkv_grad,
        proj_grad,
        fc_grad,
        out_grad,
        gains_grad,
        biases_grad,
        fc_bias_grad.reshape(FH),
    )


def solution(mesh):
    lay = Layout(mesh.shape["ctx"])
    in_specs = (
        P("fsdp", "ctx", None),
        P("ctx", "fsdp"),
        P("ctx", "fsdp"),
        P("ctx", "fsdp"),
        P("ctx", "fsdp"),
        P("fsdp", "ctx"),
        P("fsdp", "ctx"),
        P(("ctx", "fsdp")),
        P("fsdp", "ctx", None),
    )
    out_specs = (
        P("fsdp", "ctx", None),
        P("fsdp", "ctx", None),
        P("ctx", "fsdp"),
        P("ctx", "fsdp"),
        P("ctx", "fsdp"),
        P("ctx", "fsdp"),
        P("fsdp", "ctx"),
        P("fsdp", "ctx"),
        P(("ctx", "fsdp")),
    )
    return jax.shard_map(
        functools.partial(shards, lay), mesh=mesh, in_specs=in_specs, out_specs=out_specs, check_vma=False
    )
```

```python
import functools
import math

import jax
import jax.numpy as jnp
from jax import lax
from jax.experimental import pallas as pl
from jax.experimental.pallas import tpu as pltpu
from jax.sharding import PartitionSpec as P

D = 1600
HEADS = 25
HEAD_DIM = 64
FF = 6400
EPS = 1e-05
UNITS = 8
HU = -(-HEADS // UNITS)
QKV = 3 * HEAD_DIM
MESH = pl.DeviceIdType.MESH
BF = jnp.bfloat16
F32 = jnp.float32
VMEM_LIMIT = 60 * 1024 * 1024
LOG2E = 1.0 / math.log(2.0)


class Layout:
    def __init__(self, n_ctx):
        self.n_ctx = n_ctx
        a, b = n_ctx // 4, n_ctx // 2
        self.tp_bits = (b, a)
        self.dp_bits = tuple(1 << i for i in range(n_ctx.bit_length() - 3))
        self.n_dp = n_ctx // 4
        self.dp_order = list(zip(self.dp_bits, self.dp_bits[::-1]))
        self.tp_order = [(b, b), (a, a)]
        self.tp_masks = [[], [(a, a)], [(b, b)], [(a, a), (b, b)]]

    def tp_index(self, c):
        return sum(((c // b) % 2) * (1 << i) for i, b in enumerate(self.tp_bits))

    def dp_index(self, c):
        return sum(((c // b) % 2) * (1 << i) for i, b in enumerate(self.dp_bits))

    def compose(self, t, d):
        return sum(((t // (1 << i)) % 2) * b for i, b in enumerate(self.tp_bits)) + sum(
            ((d // (1 << i)) % 2) * b for i, b in enumerate(self.dp_bits)
        )

    def head_rank(self, h):
        u, j = h // HU, h % HU
        return self.compose(u // 2, j) * 2 + u % 2

    def to_natural(self, x):
        labels = list(self.dp_bits[::-1]) + list(self.tp_bits[::-1])
        k = len(labels)
        rest = x.shape[2:]
        x = x.reshape((2,) * k + rest)
        order = sorted(range(k), key=lambda i: -labels[i])
        x = jnp.transpose(x, order + list(range(k, k + len(rest))))
        return x.reshape((self.n_ctx,) + rest)

    def from_natural(self, x):
        labels = list(self.dp_bits[::-1]) + list(self.tp_bits[::-1])
        k = len(labels)
        rest = x.shape[1:]
        x = x.reshape((2,) * k + rest)
        natural = sorted(labels, reverse=True)
        order = [natural.index(b) for b in labels]
        x = jnp.transpose(x, order + list(range(k, k + len(rest))))
        return x.reshape((self.n_dp, 4) + rest)


def flip(c, sym, s):
    def one(b):
        return c + b * (1 - 2 * ((c // b) % 2))

    if sym[0] == sym[1]:
        return one(sym[0])
    return one(sym[0]) * (1 - s) + one(sym[1]) * s


def flips(c, masks, s):
    for sym in masks:
        c = flip(c, sym, s)
    return c


class Env:
    def __init__(self, layout):
        self.lay = layout
        self.c = lax.axis_index("ctx")
        self.s = lax.axis_index("fsdp")
        self.t = layout.tp_index(self.c)
        self.d = layout.dp_index(self.c)
        self.rank = self.c * 2 + self.s
        self.n_dev = layout.n_ctx * 2
        self.opened = []

    def other(self):
        return (self.c, 1 - self.s)

    def drain(self):
        for links in self.opened:
            links.drain()


class Links:
    def __init__(self, sems, env=None):
        self.send_sems, self.recv_sems, self.local_sems = sems
        if env is not None:
            env.opened.append(self)
        self.count = 0
        self.local_count = 0
        self.sent = []
        self.locals = []

    def send(self, src, dst, device):
        copy = pltpu.make_async_remote_copy(
            src_ref=src,
            dst_ref=dst,
            send_sem=self.send_sems.at[self.count],
            recv_sem=self.recv_sems.at[self.count],
            device_id=device,
            device_id_type=MESH,
        )
        copy.start()
        self.count += 1
        self.sent.append(copy)
        return copy

    def local(self, src, dst):
        copy = pltpu.make_async_copy(src, dst, self.local_sems.at[self.local_count])
        copy.start()
        self.local_count += 1
        self.locals.append(copy)
        return copy

    def settle(self):
        for copy in self.locals:
            copy.wait()
        self.locals = []

    def drain(self):
        self.settle()
        for copy in self.sent:
            copy.wait_send()


def sem_shapes(sends, local=1):
    sends = max(sends, 1)
    return [
        pltpu.SemaphoreType.DMA((sends,)),
        pltpu.SemaphoreType.DMA((sends,)),
        pltpu.SemaphoreType.DMA((local,)),
    ]


def meet(env, devices):
    barrier = pltpu.get_barrier_semaphore()
    for device in devices:
        pl.semaphore_signal(barrier, inc=1, device_id=device, device_id_type=MESH)
    pl.semaphore_wait(barrier, len(devices))


def hail_all(env):
    barrier = pltpu.get_barrier_semaphore()

    def hail(i, carry):
        rank = (env.rank + i) % env.n_dev
        pl.semaphore_signal(barrier, inc=1, device_id=(rank // 2, rank % 2), device_id_type=MESH)
        return carry

    lax.fori_loop(1, env.n_dev, hail, 0)


def near(env):
    lay = env.lay
    return (
        [(flips(env.c, m, env.s), env.s) for m in lay.tp_masks[1:]]
        + [(lay.compose(env.t, (env.d + i) % lay.n_dp), env.s) for i in range(1, lay.n_dp)]
        + [env.other()]
    )


def hail_near(env):
    barrier = pltpu.get_barrier_semaphore()
    for device in near(env):
        pl.semaphore_signal(barrier, inc=1, device_id=device, device_id_type=MESH)


def meet_near(env):
    pl.semaphore_wait(pltpu.get_barrier_semaphore(), len(near(env)))


def meet_all(env):
    pl.semaphore_wait(pltpu.get_barrier_semaphore(), env.n_dev - 1)


def tp_partners(env):
    return [(flips(env.c, m, env.s), env.s) for m in env.lay.tp_masks[1:]]


def dp_partners(env):
    return [(flip(env.c, sym, env.s), env.s) for sym in env.lay.dp_order]


def run(generators):
    active = list(generators)
    while active:
        left = []
        for g in active:
            try:
                next(g)
                left.append(g)
            except StopIteration:
                pass
        active = left


def gather_sends(bits, core):
    return (1 << bits) - 1 + (1 << bits if core else 0)


def gather(env, links, src, buf, bits, slot, core=False, half=None, placed=False):
    c, s = env.c, env.s

    def place(masks):
        return buf.at[slot(flips(c, masks, s))]

    if not placed:
        links.local(src, place([]))
    levels = [[([], None)]] + [[] for _ in bits]
    crossing = []
    for k in range(len(bits) + 1):
        for masks, copy in levels[k]:
            if copy is None:
                ref = src
            else:
                copy.wait_recv()
                ref = place(masks)
            for j in range(k, len(bits)):
                forward = links.send(ref, place(masks), (flip(c, bits[j], s), s))
                levels[j + 1].append((masks + [bits[j]], forward))
            if core:
                crossing.append(links.send(ref, place(masks), env.other()))
            if half is not None:
                there = half.at[slot(flips(c, masks, s))]
                crossing.append(links.send(ref.at[1 - s], there, env.other()))
            yield
    for copy in crossing:
        copy.wait_recv()


def gather_blocks(env, src, buf, sems, bits, slot, core=False, half=None):
    links = Links(sems, env)
    yield from gather(env, links, src, buf.at[env.s] if core else buf, bits, slot, core, half)
    links.settle()
    yield


def gather_columns(env, src, buf, sems):
    lay = env.lay
    links = Links(sems, env)
    own = buf.at[env.d]
    copies = [links.local(src.at[env.t], own.at[env.t])]
    for m in lay.tp_masks[1:]:
        there = flips(env.c, m, env.s)
        copies.append(links.send(src.at[lay.tp_index(there)], own.at[env.t], (there, env.s)))
    yield
    links.settle()
    for copy in copies[1:]:
        copy.wait_recv()
    yield from gather(env, links, own, buf, lay.dp_order, lay.dp_index, placed=True)
    links.settle()
    yield


def gather_all(env, src, buf, sems):
    lay = env.lay
    links = Links(sems, env)
    mine = buf.at[env.s]
    own = mine.at[env.d]
    yield from gather(env, links, src, own, lay.tp_order, lay.tp_index)
    links.settle()
    yield from gather(env, links, own, mine, lay.dp_order, lay.dp_index, core=True, placed=True)
    links.settle()
    yield


def reduce_sends(bits, core):
    return (1 << bits) - 1 + (1 << bits if core else 0)


def reduce_scratch(bits, core, block, dtype=BF):
    return [pltpu.VMEM((1 << j,) + block, dtype) for j in range(bits + (1 if core else 0))]


def add_into(total, term):
    if len(total.shape) == 2:
        total[...] = total[...] + term[...]
    else:
        for i in range(total.shape[0]):
            add_into(total.at[i], term.at[i])


def reduce(env, links, inp, parts, bits, slot, core=False, own=None):
    c, s = env.c, env.s
    levels = [[[]]]
    for sym in bits:
        levels.append(levels[-1] + [m + [sym] for m in levels[-1]])

    def at(side, masks):
        index = slot(flips(c, masks, side))
        return inp.at[side, index] if core else inp.at[index]

    last = levels[-1]
    if own is None:
        now = [at(s, m) for m in last]
    else:
        now = [own.at[slot(flips(c, m, s))] for m in last]
    copies = {}
    if core:
        stage = len(bits)
        for i in reversed(range(len(last))):
            copies[i] = links.send(at(1 - s, last[i]), parts[stage].at[i], env.other())
    else:
        stage = len(bits) - 1
        n = len(levels[stage])
        for i in reversed(range(n)):
            copies[i] = links.send(now[n + i], parts[stage].at[i], (flip(c, bits[stage], s), s))
    yield
    while stage >= 0:
        n = len(levels[stage])
        got = parts[stage]
        after = {}
        for i in reversed(range(n)):
            copies[i].wait_recv()
            add_into(got.at[i], now[i])
            if stage > 0 and i >= n // 2:
                after[i - n // 2] = links.send(
                    got.at[i], parts[stage - 1].at[i - n // 2], (flip(c, bits[stage - 1], s), s)
                )
            yield
        now = [got.at[i] for i in range(n)]
        copies = after
        stage -= 1
    return now[0]


def reduce_blocks(env, inp, out, parts, sems, own=None):
    links = Links(sems, env)
    total = yield from reduce(env, links, inp, parts, env.lay.tp_order, env.lay.tp_index, core=True, own=own)
    out[...] = total[...].astype(out.dtype)
    links.settle()
    yield


def reduce_columns(env, inp, out, parts, sems):
    lay = env.lay
    links = Links(sems, env)
    total = yield from reduce(env, links, inp, parts, lay.dp_order, lay.dp_index)
    local = links.local(total.at[env.t], out.at[env.s, env.t])
    copies = []
    for m in lay.tp_masks[1:]:
        there = flips(env.c, m, env.s)
        copies.append(links.send(total.at[lay.tp_index(there)], out.at[env.s, env.t], (there, env.s)))
    yield
    links.settle()
    for copy in copies:
        copy.wait_recv()
    copy = links.send(out.at[env.s], out.at[env.s], env.other())
    yield
    copy.wait_recv()
    links.settle()
    yield


def reduce_halves(env, inp, out, parts, sems):
    lay = env.lay
    links = Links(sems, env)
    total = yield from reduce(env, links, inp, parts, lay.dp_order, lay.dp_index)
    links.local(total, out.at[env.s])
    copy = links.send(total, out.at[env.s], env.other())
    yield
    copy.wait_recv()
    links.settle()
    yield


def reduce_all(env, inp, out, parts, sems):
    lay = env.lay
    links = Links(sems, env)
    n = len(lay.dp_bits) + 1
    total = yield from reduce(env, links, inp, parts[:n], lay.dp_order, lay.dp_index, core=True)
    total = yield from reduce(env, links, total, parts[n:], lay.tp_order, lay.tp_index)
    out[...] = total[...].astype(out.dtype)
    links.settle()
    yield


def own_head(env):
    h = (env.t * 2 + env.s) * HU + env.d
    return h, jnp.logical_and(env.d < HU, h < HEADS)


def wait_pieces(env, ref, count, send=None, recv=None):
    part = ref.at[pl.ds(0, count)]
    copy = pltpu.make_async_remote_copy(
        src_ref=part,
        dst_ref=part,
        send_sem=recv if send is None else send,
        recv_sem=send if recv is None else recv,
        device_id=env.other(),
        device_id_type=MESH,
    )
    if send is not None:
        copy.wait_send()
    if recv is not None:
        copy.wait_recv()


def tokens_to_heads(env, src, out, sems):
    send_sem, recv_sem, local_sem = sems[0].at[0], sems[1].at[0], sems[2].at[0]
    h, active = own_head(env)
    lay = env.lay
    place = env.s * lay.n_ctx + env.c

    def begin(i, carry):
        j = (env.rank + i) % HEADS
        rank = lay.head_rank(j)

        @pl.when(rank != env.rank)
        def _():
            pltpu.make_async_remote_copy(
                src_ref=src.at[j],
                dst_ref=out.at[place],
                send_sem=send_sem,
                recv_sem=recv_sem,
                device_id=(rank // 2, rank % 2),
                device_id_type=MESH,
            ).start()

        return carry

    lax.fori_loop(0, HEADS, begin, 0)
    yield

    @pl.when(active)
    def _():
        local = pltpu.make_async_copy(src.at[h], out.at[place], local_sem)
        local.start()
        local.wait()
        wait_pieces(env, out, env.n_dev - 1, recv=recv_sem)
        wait_pieces(env, src, HEADS - 1, send=send_sem)

    @pl.when(jnp.logical_not(active))
    def _():
        wait_pieces(env, src, HEADS, send=send_sem)


ANY = pl.BlockSpec(memory_space=pl.ANY)
VM = pl.BlockSpec(memory_space=pltpu.VMEM)


def struct(*shape, dtype=BF):
    return jax.ShapeDtypeStruct(shape, dtype)


def call(name, cid, body, args, in_specs, outs, out_specs, scratch):
    return pl.pallas_call(
        body,
        out_shape=outs,
        in_specs=in_specs,
        out_specs=out_specs,
        scratch_shapes=scratch,
        compiler_params=pltpu.CompilerParams(
            collective_id=cid, has_side_effects=True, vmem_limit_bytes=VMEM_LIMIT
        ),
        name=name,
    )(*args)


def dot(left, right, dims):
    return lax.dot_general(left, right, (dims, ((), ())), preferred_element_type=F32)


NN = ((1,), (0,))
NT = ((1,), (1,))
TN = ((0,), (0,))
SCALE = 1.0 / math.sqrt(HEAD_DIM)
TILE = 512


class Background:
    def __init__(self):
        self.active = []

    def add(self, generator):
        self.active.append(generator)

    def step(self, count=1):
        for _ in range(count):
            if not self.active:
                return
            g = self.active.pop(0)
            try:
                next(g)
                self.active.append(g)
            except StopIteration:
                pass

    def finish(self):
        while self.active:
            self.step()


def finish(generator):
    for _ in generator:
        pass


def group_to_heads(env, src, out, sems, q):
    send_sems, recv_sems, local_sems = sems
    lay = env.lay

    def copy(j, source, target):
        return pltpu.make_async_remote_copy(
            src_ref=src.at[q, j],
            dst_ref=out.at[q, source],
            send_sem=send_sems.at[q, j],
            recv_sem=recv_sems.at[q, source],
            device_id=(lay.compose(env.t, target), env.s),
            device_id_type=MESH,
        )

    for i in range(1, HU + 1):
        j = (env.d + i) % HU

        @pl.when(j != env.d)
        def _():
            copy(j, env.d, j).start()

    local = pltpu.make_async_copy(src.at[q, env.d % HU], out.at[q, env.d], local_sems.at[q])

    @pl.when(env.d < HU)
    def _():
        local.start()

    yield

    @pl.when(env.d < HU)
    def _():
        local.wait()
        for i in range(1, lay.n_dp):
            source = (env.d + i) % lay.n_dp
            copy(0, source, source).wait_recv()

    yield
    for j in range(HU):

        @pl.when(j != env.d)
        def _():
            copy(j, env.d, j).wait_send()


def heads_out(env, src, out, sems, q):
    send_sem, recv_sem = sems[0].at[q], sems[1].at[0]
    h, active = own_head(env)
    n_ctx = env.lay.n_ctx

    def copy(i):
        there = (env.c + i) % n_ctx
        return pltpu.make_async_remote_copy(
            src_ref=src.at[q, there],
            dst_ref=out.at[h],
            send_sem=send_sem,
            recv_sem=recv_sem,
            device_id=(there, q),
            device_id_type=MESH,
        )

    local = pltpu.make_async_copy(src.at[q, env.c], out.at[h], sems[2].at[q])
    mine = jnp.logical_and(active, env.s == q)
    theirs = jnp.logical_and(active, env.s != q)

    def begin(i, carry):
        copy(i).start()
        return carry

    @pl.when(mine)
    def _():
        local.start()

    @pl.when(theirs)
    def _():
        copy(0).start()

    @pl.when(active)
    def _():
        lax.fori_loop(1, n_ctx, begin, 0)

    yield

    @pl.when(mine)
    def _():
        local.wait()

    yield

    @pl.when(mine)
    def _():
        wait_pieces(env, src.at[q], n_ctx - 1, send=send_sem)

    @pl.when(theirs)
    def _():
        wait_pieces(env, src.at[q], n_ctx, send=send_sem)


def heads_in(env, out, sems):
    _, active = own_head(env)

    @pl.when(active)
    def _():
        wait_pieces(env, out, HEADS - 1, recv=sems[1].at[0])

    @pl.when(jnp.logical_not(active))
    def _():
        wait_pieces(env, out, HEADS, recv=sems[1].at[0])


def norm_stats(values):
    centre = values - jnp.mean(values, axis=-1, keepdims=True)
    spread = lax.rsqrt(jnp.mean(centre * centre, axis=-1, keepdims=True) + EPS)
    return centre * spread, spread


def attend_tile(i, tile, qt, keys, v_ref):
    def step(j, carry, masked):
        peak, total, acc = carry
        at = pl.ds(pl.multiple_of(j * tile, tile), tile)
        st = dot(keys[at, :], qt, NN) * (SCALE * LOG2E)
        if masked:
            row = lax.broadcasted_iota(jnp.int32, (tile, tile), 0)
            col = lax.broadcasted_iota(jnp.int32, (tile, tile), 1)
            st = jnp.where(row <= col, st, -1e30)
        new = jnp.maximum(peak, jnp.max(st, axis=0, keepdims=True))
        p = jnp.exp2(st - new)
        shrink = jnp.exp2(peak - new)
        total = total * shrink + jnp.sum(p, axis=0, keepdims=True)
        acc = acc * shrink + dot(v_ref[:, at], p.astype(BF), NN)
        return new, total, acc

    start = (
        jnp.full((1, tile), -1e30, F32),
        jnp.zeros((1, tile), F32),
        jnp.zeros((HEAD_DIM, tile), F32),
    )
    carry = start
    if i > 0:
        carry = lax.fori_loop(0, i, functools.partial(step, masked=False), carry)
    peak, total, acc = step(i, carry, True)
    return acc / total, peak + jnp.log2(total)


def forward(lay, x, gains, biases, fc_bias, qkv, fc, out, proj, dy):
    n_ctx, n_dp = lay.n_ctx, lay.n_dp
    n_dev = 2 * n_ctx
    k = len(lay.dp_bits)
    T = x.shape[1]
    R, FB = D // n_ctx, FF // n_ctx
    FH = FB // 2
    W = HU * HEAD_DIM
    G = 4 * T
    length = n_ctx * T
    tile = min(TILE, length)
    n_tiles = length // tile
    half = D // 2
    wide = UNITS * W

    def natural(c):
        return c

    def body(*refs):
        (x_r, gains_r, biases_r, fcb_r, qkv_r, fc_r, out_r, proj_r, dy_r) = refs[:9]
        (h1_o, wq_o, heads_o, o_o, pj_o, h2_o, fc_o, out_o, outx_o, dy_o, lse_o, ob_o, x1_o, shift_o, par_o) = refs[9:24]
        (
            pack, small, qkv_x, fc_x, qkv_s, fc_s, out_s, wq_b, wq_v, x_v, h1_v, par_w,
            parts, mine, keys, heads_v, o_v, o_low, ob_b, proj_b, pj_v, h2_s, x_s, dy_s, h1_t,
        ) = refs[24:49]
        sems = refs[49:]
        groups = [sems[3 * i : 3 * i + 3] for i in range(len(sems) // 3)]
        env = Env(lay)
        s = env.s

        hail_all(env)
        x_s[...] = x_r[...].T
        pack[...] = jnp.zeros_like(pack)
        pack[0:1, :R] = gains_r[...].astype(F32)
        pack[1:4, :R] = biases_r[...].astype(F32)
        pack[4:6, : FH // 2] = fcb_r[...].astype(F32)
        for h in range(2):
            out_s[h] = out_r[h * FH : (h + 1) * FH, :]
        par_w[...] = jnp.zeros_like(par_w)
        meet_all(env)
        links = Links(groups[0], env)
        crossing = [links.send(a, b, env.other()) for a, b in ((qkv_r, qkv_x), (fc_r, fc_x))]
        params = gather_all(env, pack, small, groups[1])
        next(params)

        def fill_qkv(a, b, side):
            q = a[:, :D]
            keys_all = jnp.concatenate([a[:, D:], b[:, : D // 2]], axis=1)
            v = b[:, D // 2 :]
            for u in range(4):
                first = (2 * u + side) * W
                width = max(0, min(W, D - first))
                for n, part in enumerate((q, keys_all, v)):
                    if width < W:
                        qkv_s[u, :, n * W : (n + 1) * W] = jnp.zeros((R, W), BF)
                    if width > 0:
                        qkv_s[u, :, n * W : n * W + width] = part[:, first : first + width]

        def fill_fc(a, b, side):
            for u in range(4):
                for d in range(n_dp):
                    first = lay.compose(u, d) * FB + side * FH
                    source, first = (a, first) if first < FF // 2 else (b, first - FF // 2)
                    fc_s[u, :, d * FH : (d + 1) * FH] = source[:, first : first + FH]

        crossing[0].wait_recv()
        by_side(s, lambda side: fill_qkv(*((qkv_r, qkv_x) if side == 0 else (qkv_x, qkv_r)), side))
        weights = gather_columns(env, qkv_s, wq_b, groups[2])
        next(weights)
        steps(params, 4)
        rows_x = gather_blocks(env, x_s, x_v, groups[3], lay.tp_order, lay.tp_index, core=True)
        next(rows_x)
        proj = gather_all(env, proj_r, proj_b, groups[7])
        next(proj)
        out_all = gather_blocks(env, out_s, out_o, groups[8], lay.dp_order, lay.dp_index, half=outx_o)
        next(out_all)
        dy_s[...] = dy_r[...].T
        crossing[1].wait_recv()
        by_side(s, lambda side: fill_fc(*((fc_r, fc_x) if side == 0 else (fc_x, fc_r)), side))
        steps(weights, 1)
        steps(params, 2)
        steps(rows_x, 1)
        steps(proj, 1)
        steps(weights, 1)
        steps(out_all, 1)
        finish(params)
        for f in range(2):
            par_o[f] = jnp.concatenate(
                [small[f, lay.dp_index(c), lay.tp_index(c)][:, :R] for c in range(n_ctx)], axis=1
            )
        par_w[:, :D] = par_o[0]
        shift_parts = []
        for d in range(n_dp):
            block = small[s, d, env.t]
            shift_parts += [block[4:5, : FH // 2], block[5:6, : FH // 2]]
        shift_o[...] = jnp.concatenate(shift_parts, axis=1)
        finish(rows_x)

        @pl.loop(0, 8)
        def _(i):
            hat, _ = norm_stats(x_v[i // 4, i % 4].astype(F32))
            low = (hat * par_o[0, 0:1, :] + par_o[0, 1:2, :]).astype(BF)
            h1_v[i // 4, i % 4] = low
            h1_t[:, pl.ds(pl.multiple_of(i * T, T), T)] = low.T

        finish(weights)
        for c in range(n_ctx):
            wq_v[c * R : (c + 1) * R, :] = wq_b[lay.dp_index(c), lay.tp_index(c)]
        leave = Links((None, None, groups[11][2]))
        leave.local(h1_t, h1_o)
        leave.local(wq_v, wq_o)
        unit = 2 * env.t + s
        cols = pl.ds(pl.multiple_of(unit * W, W), W)
        shift = jnp.concatenate(
            [par_w[2:3, cols], jnp.zeros((1, W), F32), par_w[3:4, cols]], axis=1
        )
        moving = []
        for q in range(2):
            rows = h1_v[q].reshape(G, D)
            made = (dot(rows, wq_v[...], NN) + shift).astype(BF).T
            for n in range(3):
                for j in range(HU):
                    first = n * W + j * HEAD_DIM
                    parts[q, j, n * HEAD_DIM : (n + 1) * HEAD_DIM, :] = made[first : first + HEAD_DIM]
            g = group_to_heads(env, parts, mine, groups[6], q)
            next(g)
            moving.append(g)
        steps(proj, 3)
        fc_all = gather_columns(env, fc_s, fc_o, groups[5])
        next(fc_all)
        dy_all = gather_blocks(env, dy_s, dy_o, groups[4], lay.tp_order, lay.tp_index, core=True)
        next(dy_all)
        leaving = []
        for q in range(2):
            next(moving[q])
            for c in range(n_ctx):
                tc, dc = lay.tp_index(c), lay.dp_index(c)
                for n in range(3):
                    heads_v[n, q, :, c * T : (c + 1) * T] = mine[
                        q, dc, n * HEAD_DIM : (n + 1) * HEAD_DIM, tc * T : (tc + 1) * T
                    ]
            keys[...] = heads_v[1, q].T
            for i in range(n_tiles):
                at = slice(i * tile, (i + 1) * tile)
                o, lse = attend_tile(i, tile, heads_v[0, q, :, at], keys, heads_v.at[2, q])
                o_v[q, :, at] = o
                lse_o[q, :, at] = lse
                low = o.astype(BF)
                for b in range(tile // T):
                    o_low[q, i * (tile // T) + b] = low[:, b * T : (b + 1) * T]
                if i == n_tiles - 1:
                    steps(proj, 1 if q == 0 else n_dp // 2)
            g = heads_out(env, o_low, ob_b, groups[9], q)
            next(g)
            leaving.append(g)
        leave.local(heads_v, heads_o)
        leave.local(o_v, o_o)
        finish(proj)
        for n in range(2):
            for c in range(n_ctx):
                pj_v[n, c * R : (c + 1) * R, :] = proj_b[n, lay.dp_index(c), lay.tp_index(c)]
        leave.local(pj_v, pj_o)
        for g in leaving:
            next(g)
        heads_in(env, ob_b, groups[9])
        ob_o[...] = ob_b[...].reshape(D, T).T
        branch = jnp.concatenate([dot(ob_o[...], pj_v[n], NN) for n in range(2)], axis=1)
        x1 = x_s[...].astype(F32) + branch + par_o[1, 1:2, :]
        x1_o[...] = x1
        hat, _ = norm_stats(x1)
        h2_s[...] = (hat * par_o[1, 0:1, :] + par_o[1, 2:3, :]).astype(BF)
        rows_h2 = gather_blocks(env, h2_s, h2_o, groups[10], lay.tp_order, lay.tp_index, core=True)
        next(rows_h2)
        steps(fc_all, 1)
        steps(dy_all, 1)
        steps(rows_h2, 1)
        steps(fc_all, 1)
        finish(out_all)
        finish(fc_all)
        finish(dy_all)
        finish(rows_h2)
        for g in moving + leaving:
            finish(g)
        leave.settle()
        env.drain()

    outs = [
        struct(D, 2 * G),
        struct(D, 3 * W),
        struct(3, 2, HEAD_DIM, length),
        struct(2, HEAD_DIM, length, dtype=F32),
        struct(2, D, half),
        struct(2, 4, T, D),
        struct(n_dp, 4, R, n_dp * FH),
        struct(n_dp, 2, FH, half),
        struct(n_dp, FH, half),
        struct(2, 4, T, D),
        struct(2, 1, length, dtype=F32),
        struct(T, D),
        struct(T, D, dtype=F32),
        struct(1, n_dp * FH, dtype=F32),
        struct(2, 8, D, dtype=F32),
    ]
    out_specs = [ANY] * 10 + [VM] * 5
    scratch = [
        pltpu.VMEM((8, 128), F32),
        pltpu.VMEM((2, n_dp, 4, 8, 128), F32),
        pltpu.VMEM(qkv.shape, BF),
        pltpu.VMEM(fc.shape, BF),
        pltpu.VMEM((4, R, 3 * W), BF),
        pltpu.VMEM((4, R, n_dp * FH), BF),
        pltpu.VMEM((2, FH, half), BF),
        pltpu.VMEM((n_dp, 4, R, 3 * W), BF),
        pltpu.VMEM((D, 3 * W), BF),
        pltpu.VMEM((2, 4, T, D), BF),
        pltpu.VMEM((2, 4, T, D), BF),
        pltpu.VMEM((8, wide), F32),
        pltpu.VMEM((2, HU, QKV, G), BF),
        pltpu.VMEM((2, n_dp, QKV, G), BF),
        pltpu.VMEM((length, HEAD_DIM), BF),
        pltpu.VMEM((3, 2, HEAD_DIM, length), BF),
        pltpu.VMEM((2, HEAD_DIM, length), F32),
        pltpu.VMEM((2, n_ctx, HEAD_DIM, T), BF),
        pltpu.VMEM((HEADS, HEAD_DIM, T), BF),
        pltpu.VMEM((2, n_dp, 4, R, half), BF),
        pltpu.VMEM((2, D, half), BF),
        pltpu.VMEM((T, D), BF),
        pltpu.VMEM((T, D), BF),
        pltpu.VMEM((T, D), BF),
        pltpu.VMEM((D, 2 * G), BF),
    ]
    DMA = pltpu.SemaphoreType.DMA
    columns = sem_shapes(3 + gather_sends(k, False))
    blocks = sem_shapes(gather_sends(2, True))
    every = sem_shapes(gather_sends(2, False) + gather_sends(k, True))
    scratch += sem_shapes(2) + every + columns + blocks * 2 + columns
    scratch += [DMA((2, HU)), DMA((2, n_dp)), DMA((2,))]
    scratch += every
    scratch += sem_shapes(gather_sends(k, True))
    scratch += [DMA((2,)), DMA((1,)), DMA((2,))]
    scratch += blocks
    scratch += sem_shapes(1, 5)
    in_specs = [VM] * 7 + [ANY, VM]
    return call(
        "forward", 0, body, (x, gains, biases, fc_bias, qkv, fc, out, proj, dy), in_specs, outs, out_specs, scratch
    )


def steps(generator, count):
    for _ in range(count):
        next(generator, None)


def by_side(s, f):
    for side in range(2):

        @pl.when(s == side)
        def _():
            f(side)


def spread_rows(made, first, size, block):
    end = first + made.shape[0]
    at = first
    while at < end:
        i = at // size
        stop = min(end, (i + 1) * size)
        block(i)[at - i * size : stop - i * size] = made[at - first : stop - first]
        at = stop


def middle(lay, x, h2, dy_all, fc, out, out_x, shift, x1, dy, pj, par):
    n_ctx, n_dp = lay.n_ctx, lay.n_dp
    n_dev = 2 * n_ctx
    k = len(lay.dp_bits)
    T = x.shape[1]
    R, FB = D // n_ctx, FF // n_ctx
    FH = FB // 2
    U = n_dp * FH
    G = 4 * T
    half = D // 2
    chunk = 2 * T

    def natural(c):
        return c

    def body(*refs):
        (h2_r, dya_r, fc_r, out_r, outx_r, pj_r, shift_r, x1_r, dy_r, par_r) = refs[:10]
        (mix_o, dob_o, fc_o, out_o, dx1_o, vec_o, fcb_o) = refs[10:17]
        (h2_v, dy_v, fc_b, fc_w, out_b, out_w, out_g, pj_v, gb_v, du_v, back_p, dh2_v, dob_s) = refs[17:30]
        rest = refs[30:]
        spans, first = [], 0
        for n in (3, k, k):
            spans.append((rest[first : first + n], rest[first + n : first + n + 3]))
            first += n + 3
        sems = rest[first:]
        env = Env(lay)
        s = env.s
        hail_all(env)
        loads = Links((None, None, sems[3]))
        load_fc = loads.local(fc_r, fc_b)
        load_h2 = loads.local(h2_r, h2_v)
        load_out = [loads.local(out_r.at[:, s], out_b.at[0]), loads.local(outx_r, out_b.at[1])]
        load_dy = loads.local(dya_r, dy_v)
        load_pj = loads.local(pj_r, pj_v)
        load_fc.wait()
        for c in range(n_ctx):
            fc_w[c * R : (c + 1) * R, :] = fc_b[lay.dp_index(c), lay.tp_index(c)]
        for copy in load_out:
            copy.wait()

        def fill_out(side):
            for d in range(n_dp):
                at = slice(d * FH, (d + 1) * FH)
                pair = (out_b[0, d], out_b[1, d]) if side == 0 else (out_b[1, d], out_b[0, d])
                out_w[at, :] = jnp.concatenate(pair, axis=1)

        by_side(s, fill_out)
        load_h2.wait()
        load_dy.wait()

        def forth_and_back(q):
            @pl.loop(0, G // chunk)
            def _(i):
                rows = h2_v[q, pl.ds(2 * i, 2)].reshape(chunk, D)
                u = dot(rows, fc_w[...], NN) + shift_r[...]
                square = u * u
                th = jnp.tanh(math.sqrt(2 / math.pi) * (u + 0.044715 * square * u))
                up = 0.5 * (1.0 + th)
                at = pl.ds(pl.multiple_of(i * chunk, chunk), chunk)
                gb_v[q, at, :] = (u * up).astype(BF)
                slope = up + (0.5 * math.sqrt(2 / math.pi)) * u * (1.0 - th * th) * (
                    1.0 + (3 * 0.044715) * square
                )
                dact = dot(dy_v[q, pl.ds(2 * i, 2)].reshape(chunk, D), out_w[...], NT)
                du = (dact * slope).astype(BF)
                du_v[q, at, :] = du
                back_p[q, pl.ds(2 * i, 2)] = dot(du, fc_w[...], NT).astype(BF).reshape(2, T, D)

        forth_and_back(1 - s)
        meet_all(env)
        rows = reduce_blocks(env, back_p, dh2_v, *spans[0])
        next(rows)
        forth_and_back(s)
        steps(rows, 4)
        for first in range(0, D, TILE):
            left = h2_v[:, :, :, first : min(D, first + TILE)].reshape(2 * G, -1)
            made = dot(left, du_v[...].reshape(2 * G, U), TN).astype(BF)
            spread_rows(made, first, R, lambda c: fc_b.at[lay.dp_index(c), lay.tp_index(c)])
        fc_sum = reduce_columns(env, fc_b, fc_o, *spans[1])
        next(fc_sum)
        for first in range(0, U, TILE):
            left = gb_v[:, :, first : min(U, first + TILE)].reshape(2 * G, -1)
            made = dot(left, dy_v[...].reshape(2 * G, D), TN).astype(BF)
            spread_rows(made, first, FH, lambda d: out_g.at[d])
        out_sum = reduce_halves(env, out_g, out_o, *spans[2])
        fcb_o[...] = jnp.sum(du_v[...].reshape(2 * G, U).astype(F32), axis=0, keepdims=True)
        x1 = x1_r[...]
        hat, spread = norm_stats(x1)
        dy_own = dy_r[...].T.astype(F32)
        vec_o[...] = jnp.zeros_like(vec_o)
        vec_o[3:4, :] = jnp.sum(dy_own, axis=0, keepdims=True)
        for q in range(2):

            @pl.loop(0, G // chunk)
            def _(i):
                at = pl.ds(pl.multiple_of(i * chunk, chunk), chunk)
                part = dot(gb_v[q, at, :], out_w[...], NN).astype(BF)
                h2_v[q, pl.ds(2 * i, 2)] = part.reshape(2, T, D)

        leave = loads.local(h2_v, mix_o)
        steps(rows, 1)
        steps(fc_sum, n_dp // 2)
        next(out_sum)
        finish(rows)
        dh2 = dh2_v[...].astype(F32)
        scaled = dh2 * par_r[1, 0:1, :]
        dx1 = dy_own + spread * (
            scaled
            - jnp.mean(scaled, axis=-1, keepdims=True)
            - hat * jnp.mean(scaled * hat, axis=-1, keepdims=True)
        )
        dx1_o[...] = dx1
        da = dx1.astype(BF)
        load_pj.wait()
        dob = dot(pj_v[0], da[:, :half], NT) + dot(pj_v[1], da[:, half:], NT)
        dob_s[...] = dob.astype(BF).reshape(HEADS, HEAD_DIM, T)
        heads = tokens_to_heads(env, dob_s, dob_o, sems[0:3])
        next(heads)
        vec_o[0:1, :] = jnp.sum(dh2 * hat, axis=0, keepdims=True)
        vec_o[1:2, :] = jnp.sum(da.astype(F32), axis=0, keepdims=True)
        vec_o[2:3, :] = jnp.sum(dh2, axis=0, keepdims=True)
        steps(fc_sum, n_dp // 4)
        run([fc_sum, out_sum])
        finish(heads)
        leave.wait()
        env.drain()

    outs = [
        struct(2, 4, T, D),
        struct(n_dev, HEAD_DIM, T),
        struct(2, 4, R, U),
        struct(2, FH, D),
        struct(T, D, dtype=F32),
        struct(8, D, dtype=F32),
        struct(1, U, dtype=F32),
    ]
    scratch = [
        pltpu.VMEM((2, 4, T, D), BF),
        pltpu.VMEM((2, 4, T, D), BF),
        pltpu.VMEM((n_dp, 4, R, U), BF),
        pltpu.VMEM((D, U), BF),
        pltpu.VMEM((2, n_dp, FH, half), BF),
        pltpu.VMEM((U, D), BF),
        pltpu.VMEM((n_dp, FH, D), BF),
        pltpu.VMEM((2, D, half), BF),
        pltpu.VMEM((2, G, U), BF),
        pltpu.VMEM((2, G, U), BF),
        pltpu.VMEM((2, 4, T, D), BF),
        pltpu.VMEM((T, D), BF),
        pltpu.VMEM((HEADS, HEAD_DIM, T), BF),
    ]
    scratch += reduce_scratch(2, True, (T, D)) + sem_shapes(reduce_sends(2, True))
    scratch += reduce_scratch(k, False, (4, R, U)) + sem_shapes(reduce_sends(k, False) + 4)
    scratch += reduce_scratch(k, False, (FH, D)) + sem_shapes(reduce_sends(k, False) + 1)
    DMA = pltpu.SemaphoreType.DMA
    scratch += sem_shapes(1) + [DMA((7,))]
    args = (h2, dy_all, fc, out, out_x, pj, shift, x1, dy, par)
    out_specs = [ANY] * 4 + [VM] * 3
    return call("middle", 1, body, args, [ANY] * 6 + [VM] * 4, outs, out_specs, scratch)


def heads_to_group(env, src, out, sems, q):
    send_sems, recv_sems, local_sems = sems
    lay = env.lay
    held = q % src.shape[0]

    def copy(there, j, target):
        return pltpu.make_async_remote_copy(
            src_ref=src.at[held, there],
            dst_ref=out.at[q, j],
            send_sem=send_sems.at[q, there],
            recv_sem=recv_sems.at[q, j],
            device_id=(lay.compose(env.t, target), env.s),
            device_id_type=MESH,
        )

    local = pltpu.make_async_copy(src.at[held, env.d], out.at[q, env.d % HU], local_sems.at[q])

    @pl.when(env.d < HU)
    def _():
        for i in range(1, lay.n_dp):
            there = (env.d + i) % lay.n_dp
            copy(there, env.d, there).start()
        local.start()

    yield

    @pl.when(env.d < HU)
    def _():
        local.wait()

    for j in range(HU):

        @pl.when(j != env.d)
        def _():
            copy(0, j, j).wait_recv()

    yield

    @pl.when(env.d < HU)
    def _():
        for i in range(1, lay.n_dp):
            there = (env.d + i) % lay.n_dp
            copy(there, env.d, there).wait_send()


def backward(lay, x, heads, o, lse, dob, wq, h1, ob, vec, fcb, dx1, par, mix):
    n_ctx, n_dp = lay.n_ctx, lay.n_dp
    n_dev = 2 * n_ctx
    k = len(lay.dp_bits)
    T = x.shape[1]
    R, FB = D // n_ctx, FF // n_ctx
    FH = FB // 2
    W = HU * HEAD_DIM
    G = 4 * T
    half = D // 2
    length = n_ctx * T
    tile = TILE if length <= 4 * TILE else TILE // 2
    n_tiles = length // tile
    wide = UNITS * W

    def natural(c):
        return c

    def body(*refs):
        (x_r, heads_r, o_r, lse_r, dob_r, wqh_r, h1h_r, ob_r, vec_r, fcb_r, dx1_r, par_r, mix_r) = refs[:13]
        (grad_o, q_v, proj_o, small_o, mix_s) = refs[13:18]
        (
            heads_v, o_v, dob_n, qs, dobs, delta, dq_acc, parts, land, dqkv, dh1_p, dh1_v, q_g, wide_v,
            small_s, pg, wq_r, h1_r,
        ) = refs[18:36]
        rest = refs[36:]
        spans, first = [], 0
        for n in (3, k, k + 3, 3, k + 3):
            spans.append((rest[first : first + n], rest[first + n : first + n + 3]))
            first += n + 3
        sems = rest[first:]
        env = Env(lay)
        s = env.s
        hail_near(env)
        early = Links((None, None, sems[4]))
        mix_v = dh1_p.at[0]
        load_mix = early.local(mix_r.at[s], mix_v)
        load_wq = early.local(wqh_r, wq_r)
        load_h1 = early.local(h1h_r, h1_r)
        for n in range(2):
            right = dx1_r[:, n * half : (n + 1) * half].astype(BF)
            for c in range(0, n_ctx, 4):
                made = dot(ob_r[:, c * R : (c + 4) * R], right, TN).astype(BF)
                for i in range(4):
                    pg[n, lay.dp_index(c + i), lay.tp_index(c + i)] = made[i * R : (i + 1) * R, :]
        small_s[...] = jnp.zeros_like(small_s)
        wide_v[...] = jnp.zeros_like(wide_v)
        meet_near(env)
        proj = reduce_all(env, pg, proj_o, *spans[2])
        next(proj)
        mixing = reduce_blocks(env, mix_r, mix_s, *spans[3], own=mix_v)
        next(mixing)
        load_mix.wait()
        moving = []
        _, active = own_head(env)

        def loads(q):
            copies = [pltpu.make_async_copy(heads_r.at[n, q], heads_v.at[n], sems[3].at[n]) for n in range(3)]
            copies.append(pltpu.make_async_copy(o_r.at[q], o_v, sems[3].at[3]))
            for c in range(n_ctx):
                there = dob_n.at[:, pl.ds(c * T, T)]
                copies.append(pltpu.make_async_copy(dob_r.at[q * n_ctx + c], there, sems[3].at[4 + c]))
            return copies

        for copy in loads(0):
            copy.start()
        for q in range(2):
            for copy in loads(q):
                copy.wait()

            @pl.when(jnp.logical_not(active))
            def _():
                dob_n[...] = jnp.zeros_like(dob_n)

            qs[...] = heads_v[0].T
            dobs[...] = dob_n[...].T
            delta[...] = jnp.sum(dob_n[...].astype(F32) * o_v[...], axis=0, keepdims=True)
            dq_acc[...] = jnp.zeros_like(dq_acc)

            if q == 1 and parts.shape[0] == 1:
                finish(moving[0])

            def put(n, first, block):
                for b in range(block.shape[1] // T):
                    c = first // T + b
                    tc, dc = lay.tp_index(c), lay.dp_index(c)
                    parts[q % parts.shape[0], dc, n * HEAD_DIM : (n + 1) * HEAD_DIM, tc * T : (tc + 1) * T] = block[
                        :, b * T : (b + 1) * T
                    ]

            for j in range(n_tiles):
                here = slice(j * tile, (j + 1) * tile)
                kt = heads_v[1, :, here]
                keys = kt.T
                values = heads_v[2, :, here].T

                def step(i, carry, masked):
                    dk, dv = carry
                    at = pl.ds(pl.multiple_of(i * tile, tile), tile)
                    st = dot(keys, heads_v[0, :, at], NN) * (SCALE * LOG2E)
                    p = jnp.exp2(st - lse_r[q, :, at])
                    if masked:
                        row = lax.broadcasted_iota(jnp.int32, (tile, tile), 0)
                        col = lax.broadcasted_iota(jnp.int32, (tile, tile), 1)
                        p = jnp.where(row <= col, p, 0.0)
                    dp = dot(values, dob_n[:, at], NN)
                    ds = (p * (dp - delta[:, at])).astype(BF)
                    dv = dv + dot(p.astype(BF), dobs[at, :], NN)
                    dk = dk + dot(ds, qs[at, :], NN)
                    dq_acc[:, at] += dot(kt, ds, NN)
                    return dk, dv

                zero = jnp.zeros((tile, HEAD_DIM), F32)
                carry = step(j, (zero, zero), True)
                if j + 1 < n_tiles:
                    carry = lax.fori_loop(j + 1, n_tiles, functools.partial(step, masked=False), carry)
                put(1, j * tile, (carry[0] * SCALE).T.astype(BF))
                put(2, j * tile, carry[1].T.astype(BF))
                if q == 0 and j == 0:
                    steps(proj, n_dp)
                if q == 0 and j == 1:
                    steps(mixing, 4)
                if q == 1 and j == 0:
                    steps(proj, n_dp // 2)
                if q == 1 and j >= n_tiles - 2:
                    steps(mixing, 1)
            put(0, 0, (dq_acc[...] * SCALE).astype(BF))
            if q == 0:
                for copy in loads(1):
                    copy.start()
            g = heads_to_group(env, parts, land, sems[0:3], q)
            next(g)
            moving.append(g)
        steps(proj, n_dp // 4 + 1)
        load_wq.wait()
        load_h1.wait()
        for q in range(2):
            next(moving[q], None)
            rows = []
            for n in range(3):
                for j in range(HU):
                    rows.append(land[q, j, n * HEAD_DIM : (n + 1) * HEAD_DIM, :])
            dqkv[q] = jnp.concatenate(rows, axis=0).T
            dh1_p[q] = dot(dqkv[q], wq_r[...], NT).astype(BF).reshape(4, T, D)
        rows_h1 = reduce_blocks(env, dh1_p, dh1_v, *spans[0])
        next(rows_h1)
        sums = jnp.sum(dqkv[0].astype(F32), axis=0, keepdims=True) + jnp.sum(
            dqkv[1].astype(F32), axis=0, keepdims=True
        )
        for c in range(0, n_ctx, 4):
            at = slice(c * R, (c + 4) * R)
            made = dot(h1_r[at, :], dqkv[...].reshape(2 * G, 3 * W), NN)
            low = made.astype(BF)
            for i in range(4):
                q_g[lay.dp_index(c + i), lay.tp_index(c + i)] = low[i * R : (i + 1) * R, :]
            weight = wq_r[at, :].astype(F32)
            for n, product in enumerate((made * weight, weight * sums)):
                folded = product[:, :128]
                for lane in range(128, 3 * W, 128):
                    folded = folded + product[:, lane : lane + 128]
                wide_v[n : n + 1, at] = jnp.sum(folded.T, axis=0, keepdims=True)
            if c == n_ctx // 2:
                steps(rows_h1, 4)
        grads = reduce_columns(env, q_g, q_v, *spans[1])
        next(grads)
        unit = 2 * env.t + s
        cols = pl.ds(pl.multiple_of(unit * W, W), W)
        wide_v[2:3, cols] = sums[:, :W]
        wide_v[3:4, cols] = sums[:, 2 * W :]
        wide_v[0:1, :D] = (wide_v[0:1, :D] - par_r[0, 1:2, :] * wide_v[1:2, :D]) / par_r[0, 0:1, :]
        for c in range(n_ctx):
            small_s[0, lay.dp_index(c), lay.tp_index(c), 0:4, :R] = wide_v[0:4, c * R : (c + 1) * R]
            small_s[1, lay.dp_index(c), lay.tp_index(c), 0:4, :R] = vec_r[0:4, c * R : (c + 1) * R]
        for d in range(n_dp):
            for h in range(2):
                first = d * FH + h * (FH // 2)
                small_s[s, d, env.t, 4 + h : 5 + h, : FH // 2] = fcb_r[:, first : first + FH // 2]
        small = reduce_all(env, small_s, small_o, *spans[4])
        next(small)
        hat, spread = norm_stats(x_r[...].T.astype(F32))
        steps(rows_h1, 1)
        finish(mixing)
        steps(small, n_dp)
        steps(grads, n_dp // 2)
        steps(rows_h1, 1)
        steps(small, n_dp // 2)
        steps(grads, n_dp // 4)
        finish(rows_h1)
        dh1 = dh1_v[...].astype(F32)
        scaled = dh1 * par_r[0, 0:1, :]
        grad_o[...] = dx1_r[...] + spread * (
            scaled
            - jnp.mean(scaled, axis=-1, keepdims=True)
            - hat * jnp.mean(scaled * hat, axis=-1, keepdims=True)
        )
        finish(proj)
        finish(small)
        finish(grads)
        for g in moving:
            finish(g)
        env.drain()

    outs = [
        struct(T, D, dtype=F32),
        struct(2, 4, R, 3 * W),
        struct(R, half),
        struct(8, 128, dtype=F32),
        struct(T, D),
    ]
    scratch = [
        pltpu.VMEM((3, HEAD_DIM, length), BF),
        pltpu.VMEM((HEAD_DIM, length), F32),
        pltpu.VMEM((HEAD_DIM, length), BF),
        pltpu.VMEM((length, HEAD_DIM), BF),
        pltpu.VMEM((length, HEAD_DIM), BF),
        pltpu.VMEM((1, length), F32),
        pltpu.VMEM((HEAD_DIM, length), F32),
        pltpu.VMEM((2 if n_ctx <= 16 else 1, n_dp, QKV, G), BF),
        pltpu.VMEM((2, HU, QKV, G), BF),
        pltpu.VMEM((2, G, 3 * W), BF),
        pltpu.VMEM((2, 4, T, D), BF),
        pltpu.VMEM((T, D), BF),
        pltpu.VMEM((n_dp, 4, R, 3 * W), BF),
        pltpu.VMEM((8, wide), F32),
        pltpu.VMEM((2, n_dp, 4, 8, 128), F32),
        pltpu.VMEM((2, n_dp, 4, R, half), BF),
        pltpu.VMEM((D, 3 * W), BF),
        pltpu.VMEM((D, 2 * G), BF),
    ]
    blocks = reduce_scratch(2, True, (T, D)) + sem_shapes(reduce_sends(2, True))
    scratch += blocks
    scratch += reduce_scratch(k, False, (4, R, 3 * W)) + sem_shapes(reduce_sends(k, False) + 4)
    scratch += reduce_scratch(k, True, (4, R, half)) + reduce_scratch(2, False, (R, half))
    scratch += sem_shapes(reduce_sends(k, True) + reduce_sends(2, False))
    scratch += blocks
    scratch += reduce_scratch(k, True, (4, 8, 128), F32) + reduce_scratch(2, False, (8, 128), F32)
    scratch += sem_shapes(reduce_sends(k, True) + reduce_sends(2, False))
    DMA = pltpu.SemaphoreType.DMA
    scratch += [DMA((2, n_dp)), DMA((2, HU)), DMA((2,)), DMA((4 + n_ctx,)), DMA((3,))]
    args = (x, heads, o, lse, dob, wq, h1, ob, vec, fcb, dx1, par, mix)
    in_specs = [VM, ANY, ANY, VM, ANY, ANY, ANY] + [VM] * 5 + [ANY]
    return call("backward", 2, body, args, in_specs, outs, [VM, ANY, VM, VM, VM], scratch)


def assemble(lay, q, fc, out, proj, grad, mix, x1, par, small):
    n_ctx, n_dp = lay.n_ctx, lay.n_dp
    T = grad.shape[0]
    R, FB = D // n_ctx, FF // n_ctx
    FH = FB // 2
    W = HU * HEAD_DIM
    half = D // 2

    def body(*refs):
        (q_r, fc_r, out_r, proj_r, grad_r, mix_r, x1_r, par_r, small_r) = refs[:9]
        (mixed_o, grad_o, qkv_o, proj_o, fc_o, out_o, gains_o, biases_o, fcb_o) = refs[9:]
        mixed_o[...] = (x1_r[...] + mix_r[...].astype(F32) + par_r[1, 3:4, :]).astype(BF).T
        grad_o[...] = grad_r[...].T
        proj_o[...] = proj_r[...].astype(F32)
        gains_o[...] = small_r[0:1, :R]
        biases_o[...] = small_r[1:4, :R]
        fcb_o[...] = small_r[4:6, : FH // 2]

        def last(side):
            thirds = []
            for n in range(3):
                pieces = [q_r[h, u][:, n * W : (n + 1) * W] for u in range(4) for h in range(2)]
                thirds.append(jnp.concatenate(pieces, axis=1)[:, :D])
            whole = jnp.concatenate(thirds, axis=1)
            qkv_o[...] = whole[:, side * (3 * half) : (side + 1) * (3 * half)].astype(F32)
            pieces = []
            for c in range(n_ctx // 2 * side, n_ctx // 2 * (side + 1)):
                for h in range(2):
                    first = lay.dp_index(c) * FH
                    pieces.append(fc_r[h, lay.tp_index(c)][:, first : first + FH])
            fc_o[...] = jnp.concatenate(pieces, axis=1).astype(F32)
            out_o[...] = jnp.concatenate(
                [out_r[h][:, side * half : (side + 1) * half] for h in range(2)], axis=0
            ).astype(F32)

        by_side(lax.axis_index("fsdp"), last)

    outs = [
        struct(D, T),
        struct(D, T, dtype=F32),
        struct(R, 3 * half, dtype=F32),
        struct(R, half, dtype=F32),
        struct(R, FF // 2, dtype=F32),
        struct(FB, half, dtype=F32),
        struct(1, R, dtype=F32),
        struct(3, R, dtype=F32),
        struct(2, FH // 2, dtype=F32),
    ]
    return pl.pallas_call(
        body,
        out_shape=outs,
        in_specs=[VM] * 9,
        out_specs=[VM] * 9,
        compiler_params=pltpu.CompilerParams(vmem_limit_bytes=VMEM_LIMIT),
        name="assemble",
    )(q, fc, out, proj, grad, mix, x1, par, small)


def shards(lay, tokens, qkv_weight, proj_weight, fc_weight, out_weight, gains, biases, fc_bias, cotangent):
    T = tokens.shape[1]
    R = D // lay.n_ctx
    FH = FF // lay.n_ctx // 2
    x = jnp.transpose(tokens, (0, 2, 1)).reshape(D, T)
    dy = jnp.transpose(cotangent, (0, 2, 1)).reshape(D, T)
    (h1, wq, heads, o, pj, h2, fc, out, out_x, dy_all, lse, ob, x1, shift, par) = forward(
        lay, x, gains, biases, fc_bias.reshape(2, FH // 2), qkv_weight, fc_weight, out_weight, proj_weight, dy
    )
    mix, dob, fc_sum, out_sum, dx1, vec, fcb = middle(
        lay, x, h2, dy_all, fc, out, out_x, shift, x1, dy, pj, par
    )
    grad, q_sum, proj_sum, small, mix_sum = backward(
        lay, x, heads, o, lse, dob, wq, h1, ob, vec, fcb, dx1, par, mix
    )
    (mixed, grad, qkv_grad, proj_grad, fc_grad, out_grad, gains_grad, biases_grad, fc_bias_grad) = assemble(
        lay, q_sum, fc_sum, out_sum, proj_sum, grad, mix_sum, x1, par, small
    )
    return (
        jnp.transpose(mixed.reshape(1, D, T), (0, 2, 1)),
        jnp.transpose(grad.reshape(1, D, T), (0, 2, 1)),
        qkv_grad,
        proj_grad,
        fc_grad,
        out_grad,
        gains_grad,
        biases_grad,
        fc_bias_grad.reshape(FH),
    )


def solution(mesh):
    lay = Layout(mesh.shape["ctx"])
    in_specs = (
        P("fsdp", "ctx", None),
        P("ctx", "fsdp"),
        P("ctx", "fsdp"),
        P("ctx", "fsdp"),
        P("ctx", "fsdp"),
        P("fsdp", "ctx"),
        P("fsdp", "ctx"),
        P(("ctx", "fsdp")),
        P("fsdp", "ctx", None),
    )
    out_specs = (
        P("fsdp", "ctx", None),
        P("fsdp", "ctx", None),
        P("ctx", "fsdp"),
        P("ctx", "fsdp"),
        P("ctx", "fsdp"),
        P("ctx", "fsdp"),
        P("fsdp", "ctx"),
        P("fsdp", "ctx"),
        P(("ctx", "fsdp")),
    )
    return jax.shard_map(
        functools.partial(shards, lay), mesh=mesh, in_specs=in_specs, out_specs=out_specs, check_vma=False
    )
```

```python
import functools
import math

import jax
import jax.numpy as jnp
from jax import lax
from jax.experimental import pallas as pl
from jax.experimental.pallas import tpu as pltpu
from jax.sharding import PartitionSpec as P

D = 1600
HEADS = 25
HEAD_DIM = 64
FF = 6400
EPS = 1e-05
UNITS = 8
HU = -(-HEADS // UNITS)
QKV = 3 * HEAD_DIM
MESH = pl.DeviceIdType.MESH
BF = jnp.bfloat16
F32 = jnp.float32
VMEM_LIMIT = 60 * 1024 * 1024
LOG2E = 1.0 / math.log(2.0)


class Layout:
    def __init__(self, n_ctx):
        self.n_ctx = n_ctx
        a, b = n_ctx // 4, n_ctx // 2
        self.tp_bits = (b, a)
        self.dp_bits = tuple(1 << i for i in range(n_ctx.bit_length() - 3))
        self.n_dp = n_ctx // 4
        self.dp_order = list(zip(self.dp_bits, self.dp_bits[::-1]))
        self.tp_order = [(b, b), (a, a)]
        self.tp_masks = [[], [(a, a)], [(b, b)], [(a, a), (b, b)]]

    def tp_index(self, c):
        return sum(((c // b) % 2) * (1 << i) for i, b in enumerate(self.tp_bits))

    def dp_index(self, c):
        return sum(((c // b) % 2) * (1 << i) for i, b in enumerate(self.dp_bits))

    def compose(self, t, d):
        return sum(((t // (1 << i)) % 2) * b for i, b in enumerate(self.tp_bits)) + sum(
            ((d // (1 << i)) % 2) * b for i, b in enumerate(self.dp_bits)
        )

    def head_rank(self, h):
        u, j = h // HU, h % HU
        return self.compose(u // 2, j) * 2 + u % 2

    def to_natural(self, x):
        labels = list(self.dp_bits[::-1]) + list(self.tp_bits[::-1])
        k = len(labels)
        rest = x.shape[2:]
        x = x.reshape((2,) * k + rest)
        order = sorted(range(k), key=lambda i: -labels[i])
        x = jnp.transpose(x, order + list(range(k, k + len(rest))))
        return x.reshape((self.n_ctx,) + rest)

    def from_natural(self, x):
        labels = list(self.dp_bits[::-1]) + list(self.tp_bits[::-1])
        k = len(labels)
        rest = x.shape[1:]
        x = x.reshape((2,) * k + rest)
        natural = sorted(labels, reverse=True)
        order = [natural.index(b) for b in labels]
        x = jnp.transpose(x, order + list(range(k, k + len(rest))))
        return x.reshape((self.n_dp, 4) + rest)


def flip(c, sym, s):
    def one(b):
        return c + b * (1 - 2 * ((c // b) % 2))

    if sym[0] == sym[1]:
        return one(sym[0])
    return one(sym[0]) * (1 - s) + one(sym[1]) * s


def flips(c, masks, s):
    for sym in masks:
        c = flip(c, sym, s)
    return c


class Env:
    def __init__(self, layout):
        self.lay = layout
        self.c = lax.axis_index("ctx")
        self.s = lax.axis_index("fsdp")
        self.t = layout.tp_index(self.c)
        self.d = layout.dp_index(self.c)
        self.rank = self.c * 2 + self.s
        self.n_dev = layout.n_ctx * 2
        self.opened = []

    def other(self):
        return (self.c, 1 - self.s)

    def drain(self):
        for links in self.opened:
            links.drain()


class Links:
    def __init__(self, sems, env=None):
        self.send_sems, self.recv_sems, self.local_sems = sems
        if env is not None:
            env.opened.append(self)
        self.count = 0
        self.local_count = 0
        self.sent = []
        self.locals = []

    def send(self, src, dst, device):
        copy = pltpu.make_async_remote_copy(
            src_ref=src,
            dst_ref=dst,
            send_sem=self.send_sems.at[self.count],
            recv_sem=self.recv_sems.at[self.count],
            device_id=device,
            device_id_type=MESH,
        )
        copy.start()
        self.count += 1
        self.sent.append(copy)
        return copy

    def local(self, src, dst):
        copy = pltpu.make_async_copy(src, dst, self.local_sems.at[self.local_count])
        copy.start()
        self.local_count += 1
        self.locals.append(copy)
        return copy

    def settle(self):
        for copy in self.locals:
            copy.wait()
        self.locals = []

    def drain(self):
        self.settle()
        for copy in self.sent:
            copy.wait_send()


def sem_shapes(sends, local=1):
    sends = max(sends, 1)
    return [
        pltpu.SemaphoreType.DMA((sends,)),
        pltpu.SemaphoreType.DMA((sends,)),
        pltpu.SemaphoreType.DMA((local,)),
    ]


def meet(env, devices):
    barrier = pltpu.get_barrier_semaphore()
    for device in devices:
        pl.semaphore_signal(barrier, inc=1, device_id=device, device_id_type=MESH)
    pl.semaphore_wait(barrier, len(devices))


def hail_all(env):
    barrier = pltpu.get_barrier_semaphore()

    def hail(i, carry):
        rank = (env.rank + i) % env.n_dev
        pl.semaphore_signal(barrier, inc=1, device_id=(rank // 2, rank % 2), device_id_type=MESH)
        return carry

    lax.fori_loop(1, env.n_dev, hail, 0)


def near(env):
    lay = env.lay
    return (
        [(flips(env.c, m, env.s), env.s) for m in lay.tp_masks[1:]]
        + [(lay.compose(env.t, (env.d + i) % lay.n_dp), env.s) for i in range(1, lay.n_dp)]
        + [env.other()]
    )


def hail_near(env):
    barrier = pltpu.get_barrier_semaphore()
    for device in near(env):
        pl.semaphore_signal(barrier, inc=1, device_id=device, device_id_type=MESH)


def meet_near(env):
    pl.semaphore_wait(pltpu.get_barrier_semaphore(), len(near(env)))


def meet_all(env):
    pl.semaphore_wait(pltpu.get_barrier_semaphore(), env.n_dev - 1)


def tp_partners(env):
    return [(flips(env.c, m, env.s), env.s) for m in env.lay.tp_masks[1:]]


def dp_partners(env):
    return [(flip(env.c, sym, env.s), env.s) for sym in env.lay.dp_order]


def run(generators):
    active = list(generators)
    while active:
        left = []
        for g in active:
            try:
                next(g)
                left.append(g)
            except StopIteration:
                pass
        active = left


def gather_sends(bits, core):
    return (1 << bits) - 1 + (1 << bits if core else 0)


def gather(env, links, src, buf, bits, slot, core=False, half=None, placed=False):
    c, s = env.c, env.s

    def place(masks):
        return buf.at[slot(flips(c, masks, s))]

    if not placed:
        links.local(src, place([]))
    levels = [[([], None)]] + [[] for _ in bits]
    crossing = []
    for k in range(len(bits) + 1):
        for masks, copy in levels[k]:
            if copy is None:
                ref = src
            else:
                copy.wait_recv()
                ref = place(masks)
            for j in range(k, len(bits)):
                forward = links.send(ref, place(masks), (flip(c, bits[j], s), s))
                levels[j + 1].append((masks + [bits[j]], forward))
            if core:
                crossing.append(links.send(ref, place(masks), env.other()))
            if half is not None:
                there = half.at[slot(flips(c, masks, s))]
                crossing.append(links.send(ref.at[1 - s], there, env.other()))
            yield
    for copy in crossing:
        copy.wait_recv()


def gather_blocks(env, src, buf, sems, bits, slot, core=False, half=None):
    links = Links(sems, env)
    yield from gather(env, links, src, buf.at[env.s] if core else buf, bits, slot, core, half)
    links.settle()
    yield


def gather_columns(env, src, buf, sems):
    lay = env.lay
    links = Links(sems, env)
    own = buf.at[env.d]
    copies = [links.local(src.at[env.t], own.at[env.t])]
    for m in lay.tp_masks[1:]:
        there = flips(env.c, m, env.s)
        copies.append(links.send(src.at[lay.tp_index(there)], own.at[env.t], (there, env.s)))
    yield
    links.settle()
    for copy in copies[1:]:
        copy.wait_recv()
    yield from gather(env, links, own, buf, lay.dp_order, lay.dp_index, placed=True)
    links.settle()
    yield


def gather_all(env, src, buf, sems):
    lay = env.lay
    links = Links(sems, env)
    mine = buf.at[env.s]
    own = mine.at[env.d]
    yield from gather(env, links, src, own, lay.tp_order, lay.tp_index)
    links.settle()
    yield from gather(env, links, own, mine, lay.dp_order, lay.dp_index, core=True, placed=True)
    links.settle()
    yield


def gather_small(env, src, buf, sems):
    lay = env.lay
    links = Links(sems, env)
    mine = buf.at[env.s]
    own = mine.at[env.d]
    local = links.local(src, own.at[env.t])
    copies = []
    for m in lay.tp_masks[1:]:
        copies.append(links.send(src, own.at[env.t], (flips(env.c, m, env.s), env.s)))
    yield
    links.settle()
    for copy in copies:
        copy.wait_recv()
    copies = []
    for i in range(1, lay.n_dp):
        there = lay.compose(env.t, (env.d + i) % lay.n_dp)
        copies.append(links.send(own, own, (there, env.s)))
    yield
    for copy in copies:
        copy.wait_recv()
    copy = links.send(mine, mine, env.other())
    yield
    copy.wait_recv()
    links.settle()
    yield


def reduce_sends(bits, core):
    return (1 << bits) - 1 + (1 << bits if core else 0)


def reduce_scratch(bits, core, block, dtype=BF):
    return [pltpu.VMEM((1 << j,) + block, dtype) for j in range(bits + (1 if core else 0))]


def add_into(total, term):
    if len(total.shape) == 2:
        total[...] = total[...] + term[...]
    else:
        for i in range(total.shape[0]):
            add_into(total.at[i], term.at[i])


def reduce(env, links, inp, parts, bits, slot, core=False, own=None):
    c, s = env.c, env.s
    levels = [[[]]]
    for sym in bits:
        levels.append(levels[-1] + [m + [sym] for m in levels[-1]])

    def at(side, masks):
        index = slot(flips(c, masks, side))
        return inp.at[side, index] if core else inp.at[index]

    last = levels[-1]
    if own is None:
        now = [at(s, m) for m in last]
    else:
        now = [own.at[slot(flips(c, m, s))] for m in last]
    copies = {}
    if core:
        stage = len(bits)
        for i in reversed(range(len(last))):
            copies[i] = links.send(at(1 - s, last[i]), parts[stage].at[i], env.other())
    else:
        stage = len(bits) - 1
        n = len(levels[stage])
        for i in reversed(range(n)):
            copies[i] = links.send(now[n + i], parts[stage].at[i], (flip(c, bits[stage], s), s))
    yield
    while stage >= 0:
        n = len(levels[stage])
        got = parts[stage]
        after = {}
        for i in reversed(range(n)):
            copies[i].wait_recv()
            add_into(got.at[i], now[i])
            if stage > 0 and i >= n // 2:
                after[i - n // 2] = links.send(
                    got.at[i], parts[stage - 1].at[i - n // 2], (flip(c, bits[stage - 1], s), s)
                )
            yield
        now = [got.at[i] for i in range(n)]
        copies = after
        stage -= 1
    return now[0]


def reduce_blocks(env, inp, out, parts, sems, own=None):
    links = Links(sems, env)
    total = yield from reduce(env, links, inp, parts, env.lay.tp_order, env.lay.tp_index, core=True, own=own)
    out[...] = total[...].astype(out.dtype)
    links.settle()
    yield


def reduce_columns(env, inp, out, parts, sems):
    lay = env.lay
    links = Links(sems, env)
    total = yield from reduce(env, links, inp, parts, lay.dp_order, lay.dp_index)
    local = links.local(total.at[env.t], out.at[env.s, env.t])
    copies = []
    for m in lay.tp_masks[1:]:
        there = flips(env.c, m, env.s)
        copies.append(links.send(total.at[lay.tp_index(there)], out.at[env.s, env.t], (there, env.s)))
    yield
    links.settle()
    for copy in copies:
        copy.wait_recv()
    copy = links.send(out.at[env.s], out.at[env.s], env.other())
    yield
    copy.wait_recv()
    links.settle()
    yield


def reduce_halves(env, inp, out, parts, sems):
    lay = env.lay
    links = Links(sems, env)
    total = yield from reduce(env, links, inp, parts, lay.dp_order, lay.dp_index)
    links.local(total, out.at[env.s])
    copy = links.send(total, out.at[env.s], env.other())
    yield
    copy.wait_recv()
    links.settle()
    yield


def reduce_all(env, inp, out, parts, sems):
    lay = env.lay
    links = Links(sems, env)
    n = len(lay.dp_bits) + 1
    total = yield from reduce(env, links, inp, parts[:n], lay.dp_order, lay.dp_index, core=True)
    total = yield from reduce(env, links, total, parts[n:], lay.tp_order, lay.tp_index)
    out[...] = total[...].astype(out.dtype)
    links.settle()
    yield


def own_head(env):
    h = (env.t * 2 + env.s) * HU + env.d
    return h, jnp.logical_and(env.d < HU, h < HEADS)


def wait_pieces(env, ref, count, send=None, recv=None):
    part = ref.at[pl.ds(0, count)]
    copy = pltpu.make_async_remote_copy(
        src_ref=part,
        dst_ref=part,
        send_sem=recv if send is None else send,
        recv_sem=send if recv is None else recv,
        device_id=env.other(),
        device_id_type=MESH,
    )
    if send is not None:
        copy.wait_send()
    if recv is not None:
        copy.wait_recv()


def tokens_to_heads(env, src, out, sems):
    send_sem, recv_sem, local_sem = sems[0].at[0], sems[1].at[0], sems[2].at[0]
    h, active = own_head(env)
    lay = env.lay
    place = env.s * lay.n_ctx + env.c

    def begin(i, carry):
        j = (env.rank + i) % HEADS
        rank = lay.head_rank(j)

        @pl.when(rank != env.rank)
        def _():
            pltpu.make_async_remote_copy(
                src_ref=src.at[j],
                dst_ref=out.at[place],
                send_sem=send_sem,
                recv_sem=recv_sem,
                device_id=(rank // 2, rank % 2),
                device_id_type=MESH,
            ).start()

        return carry

    lax.fori_loop(0, HEADS, begin, 0)
    yield

    @pl.when(active)
    def _():
        local = pltpu.make_async_copy(src.at[h], out.at[place], local_sem)
        local.start()
        local.wait()
        wait_pieces(env, out, env.n_dev - 1, recv=recv_sem)
        wait_pieces(env, src, HEADS - 1, send=send_sem)

    @pl.when(jnp.logical_not(active))
    def _():
        wait_pieces(env, src, HEADS, send=send_sem)


ANY = pl.BlockSpec(memory_space=pl.ANY)
VM = pl.BlockSpec(memory_space=pltpu.VMEM)


def struct(*shape, dtype=BF):
    return jax.ShapeDtypeStruct(shape, dtype)


def call(name, cid, body, args, in_specs, outs, out_specs, scratch):
    return pl.pallas_call(
        body,
        out_shape=outs,
        in_specs=in_specs,
        out_specs=out_specs,
        scratch_shapes=scratch,
        compiler_params=pltpu.CompilerParams(
            collective_id=cid, has_side_effects=True, vmem_limit_bytes=VMEM_LIMIT
        ),
        name=name,
    )(*args)


def dot(left, right, dims):
    return lax.dot_general(left, right, (dims, ((), ())), preferred_element_type=F32)


NN = ((1,), (0,))
NT = ((1,), (1,))
TN = ((0,), (0,))
SCALE = 1.0 / math.sqrt(HEAD_DIM)
TILE = 512


class Background:
    def __init__(self):
        self.active = []

    def add(self, generator):
        self.active.append(generator)

    def step(self, count=1):
        for _ in range(count):
            if not self.active:
                return
            g = self.active.pop(0)
            try:
                next(g)
                self.active.append(g)
            except StopIteration:
                pass

    def finish(self):
        while self.active:
            self.step()


def finish(generator):
    for _ in generator:
        pass


def group_to_heads(env, src, out, sems, q):
    send_sems, recv_sems, local_sems = sems
    lay = env.lay

    def copy(j, source, target):
        return pltpu.make_async_remote_copy(
            src_ref=src.at[q, j],
            dst_ref=out.at[q, source],
            send_sem=send_sems.at[q, j],
            recv_sem=recv_sems.at[q, source],
            device_id=(lay.compose(env.t, target), env.s),
            device_id_type=MESH,
        )

    for i in range(1, HU + 1):
        j = (env.d + i) % HU

        @pl.when(j != env.d)
        def _():
            copy(j, env.d, j).start()

    local = pltpu.make_async_copy(src.at[q, env.d % HU], out.at[q, env.d], local_sems.at[q])

    @pl.when(env.d < HU)
    def _():
        local.start()

    yield

    @pl.when(env.d < HU)
    def _():
        local.wait()
        for i in range(1, lay.n_dp):
            source = (env.d + i) % lay.n_dp
            copy(0, source, source).wait_recv()

    yield
    for j in range(HU):

        @pl.when(j != env.d)
        def _():
            copy(j, env.d, j).wait_send()


def heads_out(env, src, out, sems, q):
    send_sem, recv_sem = sems[0].at[q], sems[1].at[0]
    h, active = own_head(env)
    n_ctx = env.lay.n_ctx

    def copy(i):
        there = (env.c + i) % n_ctx
        return pltpu.make_async_remote_copy(
            src_ref=src.at[q, there],
            dst_ref=out.at[h],
            send_sem=send_sem,
            recv_sem=recv_sem,
            device_id=(there, q),
            device_id_type=MESH,
        )

    local = pltpu.make_async_copy(src.at[q, env.c], out.at[h], sems[2].at[q])
    mine = jnp.logical_and(active, env.s == q)
    theirs = jnp.logical_and(active, env.s != q)

    def begin(i, carry):
        copy(i).start()
        return carry

    @pl.when(mine)
    def _():
        local.start()

    @pl.when(theirs)
    def _():
        copy(0).start()

    @pl.when(active)
    def _():
        lax.fori_loop(1, n_ctx, begin, 0)

    yield

    @pl.when(mine)
    def _():
        local.wait()

    yield

    @pl.when(mine)
    def _():
        wait_pieces(env, src.at[q], n_ctx - 1, send=send_sem)

    @pl.when(theirs)
    def _():
        wait_pieces(env, src.at[q], n_ctx, send=send_sem)


def heads_in(env, out, sems):
    _, active = own_head(env)

    @pl.when(active)
    def _():
        wait_pieces(env, out, HEADS - 1, recv=sems[1].at[0])

    @pl.when(jnp.logical_not(active))
    def _():
        wait_pieces(env, out, HEADS, recv=sems[1].at[0])


def norm_stats(values):
    centre = values - jnp.mean(values, axis=-1, keepdims=True)
    spread = lax.rsqrt(jnp.mean(centre * centre, axis=-1, keepdims=True) + EPS)
    return centre * spread, spread


def attend_tile(i, tile, qt, keys, v_ref):
    def step(j, carry, masked):
        peak, total, acc = carry
        at = pl.ds(pl.multiple_of(j * tile, tile), tile)
        st = dot(keys[at, :], qt, NN) * (SCALE * LOG2E)
        if masked:
            row = lax.broadcasted_iota(jnp.int32, (tile, tile), 0)
            col = lax.broadcasted_iota(jnp.int32, (tile, tile), 1)
            st = jnp.where(row <= col, st, -1e30)
        new = jnp.maximum(peak, jnp.max(st, axis=0, keepdims=True))
        p = jnp.exp2(st - new)
        shrink = jnp.exp2(peak - new)
        total = total * shrink + jnp.sum(p, axis=0, keepdims=True)
        acc = acc * shrink + dot(v_ref[:, at], p.astype(BF), NN)
        return new, total, acc

    start = (
        jnp.full((1, tile), -1e30, F32),
        jnp.zeros((1, tile), F32),
        jnp.zeros((HEAD_DIM, tile), F32),
    )
    carry = start
    if i > 0:
        carry = lax.fori_loop(0, i, functools.partial(step, masked=False), carry)
    peak, total, acc = step(i, carry, True)
    return acc / total, peak + jnp.log2(total)


def forward(lay, x, gains, biases, fc_bias, qkv, fc, out, proj, dy):
    n_ctx, n_dp = lay.n_ctx, lay.n_dp
    n_dev = 2 * n_ctx
    k = len(lay.dp_bits)
    T = x.shape[1]
    R, FB = D // n_ctx, FF // n_ctx
    FH = FB // 2
    W = HU * HEAD_DIM
    G = 4 * T
    length = n_ctx * T
    tile = min(TILE, length)
    n_tiles = length // tile
    half = D // 2
    wide = UNITS * W

    def natural(c):
        return c

    def body(*refs):
        (x_r, gains_r, biases_r, fcb_r, qkv_r, fc_r, out_r, proj_r, dy_r) = refs[:9]
        (h1_o, wq_o, heads_o, o_o, pj_o, h2_o, fc_o, out_o, outx_o, dy_o, lse_o, ob_o, x1_o, shift_o, par_o) = refs[9:24]
        (
            pack, small, qkv_x, fc_x, qkv_s, fc_s, out_s, wq_b, wq_v, x_v, h1_v, par_w,
            parts, mine, keys, heads_v, o_v, o_low, ob_b, proj_b, pj_v, h2_s, x_s, dy_s, h1_t,
        ) = refs[24:49]
        sems = refs[49:]
        groups = [sems[3 * i : 3 * i + 3] for i in range(len(sems) // 3)]
        env = Env(lay)
        s = env.s

        hail_all(env)
        x_s[...] = x_r[...].T
        pack[...] = jnp.zeros_like(pack)
        pack[0:1, :R] = gains_r[...].astype(F32)
        pack[1:4, :R] = biases_r[...].astype(F32)
        row = fcb_r[...].astype(F32).reshape(1, FH)
        pack[4:5, : FH // 2] = row[:, : FH // 2]
        pack[5:6, : FH // 2] = row[:, FH // 2 :]
        for h in range(2):
            out_s[h] = out_r[h * FH : (h + 1) * FH, :]
        par_w[...] = jnp.zeros_like(par_w)
        meet_all(env)
        links = Links(groups[0], env)
        crossing = [links.send(a, b, env.other()) for a, b in ((qkv_r, qkv_x), (fc_r, fc_x))]
        params = gather_small(env, pack, small, groups[1])
        next(params)

        def fill_qkv(a, b, side):
            q = a[:, :D]
            keys_all = jnp.concatenate([a[:, D:], b[:, : D // 2]], axis=1)
            v = b[:, D // 2 :]
            for u in range(4):
                first = (2 * u + side) * W
                width = max(0, min(W, D - first))
                for n, part in enumerate((q, keys_all, v)):
                    if width < W:
                        qkv_s[u, :, n * W : (n + 1) * W] = jnp.zeros((R, W), BF)
                    if width > 0:
                        qkv_s[u, :, n * W : n * W + width] = part[:, first : first + width]

        def fill_fc(a, b, side):
            for u in range(4):
                for d in range(n_dp):
                    first = lay.compose(u, d) * FB + side * FH
                    source, first = (a, first) if first < FF // 2 else (b, first - FF // 2)
                    fc_s[u, :, d * FH : (d + 1) * FH] = source[:, first : first + FH]

        crossing[0].wait_recv()
        by_side(s, lambda side: fill_qkv(*((qkv_r, qkv_x) if side == 0 else (qkv_x, qkv_r)), side))
        steps(params, 1)
        weights = gather_columns(env, qkv_s, wq_b, groups[2])
        next(weights)
        rows_x = gather_blocks(env, x_s, x_v, groups[3], lay.tp_order, lay.tp_index, core=True)
        next(rows_x)
        proj = gather_all(env, proj_r, proj_b, groups[7])
        next(proj)
        out_all = gather_blocks(env, out_s, out_o, groups[8], lay.dp_order, lay.dp_index, half=outx_o)
        next(out_all)
        dy_s[...] = dy_r[...].T
        crossing[1].wait_recv()
        by_side(s, lambda side: fill_fc(*((fc_r, fc_x) if side == 0 else (fc_x, fc_r)), side))
        steps(weights, 1)
        steps(params, 1)
        steps(rows_x, 1)
        steps(proj, 1)
        steps(weights, 1)
        steps(out_all, 1)
        finish(params)
        for f in range(2):
            par_o[f] = jnp.concatenate(
                [small[f, lay.dp_index(c), lay.tp_index(c)][:, :R] for c in range(n_ctx)], axis=1
            )
        par_w[:, :D] = par_o[0]
        shift_parts = []
        for d in range(n_dp):
            block = small[s, d, env.t]
            shift_parts += [block[4:5, : FH // 2], block[5:6, : FH // 2]]
        shift_o[...] = jnp.concatenate(shift_parts, axis=1)
        finish(rows_x)

        @pl.loop(0, 8)
        def _(i):
            hat, _ = norm_stats(x_v[i // 4, i % 4].astype(F32))
            low = (hat * par_o[0, 0:1, :] + par_o[0, 1:2, :]).astype(BF)
            h1_v[i // 4, i % 4] = low
            h1_t[:, pl.ds(pl.multiple_of(i * T, T), T)] = low.T

        finish(weights)
        for c in range(n_ctx):
            wq_v[c * R : (c + 1) * R, :] = wq_b[lay.dp_index(c), lay.tp_index(c)]
        leave = Links((None, None, groups[11][2]))
        leave.local(h1_t, h1_o)
        leave.local(wq_v, wq_o)
        unit = 2 * env.t + s
        cols = pl.ds(pl.multiple_of(unit * W, W), W)
        shift = jnp.concatenate(
            [par_w[2:3, cols], jnp.zeros((1, W), F32), par_w[3:4, cols]], axis=1
        )
        moving = []
        for q in range(2):
            rows = h1_v[q].reshape(G, D)
            made = (dot(rows, wq_v[...], NN) + shift).astype(BF).T
            for n in range(3):
                for j in range(HU):
                    first = n * W + j * HEAD_DIM
                    parts[q, j, n * HEAD_DIM : (n + 1) * HEAD_DIM, :] = made[first : first + HEAD_DIM]
            g = group_to_heads(env, parts, mine, groups[6], q)
            next(g)
            moving.append(g)
        steps(proj, 3)
        fc_all = gather_columns(env, fc_s, fc_o, groups[5])
        next(fc_all)
        dy_all = gather_blocks(env, dy_s, dy_o, groups[4], lay.tp_order, lay.tp_index, core=True)
        next(dy_all)
        leaving = []
        for q in range(2):
            next(moving[q])
            for c in range(n_ctx):
                tc, dc = lay.tp_index(c), lay.dp_index(c)
                for n in range(3):
                    heads_v[n, q, :, c * T : (c + 1) * T] = mine[
                        q, dc, n * HEAD_DIM : (n + 1) * HEAD_DIM, tc * T : (tc + 1) * T
                    ]
            keys[...] = heads_v[1, q].T
            for i in range(n_tiles):
                at = slice(i * tile, (i + 1) * tile)
                o, lse = attend_tile(i, tile, heads_v[0, q, :, at], keys, heads_v.at[2, q])
                o_v[q, :, at] = o
                lse_o[q, :, at] = lse
                low = o.astype(BF)
                for b in range(tile // T):
                    o_low[q, i * (tile // T) + b] = low[:, b * T : (b + 1) * T]
                if i == n_tiles - 1:
                    steps(proj, 1 if q == 0 else n_dp // 2)
            g = heads_out(env, o_low, ob_b, groups[9], q)
            next(g)
            leaving.append(g)
        leave.local(heads_v, heads_o)
        leave.local(o_v, o_o)
        finish(proj)
        for n in range(2):
            for c in range(n_ctx):
                pj_v[n, c * R : (c + 1) * R, :] = proj_b[n, lay.dp_index(c), lay.tp_index(c)]
        leave.local(pj_v, pj_o)
        for g in leaving:
            next(g)
        heads_in(env, ob_b, groups[9])
        ob_o[...] = ob_b[...].reshape(D, T).T
        branch = jnp.concatenate([dot(ob_o[...], pj_v[n], NN) for n in range(2)], axis=1)
        x1 = x_s[...].astype(F32) + branch + par_o[1, 1:2, :]
        x1_o[...] = x1
        hat, _ = norm_stats(x1)
        h2_s[...] = (hat * par_o[1, 0:1, :] + par_o[1, 2:3, :]).astype(BF)
        rows_h2 = gather_blocks(env, h2_s, h2_o, groups[10], lay.tp_order, lay.tp_index, core=True)
        next(rows_h2)
        steps(fc_all, 1)
        steps(dy_all, 1)
        steps(rows_h2, 1)
        steps(fc_all, 1)
        finish(out_all)
        finish(fc_all)
        finish(dy_all)
        finish(rows_h2)
        for g in moving + leaving:
            finish(g)
        leave.settle()
        env.drain()

    outs = [
        struct(D, 2 * G),
        struct(D, 3 * W),
        struct(3, 2, HEAD_DIM, length),
        struct(2, HEAD_DIM, length, dtype=F32),
        struct(2, D, half),
        struct(2, 4, T, D),
        struct(n_dp, 4, R, n_dp * FH),
        struct(n_dp, 2, FH, half),
        struct(n_dp, FH, half),
        struct(2, 4, T, D),
        struct(2, 1, length, dtype=F32),
        struct(T, D),
        struct(T, D, dtype=F32),
        struct(1, n_dp * FH, dtype=F32),
        struct(2, 8, D, dtype=F32),
    ]
    out_specs = [ANY] * 10 + [VM] * 5
    scratch = [
        pltpu.VMEM((8, 128), F32),
        pltpu.VMEM((2, n_dp, 4, 8, 128), F32),
        pltpu.VMEM(qkv.shape, BF),
        pltpu.VMEM(fc.shape, BF),
        pltpu.VMEM((4, R, 3 * W), BF),
        pltpu.VMEM((4, R, n_dp * FH), BF),
        pltpu.VMEM((2, FH, half), BF),
        pltpu.VMEM((n_dp, 4, R, 3 * W), BF),
        pltpu.VMEM((D, 3 * W), BF),
        pltpu.VMEM((2, 4, T, D), BF),
        pltpu.VMEM((2, 4, T, D), BF),
        pltpu.VMEM((8, wide), F32),
        pltpu.VMEM((2, HU, QKV, G), BF),
        pltpu.VMEM((2, n_dp, QKV, G), BF),
        pltpu.VMEM((length, HEAD_DIM), BF),
        pltpu.VMEM((3, 2, HEAD_DIM, length), BF),
        pltpu.VMEM((2, HEAD_DIM, length), F32),
        pltpu.VMEM((2, n_ctx, HEAD_DIM, T), BF),
        pltpu.VMEM((HEADS, HEAD_DIM, T), BF),
        pltpu.VMEM((2, n_dp, 4, R, half), BF),
        pltpu.VMEM((2, D, half), BF),
        pltpu.VMEM((T, D), BF),
        pltpu.VMEM((T, D), BF),
        pltpu.VMEM((T, D), BF),
        pltpu.VMEM((D, 2 * G), BF),
    ]
    DMA = pltpu.SemaphoreType.DMA
    columns = sem_shapes(3 + gather_sends(k, False))
    blocks = sem_shapes(gather_sends(2, True))
    every = sem_shapes(gather_sends(2, False) + gather_sends(k, True))
    scratch += sem_shapes(2) + sem_shapes(3 + n_dp) + columns + blocks * 2 + columns
    scratch += [DMA((2, HU)), DMA((2, n_dp)), DMA((2,))]
    scratch += every
    scratch += sem_shapes(gather_sends(k, True))
    scratch += [DMA((2,)), DMA((1,)), DMA((2,))]
    scratch += blocks
    scratch += sem_shapes(1, 5)
    in_specs = [VM] * 7 + [ANY, VM]
    return call(
        "forward", 0, body, (x, gains, biases, fc_bias, qkv, fc, out, proj, dy), in_specs, outs, out_specs, scratch
    )


def steps(generator, count):
    for _ in range(count):
        next(generator, None)


def by_side(s, f):
    for side in range(2):

        @pl.when(s == side)
        def _():
            f(side)


def spread_rows(made, first, size, block):
    end = first + made.shape[0]
    at = first
    while at < end:
        i = at // size
        stop = min(end, (i + 1) * size)
        block(i)[at - i * size : stop - i * size] = made[at - first : stop - first]
        at = stop


def middle(lay, x, h2, dy_all, fc, out, out_x, shift, x1, dy, pj, par):
    n_ctx, n_dp = lay.n_ctx, lay.n_dp
    n_dev = 2 * n_ctx
    k = len(lay.dp_bits)
    T = x.shape[1]
    R, FB = D // n_ctx, FF // n_ctx
    FH = FB // 2
    U = n_dp * FH
    G = 4 * T
    half = D // 2
    chunk = 2 * T

    def natural(c):
        return c

    def body(*refs):
        (h2_r, dya_r, fc_r, out_r, outx_r, pj_r, shift_r, x1_r, dy_r, par_r) = refs[:10]
        (mix_o, dob_o, fc_o, out_o, dx1_o, vec_o, fcb_o) = refs[10:17]
        (h2_v, dy_v, fc_b, fc_w, out_b, out_w, out_g, pj_v, gb_v, du_v, back_p, dh2_v, dob_s) = refs[17:30]
        rest = refs[30:]
        spans, first = [], 0
        for n in (3, k, k):
            spans.append((rest[first : first + n], rest[first + n : first + n + 3]))
            first += n + 3
        sems = rest[first:]
        env = Env(lay)
        s = env.s
        hail_all(env)
        loads = Links((None, None, sems[3]))
        load_fc = loads.local(fc_r, fc_b)
        load_h2 = loads.local(h2_r, h2_v)
        load_out = [loads.local(out_r.at[:, s], out_b.at[0]), loads.local(outx_r, out_b.at[1])]
        load_dy = loads.local(dya_r, dy_v)
        load_pj = loads.local(pj_r, pj_v)
        load_fc.wait()
        for c in range(n_ctx):
            fc_w[c * R : (c + 1) * R, :] = fc_b[lay.dp_index(c), lay.tp_index(c)]
        for copy in load_out:
            copy.wait()

        def fill_out(side):
            for d in range(n_dp):
                at = slice(d * FH, (d + 1) * FH)
                pair = (out_b[0, d], out_b[1, d]) if side == 0 else (out_b[1, d], out_b[0, d])
                out_w[at, :] = jnp.concatenate(pair, axis=1)

        by_side(s, fill_out)
        load_h2.wait()
        load_dy.wait()

        def forth_and_back(q):
            @pl.loop(0, G // chunk)
            def _(i):
                rows = h2_v[q, pl.ds(2 * i, 2)].reshape(chunk, D)
                u = dot(rows, fc_w[...], NN) + shift_r[...]
                square = u * u
                th = jnp.tanh(math.sqrt(2 / math.pi) * (u + 0.044715 * square * u))
                up = 0.5 * (1.0 + th)
                at = pl.ds(pl.multiple_of(i * chunk, chunk), chunk)
                gb_v[q, at, :] = (u * up).astype(BF)
                slope = up + (0.5 * math.sqrt(2 / math.pi)) * u * (1.0 - th * th) * (
                    1.0 + (3 * 0.044715) * square
                )
                dact = dot(dy_v[q, pl.ds(2 * i, 2)].reshape(chunk, D), out_w[...], NT)
                du = (dact * slope).astype(BF)
                du_v[q, at, :] = du
                back_p[q, pl.ds(2 * i, 2)] = dot(du, fc_w[...], NT).astype(BF).reshape(2, T, D)

        forth_and_back(1 - s)
        meet_all(env)
        rows = reduce_blocks(env, back_p, dh2_v, *spans[0])
        next(rows)
        forth_and_back(s)
        steps(rows, 4)
        for first in range(0, D, TILE):
            left = h2_v[:, :, :, first : min(D, first + TILE)].reshape(2 * G, -1)
            made = dot(left, du_v[...].reshape(2 * G, U), TN).astype(BF)
            spread_rows(made, first, R, lambda c: fc_b.at[lay.dp_index(c), lay.tp_index(c)])
        fc_sum = reduce_columns(env, fc_b, fc_o, *spans[1])
        next(fc_sum)
        for first in range(0, U, TILE):
            left = gb_v[:, :, first : min(U, first + TILE)].reshape(2 * G, -1)
            made = dot(left, dy_v[...].reshape(2 * G, D), TN).astype(BF)
            spread_rows(made, first, FH, lambda d: out_g.at[d])
        out_sum = reduce_halves(env, out_g, out_o, *spans[2])
        fcb_o[...] = jnp.sum(du_v[...].reshape(2 * G, U).astype(F32), axis=0, keepdims=True)
        x1 = x1_r[...]
        hat, spread = norm_stats(x1)
        dy_own = dy_r[...].T.astype(F32)
        vec_o[...] = jnp.zeros_like(vec_o)
        vec_o[3:4, :] = jnp.sum(dy_own, axis=0, keepdims=True)
        for q in range(2):

            @pl.loop(0, G // chunk)
            def _(i):
                at = pl.ds(pl.multiple_of(i * chunk, chunk), chunk)
                part = dot(gb_v[q, at, :], out_w[...], NN).astype(BF)
                h2_v[q, pl.ds(2 * i, 2)] = part.reshape(2, T, D)

        leave = loads.local(h2_v, mix_o)
        steps(rows, 1)
        steps(fc_sum, n_dp // 2)
        next(out_sum)
        finish(rows)
        dh2 = dh2_v[...].astype(F32)
        scaled = dh2 * par_r[1, 0:1, :]
        dx1 = dy_own + spread * (
            scaled
            - jnp.mean(scaled, axis=-1, keepdims=True)
            - hat * jnp.mean(scaled * hat, axis=-1, keepdims=True)
        )
        dx1_o[...] = dx1
        da = dx1.astype(BF)
        load_pj.wait()
        dob = dot(pj_v[0], da[:, :half], NT) + dot(pj_v[1], da[:, half:], NT)
        dob_s[...] = dob.astype(BF).reshape(HEADS, HEAD_DIM, T)
        heads = tokens_to_heads(env, dob_s, dob_o, sems[0:3])
        next(heads)
        vec_o[0:1, :] = jnp.sum(dh2 * hat, axis=0, keepdims=True)
        vec_o[1:2, :] = jnp.sum(da.astype(F32), axis=0, keepdims=True)
        vec_o[2:3, :] = jnp.sum(dh2, axis=0, keepdims=True)
        steps(fc_sum, n_dp // 4)
        run([fc_sum, out_sum])
        finish(heads)
        leave.wait()
        env.drain()

    outs = [
        struct(2, 4, T, D),
        struct(n_dev, HEAD_DIM, T),
        struct(2, 4, R, U),
        struct(2, FH, D),
        struct(T, D, dtype=F32),
        struct(8, D, dtype=F32),
        struct(1, U, dtype=F32),
    ]
    scratch = [
        pltpu.VMEM((2, 4, T, D), BF),
        pltpu.VMEM((2, 4, T, D), BF),
        pltpu.VMEM((n_dp, 4, R, U), BF),
        pltpu.VMEM((D, U), BF),
        pltpu.VMEM((2, n_dp, FH, half), BF),
        pltpu.VMEM((U, D), BF),
        pltpu.VMEM((n_dp, FH, D), BF),
        pltpu.VMEM((2, D, half), BF),
        pltpu.VMEM((2, G, U), BF),
        pltpu.VMEM((2, G, U), BF),
        pltpu.VMEM((2, 4, T, D), BF),
        pltpu.VMEM((T, D), BF),
        pltpu.VMEM((HEADS, HEAD_DIM, T), BF),
    ]
    scratch += reduce_scratch(2, True, (T, D)) + sem_shapes(reduce_sends(2, True))
    scratch += reduce_scratch(k, False, (4, R, U)) + sem_shapes(reduce_sends(k, False) + 4)
    scratch += reduce_scratch(k, False, (FH, D)) + sem_shapes(reduce_sends(k, False) + 1)
    DMA = pltpu.SemaphoreType.DMA
    scratch += sem_shapes(1) + [DMA((7,))]
    args = (h2, dy_all, fc, out, out_x, pj, shift, x1, dy, par)
    out_specs = [ANY] * 4 + [VM] * 3
    return call("middle", 1, body, args, [ANY] * 6 + [VM] * 4, outs, out_specs, scratch)


def heads_to_group(env, src, out, sems, q):
    send_sems, recv_sems, local_sems = sems
    lay = env.lay
    held = q % src.shape[0]

    def copy(there, j, target):
        return pltpu.make_async_remote_copy(
            src_ref=src.at[held, there],
            dst_ref=out.at[q, j],
            send_sem=send_sems.at[q, there],
            recv_sem=recv_sems.at[q, j],
            device_id=(lay.compose(env.t, target), env.s),
            device_id_type=MESH,
        )

    local = pltpu.make_async_copy(src.at[held, env.d], out.at[q, env.d % HU], local_sems.at[q])

    @pl.when(env.d < HU)
    def _():
        for i in range(1, lay.n_dp):
            there = (env.d + i) % lay.n_dp
            copy(there, env.d, there).start()
        local.start()

    yield

    @pl.when(env.d < HU)
    def _():
        local.wait()

    for j in range(HU):

        @pl.when(j != env.d)
        def _():
            copy(0, j, j).wait_recv()

    yield

    @pl.when(env.d < HU)
    def _():
        for i in range(1, lay.n_dp):
            there = (env.d + i) % lay.n_dp
            copy(there, env.d, there).wait_send()


def backward(lay, x, heads, o, lse, dob, wq, h1, ob, vec, fcb, dx1, par, mix):
    n_ctx, n_dp = lay.n_ctx, lay.n_dp
    n_dev = 2 * n_ctx
    k = len(lay.dp_bits)
    T = x.shape[1]
    R, FB = D // n_ctx, FF // n_ctx
    FH = FB // 2
    W = HU * HEAD_DIM
    G = 4 * T
    half = D // 2
    length = n_ctx * T
    tile = TILE if length <= 4 * TILE else TILE // 2
    n_tiles = length // tile
    wide = UNITS * W

    def natural(c):
        return c

    def body(*refs):
        (x_r, heads_r, o_r, lse_r, dob_r, wqh_r, h1h_r, ob_r, vec_r, fcb_r, dx1_r, par_r, mix_r) = refs[:13]
        (grad_o, q_v, proj_o, small_o, mix_s) = refs[13:18]
        (
            heads_v, o_v, dob_n, qs, dobs, delta, dq_acc, parts, land, dqkv, dh1_p, dh1_v, q_g, wide_v,
            small_s, pg, wq_r, h1_r,
        ) = refs[18:36]
        rest = refs[36:]
        spans, first = [], 0
        for n in (3, k, k + 3, 3, k + 3):
            spans.append((rest[first : first + n], rest[first + n : first + n + 3]))
            first += n + 3
        sems = rest[first:]
        env = Env(lay)
        s = env.s
        hail_near(env)
        early = Links((None, None, sems[4]))
        mix_v = dh1_p.at[0]
        load_mix = early.local(mix_r.at[s], mix_v)
        load_wq = early.local(wqh_r, wq_r)
        load_h1 = early.local(h1h_r, h1_r)
        for n in range(2):
            right = dx1_r[:, n * half : (n + 1) * half].astype(BF)
            for c in range(0, n_ctx, 4):
                made = dot(ob_r[:, c * R : (c + 4) * R], right, TN).astype(BF)
                for i in range(4):
                    pg[n, lay.dp_index(c + i), lay.tp_index(c + i)] = made[i * R : (i + 1) * R, :]
        small_s[...] = jnp.zeros_like(small_s)
        wide_v[...] = jnp.zeros_like(wide_v)
        meet_near(env)
        proj = reduce_all(env, pg, proj_o, *spans[2])
        next(proj)
        mixing = reduce_blocks(env, mix_r, mix_s, *spans[3], own=mix_v)
        next(mixing)
        load_mix.wait()
        moving = []
        _, active = own_head(env)

        def loads(q):
            copies = [pltpu.make_async_copy(heads_r.at[n, q], heads_v.at[n], sems[3].at[n]) for n in range(3)]
            copies.append(pltpu.make_async_copy(o_r.at[q], o_v, sems[3].at[3]))
            for c in range(n_ctx):
                there = dob_n.at[:, pl.ds(c * T, T)]
                copies.append(pltpu.make_async_copy(dob_r.at[q * n_ctx + c], there, sems[3].at[4 + c]))
            return copies

        for copy in loads(0):
            copy.start()
        steps(proj, n_dp)
        for q in range(2):
            for copy in loads(q):
                copy.wait()

            @pl.when(jnp.logical_not(active))
            def _():
                dob_n[...] = jnp.zeros_like(dob_n)

            qs[...] = heads_v[0].T
            dobs[...] = dob_n[...].T
            delta[...] = jnp.sum(dob_n[...].astype(F32) * o_v[...], axis=0, keepdims=True)
            dq_acc[...] = jnp.zeros_like(dq_acc)

            if q == 1 and parts.shape[0] == 1:
                finish(moving[0])

            def put(n, first, block):
                for b in range(block.shape[1] // T):
                    c = first // T + b
                    tc, dc = lay.tp_index(c), lay.dp_index(c)
                    parts[q % parts.shape[0], dc, n * HEAD_DIM : (n + 1) * HEAD_DIM, tc * T : (tc + 1) * T] = block[
                        :, b * T : (b + 1) * T
                    ]

            for j in range(n_tiles):
                here = slice(j * tile, (j + 1) * tile)
                kt = heads_v[1, :, here]
                keys = kt.T
                values = heads_v[2, :, here].T

                def step(i, carry, masked):
                    dk, dv = carry
                    at = pl.ds(pl.multiple_of(i * tile, tile), tile)
                    st = dot(keys, heads_v[0, :, at], NN) * (SCALE * LOG2E)
                    p = jnp.exp2(st - lse_r[q, :, at])
                    if masked:
                        row = lax.broadcasted_iota(jnp.int32, (tile, tile), 0)
                        col = lax.broadcasted_iota(jnp.int32, (tile, tile), 1)
                        p = jnp.where(row <= col, p, 0.0)
                    dp = dot(values, dob_n[:, at], NN)
                    ds = (p * (dp - delta[:, at])).astype(BF)
                    dv = dv + dot(p.astype(BF), dobs[at, :], NN)
                    dk = dk + dot(ds, qs[at, :], NN)
                    dq_acc[:, at] += dot(kt, ds, NN)
                    return dk, dv

                zero = jnp.zeros((tile, HEAD_DIM), F32)
                carry = step(j, (zero, zero), True)
                if j + 1 < n_tiles:
                    carry = lax.fori_loop(j + 1, n_tiles, functools.partial(step, masked=False), carry)
                put(1, j * tile, (carry[0] * SCALE).T.astype(BF))
                put(2, j * tile, carry[1].T.astype(BF))
                if q == 0 and j == 1:
                    steps(mixing, 4)
                if q == 0 and j == n_tiles - 1:
                    steps(proj, n_dp // 2)
                if q == 1 and j >= n_tiles - 2:
                    steps(mixing, 1)
            put(0, 0, (dq_acc[...] * SCALE).astype(BF))
            if q == 0:
                for copy in loads(1):
                    copy.start()
            g = heads_to_group(env, parts, land, sems[0:3], q)
            next(g)
            moving.append(g)
        steps(proj, n_dp // 4 + 1)
        load_wq.wait()
        load_h1.wait()
        for q in range(2):
            next(moving[q], None)
            rows = []
            for n in range(3):
                for j in range(HU):
                    rows.append(land[q, j, n * HEAD_DIM : (n + 1) * HEAD_DIM, :])
            dqkv[q] = jnp.concatenate(rows, axis=0).T
            dh1_p[q] = dot(dqkv[q], wq_r[...], NT).astype(BF).reshape(4, T, D)
        rows_h1 = reduce_blocks(env, dh1_p, dh1_v, *spans[0])
        next(rows_h1)
        sums = jnp.sum(dqkv[0].astype(F32), axis=0, keepdims=True) + jnp.sum(
            dqkv[1].astype(F32), axis=0, keepdims=True
        )
        for c in range(0, n_ctx, 4):
            at = slice(c * R, (c + 4) * R)
            made = dot(h1_r[at, :], dqkv[...].reshape(2 * G, 3 * W), NN)
            low = made.astype(BF)
            for i in range(4):
                q_g[lay.dp_index(c + i), lay.tp_index(c + i)] = low[i * R : (i + 1) * R, :]
            weight = wq_r[at, :].astype(F32)
            for n, product in enumerate((made * weight, weight * sums)):
                folded = product[:, :128]
                for lane in range(128, 3 * W, 128):
                    folded = folded + product[:, lane : lane + 128]
                wide_v[n : n + 1, at] = jnp.sum(folded.T, axis=0, keepdims=True)
            if c == n_ctx // 2:
                steps(rows_h1, 4)
        grads = reduce_columns(env, q_g, q_v, *spans[1])
        next(grads)
        unit = 2 * env.t + s
        cols = pl.ds(pl.multiple_of(unit * W, W), W)
        wide_v[2:3, cols] = sums[:, :W]
        wide_v[3:4, cols] = sums[:, 2 * W :]
        wide_v[0:1, :D] = (wide_v[0:1, :D] - par_r[0, 1:2, :] * wide_v[1:2, :D]) / par_r[0, 0:1, :]
        for c in range(n_ctx):
            small_s[0, lay.dp_index(c), lay.tp_index(c), 0:4, :R] = wide_v[0:4, c * R : (c + 1) * R]
            small_s[1, lay.dp_index(c), lay.tp_index(c), 0:4, :R] = vec_r[0:4, c * R : (c + 1) * R]
        for d in range(n_dp):
            for h in range(2):
                first = d * FH + h * (FH // 2)
                small_s[s, d, env.t, 4 + h : 5 + h, : FH // 2] = fcb_r[:, first : first + FH // 2]
        small = reduce_all(env, small_s, small_o, *spans[4])
        next(small)
        hat, spread = norm_stats(x_r[...].T.astype(F32))
        steps(rows_h1, 1)
        finish(mixing)
        steps(small, n_dp)
        steps(grads, n_dp // 2)
        steps(rows_h1, 1)
        steps(small, n_dp // 2)
        steps(grads, n_dp // 4)
        finish(rows_h1)
        dh1 = dh1_v[...].astype(F32)
        scaled = dh1 * par_r[0, 0:1, :]
        grad_o[...] = dx1_r[...] + spread * (
            scaled
            - jnp.mean(scaled, axis=-1, keepdims=True)
            - hat * jnp.mean(scaled * hat, axis=-1, keepdims=True)
        )
        finish(proj)
        finish(small)
        finish(grads)
        for g in moving:
            finish(g)
        env.drain()

    outs = [
        struct(T, D, dtype=F32),
        struct(2, 4, R, 3 * W),
        struct(R, half),
        struct(8, 128, dtype=F32),
        struct(T, D),
    ]
    scratch = [
        pltpu.VMEM((3, HEAD_DIM, length), BF),
        pltpu.VMEM((HEAD_DIM, length), F32),
        pltpu.VMEM((HEAD_DIM, length), BF),
        pltpu.VMEM((length, HEAD_DIM), BF),
        pltpu.VMEM((length, HEAD_DIM), BF),
        pltpu.VMEM((1, length), F32),
        pltpu.VMEM((HEAD_DIM, length), F32),
        pltpu.VMEM((2 if n_ctx <= 16 else 1, n_dp, QKV, G), BF),
        pltpu.VMEM((2, HU, QKV, G), BF),
        pltpu.VMEM((2, G, 3 * W), BF),
        pltpu.VMEM((2, 4, T, D), BF),
        pltpu.VMEM((T, D), BF),
        pltpu.VMEM((n_dp, 4, R, 3 * W), BF),
        pltpu.VMEM((8, wide), F32),
        pltpu.VMEM((2, n_dp, 4, 8, 128), F32),
        pltpu.VMEM((2, n_dp, 4, R, half), BF),
        pltpu.VMEM((D, 3 * W), BF),
        pltpu.VMEM((D, 2 * G), BF),
    ]
    blocks = reduce_scratch(2, True, (T, D)) + sem_shapes(reduce_sends(2, True))
    scratch += blocks
    scratch += reduce_scratch(k, False, (4, R, 3 * W)) + sem_shapes(reduce_sends(k, False) + 4)
    scratch += reduce_scratch(k, True, (4, R, half)) + reduce_scratch(2, False, (R, half))
    scratch += sem_shapes(reduce_sends(k, True) + reduce_sends(2, False))
    scratch += blocks
    scratch += reduce_scratch(k, True, (4, 8, 128), F32) + reduce_scratch(2, False, (8, 128), F32)
    scratch += sem_shapes(reduce_sends(k, True) + reduce_sends(2, False))
    DMA = pltpu.SemaphoreType.DMA
    scratch += [DMA((2, n_dp)), DMA((2, HU)), DMA((2,)), DMA((4 + n_ctx,)), DMA((3,))]
    args = (x, heads, o, lse, dob, wq, h1, ob, vec, fcb, dx1, par, mix)
    in_specs = [VM, ANY, ANY, VM, ANY, ANY, ANY] + [VM] * 5 + [ANY]
    return call("backward", 2, body, args, in_specs, outs, [VM, ANY, VM, VM, VM], scratch)


def assemble(lay, q, fc, out, proj, grad, mix, x1, par, small):
    n_ctx, n_dp = lay.n_ctx, lay.n_dp
    T = grad.shape[0]
    R, FB = D // n_ctx, FF // n_ctx
    FH = FB // 2
    W = HU * HEAD_DIM
    half = D // 2

    def body(*refs):
        (q_r, fc_r, out_r, proj_r, grad_r, mix_r, x1_r, par_r, small_r) = refs[:9]
        (mixed_o, grad_o, qkv_o, proj_o, fc_o, out_o, gains_o, biases_o, fcb_o) = refs[9:]
        mixed_o[...] = (x1_r[...] + mix_r[...].astype(F32) + par_r[1, 3:4, :]).astype(BF).T
        grad_o[...] = grad_r[...].T
        proj_o[...] = proj_r[...].astype(F32)
        gains_o[...] = small_r[0:1, :R]
        biases_o[...] = small_r[1:4, :R]
        fcb_o[...] = small_r[4:6, : FH // 2]

        def last(side):
            thirds = []
            for n in range(3):
                pieces = [q_r[h, u][:, n * W : (n + 1) * W] for u in range(4) for h in range(2)]
                thirds.append(jnp.concatenate(pieces, axis=1)[:, :D])
            whole = jnp.concatenate(thirds, axis=1)
            qkv_o[...] = whole[:, side * (3 * half) : (side + 1) * (3 * half)].astype(F32)
            pieces = []
            for c in range(n_ctx // 2 * side, n_ctx // 2 * (side + 1)):
                for h in range(2):
                    first = lay.dp_index(c) * FH
                    pieces.append(fc_r[h, lay.tp_index(c)][:, first : first + FH])
            fc_o[...] = jnp.concatenate(pieces, axis=1).astype(F32)
            out_o[...] = jnp.concatenate(
                [out_r[h][:, side * half : (side + 1) * half] for h in range(2)], axis=0
            ).astype(F32)

        by_side(lax.axis_index("fsdp"), last)

    outs = [
        struct(D, T),
        struct(D, T, dtype=F32),
        struct(R, 3 * half, dtype=F32),
        struct(R, half, dtype=F32),
        struct(R, FF // 2, dtype=F32),
        struct(FB, half, dtype=F32),
        struct(1, R, dtype=F32),
        struct(3, R, dtype=F32),
        struct(2, FH // 2, dtype=F32),
    ]
    return pl.pallas_call(
        body,
        out_shape=outs,
        in_specs=[VM] * 9,
        out_specs=[VM] * 9,
        compiler_params=pltpu.CompilerParams(vmem_limit_bytes=VMEM_LIMIT),
        name="assemble",
    )(q, fc, out, proj, grad, mix, x1, par, small)


def shards(lay, tokens, qkv_weight, proj_weight, fc_weight, out_weight, gains, biases, fc_bias, cotangent):
    T = tokens.shape[1]
    R = D // lay.n_ctx
    FH = FF // lay.n_ctx // 2
    x = jnp.transpose(tokens, (0, 2, 1)).reshape(D, T)
    dy = jnp.transpose(cotangent, (0, 2, 1)).reshape(D, T)
    (h1, wq, heads, o, pj, h2, fc, out, out_x, dy_all, lse, ob, x1, shift, par) = forward(
        lay, x, gains, biases, fc_bias, qkv_weight, fc_weight, out_weight, proj_weight, dy
    )
    mix, dob, fc_sum, out_sum, dx1, vec, fcb = middle(
        lay, x, h2, dy_all, fc, out, out_x, shift, x1, dy, pj, par
    )
    grad, q_sum, proj_sum, small, mix_sum = backward(
        lay, x, heads, o, lse, dob, wq, h1, ob, vec, fcb, dx1, par, mix
    )
    (mixed, grad, qkv_grad, proj_grad, fc_grad, out_grad, gains_grad, biases_grad, fc_bias_grad) = assemble(
        lay, q_sum, fc_sum, out_sum, proj_sum, grad, mix_sum, x1, par, small
    )
    return (
        jnp.transpose(mixed.reshape(1, D, T), (0, 2, 1)),
        jnp.transpose(grad.reshape(1, D, T), (0, 2, 1)),
        qkv_grad,
        proj_grad,
        fc_grad,
        out_grad,
        gains_grad,
        biases_grad,
        fc_bias_grad.reshape(FH),
    )


def solution(mesh):
    lay = Layout(mesh.shape["ctx"])
    in_specs = (
        P("fsdp", "ctx", None),
        P("ctx", "fsdp"),
        P("ctx", "fsdp"),
        P("ctx", "fsdp"),
        P("ctx", "fsdp"),
        P("fsdp", "ctx"),
        P("fsdp", "ctx"),
        P(("ctx", "fsdp")),
        P("fsdp", "ctx", None),
    )
    out_specs = (
        P("fsdp", "ctx", None),
        P("fsdp", "ctx", None),
        P("ctx", "fsdp"),
        P("ctx", "fsdp"),
        P("ctx", "fsdp"),
        P("ctx", "fsdp"),
        P("fsdp", "ctx"),
        P("fsdp", "ctx"),
        P(("ctx", "fsdp")),
    )
    return jax.shard_map(
        functools.partial(shards, lay), mesh=mesh, in_specs=in_specs, out_specs=out_specs, check_vma=False
    )
```

```python
import functools
import math

import jax
import jax.numpy as jnp
from jax import lax
from jax.experimental import pallas as pl
from jax.experimental.pallas import tpu as pltpu
from jax.sharding import PartitionSpec as P

D = 1600
HEADS = 25
HEAD_DIM = 64
FF = 6400
EPS = 1e-05
UNITS = 8
HU = -(-HEADS // UNITS)
QKV = 3 * HEAD_DIM
MESH = pl.DeviceIdType.MESH
BF = jnp.bfloat16
F32 = jnp.float32
VMEM_LIMIT = 60 * 1024 * 1024
LOG2E = 1.0 / math.log(2.0)


class Layout:
    def __init__(self, n_ctx):
        self.n_ctx = n_ctx
        a, b = n_ctx // 4, n_ctx // 2
        self.tp_bits = (b, a)
        self.dp_bits = tuple(1 << i for i in range(n_ctx.bit_length() - 3))
        self.n_dp = n_ctx // 4
        self.dp_order = list(zip(self.dp_bits, self.dp_bits[::-1]))
        self.tp_order = [(b, b), (a, a)]
        self.tp_masks = [[], [(a, a)], [(b, b)], [(a, a), (b, b)]]

    def tp_index(self, c):
        return sum(((c // b) % 2) * (1 << i) for i, b in enumerate(self.tp_bits))

    def dp_index(self, c):
        return sum(((c // b) % 2) * (1 << i) for i, b in enumerate(self.dp_bits))

    def compose(self, t, d):
        return sum(((t // (1 << i)) % 2) * b for i, b in enumerate(self.tp_bits)) + sum(
            ((d // (1 << i)) % 2) * b for i, b in enumerate(self.dp_bits)
        )

    def head_rank(self, h):
        u, j = h // HU, h % HU
        return self.compose(u // 2, j) * 2 + u % 2

    def to_natural(self, x):
        labels = list(self.dp_bits[::-1]) + list(self.tp_bits[::-1])
        k = len(labels)
        rest = x.shape[2:]
        x = x.reshape((2,) * k + rest)
        order = sorted(range(k), key=lambda i: -labels[i])
        x = jnp.transpose(x, order + list(range(k, k + len(rest))))
        return x.reshape((self.n_ctx,) + rest)

    def from_natural(self, x):
        labels = list(self.dp_bits[::-1]) + list(self.tp_bits[::-1])
        k = len(labels)
        rest = x.shape[1:]
        x = x.reshape((2,) * k + rest)
        natural = sorted(labels, reverse=True)
        order = [natural.index(b) for b in labels]
        x = jnp.transpose(x, order + list(range(k, k + len(rest))))
        return x.reshape((self.n_dp, 4) + rest)


def flip(c, sym, s):
    def one(b):
        return c + b * (1 - 2 * ((c // b) % 2))

    if sym[0] == sym[1]:
        return one(sym[0])
    return one(sym[0]) * (1 - s) + one(sym[1]) * s


def flips(c, masks, s):
    for sym in masks:
        c = flip(c, sym, s)
    return c


class Env:
    def __init__(self, layout):
        self.lay = layout
        self.c = lax.axis_index("ctx")
        self.s = lax.axis_index("fsdp")
        self.t = layout.tp_index(self.c)
        self.d = layout.dp_index(self.c)
        self.rank = self.c * 2 + self.s
        self.n_dev = layout.n_ctx * 2
        self.opened = []

    def other(self):
        return (self.c, 1 - self.s)

    def drain(self):
        for links in self.opened:
            links.drain()


class Links:
    def __init__(self, sems, env=None):
        self.send_sems, self.recv_sems, self.local_sems = sems
        if env is not None:
            env.opened.append(self)
        self.count = 0
        self.local_count = 0
        self.sent = []
        self.locals = []

    def send(self, src, dst, device):
        copy = pltpu.make_async_remote_copy(
            src_ref=src,
            dst_ref=dst,
            send_sem=self.send_sems.at[self.count],
            recv_sem=self.recv_sems.at[self.count],
            device_id=device,
            device_id_type=MESH,
        )
        copy.start()
        self.count += 1
        self.sent.append(copy)
        return copy

    def local(self, src, dst):
        copy = pltpu.make_async_copy(src, dst, self.local_sems.at[self.local_count])
        copy.start()
        self.local_count += 1
        self.locals.append(copy)
        return copy

    def settle(self):
        for copy in self.locals:
            copy.wait()
        self.locals = []

    def drain(self):
        self.settle()
        for copy in self.sent:
            copy.wait_send()


def sem_shapes(sends, local=1):
    sends = max(sends, 1)
    return [
        pltpu.SemaphoreType.DMA((sends,)),
        pltpu.SemaphoreType.DMA((sends,)),
        pltpu.SemaphoreType.DMA((local,)),
    ]


def meet(env, devices):
    barrier = pltpu.get_barrier_semaphore()
    for device in devices:
        pl.semaphore_signal(barrier, inc=1, device_id=device, device_id_type=MESH)
    pl.semaphore_wait(barrier, len(devices))


def hail_all(env):
    barrier = pltpu.get_barrier_semaphore()

    def hail(i, carry):
        rank = (env.rank + i) % env.n_dev
        pl.semaphore_signal(barrier, inc=1, device_id=(rank // 2, rank % 2), device_id_type=MESH)
        return carry

    lax.fori_loop(1, env.n_dev, hail, 0)


def near(env):
    lay = env.lay
    return (
        [(flips(env.c, m, env.s), env.s) for m in lay.tp_masks[1:]]
        + [(lay.compose(env.t, (env.d + i) % lay.n_dp), env.s) for i in range(1, lay.n_dp)]
        + [env.other()]
    )


def hail_near(env):
    barrier = pltpu.get_barrier_semaphore()
    for device in near(env):
        pl.semaphore_signal(barrier, inc=1, device_id=device, device_id_type=MESH)


def meet_near(env):
    pl.semaphore_wait(pltpu.get_barrier_semaphore(), len(near(env)))


def meet_all(env):
    pl.semaphore_wait(pltpu.get_barrier_semaphore(), env.n_dev - 1)


def tp_partners(env):
    return [(flips(env.c, m, env.s), env.s) for m in env.lay.tp_masks[1:]]


def dp_partners(env):
    return [(flip(env.c, sym, env.s), env.s) for sym in env.lay.dp_order]


def run(generators):
    active = list(generators)
    while active:
        left = []
        for g in active:
            try:
                next(g)
                left.append(g)
            except StopIteration:
                pass
        active = left


def gather_sends(bits, core):
    return (1 << bits) - 1 + (1 << bits if core else 0)


def gather(env, links, src, buf, bits, slot, core=False, half=None, placed=False):
    c, s = env.c, env.s

    def place(masks):
        return buf.at[slot(flips(c, masks, s))]

    if not placed:
        links.local(src, place([]))
    levels = [[([], None)]] + [[] for _ in bits]
    crossing = []
    for k in range(len(bits) + 1):
        for masks, copy in levels[k]:
            if copy is None:
                ref = src
            else:
                copy.wait_recv()
                ref = place(masks)
            for j in range(k, len(bits)):
                forward = links.send(ref, place(masks), (flip(c, bits[j], s), s))
                levels[j + 1].append((masks + [bits[j]], forward))
            if core:
                crossing.append(links.send(ref, place(masks), env.other()))
            if half is not None:
                there = half.at[slot(flips(c, masks, s))]
                crossing.append(links.send(ref.at[1 - s], there, env.other()))
            yield
    for copy in crossing:
        copy.wait_recv()


def gather_blocks(env, src, buf, sems, bits, slot, core=False, half=None):
    links = Links(sems, env)
    yield from gather(env, links, src, buf.at[env.s] if core else buf, bits, slot, core, half)
    links.settle()
    yield


def gather_columns(env, src, buf, sems):
    lay = env.lay
    links = Links(sems, env)
    own = buf.at[env.d]
    copies = [links.local(src.at[env.t], own.at[env.t])]
    for m in lay.tp_masks[1:]:
        there = flips(env.c, m, env.s)
        copies.append(links.send(src.at[lay.tp_index(there)], own.at[env.t], (there, env.s)))
    yield
    links.settle()
    for copy in copies[1:]:
        copy.wait_recv()
    yield from gather(env, links, own, buf, lay.dp_order, lay.dp_index, placed=True)
    links.settle()
    yield


def gather_all(env, src, buf, sems):
    lay = env.lay
    links = Links(sems, env)
    mine = buf.at[env.s]
    own = mine.at[env.d]
    yield from gather(env, links, src, own, lay.tp_order, lay.tp_index)
    links.settle()
    yield from gather(env, links, own, mine, lay.dp_order, lay.dp_index, core=True, placed=True)
    links.settle()
    yield


def gather_small(env, src, buf, sems):
    lay = env.lay
    links = Links(sems, env)
    mine = buf.at[env.s]
    own = mine.at[env.d]
    local = links.local(src, own.at[env.t])
    copies = []
    for m in lay.tp_masks[1:]:
        copies.append(links.send(src, own.at[env.t], (flips(env.c, m, env.s), env.s)))
    yield
    links.settle()
    for copy in copies:
        copy.wait_recv()
    copies = []
    for i in range(1, lay.n_dp):
        there = lay.compose(env.t, (env.d + i) % lay.n_dp)
        copies.append(links.send(own, own, (there, env.s)))
    yield
    for copy in copies:
        copy.wait_recv()
    copy = links.send(mine, mine, env.other())
    yield
    copy.wait_recv()
    links.settle()
    yield


def reduce_sends(bits, core):
    return (1 << bits) - 1 + (1 << bits if core else 0)


def reduce_scratch(bits, core, block, dtype=BF):
    return [pltpu.VMEM((1 << j,) + block, dtype) for j in range(bits + (1 if core else 0))]


def add_into(total, term):
    if len(total.shape) == 2:
        total[...] = total[...] + term[...]
    else:
        for i in range(total.shape[0]):
            add_into(total.at[i], term.at[i])


def reduce(env, links, inp, parts, bits, slot, core=False, own=None):
    c, s = env.c, env.s
    levels = [[[]]]
    for sym in bits:
        levels.append(levels[-1] + [m + [sym] for m in levels[-1]])

    def at(side, masks):
        index = slot(flips(c, masks, side))
        return inp.at[side, index] if core else inp.at[index]

    last = levels[-1]
    if own is None:
        now = [at(s, m) for m in last]
    else:
        now = [own.at[slot(flips(c, m, s))] for m in last]
    copies = {}
    if core:
        stage = len(bits)
        for i in reversed(range(len(last))):
            copies[i] = links.send(at(1 - s, last[i]), parts[stage].at[i], env.other())
    else:
        stage = len(bits) - 1
        n = len(levels[stage])
        for i in reversed(range(n)):
            copies[i] = links.send(now[n + i], parts[stage].at[i], (flip(c, bits[stage], s), s))
    yield
    while stage >= 0:
        n = len(levels[stage])
        got = parts[stage]
        after = {}
        for i in reversed(range(n)):
            copies[i].wait_recv()
            add_into(got.at[i], now[i])
            if stage > 0 and i >= n // 2:
                after[i - n // 2] = links.send(
                    got.at[i], parts[stage - 1].at[i - n // 2], (flip(c, bits[stage - 1], s), s)
                )
            yield
        now = [got.at[i] for i in range(n)]
        copies = after
        stage -= 1
    return now[0]


def reduce_blocks(env, inp, out, parts, sems, own=None):
    links = Links(sems, env)
    total = yield from reduce(env, links, inp, parts, env.lay.tp_order, env.lay.tp_index, core=True, own=own)
    out[...] = total[...].astype(out.dtype)
    links.settle()
    yield


def reduce_columns(env, inp, out, parts, sems):
    lay = env.lay
    links = Links(sems, env)
    total = yield from reduce(env, links, inp, parts, lay.dp_order, lay.dp_index)
    local = links.local(total.at[env.t], out.at[env.s, env.t])
    copies = []
    for m in lay.tp_masks[1:]:
        there = flips(env.c, m, env.s)
        copies.append(links.send(total.at[lay.tp_index(there)], out.at[env.s, env.t], (there, env.s)))
    yield
    links.settle()
    for copy in copies:
        copy.wait_recv()
    copy = links.send(out.at[env.s], out.at[env.s], env.other())
    yield
    copy.wait_recv()
    links.settle()
    yield


def reduce_halves(env, inp, out, parts, sems):
    lay = env.lay
    links = Links(sems, env)
    total = yield from reduce(env, links, inp, parts, lay.dp_order, lay.dp_index)
    links.local(total, out.at[env.s])
    copy = links.send(total, out.at[env.s], env.other())
    yield
    copy.wait_recv()
    links.settle()
    yield


def reduce_all(env, inp, out, parts, sems):
    lay = env.lay
    links = Links(sems, env)
    n = len(lay.dp_bits) + 1
    total = yield from reduce(env, links, inp, parts[:n], lay.dp_order, lay.dp_index, core=True)
    total = yield from reduce(env, links, total, parts[n:], lay.tp_order, lay.tp_index)
    out[...] = total[...].astype(out.dtype)
    links.settle()
    yield


def own_head(env):
    h = (env.t * 2 + env.s) * HU + env.d
    return h, jnp.logical_and(env.d < HU, h < HEADS)


def wait_pieces(env, ref, count, send=None, recv=None):
    part = ref.at[pl.ds(0, count)]
    copy = pltpu.make_async_remote_copy(
        src_ref=part,
        dst_ref=part,
        send_sem=recv if send is None else send,
        recv_sem=send if recv is None else recv,
        device_id=env.other(),
        device_id_type=MESH,
    )
    if send is not None:
        copy.wait_send()
    if recv is not None:
        copy.wait_recv()


def tokens_to_heads(env, src, out, sems):
    send_sem, recv_sem, local_sem = sems[0].at[0], sems[1].at[0], sems[2].at[0]
    h, active = own_head(env)
    lay = env.lay
    place = env.s * lay.n_ctx + env.c

    def begin(i, carry):
        j = (env.rank + i) % HEADS
        rank = lay.head_rank(j)

        @pl.when(rank != env.rank)
        def _():
            pltpu.make_async_remote_copy(
                src_ref=src.at[j],
                dst_ref=out.at[place],
                send_sem=send_sem,
                recv_sem=recv_sem,
                device_id=(rank // 2, rank % 2),
                device_id_type=MESH,
            ).start()

        return carry

    lax.fori_loop(0, HEADS, begin, 0)
    yield

    @pl.when(active)
    def _():
        local = pltpu.make_async_copy(src.at[h], out.at[place], local_sem)
        local.start()
        local.wait()
        wait_pieces(env, out, env.n_dev - 1, recv=recv_sem)
        wait_pieces(env, src, HEADS - 1, send=send_sem)

    @pl.when(jnp.logical_not(active))
    def _():
        wait_pieces(env, src, HEADS, send=send_sem)


ANY = pl.BlockSpec(memory_space=pl.ANY)
VM = pl.BlockSpec(memory_space=pltpu.VMEM)


def struct(*shape, dtype=BF):
    return jax.ShapeDtypeStruct(shape, dtype)


def call(name, cid, body, args, in_specs, outs, out_specs, scratch):
    return pl.pallas_call(
        body,
        out_shape=outs,
        in_specs=in_specs,
        out_specs=out_specs,
        scratch_shapes=scratch,
        compiler_params=pltpu.CompilerParams(
            collective_id=cid, has_side_effects=True, vmem_limit_bytes=VMEM_LIMIT
        ),
        name=name,
    )(*args)


def dot(left, right, dims):
    return lax.dot_general(left, right, (dims, ((), ())), preferred_element_type=F32)


NN = ((1,), (0,))
NT = ((1,), (1,))
TN = ((0,), (0,))
SCALE = 1.0 / math.sqrt(HEAD_DIM)
TILE = 512


class Background:
    def __init__(self):
        self.active = []

    def add(self, generator):
        self.active.append(generator)

    def step(self, count=1):
        for _ in range(count):
            if not self.active:
                return
            g = self.active.pop(0)
            try:
                next(g)
                self.active.append(g)
            except StopIteration:
                pass

    def finish(self):
        while self.active:
            self.step()


def finish(generator):
    for _ in generator:
        pass


def group_to_heads(env, src, out, sems, q):
    send_sems, recv_sems, local_sems = sems
    lay = env.lay

    def copy(j, source, target):
        return pltpu.make_async_remote_copy(
            src_ref=src.at[q, j],
            dst_ref=out.at[q, source],
            send_sem=send_sems.at[q, j],
            recv_sem=recv_sems.at[q, source],
            device_id=(lay.compose(env.t, target), env.s),
            device_id_type=MESH,
        )

    for i in range(1, HU + 1):
        j = (env.d + i) % HU

        @pl.when(j != env.d)
        def _():
            copy(j, env.d, j).start()

    local = pltpu.make_async_copy(src.at[q, env.d % HU], out.at[q, env.d], local_sems.at[q])

    @pl.when(env.d < HU)
    def _():
        local.start()

    yield

    @pl.when(env.d < HU)
    def _():
        local.wait()
        for i in range(1, lay.n_dp):
            source = (env.d + i) % lay.n_dp
            copy(0, source, source).wait_recv()

    yield
    for j in range(HU):

        @pl.when(j != env.d)
        def _():
            copy(j, env.d, j).wait_send()


def heads_out(env, src, out, sems, q):
    send_sem, recv_sem = sems[0].at[q], sems[1].at[0]
    h, active = own_head(env)
    n_ctx = env.lay.n_ctx

    def copy(i):
        there = (env.c + i) % n_ctx
        return pltpu.make_async_remote_copy(
            src_ref=src.at[q, there],
            dst_ref=out.at[h],
            send_sem=send_sem,
            recv_sem=recv_sem,
            device_id=(there, q),
            device_id_type=MESH,
        )

    local = pltpu.make_async_copy(src.at[q, env.c], out.at[h], sems[2].at[q])
    mine = jnp.logical_and(active, env.s == q)
    theirs = jnp.logical_and(active, env.s != q)

    def begin(i, carry):
        copy(i).start()
        return carry

    @pl.when(mine)
    def _():
        local.start()

    @pl.when(theirs)
    def _():
        copy(0).start()

    @pl.when(active)
    def _():
        lax.fori_loop(1, n_ctx, begin, 0)

    yield

    @pl.when(mine)
    def _():
        local.wait()

    yield

    @pl.when(mine)
    def _():
        wait_pieces(env, src.at[q], n_ctx - 1, send=send_sem)

    @pl.when(theirs)
    def _():
        wait_pieces(env, src.at[q], n_ctx, send=send_sem)


def heads_in(env, out, sems):
    _, active = own_head(env)

    @pl.when(active)
    def _():
        wait_pieces(env, out, HEADS - 1, recv=sems[1].at[0])

    @pl.when(jnp.logical_not(active))
    def _():
        wait_pieces(env, out, HEADS, recv=sems[1].at[0])


def norm_stats(values):
    centre = values - jnp.mean(values, axis=-1, keepdims=True)
    spread = lax.rsqrt(jnp.mean(centre * centre, axis=-1, keepdims=True) + EPS)
    return centre * spread, spread


def attend_tile(i, tile, qt, keys, v_ref):
    def step(j, carry, masked):
        peak, total, acc = carry
        at = pl.ds(pl.multiple_of(j * tile, tile), tile)
        st = dot(keys[at, :], qt, NN) * (SCALE * LOG2E)
        if masked:
            row = lax.broadcasted_iota(jnp.int32, (tile, tile), 0)
            col = lax.broadcasted_iota(jnp.int32, (tile, tile), 1)
            st = jnp.where(row <= col, st, -1e30)
        new = jnp.maximum(peak, jnp.max(st, axis=0, keepdims=True))
        p = jnp.exp2(st - new)
        shrink = jnp.exp2(peak - new)
        total = total * shrink + jnp.sum(p, axis=0, keepdims=True)
        acc = acc * shrink + dot(v_ref[:, at], p.astype(BF), NN)
        return new, total, acc

    start = (
        jnp.full((1, tile), -1e30, F32),
        jnp.zeros((1, tile), F32),
        jnp.zeros((HEAD_DIM, tile), F32),
    )
    carry = start
    if i > 0:
        carry = lax.fori_loop(0, i, functools.partial(step, masked=False), carry)
    peak, total, acc = step(i, carry, True)
    return acc / total, peak + jnp.log2(total)


def forward(lay, x, gains, biases, fc_bias, qkv, fc, out, proj, dy):
    n_ctx, n_dp = lay.n_ctx, lay.n_dp
    n_dev = 2 * n_ctx
    k = len(lay.dp_bits)
    T = x.shape[1]
    R, FB = D // n_ctx, FF // n_ctx
    FH = FB // 2
    W = HU * HEAD_DIM
    G = 4 * T
    length = n_ctx * T
    tile = min(TILE, length)
    n_tiles = length // tile
    half = D // 2
    wide = UNITS * W

    def natural(c):
        return c

    def body(*refs):
        (x_r, gains_r, biases_r, fcb_r, qkv_r, fc_r, out_r, proj_r, dy_r) = refs[:9]
        (h1_o, wq_o, heads_o, o_o, pj_o, h2_o, fc_o, out_o, outx_o, dy_o, lse_o, ob_o, x1_o, shift_o, par_o) = refs[9:24]
        (
            pack, small, qkv_x, fc_x, qkv_s, fc_s, out_s, wq_b, wq_v, x_v, h1_v, par_w,
            parts, mine, keys, heads_v, o_v, o_low, ob_b, proj_b, pj_v, h2_s, x_s, dy_s, h1_t,
        ) = refs[24:49]
        sems = refs[49:]
        groups = [sems[3 * i : 3 * i + 3] for i in range(len(sems) // 3)]
        env = Env(lay)
        s = env.s

        hail_all(env)
        x_s[...] = x_r[...].T
        pack[...] = jnp.zeros_like(pack)
        pack[0:1, :R] = gains_r[...].astype(F32)
        pack[1:4, :R] = biases_r[...].astype(F32)
        row = fcb_r[...].astype(F32).reshape(1, FH)
        pack[4:5, : FH // 2] = row[:, : FH // 2]
        pack[5:6, : FH // 2] = row[:, FH // 2 :]
        for h in range(2):
            out_s[h] = out_r[h * FH : (h + 1) * FH, :]
        par_w[...] = jnp.zeros_like(par_w)
        meet_all(env)
        links = Links(groups[0], env)
        crossing = [links.send(a, b, env.other()) for a, b in ((qkv_r, qkv_x), (fc_r, fc_x))]
        params = gather_small(env, pack, small, groups[1])
        next(params)

        def fill_qkv(a, b, side):
            q = a[:, :D]
            keys_all = jnp.concatenate([a[:, D:], b[:, : D // 2]], axis=1)
            v = b[:, D // 2 :]
            for u in range(4):
                first = (2 * u + side) * W
                width = max(0, min(W, D - first))
                for n, part in enumerate((q, keys_all, v)):
                    if width < W:
                        qkv_s[u, :, n * W : (n + 1) * W] = jnp.zeros((R, W), BF)
                    if width > 0:
                        qkv_s[u, :, n * W : n * W + width] = part[:, first : first + width]

        def fill_fc(a, b, side):
            for u in range(4):
                for d in range(n_dp):
                    first = lay.compose(u, d) * FB + side * FH
                    source, first = (a, first) if first < FF // 2 else (b, first - FF // 2)
                    fc_s[u, :, d * FH : (d + 1) * FH] = source[:, first : first + FH]

        crossing[0].wait_recv()
        by_side(s, lambda side: fill_qkv(*((qkv_r, qkv_x) if side == 0 else (qkv_x, qkv_r)), side))
        steps(params, 1)
        weights = gather_columns(env, qkv_s, wq_b, groups[2])
        next(weights)
        rows_x = gather_blocks(env, x_s, x_v, groups[3], lay.tp_order, lay.tp_index, core=True)
        next(rows_x)
        proj = gather_all(env, proj_r, proj_b, groups[7])
        next(proj)
        out_all = gather_blocks(env, out_s, out_o, groups[8], lay.dp_order, lay.dp_index, half=outx_o)
        next(out_all)
        dy_s[...] = dy_r[...].T
        crossing[1].wait_recv()
        by_side(s, lambda side: fill_fc(*((fc_r, fc_x) if side == 0 else (fc_x, fc_r)), side))
        steps(weights, 1)
        steps(params, 1)
        steps(rows_x, 1)
        steps(proj, 1)
        steps(weights, 1)
        steps(out_all, 1)
        finish(params)
        for f in range(2):
            par_o[f] = jnp.concatenate(
                [small[f, lay.dp_index(c), lay.tp_index(c)][:, :R] for c in range(n_ctx)], axis=1
            )
        par_w[:, :D] = par_o[0]
        shift_parts = []
        for d in range(n_dp):
            block = small[s, d, env.t]
            shift_parts += [block[4:5, : FH // 2], block[5:6, : FH // 2]]
        shift_o[...] = jnp.concatenate(shift_parts, axis=1)
        finish(rows_x)

        @pl.loop(0, 8)
        def _(i):
            hat, _ = norm_stats(x_v[i // 4, i % 4].astype(F32))
            low = (hat * par_o[0, 0:1, :] + par_o[0, 1:2, :]).astype(BF)
            h1_v[i // 4, i % 4] = low
            h1_t[:, pl.ds(pl.multiple_of(i * T, T), T)] = low.T

        finish(weights)
        for c in range(n_ctx):
            wq_v[c * R : (c + 1) * R, :] = wq_b[lay.dp_index(c), lay.tp_index(c)]
        leave = Links((None, None, groups[11][2]))
        leave.local(h1_t, h1_o)
        leave.local(wq_v, wq_o)
        unit = 2 * env.t + s
        cols = pl.ds(pl.multiple_of(unit * W, W), W)
        shift = jnp.concatenate(
            [par_w[2:3, cols], jnp.zeros((1, W), F32), par_w[3:4, cols]], axis=1
        )
        moving = []
        for q in range(2):
            rows = h1_v[q].reshape(G, D)
            made = (dot(rows, wq_v[...], NN) + shift).astype(BF).T
            for n in range(3):
                for j in range(HU):
                    first = n * W + j * HEAD_DIM
                    parts[q, j, n * HEAD_DIM : (n + 1) * HEAD_DIM, :] = made[first : first + HEAD_DIM]
            g = group_to_heads(env, parts, mine, groups[6], q)
            next(g)
            moving.append(g)
        steps(proj, 3)
        fc_all = gather_columns(env, fc_s, fc_o, groups[5])
        next(fc_all)
        dy_all = gather_blocks(env, dy_s, dy_o, groups[4], lay.tp_order, lay.tp_index, core=True)
        next(dy_all)
        leaving = []
        for q in range(2):
            next(moving[q])
            for c in range(n_ctx):
                tc, dc = lay.tp_index(c), lay.dp_index(c)
                for n in range(3):
                    heads_v[n, q, :, c * T : (c + 1) * T] = mine[
                        q, dc, n * HEAD_DIM : (n + 1) * HEAD_DIM, tc * T : (tc + 1) * T
                    ]
            keys[...] = heads_v[1, q].T
            for i in range(n_tiles):
                at = slice(i * tile, (i + 1) * tile)
                o, lse = attend_tile(i, tile, heads_v[0, q, :, at], keys, heads_v.at[2, q])
                o_v[q, :, at] = o
                lse_o[q, :, at] = lse
                low = o.astype(BF)
                for b in range(tile // T):
                    o_low[q, i * (tile // T) + b] = low[:, b * T : (b + 1) * T]
                if i == n_tiles - 1:
                    steps(proj, 1 if q == 0 else n_dp // 2)
            g = heads_out(env, o_low, ob_b, groups[9], q)
            next(g)
            leaving.append(g)
        leave.local(heads_v, heads_o)
        leave.local(o_v, o_o)
        finish(proj)
        for n in range(2):
            for c in range(n_ctx):
                pj_v[n, c * R : (c + 1) * R, :] = proj_b[n, lay.dp_index(c), lay.tp_index(c)]
        leave.local(pj_v, pj_o)
        for g in leaving:
            next(g)
        heads_in(env, ob_b, groups[9])
        ob_o[...] = ob_b[...].reshape(D, T).T
        branch = jnp.concatenate([dot(ob_o[...], pj_v[n], NN) for n in range(2)], axis=1)
        x1 = x_s[...].astype(F32) + branch + par_o[1, 1:2, :]
        x1_o[...] = x1
        hat, _ = norm_stats(x1)
        h2_s[...] = (hat * par_o[1, 0:1, :] + par_o[1, 2:3, :]).astype(BF)
        rows_h2 = gather_blocks(env, h2_s, h2_o, groups[10], lay.tp_order, lay.tp_index, core=True)
        next(rows_h2)
        steps(fc_all, 1)
        steps(dy_all, 1)
        steps(rows_h2, 1)
        steps(fc_all, 1)
        finish(out_all)
        finish(fc_all)
        finish(dy_all)
        finish(rows_h2)
        for g in moving + leaving:
            finish(g)
        leave.settle()
        env.drain()

    outs = [
        struct(D, 2 * G),
        struct(D, 3 * W),
        struct(3, 2, HEAD_DIM, length),
        struct(2, HEAD_DIM, length, dtype=F32),
        struct(2, D, half),
        struct(2, 4, T, D),
        struct(n_dp, 4, R, n_dp * FH),
        struct(n_dp, 2, FH, half),
        struct(n_dp, FH, half),
        struct(2, 4, T, D),
        struct(2, 1, length, dtype=F32),
        struct(T, D),
        struct(T, D, dtype=F32),
        struct(1, n_dp * FH, dtype=F32),
        struct(2, 8, D, dtype=F32),
    ]
    out_specs = [ANY] * 10 + [VM] * 5
    scratch = [
        pltpu.VMEM((8, 128), F32),
        pltpu.VMEM((2, n_dp, 4, 8, 128), F32),
        pltpu.VMEM(qkv.shape, BF),
        pltpu.VMEM(fc.shape, BF),
        pltpu.VMEM((4, R, 3 * W), BF),
        pltpu.VMEM((4, R, n_dp * FH), BF),
        pltpu.VMEM((2, FH, half), BF),
        pltpu.VMEM((n_dp, 4, R, 3 * W), BF),
        pltpu.VMEM((D, 3 * W), BF),
        pltpu.VMEM((2, 4, T, D), BF),
        pltpu.VMEM((2, 4, T, D), BF),
        pltpu.VMEM((8, wide), F32),
        pltpu.VMEM((2, HU, QKV, G), BF),
        pltpu.VMEM((2, n_dp, QKV, G), BF),
        pltpu.VMEM((length, HEAD_DIM), BF),
        pltpu.VMEM((3, 2, HEAD_DIM, length), BF),
        pltpu.VMEM((2, HEAD_DIM, length), F32),
        pltpu.VMEM((2, n_ctx, HEAD_DIM, T), BF),
        pltpu.VMEM((HEADS, HEAD_DIM, T), BF),
        pltpu.VMEM((2, n_dp, 4, R, half), BF),
        pltpu.VMEM((2, D, half), BF),
        pltpu.VMEM((T, D), BF),
        pltpu.VMEM((T, D), BF),
        pltpu.VMEM((T, D), BF),
        pltpu.VMEM((D, 2 * G), BF),
    ]
    DMA = pltpu.SemaphoreType.DMA
    columns = sem_shapes(3 + gather_sends(k, False))
    blocks = sem_shapes(gather_sends(2, True))
    every = sem_shapes(gather_sends(2, False) + gather_sends(k, True))
    scratch += sem_shapes(2) + sem_shapes(3 + n_dp) + columns + blocks * 2 + columns
    scratch += [DMA((2, HU)), DMA((2, n_dp)), DMA((2,))]
    scratch += every
    scratch += sem_shapes(gather_sends(k, True))
    scratch += [DMA((2,)), DMA((1,)), DMA((2,))]
    scratch += blocks
    scratch += sem_shapes(1, 5)
    in_specs = [VM] * 7 + [ANY, VM]
    return call(
        "forward", 0, body, (x, gains, biases, fc_bias, qkv, fc, out, proj, dy), in_specs, outs, out_specs, scratch
    )


def steps(generator, count):
    for _ in range(count):
        next(generator, None)


def by_side(s, f):
    for side in range(2):

        @pl.when(s == side)
        def _():
            f(side)


def spread_rows(made, first, size, block):
    end = first + made.shape[0]
    at = first
    while at < end:
        i = at // size
        stop = min(end, (i + 1) * size)
        block(i)[at - i * size : stop - i * size] = made[at - first : stop - first]
        at = stop


def middle(lay, x, h2, dy_all, fc, out, out_x, shift, x1, dy, pj, par):
    n_ctx, n_dp = lay.n_ctx, lay.n_dp
    n_dev = 2 * n_ctx
    k = len(lay.dp_bits)
    T = x.shape[1]
    R, FB = D // n_ctx, FF // n_ctx
    FH = FB // 2
    U = n_dp * FH
    G = 4 * T
    half = D // 2
    chunk = 2 * T

    def natural(c):
        return c

    def body(*refs):
        (h2_r, dya_r, fc_r, out_r, outx_r, pj_r, shift_r, x1_r, dy_r, par_r) = refs[:10]
        (mix_o, dob_o, fc_o, out_o, dx1_o, vec_o, fcb_o) = refs[10:17]
        (h2_v, dy_v, fc_b, fc_w, out_b, out_w, out_g, pj_v, gb_v, du_v, back_p, dh2_v, dob_s) = refs[17:30]
        rest = refs[30:]
        spans, first = [], 0
        for n in (3, k, k):
            spans.append((rest[first : first + n], rest[first + n : first + n + 3]))
            first += n + 3
        sems = rest[first:]
        env = Env(lay)
        s = env.s
        hail_all(env)
        loads = Links((None, None, sems[3]))
        load_fc = loads.local(fc_r, fc_b)
        load_h2 = loads.local(h2_r, h2_v)
        load_out = [loads.local(out_r.at[:, s], out_b.at[0]), loads.local(outx_r, out_b.at[1])]
        load_dy = loads.local(dya_r, dy_v)
        load_fc.wait()
        for c in range(n_ctx):
            fc_w[c * R : (c + 1) * R, :] = fc_b[lay.dp_index(c), lay.tp_index(c)]
        for copy in load_out:
            copy.wait()

        def fill_out(side):
            for d in range(n_dp):
                at = slice(d * FH, (d + 1) * FH)
                pair = (out_b[0, d], out_b[1, d]) if side == 0 else (out_b[1, d], out_b[0, d])
                out_w[at, :] = jnp.concatenate(pair, axis=1)

        by_side(s, fill_out)
        load_h2.wait()
        load_dy.wait()

        def forth_and_back(q):
            @pl.loop(0, G // chunk)
            def _(i):
                rows = h2_v[q, pl.ds(2 * i, 2)].reshape(chunk, D)
                u = dot(rows, fc_w[...], NN) + shift_r[...]
                square = u * u
                th = jnp.tanh(math.sqrt(2 / math.pi) * (u + 0.044715 * square * u))
                up = 0.5 * (1.0 + th)
                at = pl.ds(pl.multiple_of(i * chunk, chunk), chunk)
                gb_v[q, at, :] = (u * up).astype(BF)
                slope = up + (0.5 * math.sqrt(2 / math.pi)) * u * (1.0 - th * th) * (
                    1.0 + (3 * 0.044715) * square
                )
                dact = dot(dy_v[q, pl.ds(2 * i, 2)].reshape(chunk, D), out_w[...], NT)
                du = (dact * slope).astype(BF)
                du_v[q, at, :] = du
                back_p[q, pl.ds(2 * i, 2)] = dot(du, fc_w[...], NT).astype(BF).reshape(2, T, D)

        load_pj = loads.local(pj_r, pj_v)
        forth_and_back(1 - s)
        meet_all(env)
        rows = reduce_blocks(env, back_p, dh2_v, *spans[0])
        next(rows)
        forth_and_back(s)
        steps(rows, 4)
        for first in range(0, D, TILE):
            left = h2_v[:, :, :, first : min(D, first + TILE)].reshape(2 * G, -1)
            made = dot(left, du_v[...].reshape(2 * G, U), TN).astype(BF)
            spread_rows(made, first, R, lambda c: fc_b.at[lay.dp_index(c), lay.tp_index(c)])
        fc_sum = reduce_columns(env, fc_b, fc_o, *spans[1])
        next(fc_sum)
        for first in range(0, U, TILE):
            left = gb_v[:, :, first : min(U, first + TILE)].reshape(2 * G, -1)
            made = dot(left, dy_v[...].reshape(2 * G, D), TN).astype(BF)
            spread_rows(made, first, FH, lambda d: out_g.at[d])
        out_sum = reduce_halves(env, out_g, out_o, *spans[2])
        fcb_o[...] = jnp.sum(du_v[...].reshape(2 * G, U).astype(F32), axis=0, keepdims=True)
        x1 = x1_r[...]
        hat, spread = norm_stats(x1)
        dy_own = dy_r[...].T.astype(F32)
        vec_o[...] = jnp.zeros_like(vec_o)
        vec_o[3:4, :] = jnp.sum(dy_own, axis=0, keepdims=True)
        for q in range(2):

            @pl.loop(0, G // chunk)
            def _(i):
                at = pl.ds(pl.multiple_of(i * chunk, chunk), chunk)
                part = dot(gb_v[q, at, :], out_w[...], NN).astype(BF)
                h2_v[q, pl.ds(2 * i, 2)] = part.reshape(2, T, D)

        leave = loads.local(h2_v, mix_o)
        steps(rows, 1)
        steps(fc_sum, n_dp // 2)
        next(out_sum)
        finish(rows)
        dh2 = dh2_v[...].astype(F32)
        scaled = dh2 * par_r[1, 0:1, :]
        dx1 = dy_own + spread * (
            scaled
            - jnp.mean(scaled, axis=-1, keepdims=True)
            - hat * jnp.mean(scaled * hat, axis=-1, keepdims=True)
        )
        dx1_o[...] = dx1
        da = dx1.astype(BF)
        load_pj.wait()
        dob = dot(pj_v[0], da[:, :half], NT) + dot(pj_v[1], da[:, half:], NT)
        dob_s[...] = dob.astype(BF).reshape(HEADS, HEAD_DIM, T)
        heads = tokens_to_heads(env, dob_s, dob_o, sems[0:3])
        next(heads)
        vec_o[0:1, :] = jnp.sum(dh2 * hat, axis=0, keepdims=True)
        vec_o[1:2, :] = jnp.sum(da.astype(F32), axis=0, keepdims=True)
        vec_o[2:3, :] = jnp.sum(dh2, axis=0, keepdims=True)
        steps(fc_sum, n_dp // 4)
        run([fc_sum, out_sum])
        finish(heads)
        leave.wait()
        env.drain()

    outs = [
        struct(2, 4, T, D),
        struct(n_dev, HEAD_DIM, T),
        struct(2, 4, R, U),
        struct(2, FH, D),
        struct(T, D, dtype=F32),
        struct(8, D, dtype=F32),
        struct(1, U, dtype=F32),
    ]
    scratch = [
        pltpu.VMEM((2, 4, T, D), BF),
        pltpu.VMEM((2, 4, T, D), BF),
        pltpu.VMEM((n_dp, 4, R, U), BF),
        pltpu.VMEM((D, U), BF),
        pltpu.VMEM((2, n_dp, FH, half), BF),
        pltpu.VMEM((U, D), BF),
        pltpu.VMEM((n_dp, FH, D), BF),
        pltpu.VMEM((2, D, half), BF),
        pltpu.VMEM((2, G, U), BF),
        pltpu.VMEM((2, G, U), BF),
        pltpu.VMEM((2, 4, T, D), BF),
        pltpu.VMEM((T, D), BF),
        pltpu.VMEM((HEADS, HEAD_DIM, T), BF),
    ]
    scratch += reduce_scratch(2, True, (T, D)) + sem_shapes(reduce_sends(2, True))
    scratch += reduce_scratch(k, False, (4, R, U)) + sem_shapes(reduce_sends(k, False) + 4)
    scratch += reduce_scratch(k, False, (FH, D)) + sem_shapes(reduce_sends(k, False) + 1)
    DMA = pltpu.SemaphoreType.DMA
    scratch += sem_shapes(1) + [DMA((7,))]
    args = (h2, dy_all, fc, out, out_x, pj, shift, x1, dy, par)
    out_specs = [ANY] * 4 + [VM] * 3
    return call("middle", 1, body, args, [ANY] * 6 + [VM] * 4, outs, out_specs, scratch)


def heads_to_group(env, src, out, sems, q):
    send_sems, recv_sems, local_sems = sems
    lay = env.lay
    held = q % src.shape[0]

    def copy(there, j, target):
        return pltpu.make_async_remote_copy(
            src_ref=src.at[held, there],
            dst_ref=out.at[q, j],
            send_sem=send_sems.at[q, there],
            recv_sem=recv_sems.at[q, j],
            device_id=(lay.compose(env.t, target), env.s),
            device_id_type=MESH,
        )

    local = pltpu.make_async_copy(src.at[held, env.d], out.at[q, env.d % HU], local_sems.at[q])

    @pl.when(env.d < HU)
    def _():
        for i in range(1, lay.n_dp):
            there = (env.d + i) % lay.n_dp
            copy(there, env.d, there).start()
        local.start()

    yield

    @pl.when(env.d < HU)
    def _():
        local.wait()

    for j in range(HU):

        @pl.when(j != env.d)
        def _():
            copy(0, j, j).wait_recv()

    yield

    @pl.when(env.d < HU)
    def _():
        for i in range(1, lay.n_dp):
            there = (env.d + i) % lay.n_dp
            copy(there, env.d, there).wait_send()


def backward(lay, x, heads, o, lse, dob, wq, h1, ob, vec, fcb, dx1, par, mix):
    n_ctx, n_dp = lay.n_ctx, lay.n_dp
    n_dev = 2 * n_ctx
    k = len(lay.dp_bits)
    T = x.shape[1]
    R, FB = D // n_ctx, FF // n_ctx
    FH = FB // 2
    W = HU * HEAD_DIM
    G = 4 * T
    half = D // 2
    length = n_ctx * T
    tile = TILE if length <= 4 * TILE else TILE // 2
    n_tiles = length // tile
    wide = UNITS * W

    def natural(c):
        return c

    def body(*refs):
        (x_r, heads_r, o_r, lse_r, dob_r, wqh_r, h1h_r, ob_r, vec_r, fcb_r, dx1_r, par_r, mix_r) = refs[:13]
        (grad_o, q_v, proj_o, small_o, mix_s) = refs[13:18]
        (
            heads_v, o_v, dob_n, qs, dobs, delta, dq_acc, parts, land, dqkv, dh1_p, dh1_v, q_g, wide_v,
            small_s, pg, wq_r, h1_r,
        ) = refs[18:36]
        rest = refs[36:]
        spans, first = [], 0
        for n in (3, k, k + 3, 3, k + 3):
            spans.append((rest[first : first + n], rest[first + n : first + n + 3]))
            first += n + 3
        sems = rest[first:]
        env = Env(lay)
        s = env.s
        hail_near(env)
        early = Links((None, None, sems[4]))
        mix_v = dh1_p.at[0]
        load_mix = early.local(mix_r.at[s], mix_v)
        load_wq = early.local(wqh_r, wq_r)
        load_h1 = early.local(h1h_r, h1_r)
        for n in range(2):
            right = dx1_r[:, n * half : (n + 1) * half].astype(BF)
            for c in range(0, n_ctx, 4):
                made = dot(ob_r[:, c * R : (c + 4) * R], right, TN).astype(BF)
                for i in range(4):
                    pg[n, lay.dp_index(c + i), lay.tp_index(c + i)] = made[i * R : (i + 1) * R, :]
        small_s[...] = jnp.zeros_like(small_s)
        wide_v[...] = jnp.zeros_like(wide_v)
        meet_near(env)
        proj = reduce_all(env, pg, proj_o, *spans[2])
        next(proj)
        mixing = reduce_blocks(env, mix_r, mix_s, *spans[3], own=mix_v)
        next(mixing)
        load_mix.wait()
        moving = []
        _, active = own_head(env)

        def loads(q):
            copies = [pltpu.make_async_copy(heads_r.at[n, q], heads_v.at[n], sems[3].at[n]) for n in range(3)]
            copies.append(pltpu.make_async_copy(o_r.at[q], o_v, sems[3].at[3]))
            for c in range(n_ctx):
                there = dob_n.at[:, pl.ds(c * T, T)]
                copies.append(pltpu.make_async_copy(dob_r.at[q * n_ctx + c], there, sems[3].at[4 + c]))
            return copies

        for copy in loads(0):
            copy.start()
        steps(proj, n_dp)
        for q in range(2):
            for copy in loads(q):
                copy.wait()

            @pl.when(jnp.logical_not(active))
            def _():
                dob_n[...] = jnp.zeros_like(dob_n)

            qs[...] = heads_v[0].T
            dobs[...] = dob_n[...].T
            delta[...] = jnp.sum(dob_n[...].astype(F32) * o_v[...], axis=0, keepdims=True)
            dq_acc[...] = jnp.zeros_like(dq_acc)

            if q == 1 and parts.shape[0] == 1:
                finish(moving[0])

            def put(n, first, block):
                for b in range(block.shape[1] // T):
                    c = first // T + b
                    tc, dc = lay.tp_index(c), lay.dp_index(c)
                    parts[q % parts.shape[0], dc, n * HEAD_DIM : (n + 1) * HEAD_DIM, tc * T : (tc + 1) * T] = block[
                        :, b * T : (b + 1) * T
                    ]

            for j in range(n_tiles):
                here = slice(j * tile, (j + 1) * tile)
                kt = heads_v[1, :, here]
                keys = kt.T
                values = heads_v[2, :, here].T

                def step(i, carry, masked):
                    dk, dv = carry
                    at = pl.ds(pl.multiple_of(i * tile, tile), tile)
                    st = dot(keys, heads_v[0, :, at], NN) * (SCALE * LOG2E)
                    p = jnp.exp2(st - lse_r[q, :, at])
                    if masked:
                        row = lax.broadcasted_iota(jnp.int32, (tile, tile), 0)
                        col = lax.broadcasted_iota(jnp.int32, (tile, tile), 1)
                        p = jnp.where(row <= col, p, 0.0)
                    dp = dot(values, dob_n[:, at], NN)
                    ds = (p * (dp - delta[:, at])).astype(BF)
                    dv = dv + dot(p.astype(BF), dobs[at, :], NN)
                    dk = dk + dot(ds, qs[at, :], NN)
                    dq_acc[:, at] += dot(kt, ds, NN)
                    return dk, dv

                zero = jnp.zeros((tile, HEAD_DIM), F32)
                carry = step(j, (zero, zero), True)
                if j + 1 < n_tiles:
                    carry = lax.fori_loop(j + 1, n_tiles, functools.partial(step, masked=False), carry)
                put(1, j * tile, (carry[0] * SCALE).T.astype(BF))
                put(2, j * tile, carry[1].T.astype(BF))
                if q == 0 and j == 1:
                    steps(mixing, 4)
                if q == 0 and j == n_tiles - 1:
                    steps(proj, n_dp // 2)
                if q == 1 and j >= n_tiles - 2:
                    steps(mixing, 1)
            put(0, 0, (dq_acc[...] * SCALE).astype(BF))
            if q == 0:
                for copy in loads(1):
                    copy.start()
            g = heads_to_group(env, parts, land, sems[0:3], q)
            next(g)
            moving.append(g)
        steps(proj, n_dp // 4 + 1)
        load_wq.wait()
        load_h1.wait()
        for q in range(2):
            next(moving[q], None)
            rows = []
            for n in range(3):
                for j in range(HU):
                    rows.append(land[q, j, n * HEAD_DIM : (n + 1) * HEAD_DIM, :])
            dqkv[q] = jnp.concatenate(rows, axis=0).T
            dh1_p[q] = dot(dqkv[q], wq_r[...], NT).astype(BF).reshape(4, T, D)
        rows_h1 = reduce_blocks(env, dh1_p, dh1_v, *spans[0])
        next(rows_h1)
        sums = jnp.sum(dqkv[0].astype(F32), axis=0, keepdims=True) + jnp.sum(
            dqkv[1].astype(F32), axis=0, keepdims=True
        )
        for c in range(0, n_ctx, 4):
            at = slice(c * R, (c + 4) * R)
            made = dot(h1_r[at, :], dqkv[...].reshape(2 * G, 3 * W), NN)
            low = made.astype(BF)
            for i in range(4):
                q_g[lay.dp_index(c + i), lay.tp_index(c + i)] = low[i * R : (i + 1) * R, :]
            weight = wq_r[at, :].astype(F32)
            for n, product in enumerate((made * weight, weight * sums)):
                folded = product[:, :128]
                for lane in range(128, 3 * W, 128):
                    folded = folded + product[:, lane : lane + 128]
                wide_v[n : n + 1, at] = jnp.sum(folded.T, axis=0, keepdims=True)
            if c == n_ctx // 2:
                steps(rows_h1, 4)
        grads = reduce_columns(env, q_g, q_v, *spans[1])
        next(grads)
        unit = 2 * env.t + s
        cols = pl.ds(pl.multiple_of(unit * W, W), W)
        wide_v[2:3, cols] = sums[:, :W]
        wide_v[3:4, cols] = sums[:, 2 * W :]
        wide_v[0:1, :D] = (wide_v[0:1, :D] - par_r[0, 1:2, :] * wide_v[1:2, :D]) / par_r[0, 0:1, :]
        for c in range(n_ctx):
            small_s[0, lay.dp_index(c), lay.tp_index(c), 0:4, :R] = wide_v[0:4, c * R : (c + 1) * R]
            small_s[1, lay.dp_index(c), lay.tp_index(c), 0:4, :R] = vec_r[0:4, c * R : (c + 1) * R]
        for d in range(n_dp):
            for h in range(2):
                first = d * FH + h * (FH // 2)
                small_s[s, d, env.t, 4 + h : 5 + h, : FH // 2] = fcb_r[:, first : first + FH // 2]
        small = reduce_all(env, small_s, small_o, *spans[4])
        next(small)
        hat, spread = norm_stats(x_r[...].T.astype(F32))
        steps(rows_h1, 1)
        finish(mixing)
        steps(small, n_dp)
        steps(grads, n_dp // 2)
        steps(rows_h1, 1)
        steps(small, n_dp // 2)
        steps(grads, n_dp // 4)
        finish(rows_h1)
        dh1 = dh1_v[...].astype(F32)
        scaled = dh1 * par_r[0, 0:1, :]
        grad_o[...] = dx1_r[...] + spread * (
            scaled
            - jnp.mean(scaled, axis=-1, keepdims=True)
            - hat * jnp.mean(scaled * hat, axis=-1, keepdims=True)
        )
        finish(proj)
        finish(small)
        finish(grads)
        for g in moving:
            finish(g)
        env.drain()

    outs = [
        struct(T, D, dtype=F32),
        struct(2, 4, R, 3 * W),
        struct(R, half),
        struct(8, 128, dtype=F32),
        struct(T, D),
    ]
    scratch = [
        pltpu.VMEM((3, HEAD_DIM, length), BF),
        pltpu.VMEM((HEAD_DIM, length), F32),
        pltpu.VMEM((HEAD_DIM, length), BF),
        pltpu.VMEM((length, HEAD_DIM), BF),
        pltpu.VMEM((length, HEAD_DIM), BF),
        pltpu.VMEM((1, length), F32),
        pltpu.VMEM((HEAD_DIM, length), F32),
        pltpu.VMEM((2 if n_ctx <= 16 else 1, n_dp, QKV, G), BF),
        pltpu.VMEM((2, HU, QKV, G), BF),
        pltpu.VMEM((2, G, 3 * W), BF),
        pltpu.VMEM((2, 4, T, D), BF),
        pltpu.VMEM((T, D), BF),
        pltpu.VMEM((n_dp, 4, R, 3 * W), BF),
        pltpu.VMEM((8, wide), F32),
        pltpu.VMEM((2, n_dp, 4, 8, 128), F32),
        pltpu.VMEM((2, n_dp, 4, R, half), BF),
        pltpu.VMEM((D, 3 * W), BF),
        pltpu.VMEM((D, 2 * G), BF),
    ]
    blocks = reduce_scratch(2, True, (T, D)) + sem_shapes(reduce_sends(2, True))
    scratch += blocks
    scratch += reduce_scratch(k, False, (4, R, 3 * W)) + sem_shapes(reduce_sends(k, False) + 4)
    scratch += reduce_scratch(k, True, (4, R, half)) + reduce_scratch(2, False, (R, half))
    scratch += sem_shapes(reduce_sends(k, True) + reduce_sends(2, False))
    scratch += blocks
    scratch += reduce_scratch(k, True, (4, 8, 128), F32) + reduce_scratch(2, False, (8, 128), F32)
    scratch += sem_shapes(reduce_sends(k, True) + reduce_sends(2, False))
    DMA = pltpu.SemaphoreType.DMA
    scratch += [DMA((2, n_dp)), DMA((2, HU)), DMA((2,)), DMA((4 + n_ctx,)), DMA((3,))]
    args = (x, heads, o, lse, dob, wq, h1, ob, vec, fcb, dx1, par, mix)
    in_specs = [VM, ANY, ANY, VM, ANY, ANY, ANY] + [VM] * 5 + [ANY]
    return call("backward", 2, body, args, in_specs, outs, [VM, ANY, VM, VM, VM], scratch)


def assemble(lay, q, fc, out, proj, grad, mix, x1, par, small):
    n_ctx, n_dp = lay.n_ctx, lay.n_dp
    T = grad.shape[0]
    R, FB = D // n_ctx, FF // n_ctx
    FH = FB // 2
    W = HU * HEAD_DIM
    half = D // 2

    def body(*refs):
        (q_r, fc_r, out_r, proj_r, grad_r, mix_r, x1_r, par_r, small_r) = refs[:9]
        (mixed_o, grad_o, qkv_o, proj_o, fc_o, out_o, gains_o, biases_o, fcb_o) = refs[9:]
        mixed_o[...] = (x1_r[...] + mix_r[...].astype(F32) + par_r[1, 3:4, :]).astype(BF).T
        grad_o[...] = grad_r[...].T
        proj_o[...] = proj_r[...].astype(F32)
        gains_o[...] = small_r[0:1, :R]
        biases_o[...] = small_r[1:4, :R]
        row = jnp.concatenate([small_r[4:5, : FH // 2], small_r[5:6, : FH // 2]], axis=1)
        fcb_o[...] = row.reshape(FH)

        def last(side):
            thirds = []
            for n in range(3):
                pieces = [q_r[h, u][:, n * W : (n + 1) * W] for u in range(4) for h in range(2)]
                thirds.append(jnp.concatenate(pieces, axis=1)[:, :D])
            whole = jnp.concatenate(thirds, axis=1)
            qkv_o[...] = whole[:, side * (3 * half) : (side + 1) * (3 * half)].astype(F32)
            pieces = []
            for c in range(n_ctx // 2 * side, n_ctx // 2 * (side + 1)):
                for h in range(2):
                    first = lay.dp_index(c) * FH
                    pieces.append(fc_r[h, lay.tp_index(c)][:, first : first + FH])
            fc_o[...] = jnp.concatenate(pieces, axis=1).astype(F32)
            out_o[...] = jnp.concatenate(
                [out_r[h][:, side * half : (side + 1) * half] for h in range(2)], axis=0
            ).astype(F32)

        by_side(lax.axis_index("fsdp"), last)

    outs = [
        struct(D, T),
        struct(D, T, dtype=F32),
        struct(R, 3 * half, dtype=F32),
        struct(R, half, dtype=F32),
        struct(R, FF // 2, dtype=F32),
        struct(FB, half, dtype=F32),
        struct(1, R, dtype=F32),
        struct(3, R, dtype=F32),
        struct(FH, dtype=F32),
    ]
    return pl.pallas_call(
        body,
        out_shape=outs,
        in_specs=[VM] * 9,
        out_specs=[VM] * 9,
        compiler_params=pltpu.CompilerParams(vmem_limit_bytes=VMEM_LIMIT),
        name="assemble",
    )(q, fc, out, proj, grad, mix, x1, par, small)


def shards(lay, tokens, qkv_weight, proj_weight, fc_weight, out_weight, gains, biases, fc_bias, cotangent):
    T = tokens.shape[1]
    R = D // lay.n_ctx
    FH = FF // lay.n_ctx // 2
    x = jnp.transpose(tokens, (0, 2, 1)).reshape(D, T)
    dy = jnp.transpose(cotangent, (0, 2, 1)).reshape(D, T)
    (h1, wq, heads, o, pj, h2, fc, out, out_x, dy_all, lse, ob, x1, shift, par) = forward(
        lay, x, gains, biases, fc_bias, qkv_weight, fc_weight, out_weight, proj_weight, dy
    )
    mix, dob, fc_sum, out_sum, dx1, vec, fcb = middle(
        lay, x, h2, dy_all, fc, out, out_x, shift, x1, dy, pj, par
    )
    grad, q_sum, proj_sum, small, mix_sum = backward(
        lay, x, heads, o, lse, dob, wq, h1, ob, vec, fcb, dx1, par, mix
    )
    (mixed, grad, qkv_grad, proj_grad, fc_grad, out_grad, gains_grad, biases_grad, fc_bias_grad) = assemble(
        lay, q_sum, fc_sum, out_sum, proj_sum, grad, mix_sum, x1, par, small
    )
    return (
        jnp.transpose(mixed.reshape(1, D, T), (0, 2, 1)),
        jnp.transpose(grad.reshape(1, D, T), (0, 2, 1)),
        qkv_grad,
        proj_grad,
        fc_grad,
        out_grad,
        gains_grad,
        biases_grad,
        fc_bias_grad,
    )


def solution(mesh):
    lay = Layout(mesh.shape["ctx"])
    in_specs = (
        P("fsdp", "ctx", None),
        P("ctx", "fsdp"),
        P("ctx", "fsdp"),
        P("ctx", "fsdp"),
        P("ctx", "fsdp"),
        P("fsdp", "ctx"),
        P("fsdp", "ctx"),
        P(("ctx", "fsdp")),
        P("fsdp", "ctx", None),
    )
    out_specs = (
        P("fsdp", "ctx", None),
        P("fsdp", "ctx", None),
        P("ctx", "fsdp"),
        P("ctx", "fsdp"),
        P("ctx", "fsdp"),
        P("ctx", "fsdp"),
        P("fsdp", "ctx"),
        P("fsdp", "ctx"),
        P(("ctx", "fsdp")),
    )
    return jax.shard_map(
        functools.partial(shards, lay), mesh=mesh, in_specs=in_specs, out_specs=out_specs, check_vma=False
    )
```

```python
import functools
import math

import jax
import jax.numpy as jnp
from jax import lax
from jax.experimental import pallas as pl
from jax.experimental.pallas import tpu as pltpu
from jax.sharding import PartitionSpec as P

D = 1600
HEADS = 25
HEAD_DIM = 64
FF = 6400
EPS = 1e-05
UNITS = 8
HU = -(-HEADS // UNITS)
QKV = 3 * HEAD_DIM
MESH = pl.DeviceIdType.MESH
BF = jnp.bfloat16
F32 = jnp.float32
VMEM_LIMIT = 60 * 1024 * 1024
LOG2E = 1.0 / math.log(2.0)


class Layout:
    def __init__(self, n_ctx):
        self.n_ctx = n_ctx
        a, b = n_ctx // 4, n_ctx // 2
        self.tp_bits = (b, a)
        self.dp_bits = tuple(1 << i for i in range(n_ctx.bit_length() - 3))
        self.n_dp = n_ctx // 4
        self.dp_order = list(zip(self.dp_bits, self.dp_bits[::-1]))
        self.tp_order = [(b, b), (a, a)]
        self.tp_masks = [[], [(a, a)], [(b, b)], [(a, a), (b, b)]]

    def tp_index(self, c):
        return sum(((c // b) % 2) * (1 << i) for i, b in enumerate(self.tp_bits))

    def dp_index(self, c):
        return sum(((c // b) % 2) * (1 << i) for i, b in enumerate(self.dp_bits))

    def compose(self, t, d):
        return sum(((t // (1 << i)) % 2) * b for i, b in enumerate(self.tp_bits)) + sum(
            ((d // (1 << i)) % 2) * b for i, b in enumerate(self.dp_bits)
        )

    def head_rank(self, h):
        u, j = h // HU, h % HU
        return self.compose(u // 2, j) * 2 + u % 2

    def to_natural(self, x):
        labels = list(self.dp_bits[::-1]) + list(self.tp_bits[::-1])
        k = len(labels)
        rest = x.shape[2:]
        x = x.reshape((2,) * k + rest)
        order = sorted(range(k), key=lambda i: -labels[i])
        x = jnp.transpose(x, order + list(range(k, k + len(rest))))
        return x.reshape((self.n_ctx,) + rest)

    def from_natural(self, x):
        labels = list(self.dp_bits[::-1]) + list(self.tp_bits[::-1])
        k = len(labels)
        rest = x.shape[1:]
        x = x.reshape((2,) * k + rest)
        natural = sorted(labels, reverse=True)
        order = [natural.index(b) for b in labels]
        x = jnp.transpose(x, order + list(range(k, k + len(rest))))
        return x.reshape((self.n_dp, 4) + rest)


def flip(c, sym, s):
    def one(b):
        return c + b * (1 - 2 * ((c // b) % 2))

    if sym[0] == sym[1]:
        return one(sym[0])
    return one(sym[0]) * (1 - s) + one(sym[1]) * s


def flips(c, masks, s):
    for sym in masks:
        c = flip(c, sym, s)
    return c


class Env:
    def __init__(self, layout):
        self.lay = layout
        self.c = lax.axis_index("ctx")
        self.s = lax.axis_index("fsdp")
        self.t = layout.tp_index(self.c)
        self.d = layout.dp_index(self.c)
        self.rank = self.c * 2 + self.s
        self.n_dev = layout.n_ctx * 2
        self.opened = []

    def other(self):
        return (self.c, 1 - self.s)

    def drain(self):
        for links in self.opened:
            links.drain()


class Links:
    def __init__(self, sems, env=None):
        self.send_sems, self.recv_sems, self.local_sems = sems
        if env is not None:
            env.opened.append(self)
        self.count = 0
        self.local_count = 0
        self.sent = []
        self.locals = []

    def send(self, src, dst, device):
        copy = pltpu.make_async_remote_copy(
            src_ref=src,
            dst_ref=dst,
            send_sem=self.send_sems.at[self.count],
            recv_sem=self.recv_sems.at[self.count],
            device_id=device,
            device_id_type=MESH,
        )
        copy.start()
        self.count += 1
        self.sent.append(copy)
        return copy

    def local(self, src, dst):
        copy = pltpu.make_async_copy(src, dst, self.local_sems.at[self.local_count])
        copy.start()
        self.local_count += 1
        self.locals.append(copy)
        return copy

    def settle(self):
        for copy in self.locals:
            copy.wait()
        self.locals = []

    def drain(self):
        self.settle()
        for copy in self.sent:
            copy.wait_send()


def sem_shapes(sends, local=1):
    sends = max(sends, 1)
    return [
        pltpu.SemaphoreType.DMA((sends,)),
        pltpu.SemaphoreType.DMA((sends,)),
        pltpu.SemaphoreType.DMA((local,)),
    ]


def meet(env, devices):
    barrier = pltpu.get_barrier_semaphore()
    for device in devices:
        pl.semaphore_signal(barrier, inc=1, device_id=device, device_id_type=MESH)
    pl.semaphore_wait(barrier, len(devices))


def hail_all(env):
    barrier = pltpu.get_barrier_semaphore()

    def hail(i, carry):
        rank = (env.rank + i) % env.n_dev
        pl.semaphore_signal(barrier, inc=1, device_id=(rank // 2, rank % 2), device_id_type=MESH)
        return carry

    lax.fori_loop(1, env.n_dev, hail, 0)


def near(env):
    lay = env.lay
    return (
        [(flips(env.c, m, env.s), env.s) for m in lay.tp_masks[1:]]
        + [(lay.compose(env.t, (env.d + i) % lay.n_dp), env.s) for i in range(1, lay.n_dp)]
        + [env.other()]
    )


def hail_near(env):
    barrier = pltpu.get_barrier_semaphore()
    for device in near(env):
        pl.semaphore_signal(barrier, inc=1, device_id=device, device_id_type=MESH)


def meet_near(env):
    pl.semaphore_wait(pltpu.get_barrier_semaphore(), len(near(env)))


def meet_all(env):
    pl.semaphore_wait(pltpu.get_barrier_semaphore(), env.n_dev - 1)


def tp_partners(env):
    return [(flips(env.c, m, env.s), env.s) for m in env.lay.tp_masks[1:]]


def dp_partners(env):
    return [(flip(env.c, sym, env.s), env.s) for sym in env.lay.dp_order]


def run(generators):
    active = list(generators)
    while active:
        left = []
        for g in active:
            try:
                next(g)
                left.append(g)
            except StopIteration:
                pass
        active = left


def gather_sends(bits, core):
    return (1 << bits) - 1 + (1 << bits if core else 0)


def gather(env, links, src, buf, bits, slot, core=False, half=None, placed=False):
    c, s = env.c, env.s

    def place(masks):
        return buf.at[slot(flips(c, masks, s))]

    if not placed:
        links.local(src, place([]))
    levels = [[([], None)]] + [[] for _ in bits]
    crossing = []
    for k in range(len(bits) + 1):
        for masks, copy in levels[k]:
            if copy is None:
                ref = src
            else:
                copy.wait_recv()
                ref = place(masks)
            for j in range(k, len(bits)):
                forward = links.send(ref, place(masks), (flip(c, bits[j], s), s))
                levels[j + 1].append((masks + [bits[j]], forward))
            if core:
                crossing.append(links.send(ref, place(masks), env.other()))
            if half is not None:
                there = half.at[slot(flips(c, masks, s))]
                crossing.append(links.send(ref.at[1 - s], there, env.other()))
            yield
    for copy in crossing:
        copy.wait_recv()


def gather_blocks(env, src, buf, sems, bits, slot, core=False, half=None):
    links = Links(sems, env)
    yield from gather(env, links, src, buf.at[env.s] if core else buf, bits, slot, core, half)
    links.settle()
    yield


def gather_columns(env, src, buf, sems):
    lay = env.lay
    links = Links(sems, env)
    own = buf.at[env.d]
    copies = [links.local(src.at[env.t], own.at[env.t])]
    for m in lay.tp_masks[1:]:
        there = flips(env.c, m, env.s)
        copies.append(links.send(src.at[lay.tp_index(there)], own.at[env.t], (there, env.s)))
    yield
    links.settle()
    for copy in copies[1:]:
        copy.wait_recv()
    yield from gather(env, links, own, buf, lay.dp_order, lay.dp_index, placed=True)
    links.settle()
    yield


def gather_all(env, src, buf, sems):
    lay = env.lay
    links = Links(sems, env)
    mine = buf.at[env.s]
    own = mine.at[env.d]
    yield from gather(env, links, src, own, lay.tp_order, lay.tp_index)
    links.settle()
    yield from gather(env, links, own, mine, lay.dp_order, lay.dp_index, core=True, placed=True)
    links.settle()
    yield


def gather_small(env, src, buf, sems):
    lay = env.lay
    links = Links(sems, env)
    mine = buf.at[env.s]
    own = mine.at[env.d]
    local = links.local(src, own.at[env.t])
    copies = []
    for m in lay.tp_masks[1:]:
        copies.append(links.send(src, own.at[env.t], (flips(env.c, m, env.s), env.s)))
    yield
    links.settle()
    for copy in copies:
        copy.wait_recv()
    copies = []
    for i in range(1, lay.n_dp):
        there = lay.compose(env.t, (env.d + i) % lay.n_dp)
        copies.append(links.send(own, own, (there, env.s)))
    yield
    for copy in copies:
        copy.wait_recv()
    copy = links.send(mine, mine, env.other())
    yield
    copy.wait_recv()
    links.settle()
    yield


def reduce_sends(bits, core):
    return (1 << bits) - 1 + (1 << bits if core else 0)


def reduce_scratch(bits, core, block, dtype=BF):
    return [pltpu.VMEM((1 << j,) + block, dtype) for j in range(bits + (1 if core else 0))]


def add_into(total, term):
    if len(total.shape) == 2:
        total[...] = total[...] + term[...]
    else:
        for i in range(total.shape[0]):
            add_into(total.at[i], term.at[i])


def reduce(env, links, inp, parts, bits, slot, core=False, own=None):
    c, s = env.c, env.s
    levels = [[[]]]
    for sym in bits:
        levels.append(levels[-1] + [m + [sym] for m in levels[-1]])

    def at(side, masks):
        index = slot(flips(c, masks, side))
        return inp.at[side, index] if core else inp.at[index]

    last = levels[-1]
    if own is None:
        now = [at(s, m) for m in last]
    else:
        now = [own.at[slot(flips(c, m, s))] for m in last]
    copies = {}
    if core:
        stage = len(bits)
        for i in reversed(range(len(last))):
            copies[i] = links.send(at(1 - s, last[i]), parts[stage].at[i], env.other())
    else:
        stage = len(bits) - 1
        n = len(levels[stage])
        for i in reversed(range(n)):
            copies[i] = links.send(now[n + i], parts[stage].at[i], (flip(c, bits[stage], s), s))
    yield
    while stage >= 0:
        n = len(levels[stage])
        got = parts[stage]
        after = {}
        for i in reversed(range(n)):
            copies[i].wait_recv()
            add_into(got.at[i], now[i])
            if stage > 0 and i >= n // 2:
                after[i - n // 2] = links.send(
                    got.at[i], parts[stage - 1].at[i - n // 2], (flip(c, bits[stage - 1], s), s)
                )
            yield
        now = [got.at[i] for i in range(n)]
        copies = after
        stage -= 1
    return now[0]


def reduce_blocks(env, inp, out, parts, sems, own=None):
    links = Links(sems, env)
    total = yield from reduce(env, links, inp, parts, env.lay.tp_order, env.lay.tp_index, core=True, own=own)
    out[...] = total[...].astype(out.dtype)
    links.settle()
    yield


def reduce_columns(env, inp, out, parts, sems):
    lay = env.lay
    links = Links(sems, env)
    total = yield from reduce(env, links, inp, parts, lay.dp_order, lay.dp_index)
    local = links.local(total.at[env.t], out.at[env.s, env.t])
    copies = []
    for m in lay.tp_masks[1:]:
        there = flips(env.c, m, env.s)
        copies.append(links.send(total.at[lay.tp_index(there)], out.at[env.s, env.t], (there, env.s)))
    yield
    links.settle()
    for copy in copies:
        copy.wait_recv()
    copy = links.send(out.at[env.s], out.at[env.s], env.other())
    yield
    copy.wait_recv()
    links.settle()
    yield


def reduce_halves(env, inp, out, parts, sems):
    lay = env.lay
    links = Links(sems, env)
    total = yield from reduce(env, links, inp, parts, lay.dp_order, lay.dp_index)
    links.local(total, out.at[env.s])
    copy = links.send(total, out.at[env.s], env.other())
    yield
    copy.wait_recv()
    links.settle()
    yield


def reduce_all(env, inp, out, parts, sems):
    lay = env.lay
    links = Links(sems, env)
    n = len(lay.dp_bits) + 1
    total = yield from reduce(env, links, inp, parts[:n], lay.dp_order, lay.dp_index, core=True)
    total = yield from reduce(env, links, total, parts[n:], lay.tp_order, lay.tp_index)
    out[...] = total[...].astype(out.dtype)
    links.settle()
    yield


def own_head(env):
    h = (env.t * 2 + env.s) * HU + env.d
    return h, jnp.logical_and(env.d < HU, h < HEADS)


def wait_pieces(env, ref, count, send=None, recv=None):
    part = ref.at[pl.ds(0, count)]
    copy = pltpu.make_async_remote_copy(
        src_ref=part,
        dst_ref=part,
        send_sem=recv if send is None else send,
        recv_sem=send if recv is None else recv,
        device_id=env.other(),
        device_id_type=MESH,
    )
    if send is not None:
        copy.wait_send()
    if recv is not None:
        copy.wait_recv()


def tokens_to_heads(env, src, out, sems):
    send_sem, recv_sem, local_sem = sems[0].at[0], sems[1].at[0], sems[2].at[0]
    h, active = own_head(env)
    lay = env.lay
    place = env.s * lay.n_ctx + env.c

    def begin(i, carry):
        j = (env.rank + i) % HEADS
        rank = lay.head_rank(j)

        @pl.when(rank != env.rank)
        def _():
            pltpu.make_async_remote_copy(
                src_ref=src.at[j],
                dst_ref=out.at[place],
                send_sem=send_sem,
                recv_sem=recv_sem,
                device_id=(rank // 2, rank % 2),
                device_id_type=MESH,
            ).start()

        return carry

    lax.fori_loop(0, HEADS, begin, 0)
    yield

    @pl.when(active)
    def _():
        local = pltpu.make_async_copy(src.at[h], out.at[place], local_sem)
        local.start()
        local.wait()
        wait_pieces(env, out, env.n_dev - 1, recv=recv_sem)
        wait_pieces(env, src, HEADS - 1, send=send_sem)

    @pl.when(jnp.logical_not(active))
    def _():
        wait_pieces(env, src, HEADS, send=send_sem)


ANY = pl.BlockSpec(memory_space=pl.ANY)
VM = pl.BlockSpec(memory_space=pltpu.VMEM)


def struct(*shape, dtype=BF):
    return jax.ShapeDtypeStruct(shape, dtype)


def call(name, cid, body, args, in_specs, outs, out_specs, scratch):
    return pl.pallas_call(
        body,
        out_shape=outs,
        in_specs=in_specs,
        out_specs=out_specs,
        scratch_shapes=scratch,
        compiler_params=pltpu.CompilerParams(
            collective_id=cid, has_side_effects=True, vmem_limit_bytes=VMEM_LIMIT
        ),
        name=name,
    )(*args)


def dot(left, right, dims):
    return lax.dot_general(left, right, (dims, ((), ())), preferred_element_type=F32)


NN = ((1,), (0,))
NT = ((1,), (1,))
TN = ((0,), (0,))
SCALE = 1.0 / math.sqrt(HEAD_DIM)
TILE = 512


class Background:
    def __init__(self):
        self.active = []

    def add(self, generator):
        self.active.append(generator)

    def step(self, count=1):
        for _ in range(count):
            if not self.active:
                return
            g = self.active.pop(0)
            try:
                next(g)
                self.active.append(g)
            except StopIteration:
                pass

    def finish(self):
        while self.active:
            self.step()


def finish(generator):
    for _ in generator:
        pass


def group_to_heads(env, src, out, sems, q):
    send_sems, recv_sems, local_sems = sems
    lay = env.lay

    def copy(j, source, target):
        return pltpu.make_async_remote_copy(
            src_ref=src.at[q, j],
            dst_ref=out.at[q, source],
            send_sem=send_sems.at[q, j],
            recv_sem=recv_sems.at[q, source],
            device_id=(lay.compose(env.t, target), env.s),
            device_id_type=MESH,
        )

    for i in range(1, HU + 1):
        j = (env.d + i) % HU

        @pl.when(j != env.d)
        def _():
            copy(j, env.d, j).start()

    local = pltpu.make_async_copy(src.at[q, env.d % HU], out.at[q, env.d], local_sems.at[q])

    @pl.when(env.d < HU)
    def _():
        local.start()

    yield

    @pl.when(env.d < HU)
    def _():
        local.wait()
        for i in range(1, lay.n_dp):
            source = (env.d + i) % lay.n_dp
            copy(0, source, source).wait_recv()

    yield
    for j in range(HU):

        @pl.when(j != env.d)
        def _():
            copy(j, env.d, j).wait_send()


def heads_out(env, src, out, sems, q):
    send_sem, recv_sem = sems[0].at[q], sems[1].at[0]
    h, active = own_head(env)
    n_ctx = env.lay.n_ctx

    def copy(i):
        there = (env.c + i) % n_ctx
        return pltpu.make_async_remote_copy(
            src_ref=src.at[q, there],
            dst_ref=out.at[h],
            send_sem=send_sem,
            recv_sem=recv_sem,
            device_id=(there, q),
            device_id_type=MESH,
        )

    local = pltpu.make_async_copy(src.at[q, env.c], out.at[h], sems[2].at[q])
    mine = jnp.logical_and(active, env.s == q)
    theirs = jnp.logical_and(active, env.s != q)

    def begin(i, carry):
        copy(i).start()
        return carry

    @pl.when(mine)
    def _():
        local.start()

    @pl.when(theirs)
    def _():
        copy(0).start()

    @pl.when(active)
    def _():
        lax.fori_loop(1, n_ctx, begin, 0)

    yield

    @pl.when(mine)
    def _():
        local.wait()

    yield

    @pl.when(mine)
    def _():
        wait_pieces(env, src.at[q], n_ctx - 1, send=send_sem)

    @pl.when(theirs)
    def _():
        wait_pieces(env, src.at[q], n_ctx, send=send_sem)


def heads_in(env, out, sems):
    _, active = own_head(env)

    @pl.when(active)
    def _():
        wait_pieces(env, out, HEADS - 1, recv=sems[1].at[0])

    @pl.when(jnp.logical_not(active))
    def _():
        wait_pieces(env, out, HEADS, recv=sems[1].at[0])


def norm_stats(values):
    centre = values - jnp.mean(values, axis=-1, keepdims=True)
    spread = lax.rsqrt(jnp.mean(centre * centre, axis=-1, keepdims=True) + EPS)
    return centre * spread, spread


def attend_tile(i, tile, qt, keys, v_ref):
    def step(j, carry, masked):
        peak, total, acc = carry
        at = pl.ds(pl.multiple_of(j * tile, tile), tile)
        st = dot(keys[at, :], qt, NN) * (SCALE * LOG2E)
        if masked:
            row = lax.broadcasted_iota(jnp.int32, (tile, tile), 0)
            col = lax.broadcasted_iota(jnp.int32, (tile, tile), 1)
            st = jnp.where(row <= col, st, -1e30)
        new = jnp.maximum(peak, jnp.max(st, axis=0, keepdims=True))
        p = jnp.exp2(st - new)
        shrink = jnp.exp2(peak - new)
        total = total * shrink + jnp.sum(p, axis=0, keepdims=True)
        acc = acc * shrink + dot(v_ref[:, at], p.astype(BF), NN)
        return new, total, acc

    start = (
        jnp.full((1, tile), -1e30, F32),
        jnp.zeros((1, tile), F32),
        jnp.zeros((HEAD_DIM, tile), F32),
    )
    carry = start
    if i > 0:
        carry = lax.fori_loop(0, i, functools.partial(step, masked=False), carry)
    peak, total, acc = step(i, carry, True)
    return acc / total, peak + jnp.log2(total)


def forward(lay, x, gains, biases, fc_bias, qkv, fc, out, proj, dy):
    n_ctx, n_dp = lay.n_ctx, lay.n_dp
    n_dev = 2 * n_ctx
    k = len(lay.dp_bits)
    T = x.shape[1]
    R, FB = D // n_ctx, FF // n_ctx
    FH = FB // 2
    W = HU * HEAD_DIM
    G = 4 * T
    length = n_ctx * T
    tile = min(TILE, length)
    n_tiles = length // tile
    half = D // 2
    wide = UNITS * W

    def natural(c):
        return c

    def body(*refs):
        (x_r, gains_r, biases_r, fcb_r, qkv_r, fc_r, out_r, proj_r, dy_r) = refs[:9]
        (h1_o, wq_o, heads_o, o_o, pj_o, h2_o, fc_o, out_o, outx_o, dy_o, lse_o, ob_o, x1_o, shift_o, par_o) = refs[9:24]
        (
            pack, small, qkv_x, fc_x, qkv_s, fc_s, out_s, wq_b, wq_v, x_v, h1_v, par_w,
            parts, mine, keys, heads_v, o_v, o_low, ob_b, proj_b, pj_v, h2_s, x_s, dy_s, h1_t,
        ) = refs[24:49]
        sems = refs[49:]
        groups = [sems[3 * i : 3 * i + 3] for i in range(len(sems) // 3)]
        env = Env(lay)
        s = env.s

        hail_all(env)
        x_s[...] = x_r[...].T
        pack[...] = jnp.zeros_like(pack)
        pack[0:1, :R] = gains_r[...].astype(F32)
        pack[1:4, :R] = biases_r[...].astype(F32)
        row = fcb_r[...].astype(F32).reshape(1, FH)
        pack[4:5, : FH // 2] = row[:, : FH // 2]
        pack[5:6, : FH // 2] = row[:, FH // 2 :]
        for h in range(2):
            out_s[h] = out_r[h * FH : (h + 1) * FH, :]
        par_w[...] = jnp.zeros_like(par_w)
        meet_all(env)
        links = Links(groups[0], env)
        crossing = [links.send(a, b, env.other()) for a, b in ((qkv_r, qkv_x), (fc_r, fc_x))]
        params = gather_small(env, pack, small, groups[1])
        next(params)

        def fill_qkv(a, b, side):
            q = a[:, :D]
            keys_all = jnp.concatenate([a[:, D:], b[:, : D // 2]], axis=1)
            v = b[:, D // 2 :]
            for u in range(4):
                first = (2 * u + side) * W
                width = max(0, min(W, D - first))
                for n, part in enumerate((q, keys_all, v)):
                    if width < W:
                        qkv_s[u, :, n * W : (n + 1) * W] = jnp.zeros((R, W), BF)
                    if width > 0:
                        qkv_s[u, :, n * W : n * W + width] = part[:, first : first + width]

        def fill_fc(a, b, side):
            for u in range(4):
                for d in range(n_dp):
                    first = lay.compose(u, d) * FB + side * FH
                    source, first = (a, first) if first < FF // 2 else (b, first - FF // 2)
                    fc_s[u, :, d * FH : (d + 1) * FH] = source[:, first : first + FH]

        crossing[0].wait_recv()
        by_side(s, lambda side: fill_qkv(*((qkv_r, qkv_x) if side == 0 else (qkv_x, qkv_r)), side))
        steps(params, 1)
        weights = gather_columns(env, qkv_s, wq_b, groups[2])
        next(weights)
        rows_x = gather_blocks(env, x_s, x_v, groups[3], lay.tp_order, lay.tp_index, core=True)
        next(rows_x)
        proj = gather_all(env, proj_r, proj_b, groups[7])
        next(proj)
        out_all = gather_blocks(env, out_s, out_o, groups[8], lay.dp_order, lay.dp_index, half=outx_o)
        next(out_all)
        dy_s[...] = dy_r[...].T
        crossing[1].wait_recv()
        by_side(s, lambda side: fill_fc(*((fc_r, fc_x) if side == 0 else (fc_x, fc_r)), side))
        steps(weights, 1)
        steps(params, 1)
        steps(rows_x, 1)
        steps(proj, 1)
        steps(weights, 1)
        steps(out_all, 1)
        finish(params)
        for f in range(2):
            par_o[f] = jnp.concatenate(
                [small[f, lay.dp_index(c), lay.tp_index(c)][:, :R] for c in range(n_ctx)], axis=1
            )
        par_w[:, :D] = par_o[0]
        shift_parts = []
        for d in range(n_dp):
            block = small[s, d, env.t]
            shift_parts += [block[4:5, : FH // 2], block[5:6, : FH // 2]]
        shift_o[...] = jnp.concatenate(shift_parts, axis=1)
        finish(rows_x)

        @pl.loop(0, 8)
        def _(i):
            hat, _ = norm_stats(x_v[i // 4, i % 4].astype(F32))
            low = (hat * par_o[0, 0:1, :] + par_o[0, 1:2, :]).astype(BF)
            h1_v[i // 4, i % 4] = low
            h1_t[:, pl.ds(pl.multiple_of(i * T, T), T)] = low.T

        finish(weights)
        for c in range(n_ctx):
            wq_v[c * R : (c + 1) * R, :] = wq_b[lay.dp_index(c), lay.tp_index(c)]
        leave = Links((None, None, groups[11][2]))
        leave.local(h1_t, h1_o)
        leave.local(wq_v, wq_o)
        unit = 2 * env.t + s
        cols = pl.ds(pl.multiple_of(unit * W, W), W)
        shift = jnp.concatenate(
            [par_w[2:3, cols], jnp.zeros((1, W), F32), par_w[3:4, cols]], axis=1
        )
        moving = []
        for q in range(2):
            rows = h1_v[q].reshape(G, D)
            made = (dot(rows, wq_v[...], NN) + shift).astype(BF).T
            for n in range(3):
                for j in range(HU):
                    first = n * W + j * HEAD_DIM
                    parts[q, j, n * HEAD_DIM : (n + 1) * HEAD_DIM, :] = made[first : first + HEAD_DIM]
            g = group_to_heads(env, parts, mine, groups[6], q)
            next(g)
            moving.append(g)
        steps(proj, 3)
        fc_all = gather_columns(env, fc_s, fc_o, groups[5])
        next(fc_all)
        dy_all = gather_blocks(env, dy_s, dy_o, groups[4], lay.tp_order, lay.tp_index, core=True)
        next(dy_all)
        leaving = []
        for q in range(2):
            next(moving[q])
            for c in range(n_ctx):
                tc, dc = lay.tp_index(c), lay.dp_index(c)
                for n in range(3):
                    heads_v[n, q, :, c * T : (c + 1) * T] = mine[
                        q, dc, n * HEAD_DIM : (n + 1) * HEAD_DIM, tc * T : (tc + 1) * T
                    ]
            keys[...] = heads_v[1, q].T
            for i in range(n_tiles):
                at = slice(i * tile, (i + 1) * tile)
                o, lse = attend_tile(i, tile, heads_v[0, q, :, at], keys, heads_v.at[2, q])
                o_v[q, :, at] = o
                lse_o[q, :, at] = lse
                low = o.astype(BF)
                for b in range(tile // T):
                    o_low[q, i * (tile // T) + b] = low[:, b * T : (b + 1) * T]
                if i == n_tiles - 1:
                    steps(proj, 1 if q == 0 else n_dp // 2)
            g = heads_out(env, o_low, ob_b, groups[9], q)
            next(g)
            leaving.append(g)
        leave.local(heads_v, heads_o)
        leave.local(o_v, o_o)
        finish(proj)
        for n in range(2):
            for c in range(n_ctx):
                pj_v[n, c * R : (c + 1) * R, :] = proj_b[n, lay.dp_index(c), lay.tp_index(c)]
        leave.local(pj_v, pj_o)
        for g in leaving:
            next(g)
        heads_in(env, ob_b, groups[9])
        ob_o[...] = ob_b[...].reshape(D, T).T
        branch = jnp.concatenate([dot(ob_o[...], pj_v[n], NN) for n in range(2)], axis=1)
        x1 = x_s[...].astype(F32) + branch + par_o[1, 1:2, :]
        x1_o[...] = x1
        hat, _ = norm_stats(x1)
        h2_s[...] = (hat * par_o[1, 0:1, :] + par_o[1, 2:3, :]).astype(BF)
        rows_h2 = gather_blocks(env, h2_s, h2_o, groups[10], lay.tp_order, lay.tp_index, core=True)
        next(rows_h2)
        steps(fc_all, 1)
        steps(dy_all, 1)
        steps(rows_h2, 1)
        steps(fc_all, 1)
        finish(out_all)
        finish(fc_all)
        finish(dy_all)
        finish(rows_h2)
        for g in moving + leaving:
            finish(g)
        leave.settle()
        env.drain()

    outs = [
        struct(D, 2 * G),
        struct(D, 3 * W),
        struct(3, 2, HEAD_DIM, length),
        struct(2, HEAD_DIM, length, dtype=F32),
        struct(2, D, half),
        struct(2, 4, T, D),
        struct(n_dp, 4, R, n_dp * FH),
        struct(n_dp, 2, FH, half),
        struct(n_dp, FH, half),
        struct(2, 4, T, D),
        struct(2, 1, length, dtype=F32),
        struct(T, D),
        struct(T, D, dtype=F32),
        struct(1, n_dp * FH, dtype=F32),
        struct(2, 8, D, dtype=F32),
    ]
    out_specs = [ANY] * 10 + [VM] * 5
    scratch = [
        pltpu.VMEM((8, 128), F32),
        pltpu.VMEM((2, n_dp, 4, 8, 128), F32),
        pltpu.VMEM(qkv.shape, BF),
        pltpu.VMEM(fc.shape, BF),
        pltpu.VMEM((4, R, 3 * W), BF),
        pltpu.VMEM((4, R, n_dp * FH), BF),
        pltpu.VMEM((2, FH, half), BF),
        pltpu.VMEM((n_dp, 4, R, 3 * W), BF),
        pltpu.VMEM((D, 3 * W), BF),
        pltpu.VMEM((2, 4, T, D), BF),
        pltpu.VMEM((2, 4, T, D), BF),
        pltpu.VMEM((8, wide), F32),
        pltpu.VMEM((2, HU, QKV, G), BF),
        pltpu.VMEM((2, n_dp, QKV, G), BF),
        pltpu.VMEM((length, HEAD_DIM), BF),
        pltpu.VMEM((3, 2, HEAD_DIM, length), BF),
        pltpu.VMEM((2, HEAD_DIM, length), F32),
        pltpu.VMEM((2, n_ctx, HEAD_DIM, T), BF),
        pltpu.VMEM((HEADS, HEAD_DIM, T), BF),
        pltpu.VMEM((2, n_dp, 4, R, half), BF),
        pltpu.VMEM((2, D, half), BF),
        pltpu.VMEM((T, D), BF),
        pltpu.VMEM((T, D), BF),
        pltpu.VMEM((T, D), BF),
        pltpu.VMEM((D, 2 * G), BF),
    ]
    DMA = pltpu.SemaphoreType.DMA
    columns = sem_shapes(3 + gather_sends(k, False))
    blocks = sem_shapes(gather_sends(2, True))
    every = sem_shapes(gather_sends(2, False) + gather_sends(k, True))
    scratch += sem_shapes(2) + sem_shapes(3 + n_dp) + columns + blocks * 2 + columns
    scratch += [DMA((2, HU)), DMA((2, n_dp)), DMA((2,))]
    scratch += every
    scratch += sem_shapes(gather_sends(k, True))
    scratch += [DMA((2,)), DMA((1,)), DMA((2,))]
    scratch += blocks
    scratch += sem_shapes(1, 5)
    in_specs = [VM] * 7 + [ANY, VM]
    return call(
        "forward", 0, body, (x, gains, biases, fc_bias, qkv, fc, out, proj, dy), in_specs, outs, out_specs, scratch
    )


def steps(generator, count):
    for _ in range(count):
        next(generator, None)


def by_side(s, f):
    for side in range(2):

        @pl.when(s == side)
        def _():
            f(side)


def spread_rows(made, first, size, block):
    end = first + made.shape[0]
    at = first
    while at < end:
        i = at // size
        stop = min(end, (i + 1) * size)
        block(i)[at - i * size : stop - i * size] = made[at - first : stop - first]
        at = stop


def middle(lay, x, h2, dy_all, fc, out, out_x, shift, x1, dy, pj, par):
    n_ctx, n_dp = lay.n_ctx, lay.n_dp
    n_dev = 2 * n_ctx
    k = len(lay.dp_bits)
    T = x.shape[1]
    R, FB = D // n_ctx, FF // n_ctx
    FH = FB // 2
    U = n_dp * FH
    G = 4 * T
    half = D // 2
    chunk = 4 * T

    def natural(c):
        return c

    def body(*refs):
        (h2_r, dya_r, fc_r, out_r, outx_r, pj_r, shift_r, x1_r, dy_r, par_r) = refs[:10]
        (mix_o, dob_o, fc_o, out_o, dx1_o, vec_o, fcb_o) = refs[10:17]
        (h2_v, dy_v, fc_b, fc_w, out_b, out_w, out_g, pj_v, gb_v, du_v, back_p, dh2_v, dob_s) = refs[17:30]
        rest = refs[30:]
        spans, first = [], 0
        for n in (3, k, k):
            spans.append((rest[first : first + n], rest[first + n : first + n + 3]))
            first += n + 3
        sems = rest[first:]
        env = Env(lay)
        s = env.s
        hail_all(env)
        loads = Links((None, None, sems[3]))
        load_fc = loads.local(fc_r, fc_b)
        load_h2 = loads.local(h2_r, h2_v)
        load_out = [loads.local(out_r.at[:, s], out_b.at[0]), loads.local(outx_r, out_b.at[1])]
        load_dy = loads.local(dya_r, dy_v)
        load_fc.wait()
        for c in range(n_ctx):
            fc_w[c * R : (c + 1) * R, :] = fc_b[lay.dp_index(c), lay.tp_index(c)]
        for copy in load_out:
            copy.wait()

        def fill_out(side):
            for d in range(n_dp):
                at = slice(d * FH, (d + 1) * FH)
                pair = (out_b[0, d], out_b[1, d]) if side == 0 else (out_b[1, d], out_b[0, d])
                out_w[at, :] = jnp.concatenate(pair, axis=1)

        by_side(s, fill_out)
        load_h2.wait()
        load_dy.wait()

        def forth_and_back(q):
            @pl.loop(0, G // chunk)
            def _(i):
                rows = h2_v[q, pl.ds(4 * i, 4)].reshape(chunk, D)
                u = dot(rows, fc_w[...], NN) + shift_r[...]
                square = u * u
                th = jnp.tanh(math.sqrt(2 / math.pi) * (u + 0.044715 * square * u))
                up = 0.5 * (1.0 + th)
                at = pl.ds(pl.multiple_of(i * chunk, chunk), chunk)
                gb_v[q, at, :] = (u * up).astype(BF)
                slope = up + (0.5 * math.sqrt(2 / math.pi)) * u * (1.0 - th * th) * (
                    1.0 + (3 * 0.044715) * square
                )
                dact = dot(dy_v[q, pl.ds(4 * i, 4)].reshape(chunk, D), out_w[...], NT)
                du = (dact * slope).astype(BF)
                du_v[q, at, :] = du
                back_p[q, pl.ds(4 * i, 4)] = dot(du, fc_w[...], NT).astype(BF).reshape(4, T, D)

        load_pj = loads.local(pj_r, pj_v)
        forth_and_back(1 - s)
        meet_all(env)
        rows = reduce_blocks(env, back_p, dh2_v, *spans[0])
        next(rows)
        forth_and_back(s)
        steps(rows, 4)
        for first in range(0, D, TILE):
            left = h2_v[:, :, :, first : min(D, first + TILE)].reshape(2 * G, -1)
            made = dot(left, du_v[...].reshape(2 * G, U), TN).astype(BF)
            spread_rows(made, first, R, lambda c: fc_b.at[lay.dp_index(c), lay.tp_index(c)])
        fc_sum = reduce_columns(env, fc_b, fc_o, *spans[1])
        next(fc_sum)
        for first in range(0, U, TILE):
            left = gb_v[:, :, first : min(U, first + TILE)].reshape(2 * G, -1)
            made = dot(left, dy_v[...].reshape(2 * G, D), TN).astype(BF)
            spread_rows(made, first, FH, lambda d: out_g.at[d])
        out_sum = reduce_halves(env, out_g, out_o, *spans[2])
        fcb_o[...] = jnp.sum(du_v[...].reshape(2 * G, U).astype(F32), axis=0, keepdims=True)
        x1 = x1_r[...]
        hat, spread = norm_stats(x1)
        dy_own = dy_r[...].T.astype(F32)
        vec_o[...] = jnp.zeros_like(vec_o)
        vec_o[3:4, :] = jnp.sum(dy_own, axis=0, keepdims=True)
        for q in range(2):

            @pl.loop(0, G // chunk)
            def _(i):
                at = pl.ds(pl.multiple_of(i * chunk, chunk), chunk)
                part = dot(gb_v[q, at, :], out_w[...], NN).astype(BF)
                h2_v[q, pl.ds(4 * i, 4)] = part.reshape(4, T, D)

        leave = loads.local(h2_v, mix_o)
        steps(rows, 1)
        steps(fc_sum, n_dp // 2)
        next(out_sum)
        finish(rows)
        dh2 = dh2_v[...].astype(F32)
        scaled = dh2 * par_r[1, 0:1, :]
        dx1 = dy_own + spread * (
            scaled
            - jnp.mean(scaled, axis=-1, keepdims=True)
            - hat * jnp.mean(scaled * hat, axis=-1, keepdims=True)
        )
        dx1_o[...] = dx1
        da = dx1.astype(BF)
        load_pj.wait()
        dob = dot(pj_v[0], da[:, :half], NT) + dot(pj_v[1], da[:, half:], NT)
        dob_s[...] = dob.astype(BF).reshape(HEADS, HEAD_DIM, T)
        heads = tokens_to_heads(env, dob_s, dob_o, sems[0:3])
        next(heads)
        vec_o[0:1, :] = jnp.sum(dh2 * hat, axis=0, keepdims=True)
        vec_o[1:2, :] = jnp.sum(da.astype(F32), axis=0, keepdims=True)
        vec_o[2:3, :] = jnp.sum(dh2, axis=0, keepdims=True)
        steps(fc_sum, n_dp // 4)
        run([fc_sum, out_sum])
        finish(heads)
        leave.wait()
        env.drain()

    outs = [
        struct(2, 4, T, D),
        struct(n_dev, HEAD_DIM, T),
        struct(2, 4, R, U),
        struct(2, FH, D),
        struct(T, D, dtype=F32),
        struct(8, D, dtype=F32),
        struct(1, U, dtype=F32),
    ]
    scratch = [
        pltpu.VMEM((2, 4, T, D), BF),
        pltpu.VMEM((2, 4, T, D), BF),
        pltpu.VMEM((n_dp, 4, R, U), BF),
        pltpu.VMEM((D, U), BF),
        pltpu.VMEM((2, n_dp, FH, half), BF),
        pltpu.VMEM((U, D), BF),
        pltpu.VMEM((n_dp, FH, D), BF),
        pltpu.VMEM((2, D, half), BF),
        pltpu.VMEM((2, G, U), BF),
        pltpu.VMEM((2, G, U), BF),
        pltpu.VMEM((2, 4, T, D), BF),
        pltpu.VMEM((T, D), BF),
        pltpu.VMEM((HEADS, HEAD_DIM, T), BF),
    ]
    scratch += reduce_scratch(2, True, (T, D)) + sem_shapes(reduce_sends(2, True))
    scratch += reduce_scratch(k, False, (4, R, U)) + sem_shapes(reduce_sends(k, False) + 4)
    scratch += reduce_scratch(k, False, (FH, D)) + sem_shapes(reduce_sends(k, False) + 1)
    DMA = pltpu.SemaphoreType.DMA
    scratch += sem_shapes(1) + [DMA((7,))]
    args = (h2, dy_all, fc, out, out_x, pj, shift, x1, dy, par)
    out_specs = [ANY] * 4 + [VM] * 3
    return call("middle", 1, body, args, [ANY] * 6 + [VM] * 4, outs, out_specs, scratch)


def heads_to_group(env, src, out, sems, q):
    send_sems, recv_sems, local_sems = sems
    lay = env.lay
    held = q % src.shape[0]

    def copy(there, j, target):
        return pltpu.make_async_remote_copy(
            src_ref=src.at[held, there],
            dst_ref=out.at[q, j],
            send_sem=send_sems.at[q, there],
            recv_sem=recv_sems.at[q, j],
            device_id=(lay.compose(env.t, target), env.s),
            device_id_type=MESH,
        )

    local = pltpu.make_async_copy(src.at[held, env.d], out.at[q, env.d % HU], local_sems.at[q])

    @pl.when(env.d < HU)
    def _():
        for i in range(1, lay.n_dp):
            there = (env.d + i) % lay.n_dp
            copy(there, env.d, there).start()
        local.start()

    yield

    @pl.when(env.d < HU)
    def _():
        local.wait()

    for j in range(HU):

        @pl.when(j != env.d)
        def _():
            copy(0, j, j).wait_recv()

    yield

    @pl.when(env.d < HU)
    def _():
        for i in range(1, lay.n_dp):
            there = (env.d + i) % lay.n_dp
            copy(there, env.d, there).wait_send()


def backward(lay, x, heads, o, lse, dob, wq, h1, ob, vec, fcb, dx1, par, mix):
    n_ctx, n_dp = lay.n_ctx, lay.n_dp
    n_dev = 2 * n_ctx
    k = len(lay.dp_bits)
    T = x.shape[1]
    R, FB = D // n_ctx, FF // n_ctx
    FH = FB // 2
    W = HU * HEAD_DIM
    G = 4 * T
    half = D // 2
    length = n_ctx * T
    tile = TILE if length <= 4 * TILE else TILE // 2
    n_tiles = length // tile
    wide = UNITS * W

    def natural(c):
        return c

    def body(*refs):
        (x_r, heads_r, o_r, lse_r, dob_r, wqh_r, h1h_r, ob_r, vec_r, fcb_r, dx1_r, par_r, mix_r) = refs[:13]
        (grad_o, q_v, proj_o, small_o, mix_s) = refs[13:18]
        (
            heads_v, o_v, dob_n, qs, dobs, delta, dq_acc, parts, land, dqkv, dh1_p, dh1_v, q_g, wide_v,
            small_s, pg, wq_r, h1_r,
        ) = refs[18:36]
        rest = refs[36:]
        spans, first = [], 0
        for n in (3, k, k + 3, 3, k + 3):
            spans.append((rest[first : first + n], rest[first + n : first + n + 3]))
            first += n + 3
        sems = rest[first:]
        env = Env(lay)
        s = env.s
        hail_near(env)
        early = Links((None, None, sems[4]))
        mix_v = dh1_p.at[0]
        load_mix = early.local(mix_r.at[s], mix_v)
        load_wq = early.local(wqh_r, wq_r)
        load_h1 = early.local(h1h_r, h1_r)
        for n in range(2):
            right = dx1_r[:, n * half : (n + 1) * half].astype(BF)
            for c in range(0, n_ctx, 4):
                made = dot(ob_r[:, c * R : (c + 4) * R], right, TN).astype(BF)
                for i in range(4):
                    pg[n, lay.dp_index(c + i), lay.tp_index(c + i)] = made[i * R : (i + 1) * R, :]
        small_s[...] = jnp.zeros_like(small_s)
        wide_v[...] = jnp.zeros_like(wide_v)
        meet_near(env)
        proj = reduce_all(env, pg, proj_o, *spans[2])
        next(proj)
        mixing = reduce_blocks(env, mix_r, mix_s, *spans[3], own=mix_v)
        next(mixing)
        load_mix.wait()
        moving = []
        _, active = own_head(env)

        def loads(q):
            copies = [pltpu.make_async_copy(heads_r.at[n, q], heads_v.at[n], sems[3].at[n]) for n in range(3)]
            copies.append(pltpu.make_async_copy(o_r.at[q], o_v, sems[3].at[3]))
            for c in range(n_ctx):
                there = dob_n.at[:, pl.ds(c * T, T)]
                copies.append(pltpu.make_async_copy(dob_r.at[q * n_ctx + c], there, sems[3].at[4 + c]))
            return copies

        for copy in loads(0):
            copy.start()
        steps(proj, n_dp)
        for q in range(2):
            for copy in loads(q):
                copy.wait()

            @pl.when(jnp.logical_not(active))
            def _():
                dob_n[...] = jnp.zeros_like(dob_n)

            qs[...] = heads_v[0].T
            dobs[...] = dob_n[...].T
            delta[...] = jnp.sum(dob_n[...].astype(F32) * o_v[...], axis=0, keepdims=True)
            dq_acc[...] = jnp.zeros_like(dq_acc)

            if q == 1 and parts.shape[0] == 1:
                finish(moving[0])

            def put(n, first, block):
                for b in range(block.shape[1] // T):
                    c = first // T + b
                    tc, dc = lay.tp_index(c), lay.dp_index(c)
                    parts[q % parts.shape[0], dc, n * HEAD_DIM : (n + 1) * HEAD_DIM, tc * T : (tc + 1) * T] = block[
                        :, b * T : (b + 1) * T
                    ]

            for j in range(n_tiles):
                here = slice(j * tile, (j + 1) * tile)
                kt = heads_v[1, :, here]
                keys = kt.T
                values = heads_v[2, :, here].T

                def step(i, carry, masked):
                    dk, dv = carry
                    at = pl.ds(pl.multiple_of(i * tile, tile), tile)
                    st = dot(keys, heads_v[0, :, at], NN) * (SCALE * LOG2E)
                    p = jnp.exp2(st - lse_r[q, :, at])
                    if masked:
                        row = lax.broadcasted_iota(jnp.int32, (tile, tile), 0)
                        col = lax.broadcasted_iota(jnp.int32, (tile, tile), 1)
                        p = jnp.where(row <= col, p, 0.0)
                    dp = dot(values, dob_n[:, at], NN)
                    ds = (p * (dp - delta[:, at])).astype(BF)
                    dv = dv + dot(p.astype(BF), dobs[at, :], NN)
                    dk = dk + dot(ds, qs[at, :], NN)
                    dq_acc[:, at] += dot(kt, ds, NN)
                    return dk, dv

                zero = jnp.zeros((tile, HEAD_DIM), F32)
                carry = step(j, (zero, zero), True)
                if j + 1 < n_tiles:
                    carry = lax.fori_loop(j + 1, n_tiles, functools.partial(step, masked=False), carry)
                put(1, j * tile, (carry[0] * SCALE).T.astype(BF))
                put(2, j * tile, carry[1].T.astype(BF))
                if q == 0 and j == 1:
                    steps(mixing, 4)
                if q == 0 and j == n_tiles - 1:
                    steps(proj, n_dp // 2)
                if q == 1 and j >= n_tiles - 2:
                    steps(mixing, 1)
            put(0, 0, (dq_acc[...] * SCALE).astype(BF))
            if q == 0:
                for copy in loads(1):
                    copy.start()
            g = heads_to_group(env, parts, land, sems[0:3], q)
            next(g)
            moving.append(g)
        steps(proj, n_dp // 4 + 1)
        load_wq.wait()
        load_h1.wait()
        for q in range(2):
            next(moving[q], None)
            rows = []
            for n in range(3):
                for j in range(HU):
                    rows.append(land[q, j, n * HEAD_DIM : (n + 1) * HEAD_DIM, :])
            dqkv[q] = jnp.concatenate(rows, axis=0).T
            dh1_p[q] = dot(dqkv[q], wq_r[...], NT).astype(BF).reshape(4, T, D)
        rows_h1 = reduce_blocks(env, dh1_p, dh1_v, *spans[0])
        next(rows_h1)
        sums = jnp.sum(dqkv[0].astype(F32), axis=0, keepdims=True) + jnp.sum(
            dqkv[1].astype(F32), axis=0, keepdims=True
        )
        for c in range(0, n_ctx, 4):
            at = slice(c * R, (c + 4) * R)
            made = dot(h1_r[at, :], dqkv[...].reshape(2 * G, 3 * W), NN)
            low = made.astype(BF)
            for i in range(4):
                q_g[lay.dp_index(c + i), lay.tp_index(c + i)] = low[i * R : (i + 1) * R, :]
            weight = wq_r[at, :].astype(F32)
            for n, product in enumerate((made * weight, weight * sums)):
                folded = product[:, :128]
                for lane in range(128, 3 * W, 128):
                    folded = folded + product[:, lane : lane + 128]
                wide_v[n : n + 1, at] = jnp.sum(folded.T, axis=0, keepdims=True)
            if c == n_ctx // 2:
                steps(rows_h1, 4)
        grads = reduce_columns(env, q_g, q_v, *spans[1])
        next(grads)
        unit = 2 * env.t + s
        cols = pl.ds(pl.multiple_of(unit * W, W), W)
        wide_v[2:3, cols] = sums[:, :W]
        wide_v[3:4, cols] = sums[:, 2 * W :]
        wide_v[0:1, :D] = (wide_v[0:1, :D] - par_r[0, 1:2, :] * wide_v[1:2, :D]) / par_r[0, 0:1, :]
        for c in range(n_ctx):
            small_s[0, lay.dp_index(c), lay.tp_index(c), 0:4, :R] = wide_v[0:4, c * R : (c + 1) * R]
            small_s[1, lay.dp_index(c), lay.tp_index(c), 0:4, :R] = vec_r[0:4, c * R : (c + 1) * R]
        for d in range(n_dp):
            for h in range(2):
                first = d * FH + h * (FH // 2)
                small_s[s, d, env.t, 4 + h : 5 + h, : FH // 2] = fcb_r[:, first : first + FH // 2]
        small = reduce_all(env, small_s, small_o, *spans[4])
        next(small)
        hat, spread = norm_stats(x_r[...].T.astype(F32))
        steps(rows_h1, 1)
        finish(mixing)
        steps(small, n_dp)
        steps(grads, n_dp // 2)
        steps(rows_h1, 1)
        steps(small, n_dp // 2)
        steps(grads, n_dp // 4)
        finish(rows_h1)
        dh1 = dh1_v[...].astype(F32)
        scaled = dh1 * par_r[0, 0:1, :]
        grad_o[...] = dx1_r[...] + spread * (
            scaled
            - jnp.mean(scaled, axis=-1, keepdims=True)
            - hat * jnp.mean(scaled * hat, axis=-1, keepdims=True)
        )
        finish(proj)
        finish(small)
        finish(grads)
        for g in moving:
            finish(g)
        env.drain()

    outs = [
        struct(T, D, dtype=F32),
        struct(2, 4, R, 3 * W),
        struct(R, half),
        struct(8, 128, dtype=F32),
        struct(T, D),
    ]
    scratch = [
        pltpu.VMEM((3, HEAD_DIM, length), BF),
        pltpu.VMEM((HEAD_DIM, length), F32),
        pltpu.VMEM((HEAD_DIM, length), BF),
        pltpu.VMEM((length, HEAD_DIM), BF),
        pltpu.VMEM((length, HEAD_DIM), BF),
        pltpu.VMEM((1, length), F32),
        pltpu.VMEM((HEAD_DIM, length), F32),
        pltpu.VMEM((2 if n_ctx <= 16 else 1, n_dp, QKV, G), BF),
        pltpu.VMEM((2, HU, QKV, G), BF),
        pltpu.VMEM((2, G, 3 * W), BF),
        pltpu.VMEM((2, 4, T, D), BF),
        pltpu.VMEM((T, D), BF),
        pltpu.VMEM((n_dp, 4, R, 3 * W), BF),
        pltpu.VMEM((8, wide), F32),
        pltpu.VMEM((2, n_dp, 4, 8, 128), F32),
        pltpu.VMEM((2, n_dp, 4, R, half), BF),
        pltpu.VMEM((D, 3 * W), BF),
        pltpu.VMEM((D, 2 * G), BF),
    ]
    blocks = reduce_scratch(2, True, (T, D)) + sem_shapes(reduce_sends(2, True))
    scratch += blocks
    scratch += reduce_scratch(k, False, (4, R, 3 * W)) + sem_shapes(reduce_sends(k, False) + 4)
    scratch += reduce_scratch(k, True, (4, R, half)) + reduce_scratch(2, False, (R, half))
    scratch += sem_shapes(reduce_sends(k, True) + reduce_sends(2, False))
    scratch += blocks
    scratch += reduce_scratch(k, True, (4, 8, 128), F32) + reduce_scratch(2, False, (8, 128), F32)
    scratch += sem_shapes(reduce_sends(k, True) + reduce_sends(2, False))
    DMA = pltpu.SemaphoreType.DMA
    scratch += [DMA((2, n_dp)), DMA((2, HU)), DMA((2,)), DMA((4 + n_ctx,)), DMA((3,))]
    args = (x, heads, o, lse, dob, wq, h1, ob, vec, fcb, dx1, par, mix)
    in_specs = [VM, ANY, ANY, VM, ANY, ANY, ANY] + [VM] * 5 + [ANY]
    return call("backward", 2, body, args, in_specs, outs, [VM, ANY, VM, VM, VM], scratch)


def assemble(lay, q, fc, out, proj, grad, mix, x1, par, small):
    n_ctx, n_dp = lay.n_ctx, lay.n_dp
    T = grad.shape[0]
    R, FB = D // n_ctx, FF // n_ctx
    FH = FB // 2
    W = HU * HEAD_DIM
    half = D // 2

    def body(*refs):
        (q_r, fc_r, out_r, proj_r, grad_r, mix_r, x1_r, par_r, small_r) = refs[:9]
        (mixed_o, grad_o, qkv_o, proj_o, fc_o, out_o, gains_o, biases_o, fcb_o) = refs[9:]
        mixed_o[...] = (x1_r[...] + mix_r[...].astype(F32) + par_r[1, 3:4, :]).astype(BF).T
        grad_o[...] = grad_r[...].T
        proj_o[...] = proj_r[...].astype(F32)
        gains_o[...] = small_r[0:1, :R]
        biases_o[...] = small_r[1:4, :R]
        row = jnp.concatenate([small_r[4:5, : FH // 2], small_r[5:6, : FH // 2]], axis=1)
        fcb_o[...] = row.reshape(FH)

        def last(side):
            thirds = []
            for n in range(3):
                pieces = [q_r[h, u][:, n * W : (n + 1) * W] for u in range(4) for h in range(2)]
                thirds.append(jnp.concatenate(pieces, axis=1)[:, :D])
            whole = jnp.concatenate(thirds, axis=1)
            qkv_o[...] = whole[:, side * (3 * half) : (side + 1) * (3 * half)].astype(F32)
            pieces = []
            for c in range(n_ctx // 2 * side, n_ctx // 2 * (side + 1)):
                for h in range(2):
                    first = lay.dp_index(c) * FH
                    pieces.append(fc_r[h, lay.tp_index(c)][:, first : first + FH])
            fc_o[...] = jnp.concatenate(pieces, axis=1).astype(F32)
            out_o[...] = jnp.concatenate(
                [out_r[h][:, side * half : (side + 1) * half] for h in range(2)], axis=0
            ).astype(F32)

        by_side(lax.axis_index("fsdp"), last)

    outs = [
        struct(D, T),
        struct(D, T, dtype=F32),
        struct(R, 3 * half, dtype=F32),
        struct(R, half, dtype=F32),
        struct(R, FF // 2, dtype=F32),
        struct(FB, half, dtype=F32),
        struct(1, R, dtype=F32),
        struct(3, R, dtype=F32),
        struct(FH, dtype=F32),
    ]
    return pl.pallas_call(
        body,
        out_shape=outs,
        in_specs=[VM] * 9,
        out_specs=[VM] * 9,
        compiler_params=pltpu.CompilerParams(vmem_limit_bytes=VMEM_LIMIT),
        name="assemble",
    )(q, fc, out, proj, grad, mix, x1, par, small)


def shards(lay, tokens, qkv_weight, proj_weight, fc_weight, out_weight, gains, biases, fc_bias, cotangent):
    T = tokens.shape[1]
    R = D // lay.n_ctx
    FH = FF // lay.n_ctx // 2
    x = jnp.transpose(tokens, (0, 2, 1)).reshape(D, T)
    dy = jnp.transpose(cotangent, (0, 2, 1)).reshape(D, T)
    (h1, wq, heads, o, pj, h2, fc, out, out_x, dy_all, lse, ob, x1, shift, par) = forward(
        lay, x, gains, biases, fc_bias, qkv_weight, fc_weight, out_weight, proj_weight, dy
    )
    mix, dob, fc_sum, out_sum, dx1, vec, fcb = middle(
        lay, x, h2, dy_all, fc, out, out_x, shift, x1, dy, pj, par
    )
    grad, q_sum, proj_sum, small, mix_sum = backward(
        lay, x, heads, o, lse, dob, wq, h1, ob, vec, fcb, dx1, par, mix
    )
    (mixed, grad, qkv_grad, proj_grad, fc_grad, out_grad, gains_grad, biases_grad, fc_bias_grad) = assemble(
        lay, q_sum, fc_sum, out_sum, proj_sum, grad, mix_sum, x1, par, small
    )
    return (
        jnp.transpose(mixed.reshape(1, D, T), (0, 2, 1)),
        jnp.transpose(grad.reshape(1, D, T), (0, 2, 1)),
        qkv_grad,
        proj_grad,
        fc_grad,
        out_grad,
        gains_grad,
        biases_grad,
        fc_bias_grad,
    )


def solution(mesh):
    lay = Layout(mesh.shape["ctx"])
    in_specs = (
        P("fsdp", "ctx", None),
        P("ctx", "fsdp"),
        P("ctx", "fsdp"),
        P("ctx", "fsdp"),
        P("ctx", "fsdp"),
        P("fsdp", "ctx"),
        P("fsdp", "ctx"),
        P(("ctx", "fsdp")),
        P("fsdp", "ctx", None),
    )
    out_specs = (
        P("fsdp", "ctx", None),
        P("fsdp", "ctx", None),
        P("ctx", "fsdp"),
        P("ctx", "fsdp"),
        P("ctx", "fsdp"),
        P("ctx", "fsdp"),
        P("fsdp", "ctx"),
        P("fsdp", "ctx"),
        P(("ctx", "fsdp")),
    )
    return jax.shard_map(
        functools.partial(shards, lay), mesh=mesh, in_specs=in_specs, out_specs=out_specs, check_vma=False
    )
```
